32 devices in a mesh: groups: 2 (over x), blk: 8 (over z, y), sub: 2 (over core).
Axes of the slice: x: 2, y: 2, z: 4, core: 2. Of those that a mesh axis runs over, the one named last changes fastest.
Arguments:
- embeddings: bfloat16 [16384, 512], P(('groups', 'blk'), 'sub'), parts along dimension 0, may hold values from -60 to 60
- vectors: bfloat16 [32, 16384], P('sub', ('groups', 'blk')), parts along dimension 1, may hold values from -6 to 6
- boxes: int32 [4, 16384], P(None, ('groups', 'blk')), parts along dimension 1, may hold values from 0 to 1023
- spans: int32 [2, 16384], P(None, ('groups', 'blk')), parts along dimension 1, may hold values from 0 to 17999
- camera: int32 [16384], P(('groups', 'blk')), parts along dimension 0, may hold values from 0 to 7
Outputs:
- basis: float32 [32, 16384], P('sub', ('groups', 'blk')), parts along dimension 1
The draws below stay inside these ranges and needn't reach their ends.
There are 2 independent parts, one for each index of `groups`. The reference program is written for one: setup_inputs(seed, part) draws one part's arguments, and reference() takes and returns one part's arrays. A program takes and returns all parts, laid end to end along the dimension named above; each array names one. Nothing has to cross between parts.
Inputs may be any that keep to these rules, and one draw needn't show every extreme that they name: `boxes`: coordinates are whole pixels and may travel packed several to a word. `spans`: frame numbers are whole and may travel packed two to a word. `camera`: camera ids may travel packed several to a word.
All inputs are finite; a program needn't handle non-finite values.
Results may differ from the reference program's by a relative error of at most 0.0005.
Values may be sent and summed in bfloat16 or wider, within the bound.
No kernel may reach another device: no remote copies, remote signals or barrier semaphores. Data moves between devices by JAX's collectives and lax.ppermute only.
A program may use at most 64 MiB of HBM per device.

```python
import math
import jax
import jax.numpy as jnp
from jax import lax

EMB = 512
VECS = 32
TRACKS = 8192


def draw_embeddings(key, part):
    key = jax.random.fold_in(key, 11)
    key_ids, key_shared, key_family, key_protos, key_noise = jax.random.split(key, 5)
    identities = max(TRACKS // 8, 2)
    families = max(TRACKS // 64, 2)
    identity = jax.random.randint(key_ids, (TRACKS,), 0, identities)
    family = identity % families
    shared = jax.random.normal(key_shared, (1, EMB), jnp.float32)
    family_protos = jax.random.normal(key_family, (families, EMB), jnp.float32)
    prototypes = jax.random.normal(key_protos, (identities, EMB), jnp.float32)
    family_rows = jnp.take(family_protos, family, axis=0)
    identity_rows = jnp.take(prototypes, identity, axis=0)
    centers = 0.548 * shared + 0.316 * family_rows + 0.671 * identity_rows
    noise = 0.387 * jax.random.normal(key_noise, (TRACKS, EMB), jnp.float32)
    return jnp.clip(centers + noise, -60.0, 60.0).astype(jnp.bfloat16)


def plant(entries, stream_key, least, largest):
    dims = entries.shape
    place = [jax.random.randint(jax.random.fold_in(stream_key, axis), (), 0, dims[axis]) for axis in range(len(dims))]
    entries = entries.at[tuple(place)].set(least)
    longest = dims.index(max(dims))
    place[longest] = (place[longest] + 1) % dims[longest]
    return entries.at[tuple(place)].set(largest)


def block_levels(key, dims, cuts, least, largest):
    factor_of = 1.0
    for dim, shards_of in cuts:
        steps = jax.random.uniform(jax.random.fold_in(jax.random.fold_in(key, 6), dim), (shards_of,), jnp.float32, least / len(cuts), largest / len(cuts))
        factor_of = factor_of * jnp.repeat(jnp.exp(steps), dims[dim] // shards_of).reshape((-1,) + (1,) * (len(dims) - 1 - dim))
    return factor_of


def centred(key, extent, deviation, limit, cuts=(), kind=jnp.bfloat16):
    drawn = jax.random.normal(key, extent, jnp.float32) * deviation
    if len(cuts) > 0:
        drawn = block_levels(key, extent, cuts, -0.22, 0.18) * drawn
    return jnp.clip(drawn, min=-limit, max=limit).astype(kind)


def setup_inputs(seed: int = 0, part: int = 0) -> dict:
    splits = jax.random.split(jax.random.key(seed), 6)
    part_splits = jax.random.split(jax.random.fold_in(splits[5], part), 6)
    embeddings = draw_embeddings(jax.random.fold_in(jax.random.fold_in(splits[5], part), 71), part)
    vectors = centred(part_splits[1], (VECS, TRACKS), 1.0, 6.0, ((0, 2), (1, 8)))
    boxes = plant(jax.random.randint(part_splits[2], (4, TRACKS), 0, 1024), jax.random.fold_in(part_splits[2], 1), 0, 1023).astype(jnp.int32)
    spans = plant(jax.random.randint(part_splits[3], (2, TRACKS), 0, 18000), jax.random.fold_in(part_splits[3], 1), 0, 17999).astype(jnp.int32)
    camera = plant(jax.random.randint(part_splits[4], (TRACKS,), 0, 8), jax.random.fold_in(part_splits[4], 1), 0, 7).astype(jnp.int32)
    return dict(embeddings=embeddings, vectors=vectors, boxes=boxes, spans=spans, camera=camera)


SHARPNESS = 10.0
IOU_FLOOR = 0.5
HORIZON = 2000.0
MARGIN = 8.0
EPSILON = 1e-06

def inverse_norms(values, axis_number):
    squares = lax.optimization_barrier(jnp.sum(jnp.square(values.astype(jnp.float32)), axis=axis_number))
    return lax.rsqrt(squares + EPSILON)

def track_fields(track_meta):
    left = jnp.minimum(track_meta[0], track_meta[2]).astype(jnp.float32)
    right = jnp.maximum(track_meta[0], track_meta[2]).astype(jnp.float32) + MARGIN
    bottom = jnp.minimum(track_meta[1], track_meta[3]).astype(jnp.float32)
    top = jnp.maximum(track_meta[1], track_meta[3]).astype(jnp.float32) + MARGIN
    first = jnp.minimum(track_meta[4], track_meta[5])
    last = jnp.maximum(track_meta[4], track_meta[5])
    return (left, right, bottom, top, first, last, track_meta[6], track_meta[7])

def affinity(row_emb, row_inv, row_meta, col_embt, col_inv, col_meta):
    products = jnp.dot(row_emb.astype(jnp.float32), col_embt.astype(jnp.float32), preferred_element_type=jnp.float32)
    cosine = products * row_inv[:, None] * col_inv[None, :]
    row_left, row_right, row_bottom, row_top, row_first, row_last, row_cam, row_ids = track_fields(row_meta)
    col_left, col_right, col_bottom, col_top, col_first, col_last, col_cam, col_ids = track_fields(col_meta)
    inter_width = jnp.maximum(jnp.minimum(row_right[:, None], col_right[None, :]) - jnp.maximum(row_left[:, None], col_left[None, :]), 0.0)
    inter_height = jnp.maximum(jnp.minimum(row_top[:, None], col_top[None, :]) - jnp.maximum(row_bottom[:, None], col_bottom[None, :]), 0.0)
    inter_area = inter_width * inter_height
    row_area = (row_right - row_left) * (row_top - row_bottom)
    col_area = (col_right - col_left) * (col_top - col_bottom)
    union_area = row_area[:, None] + col_area[None, :] - inter_area
    iou_value = inter_area / union_area
    gap_frames = jnp.maximum(col_first[None, :] - row_last[:, None], row_first[:, None] - col_last[None, :])
    temporal = jnp.exp(-jnp.maximum(gap_frames, 0).astype(jnp.float32) / HORIZON)
    barred = (row_cam[:, None] == col_cam[None, :]) & (gap_frames < 0) & (row_ids[:, None] != col_ids[None, :])
    weight = jnp.exp(SHARPNESS * (cosine - 1.0)) * (IOU_FLOOR + iou_value) * temporal
    return jnp.where(barred, 0.0, weight)

def reference(embeddings, vectors, boxes, spans, camera):
    track_ids = jnp.arange(TRACKS, dtype=jnp.int32)
    track_meta = jnp.concatenate([boxes, spans, camera[None, :], track_ids[None, :]], axis=0).astype(jnp.int32)
    inv_norms = inverse_norms(embeddings, 1)
    columns = embeddings.T
    block_rows = math.gcd(TRACKS, 512)
    block_total = TRACKS // block_rows

    def one_block(block_number):
        offset = (block_number * block_rows).astype(jnp.int32)
        row_emb = lax.dynamic_slice_in_dim(embeddings, offset, block_rows, 0)
        row_inv = lax.dynamic_slice_in_dim(inv_norms, offset, block_rows, 0)
        row_meta = lax.dynamic_slice_in_dim(track_meta, offset, block_rows, 1)
        block_tile = affinity(row_emb, row_inv, row_meta, columns, inv_norms, track_meta)
        degree = lax.optimization_barrier(jnp.sum(block_tile, axis=1))
        partial_image = lax.dot_general(vectors.astype(jnp.float32), block_tile.astype(jnp.bfloat16).astype(jnp.float32), (((1,), (1,)), ((), ())), preferred_element_type=jnp.float32)
        return (partial_image, degree)
    pieces, degrees = lax.map(one_block, jnp.arange(block_total, dtype=jnp.int32))
    image_sums = jnp.transpose(pieces, (1, 0, 2)).reshape(VECS, TRACKS)
    image = image_sums / degrees.reshape(TRACKS)[None, :]
    gram = jnp.dot(image.astype(jnp.float32), image.T.astype(jnp.float32), precision=lax.Precision.HIGHEST, preferred_element_type=jnp.float32) / TRACKS
    lower = jnp.linalg.cholesky(gram)
    return jax.scipy.linalg.solve_triangular(lower, image, lower=True)
```

```python
import functools
import math

import jax
import jax.numpy as jnp
from jax import lax
from jax.experimental import pallas as pl
from jax.experimental.pallas import tpu as pltpu
from jax.sharding import PartitionSpec as P

SHARPNESS = 10.0
HORIZON = 2000.0
MARGIN = 8.0
EPSILON = 1e-06

LOG2E = math.log2(math.e)
COS_SCALE = math.sqrt(SHARPNESS * LOG2E)
GAP_SCALE = LOG2E / HORIZON
BASE = SHARPNESS * LOG2E + 1.0
BARRED_BELOW = BASE - 0.5 * GAP_SCALE

FIELDS = 8
LEFT, RIGHT, BOTTOM, TOP, FIRST, LAST, CAMERA, NORM = range(FIELDS)
LANES = 128
CHUNK = 256
GROUP = 32
OUT_ROWS = 40
VMEM_LIMIT = 48 * 1024 * 1024

NT = (((1,), (1,)), ((), ()))
VMEM_SPEC = pl.BlockSpec(memory_space=pltpu.VMEM)


def params():
    return pltpu.CompilerParams(vmem_limit_bytes=VMEM_LIMIT)


def dot_nt(a, b, precision=None):
    return lax.dot_general(a, b, NT, precision=precision, preferred_element_type=jnp.float32)


def prepare_kernel(mine_ref, other_ref, vec_mine_ref, vec_other_ref, boxes_ref, spans_ref, camera_ref, out_ref):
    sub = lax.axis_index("sub")
    rows = mine_ref.shape[0]
    half_vecs = vec_mine_ref.shape[0]
    ones = jnp.ones((FIELDS, mine_ref.shape[1]), jnp.bfloat16)
    for start in range(0, rows, CHUNK):
        part = pl.ds(start, CHUNK)
        total = jnp.zeros((FIELDS, CHUNK), jnp.float32)
        for ref in (mine_ref, other_ref):
            values = ref[part, :].astype(jnp.float32)
            square = values * values
            high = square.astype(jnp.bfloat16)
            low = (square - high.astype(jnp.float32)).astype(jnp.bfloat16)
            total = total + dot_nt(ones, high) + dot_nt(ones, low)
        out_ref[NORM : NORM + 1, part] = (lax.rsqrt(total + EPSILON) * COS_SCALE)[0:1]
    corner_x, corner_y = boxes_ref[0:1, :], boxes_ref[1:2, :]
    other_x, other_y = boxes_ref[2:3, :], boxes_ref[3:4, :]
    begin, end = spans_ref[0:1, :], spans_ref[1:2, :]
    out_ref[LEFT : LEFT + 1, :] = jnp.minimum(corner_x, other_x).astype(jnp.float32)
    out_ref[RIGHT : RIGHT + 1, :] = jnp.maximum(corner_x, other_x).astype(jnp.float32) + MARGIN
    out_ref[BOTTOM : BOTTOM + 1, :] = jnp.minimum(corner_y, other_y).astype(jnp.float32)
    out_ref[TOP : TOP + 1, :] = jnp.maximum(corner_y, other_y).astype(jnp.float32) + MARGIN
    out_ref[FIRST : FIRST + 1, :] = jnp.minimum(begin, end).astype(jnp.float32) * GAP_SCALE + BASE
    out_ref[LAST : LAST + 1, :] = jnp.maximum(begin, end).astype(jnp.float32) * GAP_SCALE
    out_ref[CAMERA : CAMERA + 1, :] = camera_ref[...].astype(jnp.float32)
    own_place = pl.multiple_of(FIELDS + sub * half_vecs, 8)
    other_place = pl.multiple_of(FIELDS + (1 - sub) * half_vecs, 8)
    out_ref[pl.ds(own_place, half_vecs), :] = vec_mine_ref[...].astype(jnp.float32)
    out_ref[pl.ds(other_place, half_vecs), :] = vec_other_ref[...].astype(jnp.float32)


def prepare(mine, other, vec_mine, vec_other, boxes, spans, camera):
    rows = mine.shape[0]
    return pl.pallas_call(
        prepare_kernel,
        out_shape=jax.ShapeDtypeStruct((FIELDS + 2 * vec_mine.shape[0], rows), jnp.float32),
        in_specs=[VMEM_SPEC] * 7,
        out_specs=VMEM_SPEC,
        compiler_params=params(),
        name="prepare",
    )(mine, other, vec_mine, vec_other, boxes, spans, camera[None, :])


def weights_of(products, row, col, same):
    logit = products * row[NORM] * col[NORM]
    gap = jnp.maximum(col[FIRST] - row[LAST], row[FIRST] - col[LAST])
    width = jnp.maximum(jnp.minimum(row[RIGHT], col[RIGHT]) - jnp.maximum(row[LEFT], col[LEFT]), 0.0)
    height = jnp.maximum(jnp.minimum(row[TOP], col[TOP]) - jnp.maximum(row[BOTTOM], col[BOTTOM]), 0.0)
    inter = width * height
    both = row[FIELDS] + col[FIELDS]
    share = (both + inter) * pl.reciprocal(both - inter, approx=True)
    value = jnp.exp2(logit - jnp.maximum(gap, BASE)) * share
    barred = (row[CAMERA] == col[CAMERA]) & (gap < BARRED_BELOW)
    if same is not None:
        barred = barred & jnp.logical_not(same)
    return jnp.where(barred, 0.0, value)


def tile_kernel(blocks, own_block, receivers, *refs):
    row_mine_ref, row_other_ref, row_packet_ref = refs[:3]
    col_refs = [refs[3 + 3 * number : 6 + 3 * number] for number in range(blocks)]
    row_out_ref, col_out_ref, spread_ref, product_ref, weight_ref = refs[3 + 3 * blocks :]
    rows = row_mine_ref.shape[0]
    vecs = row_packet_ref.shape[0] - FIELDS
    row_out_ref[...] = jnp.zeros_like(row_out_ref)

    def with_ones(packet, count):
        tail = jnp.where(lax.broadcasted_iota(jnp.int32, (OUT_ROWS - vecs, count), 0) == 0, 1.0, 0.0)
        return jnp.concatenate([packet, tail], axis=0).astype(jnp.bfloat16)

    def compute():
        row_fields = row_packet_ref[0:FIELDS, :]
        turned = jnp.concatenate([row_fields] * (LANES // FIELDS), axis=0).T
        for field in range(FIELDS):
            spread_ref[field] = jnp.broadcast_to(turned[:, field : field + 1], (rows, LANES))
        spread_ref[FIELDS] = (spread_ref[RIGHT] - spread_ref[LEFT]) * (spread_ref[TOP] - spread_ref[BOTTOM])
        row_vecs = with_ones(row_packet_ref[FIELDS:, :], rows)
        sub = lax.axis_index("sub")
        done = 0
        for number, (col_mine_ref, col_other_ref, col_packet_ref) in enumerate(col_refs):
            cols = col_mine_ref.shape[0]

            def chunk(step, carry, col_mine_ref=col_mine_ref, col_other_ref=col_other_ref, col_packet_ref=col_packet_ref, number=number, done=done):
                start = pl.multiple_of(step * CHUNK, CHUNK)
                part = pl.ds(start, CHUNK)
                product_ref[...] = dot_nt(row_mine_ref[...], col_mine_ref[part, :]) + dot_nt(
                    row_other_ref[...], col_other_ref[part, :]
                )
                col = [col_packet_ref[field : field + 1, part] for field in range(FIELDS)]
                col.append((col[RIGHT] - col[LEFT]) * (col[TOP] - col[BOTTOM]))

                def group(index, inner):
                    first_row = pl.multiple_of(index * GROUP, GROUP)
                    row_part = pl.ds(first_row, GROUP)
                    row = [
                        jnp.concatenate([spread_ref[field, row_part, :]] * (CHUNK // LANES), axis=1)
                        for field in range(FIELDS + 1)
                    ]
                    same = None
                    if own_block and number == 0:
                        row_ids = lax.broadcasted_iota(jnp.int32, (GROUP, CHUNK), 0) + (sub * rows + first_row - start)
                        same = row_ids == lax.broadcasted_iota(jnp.int32, (GROUP, CHUNK), 1)
                    weight_ref[row_part, :] = weights_of(product_ref[row_part, :], row, col, same).astype(jnp.bfloat16)
                    return inner

                lax.fori_loop(0, rows // GROUP, group, 0, unroll=2)
                col_vecs = with_ones(col_packet_ref[FIELDS:, part], CHUNK)
                row_out_ref[...] += dot_nt(col_vecs, weight_ref[...])
                if col_out_ref is not None:
                    col_out_ref[:, pl.ds(pl.multiple_of(done + start, CHUNK), CHUNK)] = jnp.dot(
                        row_vecs, weight_ref[...], preferred_element_type=jnp.float32
                    )
                return carry

            lax.fori_loop(0, cols // CHUNK, chunk, 0)
            done += cols

    if receivers is None:
        compute()
        return
    pair = lax.axis_index("blk") // 2
    takes_part = functools.reduce(jnp.logical_or, [pair == one for one in receivers])

    @pl.when(takes_part)
    def _():
        compute()

    @pl.when(jnp.logical_not(takes_part))
    def _():
        col_out_ref[...] = jnp.zeros_like(col_out_ref)


def tile(row, columns, own_block=False, col_sums=True, receivers=None):
    row_mine, row_other, row_packet = row
    rows, features = row_mine.shape
    cols = sum(part[0].shape[0] for part in columns)
    shapes = [jax.ShapeDtypeStruct((OUT_ROWS, rows), jnp.float32)]
    if col_sums:
        shapes.append(jax.ShapeDtypeStruct((OUT_ROWS, cols), jnp.float32))

    def body(*refs):
        inputs = 3 + 3 * len(columns)
        refs = list(refs)
        if not col_sums:
            refs.insert(inputs + 1, None)
        tile_kernel(len(columns), own_block, receivers, *refs)

    pairs = rows * cols
    return pl.pallas_call(
        body,
        out_shape=shapes,
        in_specs=[VMEM_SPEC] * (3 + 3 * len(columns)),
        out_specs=[VMEM_SPEC] * len(shapes),
        scratch_shapes=[
            pltpu.VMEM((FIELDS + 1, rows, LANES), jnp.float32),
            pltpu.VMEM((rows, CHUNK), jnp.float32),
            pltpu.VMEM((rows, CHUNK), jnp.bfloat16),
        ],
        cost_estimate=pl.CostEstimate(
            flops=4 * pairs * features, bytes_accessed=4 * cols * features + 4 * rows * features, transcendentals=2 * pairs
        ),
        compiler_params=params(),
        name="tile",
    )(row_mine, row_other, row_packet, *[array for part in columns for array in part])


def image_kernel(*refs):
    parts, image_ref, gram_ref = refs[:-2], refs[-2], refs[-1]
    total = parts[0][...]
    for part in parts[1:]:
        total = total + part[...]
    vecs = image_ref.shape[0]
    image = total[0:vecs] / total[vecs : vecs + 1]
    image_ref[...] = image
    packed = jnp.zeros((8, LANES), jnp.float32)
    for piece in range(LANES // vecs):
        shifted = [image]
        if piece > 0:
            shifted.insert(0, jnp.zeros((piece * vecs, image.shape[1]), jnp.float32))
        if piece < LANES // vecs - 1:
            shifted.append(jnp.zeros((LANES - (piece + 1) * vecs, image.shape[1]), jnp.float32))
        packed = packed + dot_nt(image[8 * piece : 8 * piece + 8], jnp.concatenate(shifted, axis=0), lax.Precision.HIGHEST)
    gram_ref[...] = packed


def image_of(parts, vecs):
    cols = parts[0].shape[1]
    return pl.pallas_call(
        image_kernel,
        out_shape=[
            jax.ShapeDtypeStruct((vecs, cols), jnp.float32),
            jax.ShapeDtypeStruct((8, LANES), jnp.float32),
        ],
        in_specs=[VMEM_SPEC] * len(parts),
        out_specs=[VMEM_SPEC] * 2,
        compiler_params=params(),
        name="image",
    )(*parts)


def basis_kernel(total_rows, grams_ref, mine_ref, other_ref, out_ref, inverse_ref):
    vecs, half = mine_ref.shape
    sub = lax.axis_index("sub")
    packed = jnp.sum(grams_ref[...], axis=0) / total_rows
    lane = lax.broadcasted_iota(jnp.int32, (vecs, LANES), 1)
    line = lax.broadcasted_iota(jnp.int32, (vecs, LANES), 0)
    pieces = [packed] + [pltpu.roll(packed, LANES - piece * vecs, 1) for piece in range(1, LANES // vecs)]
    matrix = jnp.where(lane < vecs, jnp.concatenate(pieces, axis=0), 0.0)
    matrix = jnp.where(lane == line + vecs, 1.0, matrix)
    for step in range(vecs - 1):
        column = jnp.broadcast_to(matrix[:, step : step + 1], (vecs, LANES))
        scaled = matrix[step : step + 1, :] / column[step : step + 1, :]
        matrix = jnp.where(line > step, matrix - column * scaled, matrix)
    pivots = jnp.sum(jnp.where(lane == line, matrix, 0.0), axis=1, keepdims=True)
    inverse_ref[...] = pltpu.roll(matrix / jnp.sqrt(pivots), LANES - vecs, 1)
    share = vecs // 2
    own_rows = inverse_ref[pl.ds(pl.multiple_of(sub * share, 8), share), :][:, 0:vecs]
    for ref, place in ((mine_ref, sub), (other_ref, 1 - sub)):
        out_ref[:, pl.ds(pl.multiple_of(place * half, LANES), half)] = jnp.dot(
            own_rows, ref[...], precision=lax.Precision.HIGHEST, preferred_element_type=jnp.float32
        )


def basis_of(grams, mine, other, total_rows):
    vecs, half = mine.shape
    return pl.pallas_call(
        functools.partial(basis_kernel, total_rows),
        out_shape=jax.ShapeDtypeStruct((vecs // 2, 2 * half), jnp.float32),
        in_specs=[VMEM_SPEC] * 3,
        out_specs=VMEM_SPEC,
        scratch_shapes=[pltpu.VMEM((vecs, LANES), jnp.float32)],
        compiler_params=params(),
        name="basis",
    )(grams, mine, other)


def exchanges(pairs):
    plans = []
    for distance in range(1, pairs // 2):
        plans.append(([((p + distance) % pairs, p) for p in range(pairs)], None))
    if pairs > 1:
        half = pairs // 2
        last = [(p, p + half) if p % 2 == 0 else (p + half, p) for p in range(half)]
        plans.append((last, sorted(taker for _, taker in last)))
    return plans


def block_moves(pair_moves):
    return [(2 * source + member, 2 * target + member) for source, target in pair_moves for member in range(2)]


def back(moves):
    return [(target, source) for source, target in moves]


def local(embeddings, vectors, boxes, spans, camera):
    rows = embeddings.shape[0]
    half = rows // 2
    vecs = 2 * vectors.shape[0]
    blocks = lax.axis_size("blk")
    devices = 2 * blocks
    sub = lax.axis_index("sub")
    swap = [(0, 1), (1, 0)]
    beside = [(block, block ^ 1) for block in range(blocks)]
    plans = [(block_moves(moves), takers) for moves, takers in exchanges(blocks // 2)]

    def half_rows(array):
        return lax.dynamic_slice_in_dim(array, sub * half, half, 0)

    other = lax.ppermute(embeddings, "sub", swap)
    vec_other = lax.ppermute(vectors, "sub", swap)
    beside_mine = lax.ppermute(embeddings, "blk", beside)
    row_mine = half_rows(embeddings)
    sent_mine = [lax.ppermute(row_mine, "blk", moves) for moves, _ in plans]
    row_other = half_rows(other)
    sent_other = [lax.ppermute(row_other, "blk", moves) for moves, _ in plans]
    packet = prepare(embeddings, other, vectors, vec_other, boxes, spans, camera)
    row_packet = lax.dynamic_slice_in_dim(packet, sub * half, half, 1)
    beside_packet = lax.ppermute(packet, "blk", beside)
    sent_packet = [lax.ppermute(row_packet, "blk", moves) for moves, _ in plans]
    beside_other = lax.ppermute(beside_mine, "sub", swap)

    own_row = (row_mine, row_other, row_packet)
    own_cols = (embeddings, other, packet)
    beside_cols = (beside_mine, beside_other, beside_packet)
    parts = [
        tile(own_row, [own_cols], own_block=True, col_sums=False)[0],
        tile(own_row, [beside_cols], col_sums=False)[0],
    ]
    col_sums = None
    for (moves, takers), mine, rest, meta in zip(plans, sent_mine, sent_other, sent_packet):
        row_sums, sums = tile((mine, rest, meta), [own_cols, beside_cols], receivers=takers)
        parts.append(lax.ppermute(row_sums, "blk", back(moves)))
        col_sums = sums if col_sums is None else col_sums + sums

    def piece(place):
        return lax.dynamic_slice_in_dim(col_sums, place * half, half, 1)

    if col_sums is not None:
        crossed = [(2 * block + core, 2 * (block ^ 1) + 1 - core) for block in range(blocks) for core in range(2)]
        parts.append(piece(sub))
        parts.append(lax.ppermute(piece(1 - sub), "sub", swap))
        parts.append(lax.ppermute(piece(2 + sub), "blk", beside))
        parts.append(lax.ppermute(piece(3 - sub), ("blk", "sub"), crossed))

    image, gram = image_of(parts, vecs)
    image_other = lax.ppermute(image, "sub", swap)
    copies = jnp.broadcast_to(gram[None], (devices,) + gram.shape)
    grams = lax.all_to_all(copies, ("blk", "sub"), 0, 0, tiled=True)
    return basis_of(grams, image, image_other, blocks * rows)


def solution(mesh):
    placed = (
        P(("groups", "blk"), "sub"),
        P("sub", ("groups", "blk")),
        P(None, ("groups", "blk")),
        P(None, ("groups", "blk")),
        P(("groups", "blk")),
    )
    return jax.shard_map(
        local, mesh=mesh, in_specs=placed, out_specs=P("sub", ("groups", "blk")), check_vma=False
    )
```

```python
import functools
import math

import jax
import jax.numpy as jnp
from jax import lax
from jax.experimental import pallas as pl
from jax.experimental.pallas import tpu as pltpu
from jax.sharding import PartitionSpec as P

SHARPNESS = 10.0
HORIZON = 2000.0
MARGIN = 8.0
EPSILON = 1e-06

LOG2E = math.log2(math.e)
COS_SCALE = math.sqrt(SHARPNESS * LOG2E)
GAP_SCALE = LOG2E / HORIZON
BASE = SHARPNESS * LOG2E + 1.0
BARRED_BELOW = BASE - 0.5 * GAP_SCALE

FIELDS = 8
LEFT, RIGHT, BOTTOM, TOP, FIRST, LAST, CAMERA, NORM = range(FIELDS)
LANES = 128
CHUNK = 256
OUT_ROWS = 40
VMEM_LIMIT = 48 * 1024 * 1024

NT = (((1,), (1,)), ((), ()))
VMEM_SPEC = pl.BlockSpec(memory_space=pltpu.VMEM)


def params():
    return pltpu.CompilerParams(vmem_limit_bytes=VMEM_LIMIT)


def dot_nt(a, b, precision=None):
    return lax.dot_general(a, b, NT, precision=precision, preferred_element_type=jnp.float32)


def prepare_kernel(mine_ref, other_ref, vec_mine_ref, vec_other_ref, boxes_ref, spans_ref, camera_ref, out_ref):
    sub = lax.axis_index("sub")
    rows = mine_ref.shape[0]
    half_vecs = vec_mine_ref.shape[0]
    ones = jnp.ones((FIELDS, mine_ref.shape[1]), jnp.bfloat16)
    for start in range(0, rows, CHUNK):
        part = pl.ds(start, CHUNK)
        total = jnp.zeros((FIELDS, CHUNK), jnp.float32)
        for ref in (mine_ref, other_ref):
            values = ref[part, :].astype(jnp.float32)
            square = values * values
            high = square.astype(jnp.bfloat16)
            low = (square - high.astype(jnp.float32)).astype(jnp.bfloat16)
            total = total + dot_nt(ones, high) + dot_nt(ones, low)
        out_ref[NORM : NORM + 1, part] = (lax.rsqrt(total + EPSILON) * COS_SCALE)[0:1]
    corner_x, corner_y = boxes_ref[0:1, :], boxes_ref[1:2, :]
    other_x, other_y = boxes_ref[2:3, :], boxes_ref[3:4, :]
    begin, end = spans_ref[0:1, :], spans_ref[1:2, :]
    out_ref[LEFT : LEFT + 1, :] = jnp.minimum(corner_x, other_x).astype(jnp.float32)
    out_ref[RIGHT : RIGHT + 1, :] = jnp.maximum(corner_x, other_x).astype(jnp.float32) + MARGIN
    out_ref[BOTTOM : BOTTOM + 1, :] = jnp.minimum(corner_y, other_y).astype(jnp.float32)
    out_ref[TOP : TOP + 1, :] = jnp.maximum(corner_y, other_y).astype(jnp.float32) + MARGIN
    out_ref[FIRST : FIRST + 1, :] = jnp.minimum(begin, end).astype(jnp.float32) * GAP_SCALE + BASE
    out_ref[LAST : LAST + 1, :] = jnp.maximum(begin, end).astype(jnp.float32) * GAP_SCALE
    out_ref[CAMERA : CAMERA + 1, :] = camera_ref[...].astype(jnp.float32)
    own_place = pl.multiple_of(FIELDS + sub * half_vecs, 8)
    other_place = pl.multiple_of(FIELDS + (1 - sub) * half_vecs, 8)
    out_ref[pl.ds(own_place, half_vecs), :] = vec_mine_ref[...].astype(jnp.float32)
    out_ref[pl.ds(other_place, half_vecs), :] = vec_other_ref[...].astype(jnp.float32)


def prepare(mine, other, vec_mine, vec_other, boxes, spans, camera):
    rows = mine.shape[0]
    return pl.pallas_call(
        prepare_kernel,
        out_shape=jax.ShapeDtypeStruct((FIELDS + 2 * vec_mine.shape[0], rows), jnp.float32),
        in_specs=[VMEM_SPEC] * 7,
        out_specs=VMEM_SPEC,
        compiler_params=params(),
        name="prepare",
    )(mine, other, vec_mine, vec_other, boxes, spans, camera[None, :])


def weights_of(products, row, col, same):
    logit = products * row[NORM] * col[NORM]
    gap = jnp.maximum(col[FIRST] - row[LAST], row[FIRST] - col[LAST])
    width = jnp.maximum(jnp.minimum(row[RIGHT], col[RIGHT]) - jnp.maximum(row[LEFT], col[LEFT]), 0.0)
    height = jnp.maximum(jnp.minimum(row[TOP], col[TOP]) - jnp.maximum(row[BOTTOM], col[BOTTOM]), 0.0)
    inter = width * height
    both = row[FIELDS] + col[FIELDS]
    share = (both + inter) * pl.reciprocal(both - inter, approx=True)
    value = jnp.exp2(logit - jnp.maximum(gap, BASE)) * share
    barred = (row[CAMERA] == col[CAMERA]) & (gap < BARRED_BELOW)
    if same is not None:
        barred = barred & jnp.logical_not(same)
    return jnp.where(barred, 0.0, value)


def tile_kernel(blocks, own_rows, own_block, receivers, *refs):
    row_mine_ref, row_other_ref, row_packet_ref = refs[:3]
    col_refs = [refs[3 + 3 * number : 6 + 3 * number] for number in range(blocks)]
    row_out_ref, col_out_ref, spread_ref = refs[3 + 3 * blocks : 6 + 3 * blocks]
    products, weights = refs[6 + 3 * blocks : 8 + 3 * blocks], refs[8 + 3 * blocks :]
    rows = row_out_ref.shape[1]
    vecs = row_packet_ref.shape[0] - FIELDS
    sub = lax.axis_index("sub")
    row_part, packet_part = pl.ds(0, rows), pl.ds(0, rows)
    if own_rows:
        row_part = packet_part = pl.ds(pl.multiple_of(sub * rows, rows), rows)
    row_out_ref[...] = jnp.zeros_like(row_out_ref)

    def with_ones(packet, count):
        tail = jnp.where(lax.broadcasted_iota(jnp.int32, (OUT_ROWS - vecs, count), 0) == 0, 1.0, 0.0)
        return jnp.concatenate([packet, tail], axis=0).astype(jnp.bfloat16)

    def block(number, done, row_vecs):
        col_mine_ref, col_other_ref, col_packet_ref = col_refs[number]
        chunks = col_mine_ref.shape[0] // CHUNK

        def place(step, base=0):
            return pl.ds(pl.multiple_of(base + step * CHUNK, CHUNK), CHUNK)

        def multiply(step, product_ref):
            part = place(step)
            columns = jnp.concatenate([col_mine_ref[part, :], col_other_ref[part, :]], axis=1)
            lines = jnp.concatenate([row_mine_ref[row_part, :], row_other_ref[row_part, :]], axis=1)
            product_ref[...] = dot_nt(lines, columns)

        def weigh(step, product_ref, weight_ref):
            col = [col_packet_ref[field : field + 1, place(step)] for field in range(FIELDS)]
            col.append((col[RIGHT] - col[LEFT]) * (col[TOP] - col[BOTTOM]))
            col = [jnp.broadcast_to(field, (8, CHUNK)) for field in col]
            for first_row in range(0, rows, 16):
                both = []
                for line in (first_row, first_row + 8):
                    row = [
                        jnp.concatenate([spread_ref[field, line : line + 8, :]] * (CHUNK // LANES), axis=1)
                        for field in range(FIELDS + 1)
                    ]
                    same = None
                    if own_block:
                        row_ids = lax.broadcasted_iota(jnp.int32, (8, CHUNK), 0) + (sub * rows + line - step * CHUNK)
                        same = row_ids == lax.broadcasted_iota(jnp.int32, (8, CHUNK), 1)
                    both.append(weights_of(product_ref[line : line + 8, :], row, col, same))
                weight_ref[first_row : first_row + 16, :] = jnp.concatenate(both, axis=0).astype(jnp.bfloat16)

        def total(step, weight_ref):
            col_vecs = with_ones(col_packet_ref[FIELDS:, place(step)], CHUNK)
            row_out_ref[...] += dot_nt(col_vecs, weight_ref[...])
            if col_out_ref is not None:
                col_out_ref[:, place(step, done)] = jnp.dot(
                    row_vecs, weight_ref[...], preferred_element_type=jnp.float32
                )

        def steps(index, carry):
            for parity in range(2):
                step = 2 * index + parity
                multiply(lax.rem(step + 1, chunks), products[1 - parity])
                weigh(step, products[parity], weights[parity])
                total(lax.rem(step + chunks - 1, chunks), weights[1 - parity])
            return carry

        multiply(0, products[0])
        weights[1][...] = jnp.zeros_like(weights[1])
        lax.fori_loop(0, chunks // 2, steps, 0)
        total(chunks - 1, weights[1])

    def compute():
        row_fields = row_packet_ref[0:FIELDS, packet_part]
        turned = jnp.concatenate([row_fields] * (LANES // FIELDS), axis=0).T
        for field in range(FIELDS):
            spread_ref[field] = jnp.broadcast_to(turned[:, field : field + 1], (rows, LANES))
        spread_ref[FIELDS] = (spread_ref[RIGHT] - spread_ref[LEFT]) * (spread_ref[TOP] - spread_ref[BOTTOM])
        row_vecs = with_ones(row_packet_ref[FIELDS:, packet_part], rows)
        done = 0
        for number in range(blocks):
            block(number, done, row_vecs)
            done += col_refs[number][0].shape[0]

    if receivers is None:
        compute()
        return
    pair = lax.axis_index("blk") // 2
    takes_part = functools.reduce(jnp.logical_or, [pair == one for one in receivers])

    @pl.when(takes_part)
    def _():
        compute()

    @pl.when(jnp.logical_not(takes_part))
    def _():
        col_out_ref[...] = jnp.zeros_like(col_out_ref)


def tile(row, columns, rows, own_rows=False, own_block=False, col_sums=True, receivers=None):
    features = 2 * row[0].shape[1]
    cols = sum(part[0].shape[0] for part in columns)
    shapes = [jax.ShapeDtypeStruct((OUT_ROWS, rows), jnp.float32)]
    if col_sums:
        shapes.append(jax.ShapeDtypeStruct((OUT_ROWS, cols), jnp.float32))

    def body(*refs):
        inputs = 3 + 3 * len(columns)
        refs = list(refs)
        if not col_sums:
            refs.insert(inputs + 1, None)
        tile_kernel(len(columns), own_rows, own_block, receivers, *refs)

    pairs = rows * cols
    return pl.pallas_call(
        body,
        out_shape=shapes,
        in_specs=[VMEM_SPEC] * (3 + 3 * len(columns)),
        out_specs=[VMEM_SPEC] * len(shapes),
        scratch_shapes=[
            pltpu.VMEM((FIELDS + 1, rows, LANES), jnp.float32),
            pltpu.VMEM((rows, CHUNK), jnp.float32),
            pltpu.VMEM((rows, CHUNK), jnp.float32),
            pltpu.VMEM((rows, CHUNK), jnp.bfloat16),
            pltpu.VMEM((rows, CHUNK), jnp.bfloat16),
        ],
        cost_estimate=pl.CostEstimate(
            flops=4 * pairs * features, bytes_accessed=4 * cols * features + 4 * rows * features, transcendentals=2 * pairs
        ),
        compiler_params=params(),
        name="tile",
    )(*row, *[array for part in columns for array in part])


def image_kernel(*refs):
    parts, image_ref, grams_ref = refs[:-2], refs[-2], refs[-1]
    total = parts[0][...]
    for part in parts[1:]:
        total = total + part[...]
    vecs = image_ref.shape[0]
    image = total[0:vecs] / total[vecs : vecs + 1]
    image_ref[...] = image
    packed = jnp.zeros((8, LANES), jnp.float32)
    for piece in range(LANES // vecs):
        shifted = [image]
        if piece > 0:
            shifted.insert(0, jnp.zeros((piece * vecs, image.shape[1]), jnp.float32))
        if piece < LANES // vecs - 1:
            shifted.append(jnp.zeros((LANES - (piece + 1) * vecs, image.shape[1]), jnp.float32))
        packed = packed + dot_nt(image[8 * piece : 8 * piece + 8], jnp.concatenate(shifted, axis=0), lax.Precision.HIGHEST)
    for copy in range(grams_ref.shape[0]):
        grams_ref[copy] = packed


def image_of(parts, vecs, copies):
    cols = parts[0].shape[1]
    return pl.pallas_call(
        image_kernel,
        out_shape=[
            jax.ShapeDtypeStruct((vecs, cols), jnp.float32),
            jax.ShapeDtypeStruct((copies, 8, LANES), jnp.float32),
        ],
        in_specs=[VMEM_SPEC] * len(parts),
        out_specs=[VMEM_SPEC] * 2,
        compiler_params=params(),
        name="image",
    )(*parts)


def basis_kernel(total_rows, grams_ref, mine_ref, other_ref, out_ref, inverse_ref):
    vecs, half = mine_ref.shape
    sub = lax.axis_index("sub")
    packed = jnp.sum(grams_ref[...], axis=0) / total_rows
    lane = lax.broadcasted_iota(jnp.int32, (vecs, LANES), 1)
    line = lax.broadcasted_iota(jnp.int32, (vecs, LANES), 0)
    pieces = [packed] + [pltpu.roll(packed, LANES - piece * vecs, 1) for piece in range(1, LANES // vecs)]
    matrix = jnp.where(lane < vecs, jnp.concatenate(pieces, axis=0), 0.0)
    matrix = jnp.where(lane == line + vecs, 1.0, matrix)
    for step in range(vecs - 1):
        column = jnp.broadcast_to(matrix[:, step : step + 1], (vecs, LANES))
        scaled = matrix[step : step + 1, :] / column[step : step + 1, :]
        matrix = jnp.where(line > step, matrix - column * scaled, matrix)
    pivots = jnp.sum(jnp.where(lane == line, matrix, 0.0), axis=1, keepdims=True)
    inverse_ref[...] = pltpu.roll(matrix / jnp.sqrt(pivots), LANES - vecs, 1)
    share = vecs // 2
    own_rows = inverse_ref[pl.ds(pl.multiple_of(sub * share, 8), share), :][:, 0:vecs]
    for ref, place in ((mine_ref, sub), (other_ref, 1 - sub)):
        out_ref[:, pl.ds(pl.multiple_of(place * half, LANES), half)] = jnp.dot(
            own_rows, ref[...], precision=lax.Precision.HIGHEST, preferred_element_type=jnp.float32
        )


def basis_of(grams, mine, other, total_rows):
    vecs, half = mine.shape
    return pl.pallas_call(
        functools.partial(basis_kernel, total_rows),
        out_shape=jax.ShapeDtypeStruct((vecs // 2, 2 * half), jnp.float32),
        in_specs=[VMEM_SPEC] * 3,
        out_specs=VMEM_SPEC,
        scratch_shapes=[pltpu.VMEM((vecs, LANES), jnp.float32)],
        compiler_params=params(),
        name="basis",
    )(grams, mine, other)


def exchanges(pairs):
    plans = []
    for distance in range(1, pairs // 2):
        plans.append(([((p + distance) % pairs, p) for p in range(pairs)], None))
    if pairs > 1:
        half = pairs // 2
        last = [(p, p + half) if p % 2 == 0 else (p + half, p) for p in range(half)]
        plans.append((last, sorted(taker for _, taker in last)))
    return plans


def block_moves(pair_moves):
    return [(2 * source + member, 2 * target + member) for source, target in pair_moves for member in range(2)]


def back(moves):
    return [(target, source) for source, target in moves]


def local(embeddings, vectors, boxes, spans, camera):
    rows = embeddings.shape[0]
    half = rows // 2
    vecs = 2 * vectors.shape[0]
    blocks = lax.axis_size("blk")
    devices = 2 * blocks
    sub = lax.axis_index("sub")
    swap = [(0, 1), (1, 0)]
    beside = [(block, block ^ 1) for block in range(blocks)]
    plans = [(block_moves(moves), takers) for moves, takers in exchanges(blocks // 2)]

    def half_rows(place):
        return lax.dynamic_slice_in_dim(embeddings, place * half, half, 0)

    def crossed(moves):
        return [(2 * source + 1 - core, 2 * target + core) for source, target in moves for core in range(2)]

    other = lax.ppermute(embeddings, "sub", swap)
    vec_other = lax.ppermute(vectors, "sub", swap)
    to_same, to_cross = half_rows(sub), half_rows(1 - sub)
    sent = [
        (lax.ppermute(to_same, "blk", moves), lax.ppermute(to_cross, ("blk", "sub"), crossed(moves)))
        for moves, _ in plans
    ]
    beside_mine = lax.ppermute(embeddings, "blk", beside)
    beside_other = lax.ppermute(embeddings, ("blk", "sub"), crossed(beside))
    packet = prepare(embeddings, other, vectors, vec_other, boxes, spans, camera)
    row_packet = lax.dynamic_slice_in_dim(packet, sub * half, half, 1)
    beside_packet = lax.ppermute(packet, "blk", beside)
    sent_packet = [lax.ppermute(row_packet, "blk", moves) for moves, _ in plans]

    own = (embeddings, other, packet)
    next_to = (beside_mine, beside_other, beside_packet)
    parts = [
        tile(own, [own], half, own_rows=True, own_block=True, col_sums=False)[0],
        tile(own, [next_to], half, own_rows=True, col_sums=False)[0],
    ]
    col_sums = None
    for (moves, takers), halves, meta in zip(plans, sent, sent_packet):
        row_sums, sums = tile((*halves, meta), [own, next_to], half, receivers=takers)
        parts.append(lax.ppermute(row_sums, "blk", back(moves)))
        col_sums = sums if col_sums is None else col_sums + sums

    def piece(place):
        return lax.dynamic_slice_in_dim(col_sums, place * half, half, 1)

    if col_sums is not None:
        parts.append(piece(sub))
        parts.append(lax.ppermute(piece(1 - sub), "sub", swap))
        parts.append(lax.ppermute(piece(2 + sub), "blk", beside))
        parts.append(lax.ppermute(piece(3 - sub), ("blk", "sub"), crossed(beside)))

    image, copies = image_of(parts, vecs, devices)
    image_other = lax.ppermute(image, "sub", swap)
    grams = lax.all_to_all(copies, ("blk", "sub"), 0, 0, tiled=True)
    return basis_of(grams, image, image_other, blocks * rows)


def solution(mesh):
    placed = (
        P(("groups", "blk"), "sub"),
        P("sub", ("groups", "blk")),
        P(None, ("groups", "blk")),
        P(None, ("groups", "blk")),
        P(("groups", "blk")),
    )
    return jax.shard_map(
        local, mesh=mesh, in_specs=placed, out_specs=P("sub", ("groups", "blk")), check_vma=False
    )
```

```python
import functools
import math

import jax
import jax.numpy as jnp
from jax import lax
from jax.experimental import pallas as pl
from jax.experimental.pallas import tpu as pltpu
from jax.sharding import PartitionSpec as P

SHARPNESS = 10.0
HORIZON = 2000.0
MARGIN = 8.0
EPSILON = 1e-06

LOG2E = math.log2(math.e)
COS_SCALE = math.sqrt(SHARPNESS * LOG2E)
GAP_SCALE = LOG2E / HORIZON
BASE = SHARPNESS * LOG2E + 1.0
BARRED_BELOW = BASE - 0.5 * GAP_SCALE

FIELDS = 9
LEFT, RIGHT, BOTTOM, TOP, FIRST, LAST, CAMERA, NORM, AREA = range(FIELDS)
CODE_ROWS = 16
LANES = 128
CHUNK = 256
OUT_ROWS = 40
VMEM_LIMIT = 48 * 1024 * 1024

NT = (((1,), (1,)), ((), ()))
VMEM_SPEC = pl.BlockSpec(memory_space=pltpu.VMEM)


def params():
    return pltpu.CompilerParams(vmem_limit_bytes=VMEM_LIMIT)


def dot_nt(a, b, precision=None):
    return lax.dot_general(a, b, NT, precision=precision, preferred_element_type=jnp.float32)


def pack_rows(rows, half_vecs):
    return rows + rows // CHUNK * (half_vecs + CODE_ROWS)


def vec_place(total, half_vecs, chunk):
    return pl.ds(pl.multiple_of(total + chunk * half_vecs, 16), half_vecs)


def code_place(total, half_vecs, chunk):
    return pl.ds(pl.multiple_of(total + total // CHUNK * half_vecs + chunk * CODE_ROWS, 16), CODE_ROWS)


def pack_kernel(emb_ref, vec_ref, boxes_ref, spans_ref, camera_ref, full_ref, same_ref, cross_ref):
    sub = lax.axis_index("sub")
    rows = emb_ref.shape[0]
    half = same_ref.shape[0] * rows // full_ref.shape[0]
    half_vecs = vec_ref.shape[0]
    full_ref[0:rows, :] = emb_ref[...]
    same_ref[0:half, :] = emb_ref[pl.ds(pl.multiple_of(sub * half, half), half), :]
    cross_ref[0:half, :] = emb_ref[pl.ds(pl.multiple_of((1 - sub) * half, half), half), :]
    ones = jnp.ones((8, CHUNK), jnp.bfloat16)
    for chunk in range(rows // CHUNK):
        part = pl.ds(chunk * CHUNK, CHUNK)
        codes = []

        def whole(number, low_bits):
            codes.append((number >> low_bits) << low_bits)
            codes.append(number & ((1 << low_bits) - 1))

        boxes, spans = boxes_ref[:, part], spans_ref[:, part]
        for axis in range(2):
            whole(jnp.minimum(boxes[axis : axis + 1], boxes[axis + 2 : axis + 3]), 5)
            whole(jnp.maximum(boxes[axis : axis + 1], boxes[axis + 2 : axis + 3]), 5)
        whole(jnp.minimum(spans[0:1], spans[1:2]), 7)
        whole(jnp.maximum(spans[0:1], spans[1:2]), 7)
        codes.append(camera_ref[:, part])
        codes = [code.astype(jnp.float32) for code in codes]
        values = emb_ref[part, :].astype(jnp.float32)
        square = values * values
        high = square.astype(jnp.bfloat16)
        low = (square - high.astype(jnp.float32)).astype(jnp.bfloat16)
        rest = (dot_nt(ones, high) + dot_nt(ones, low))[0:1]
        for _ in range(3):
            piece = rest.astype(jnp.bfloat16).astype(jnp.float32)
            codes.append(piece)
            rest = rest - piece
        coded = jnp.concatenate(codes, axis=0).astype(jnp.bfloat16)
        vecs = vec_ref[:, part]
        full_ref[vec_place(rows, half_vecs, chunk), :] = vecs
        full_ref[code_place(rows, half_vecs, chunk), :] = coded
        in_half = chunk % (half // CHUNK)
        first_half = chunk < half // CHUNK

        def put(ref):
            ref[vec_place(half, half_vecs, in_half), :] = vecs
            ref[code_place(half, half_vecs, in_half), :] = coded

        pl.when((sub == 0) == first_half)(functools.partial(put, same_ref))
        pl.when((sub == 0) != first_half)(functools.partial(put, cross_ref))


def packs_of(embeddings, vectors, boxes, spans, camera):
    rows, width = embeddings.shape
    half_vecs = vectors.shape[0]
    sizes = [pack_rows(rows, half_vecs)] + [pack_rows(rows // 2, half_vecs)] * 2
    return pl.pallas_call(
        pack_kernel,
        out_shape=[jax.ShapeDtypeStruct((size, width), jnp.bfloat16) for size in sizes],
        in_specs=[VMEM_SPEC] * 5,
        out_specs=[VMEM_SPEC] * 3,
        compiler_params=params(),
        name="pack",
    )(embeddings, vectors, boxes, spans, camera[None, :])


def decode(mine_ref, other_ref, place):
    mine, other = mine_ref[place, :].astype(jnp.float32), other_ref[place, :].astype(jnp.float32)
    numbers = [mine[2 * index : 2 * index + 1] + mine[2 * index + 1 : 2 * index + 2] for index in range(6)]
    left, right, bottom, top, first, last = numbers
    right, top = right + MARGIN, top + MARGIN
    square = jnp.zeros_like(left)
    for index in (15, 14, 13):
        square = square + (mine[index : index + 1] + other[index : index + 1])
    norm = lax.rsqrt(square + EPSILON) * COS_SCALE
    area = (right - left) * (top - bottom)
    return [left, right, bottom, top, first * GAP_SCALE + BASE, last * GAP_SCALE, mine[12:13], norm, area]


def vectors_of(mine_ref, other_ref, place):
    mine, other = mine_ref[place, :].astype(jnp.float32), other_ref[place, :].astype(jnp.float32)
    swapped = lax.axis_index("sub") != 0
    tail = jnp.where(lax.broadcasted_iota(jnp.int32, mine.shape, 0) == 0, 1.0, 0.0)
    ordered = [jnp.where(swapped, other, mine), jnp.where(swapped, mine, other), tail]
    return jnp.concatenate(ordered, axis=0).astype(jnp.bfloat16)


def weights_of(products, row, col, same):
    logit = products * row[NORM] * col[NORM]
    gap = jnp.maximum(col[FIRST] - row[LAST], row[FIRST] - col[LAST])
    width = jnp.maximum(jnp.minimum(row[RIGHT], col[RIGHT]) - jnp.maximum(row[LEFT], col[LEFT]), 0.0)
    height = jnp.maximum(jnp.minimum(row[TOP], col[TOP]) - jnp.maximum(row[BOTTOM], col[BOTTOM]), 0.0)
    inter = width * height
    both = row[AREA] + col[AREA]
    share = (both + inter) * pl.reciprocal(both - inter, approx=True)
    value = jnp.exp2(logit - jnp.maximum(gap, BASE)) * share
    barred = (row[CAMERA] == col[CAMERA]) & (gap < BARRED_BELOW)
    if same is not None:
        barred = barred & jnp.logical_not(same)
    return jnp.where(barred, 0.0, value)


def tile_kernel(blocks, own_rows, own_block, receivers, half_vecs, *refs):
    row_mine_ref, row_other_ref = refs[:2]
    col_refs = [refs[2 + 2 * number : 4 + 2 * number] for number in range(blocks)]
    row_out_ref, col_out_ref, field_ref, spread_ref = refs[2 + 2 * blocks : 6 + 2 * blocks]
    products, weights = refs[6 + 2 * blocks : 8 + 2 * blocks], refs[8 + 2 * blocks :]
    rows = row_out_ref.shape[1]
    sub = lax.axis_index("sub")
    row_total, first_chunk = rows, 0
    row_part = pl.ds(0, rows)
    if own_rows:
        row_total, first_chunk = 2 * rows, sub * (rows // CHUNK)
        row_part = pl.ds(pl.multiple_of(sub * rows, rows), rows)
    row_out_ref[...] = jnp.zeros_like(row_out_ref)

    def block(number, done, row_vecs):
        col_mine_ref, col_other_ref = col_refs[number]
        cols = 2 * rows
        chunks = cols // CHUNK

        def place(step, base=0):
            return pl.ds(pl.multiple_of(base + step * CHUNK, CHUNK), CHUNK)

        def multiply(step, product_ref):
            part = place(step)
            columns = jnp.concatenate([col_mine_ref[part, :], col_other_ref[part, :]], axis=1)
            lines = jnp.concatenate([row_mine_ref[row_part, :], row_other_ref[row_part, :]], axis=1)
            product_ref[...] = dot_nt(lines, columns)

        def weigh(step, product_ref, weight_ref):
            col = decode(col_mine_ref, col_other_ref, code_place(cols, half_vecs, step))
            col = [jnp.broadcast_to(field, (8, CHUNK)) for field in col]
            for first_row in range(0, rows, 16):
                both = []
                for line in (first_row, first_row + 8):
                    row = [
                        jnp.concatenate([spread_ref[field, line : line + 8, :]] * (CHUNK // LANES), axis=1)
                        for field in range(FIELDS)
                    ]
                    same = None
                    if own_block:
                        row_ids = lax.broadcasted_iota(jnp.int32, (8, CHUNK), 0) + (sub * rows + line - step * CHUNK)
                        same = row_ids == lax.broadcasted_iota(jnp.int32, (8, CHUNK), 1)
                    both.append(weights_of(product_ref[line : line + 8, :], row, col, same))
                weight_ref[first_row : first_row + 16, :] = jnp.concatenate(both, axis=0).astype(jnp.bfloat16)

        def total(step, weight_ref):
            col_vecs = vectors_of(col_mine_ref, col_other_ref, vec_place(cols, half_vecs, step))
            row_out_ref[...] += dot_nt(col_vecs, weight_ref[...])[0:OUT_ROWS]
            if col_out_ref is not None:
                col_out_ref[:, place(step, done)] = jnp.dot(
                    row_vecs, weight_ref[...], preferred_element_type=jnp.float32
                )[0:OUT_ROWS]

        def steps(index, carry):
            for parity in range(2):
                step = 2 * index + parity
                multiply(lax.rem(step + 1, chunks), products[1 - parity])
                weigh(step, products[parity], weights[parity])
                total(lax.rem(step + chunks - 1, chunks), weights[1 - parity])
            return carry

        multiply(0, products[0])
        weights[1][...] = jnp.zeros_like(weights[1])
        lax.fori_loop(0, chunks // 2, steps, 0)
        total(chunks - 1, weights[1])

    def compute():
        row_vecs = []
        for chunk in range(rows // CHUNK):
            codes = code_place(row_total, half_vecs, first_chunk + chunk)
            for field, values in enumerate(decode(row_mine_ref, row_other_ref, codes)):
                field_ref[field : field + 1, chunk * CHUNK : (chunk + 1) * CHUNK] = values
            row_vecs.append(vectors_of(row_mine_ref, row_other_ref, vec_place(row_total, half_vecs, first_chunk + chunk)))
        row_vecs = jnp.concatenate(row_vecs, axis=1)
        turned = field_ref[...].T
        for field in range(FIELDS):
            spread_ref[field] = jnp.broadcast_to(turned[:, field : field + 1], (rows, LANES))
        for number in range(blocks):
            block(number, number * 2 * rows, row_vecs)

    if receivers is None:
        compute()
        return
    pair = lax.axis_index("blk") // 2
    takes_part = functools.reduce(jnp.logical_or, [pair == one for one in receivers])

    @pl.when(takes_part)
    def _():
        compute()

    @pl.when(jnp.logical_not(takes_part))
    def _():
        col_out_ref[...] = jnp.zeros_like(col_out_ref)


def tile(row, columns, rows, half_vecs, own_rows=False, own_block=False, col_sums=True, receivers=None):
    features = 2 * row[0].shape[1]
    cols = 2 * rows * len(columns)
    shapes = [jax.ShapeDtypeStruct((OUT_ROWS, rows), jnp.float32)]
    if col_sums:
        shapes.append(jax.ShapeDtypeStruct((OUT_ROWS, cols), jnp.float32))

    def body(*refs):
        inputs = 2 + 2 * len(columns)
        refs = list(refs)
        if not col_sums:
            refs.insert(inputs + 1, None)
        tile_kernel(len(columns), own_rows, own_block, receivers, half_vecs, *refs)

    pairs = rows * cols
    return pl.pallas_call(
        body,
        out_shape=shapes,
        in_specs=[VMEM_SPEC] * (2 + 2 * len(columns)),
        out_specs=[VMEM_SPEC] * len(shapes),
        scratch_shapes=[
            pltpu.VMEM((LANES, rows), jnp.float32),
            pltpu.VMEM((FIELDS, rows, LANES), jnp.float32),
            pltpu.VMEM((rows, CHUNK), jnp.float32),
            pltpu.VMEM((rows, CHUNK), jnp.float32),
            pltpu.VMEM((rows, CHUNK), jnp.bfloat16),
            pltpu.VMEM((rows, CHUNK), jnp.bfloat16),
        ],
        cost_estimate=pl.CostEstimate(
            flops=4 * pairs * features, bytes_accessed=4 * cols * features + 4 * rows * features, transcendentals=2 * pairs
        ),
        compiler_params=params(),
        name="tile",
    )(*row, *[array for part in columns for array in part])


def image_kernel(*refs):
    parts, image_ref, grams_ref = refs[:-2], refs[-2], refs[-1]
    total = parts[0][...]
    for part in parts[1:]:
        total = total + part[...]
    vecs = image_ref.shape[0]
    image = total[0:vecs] / total[vecs : vecs + 1]
    image_ref[...] = image
    packed = jnp.zeros((8, LANES), jnp.float32)
    for piece in range(LANES // vecs):
        shifted = [image]
        if piece > 0:
            shifted.insert(0, jnp.zeros((piece * vecs, image.shape[1]), jnp.float32))
        if piece < LANES // vecs - 1:
            shifted.append(jnp.zeros((LANES - (piece + 1) * vecs, image.shape[1]), jnp.float32))
        packed = packed + dot_nt(image[8 * piece : 8 * piece + 8], jnp.concatenate(shifted, axis=0), lax.Precision.HIGHEST)
    for copy in range(grams_ref.shape[0]):
        grams_ref[copy] = packed


def image_of(parts, vecs, copies):
    cols = parts[0].shape[1]
    return pl.pallas_call(
        image_kernel,
        out_shape=[
            jax.ShapeDtypeStruct((vecs, cols), jnp.float32),
            jax.ShapeDtypeStruct((copies, 8, LANES), jnp.float32),
        ],
        in_specs=[VMEM_SPEC] * len(parts),
        out_specs=[VMEM_SPEC] * 2,
        compiler_params=params(),
        name="image",
    )(*parts)


def basis_kernel(total_rows, grams_ref, mine_ref, other_ref, out_ref, inverse_ref):
    vecs, half = mine_ref.shape
    sub = lax.axis_index("sub")
    packed = jnp.sum(grams_ref[...], axis=0) / total_rows
    lane = lax.broadcasted_iota(jnp.int32, (vecs, LANES), 1)
    line = lax.broadcasted_iota(jnp.int32, (vecs, LANES), 0)
    pieces = [packed] + [pltpu.roll(packed, LANES - piece * vecs, 1) for piece in range(1, LANES // vecs)]
    matrix = jnp.where(lane < vecs, jnp.concatenate(pieces, axis=0), 0.0)
    matrix = jnp.where(lane == line + vecs, 1.0, matrix)
    for step in range(vecs - 1):
        column = jnp.broadcast_to(matrix[:, step : step + 1], (vecs, LANES))
        scaled = matrix[step : step + 1, :] / column[step : step + 1, :]
        matrix = jnp.where(line > step, matrix - column * scaled, matrix)
    pivots = jnp.sum(jnp.where(lane == line, matrix, 0.0), axis=1, keepdims=True)
    inverse_ref[...] = pltpu.roll(matrix / jnp.sqrt(pivots), LANES - vecs, 1)
    share = vecs // 2
    own_rows = inverse_ref[pl.ds(pl.multiple_of(sub * share, 8), share), :][:, 0:vecs]
    for ref, place in ((mine_ref, sub), (other_ref, 1 - sub)):
        out_ref[:, pl.ds(pl.multiple_of(place * half, LANES), half)] = jnp.dot(
            own_rows, ref[...], precision=lax.Precision.HIGHEST, preferred_element_type=jnp.float32
        )


def basis_of(grams, mine, other, total_rows):
    vecs, half = mine.shape
    return pl.pallas_call(
        functools.partial(basis_kernel, total_rows),
        out_shape=jax.ShapeDtypeStruct((vecs // 2, 2 * half), jnp.float32),
        in_specs=[VMEM_SPEC] * 3,
        out_specs=VMEM_SPEC,
        scratch_shapes=[pltpu.VMEM((vecs, LANES), jnp.float32)],
        compiler_params=params(),
        name="basis",
    )(grams, mine, other)


def exchanges(pairs):
    plans = []
    for distance in range(1, pairs // 2):
        plans.append(([((p + distance) % pairs, p) for p in range(pairs)], None))
    if pairs > 1:
        half = pairs // 2
        last = [(p, p + half) if p % 2 == 0 else (p + half, p) for p in range(half)]
        plans.append((last, sorted(taker for _, taker in last)))
    return plans


def block_moves(pair_moves):
    return [(2 * source + member, 2 * target + member) for source, target in pair_moves for member in range(2)]


def back(moves):
    return [(target, source) for source, target in moves]


def local(embeddings, vectors, boxes, spans, camera):
    rows = embeddings.shape[0]
    half = rows // 2
    vecs = 2 * vectors.shape[0]
    blocks = lax.axis_size("blk")
    devices = 2 * blocks
    sub = lax.axis_index("sub")
    swap = [(0, 1), (1, 0)]
    beside = [(block, block ^ 1) for block in range(blocks)]
    plans = [(block_moves(moves), takers) for moves, takers in exchanges(blocks // 2)]

    def crossed(moves):
        return [(2 * source + 1 - core, 2 * target + core) for source, target in moves for core in range(2)]

    full, to_same, to_cross = packs_of(embeddings, vectors, boxes, spans, camera)
    sent = [
        (lax.ppermute(to_same, "blk", moves), lax.ppermute(to_cross, ("blk", "sub"), crossed(moves)))
        for moves, _ in plans
    ]
    own = (full, lax.ppermute(full, "sub", swap))
    next_to = (lax.ppermute(full, "blk", beside), lax.ppermute(full, ("blk", "sub"), crossed(beside)))
    weigh = functools.partial(tile, rows=half, half_vecs=vecs // 2)
    parts = [
        weigh(own, [own], own_rows=True, own_block=True, col_sums=False)[0],
        weigh(own, [next_to], own_rows=True, col_sums=False)[0],
    ]
    col_sums = None
    for (moves, takers), halves in zip(plans, sent):
        row_sums, sums = weigh(halves, [own, next_to], receivers=takers)
        parts.append(lax.ppermute(row_sums, "blk", back(moves)))
        col_sums = sums if col_sums is None else col_sums + sums

    def piece(place):
        return lax.dynamic_slice_in_dim(col_sums, place * half, half, 1)

    if col_sums is not None:
        parts.append(piece(sub))
        parts.append(lax.ppermute(piece(1 - sub), "sub", swap))
        parts.append(lax.ppermute(piece(2 + sub), "blk", beside))
        parts.append(lax.ppermute(piece(3 - sub), ("blk", "sub"), crossed(beside)))

    image, copies = image_of(parts, vecs, devices)
    image_other = lax.ppermute(image, "sub", swap)
    grams = lax.all_to_all(copies, ("blk", "sub"), 0, 0, tiled=True)
    return basis_of(grams, image, image_other, blocks * rows)


def solution(mesh):
    placed = (
        P(("groups", "blk"), "sub"),
        P("sub", ("groups", "blk")),
        P(None, ("groups", "blk")),
        P(None, ("groups", "blk")),
        P(("groups", "blk")),
    )
    return jax.shard_map(
        local, mesh=mesh, in_specs=placed, out_specs=P("sub", ("groups", "blk")), check_vma=False
    )
```

```python
import functools
import math

import jax
import jax.numpy as jnp
from jax import lax
from jax.experimental import pallas as pl
from jax.experimental.pallas import tpu as pltpu
from jax.sharding import PartitionSpec as P

SHARPNESS = 10.0
HORIZON = 2000.0
MARGIN = 8.0
EPSILON = 1e-06

LOG2E = math.log2(math.e)
COS_SCALE = math.sqrt(SHARPNESS * LOG2E)
GAP_SCALE = LOG2E / HORIZON
BASE = SHARPNESS * LOG2E + 1.0
BARRED_BELOW = BASE - 0.5 * GAP_SCALE

FIELDS = 9
LEFT, RIGHT, BOTTOM, TOP, FIRST, LAST, CAMERA, NORM, AREA = range(FIELDS)
CODE_ROWS = 16
LANES = 128
CHUNK = 256
OUT_ROWS = 40
COST = 1
VMEM_LIMIT = 48 * 1024 * 1024
PACK_VMEM_LIMIT = 63 * 1024 * 1024

NT = (((1,), (1,)), ((), ()))
VMEM_SPEC = pl.BlockSpec(memory_space=pltpu.VMEM)


def params():
    return pltpu.CompilerParams(vmem_limit_bytes=VMEM_LIMIT)


def dot_nt(a, b, precision=None):
    return lax.dot_general(a, b, NT, precision=precision, preferred_element_type=jnp.float32)


def pack_rows(rows, half_vecs):
    return rows + rows // CHUNK * (half_vecs + CODE_ROWS)


def vec_place(total, half_vecs, chunk):
    return pl.ds(pl.multiple_of(total + chunk * half_vecs, 16), half_vecs)


def code_place(total, half_vecs, chunk):
    return pl.ds(pl.multiple_of(total + total // CHUNK * half_vecs + chunk * CODE_ROWS, 16), CODE_ROWS)


def pack_kernel(*refs):
    sources, (full_ref, same_ref, cross_ref), loaded, side_ref, sems = refs[:5], refs[5:8], refs[8:13], refs[13], refs[14]
    emb_ref, vec_ref, boxes_ref, spans_ref, camera_ref = loaded
    sub = lax.axis_index("sub")
    rows = emb_ref.shape[0]
    half = rows // 2
    half_vecs = vec_ref.shape[0]
    halves = ((same_ref, sub), (cross_ref, 1 - sub))
    number = iter(range(sems.shape[0]))

    def start(source, target):
        copy = pltpu.make_async_copy(source, target, sems.at[next(number)])
        copy.start()
        return copy

    loads = [start(source, target) for source, target in zip(sources, loaded)]
    moves = [start(sources[0].at[pl.ds(pl.multiple_of(place * half, half), half)], ref.at[pl.ds(0, half)]) for ref, place in halves]
    moves.append(start(sources[0], full_ref.at[pl.ds(0, rows)]))
    for load in loads:
        load.wait()
    ones = jnp.ones((8, CHUNK), jnp.bfloat16)
    for chunk in range(rows // CHUNK):
        part = pl.ds(chunk * CHUNK, CHUNK)
        codes = []

        def whole(number, low_bits):
            codes.append((number >> low_bits) << low_bits)
            codes.append(number & ((1 << low_bits) - 1))

        boxes, spans = boxes_ref[:, part], spans_ref[:, part]
        for axis in range(2):
            whole(jnp.minimum(boxes[axis : axis + 1], boxes[axis + 2 : axis + 3]), 5)
            whole(jnp.maximum(boxes[axis : axis + 1], boxes[axis + 2 : axis + 3]), 5)
        whole(jnp.minimum(spans[0:1], spans[1:2]), 7)
        whole(jnp.maximum(spans[0:1], spans[1:2]), 7)
        codes.append(camera_ref[:, part])
        codes = [code.astype(jnp.float32) for code in codes]
        values = emb_ref[part, :].astype(jnp.float32)
        square = values * values
        high = square.astype(jnp.bfloat16)
        low = (square - high.astype(jnp.float32)).astype(jnp.bfloat16)
        rest = (dot_nt(ones, high) + dot_nt(ones, low))[0:1]
        for _ in range(3):
            piece = rest.astype(jnp.bfloat16).astype(jnp.float32)
            codes.append(piece)
            rest = rest - piece
        coded = jnp.concatenate(codes, axis=0).astype(jnp.bfloat16)
        side_ref[vec_place(0, half_vecs, chunk), :] = vec_ref[:, part]
        first_code = rows // CHUNK * half_vecs + chunk * CODE_ROWS
        side_ref[first_code : first_code + CODE_ROWS, :] = coded
    side_rows = side_ref.shape[0]
    moves.append(start(side_ref, full_ref.at[pl.ds(rows, side_rows)]))
    vec_rows, code_rows = half // CHUNK * half_vecs, half // CHUNK * CODE_ROWS
    for ref, place in halves:
        vec_start = pl.multiple_of(place * vec_rows, 16)
        code_start = pl.multiple_of(2 * vec_rows + place * code_rows, 16)
        moves.append(start(side_ref.at[pl.ds(vec_start, vec_rows)], ref.at[pl.ds(half, vec_rows)]))
        moves.append(start(side_ref.at[pl.ds(code_start, code_rows)], ref.at[pl.ds(half + vec_rows, code_rows)]))
    for move in moves:
        move.wait()


def packs_of(embeddings, vectors, boxes, spans, camera):
    rows, width = embeddings.shape
    half_vecs = vectors.shape[0]
    sizes = [pack_rows(rows, half_vecs)] + [pack_rows(rows // 2, half_vecs)] * 2
    inputs = (embeddings, vectors, boxes, spans, camera[None, :])
    return pl.pallas_call(
        pack_kernel,
        out_shape=[jax.ShapeDtypeStruct((size, width), jnp.bfloat16) for size in sizes],
        in_specs=[pl.BlockSpec(memory_space=pltpu.HBM)] * 5,
        out_specs=[pl.BlockSpec(memory_space=pltpu.HBM)] * 3,
        scratch_shapes=[pltpu.VMEM(array.shape, array.dtype) for array in inputs]
        + [pltpu.VMEM((sizes[0] - rows, width), jnp.bfloat16), pltpu.SemaphoreType.DMA((13,))],
        compiler_params=pltpu.CompilerParams(vmem_limit_bytes=PACK_VMEM_LIMIT),
        name="pack",
    )(*inputs)


def decode(mine_ref, other_ref, place):
    mine, other = mine_ref[place, :].astype(jnp.float32), other_ref[place, :].astype(jnp.float32)
    numbers = [mine[2 * index : 2 * index + 1] + mine[2 * index + 1 : 2 * index + 2] for index in range(6)]
    left, right, bottom, top, first, last = numbers
    right, top = right + MARGIN, top + MARGIN
    square = jnp.zeros_like(left)
    for index in (15, 14, 13):
        square = square + (mine[index : index + 1] + other[index : index + 1])
    norm = lax.rsqrt(square + EPSILON) * COS_SCALE
    area = (right - left) * (top - bottom)
    return [left, right, bottom, top, first * GAP_SCALE + BASE, last * GAP_SCALE, mine[12:13], norm, area]


def vectors_of(mine_ref, other_ref, place):
    mine, other = mine_ref[place, :].astype(jnp.float32), other_ref[place, :].astype(jnp.float32)
    swapped = lax.axis_index("sub") != 0
    tail = jnp.where(lax.broadcasted_iota(jnp.int32, mine.shape, 0) == 0, 1.0, 0.0)
    ordered = [jnp.where(swapped, other, mine), jnp.where(swapped, mine, other), tail]
    return jnp.concatenate(ordered, axis=0).astype(jnp.bfloat16)


def weights_of(products, row, col, same):
    logit = products * row[NORM] * col[NORM]
    gap = jnp.maximum(col[FIRST] - row[LAST], row[FIRST] - col[LAST])
    width = jnp.maximum(jnp.minimum(row[RIGHT], col[RIGHT]) - jnp.maximum(row[LEFT], col[LEFT]), 0.0)
    height = jnp.maximum(jnp.minimum(row[TOP], col[TOP]) - jnp.maximum(row[BOTTOM], col[BOTTOM]), 0.0)
    inter = width * height
    both = row[AREA] + col[AREA]
    share = (both + inter) * pl.reciprocal(both - inter, approx=True)
    value = jnp.exp2(logit - jnp.maximum(gap, BASE)) * share
    barred = (row[CAMERA] == col[CAMERA]) & (gap < BARRED_BELOW)
    if same is not None:
        barred = barred & jnp.logical_not(same)
    return jnp.where(barred, 0.0, value)


def tile_kernel(blocks, own_rows, own_block, receivers, half_vecs, *refs):
    row_mine_ref, row_other_ref = refs[:2]
    col_refs = [refs[2 + 2 * number : 4 + 2 * number] for number in range(blocks)]
    row_out_ref, col_out_ref, field_ref, spread_ref = refs[2 + 2 * blocks : 6 + 2 * blocks]
    products, weights = refs[6 + 2 * blocks : 8 + 2 * blocks], refs[8 + 2 * blocks :]
    rows = row_out_ref.shape[1]
    sub = lax.axis_index("sub")
    row_total, first_chunk = rows, 0
    row_part = pl.ds(0, rows)
    if own_rows:
        row_total, first_chunk = 2 * rows, sub * (rows // CHUNK)
        row_part = pl.ds(pl.multiple_of(sub * rows, rows), rows)
    row_out_ref[...] = jnp.zeros_like(row_out_ref)

    def block(number, done, row_vecs):
        col_mine_ref, col_other_ref = col_refs[number]
        cols = 2 * rows
        chunks = cols // CHUNK

        def place(step, base=0):
            return pl.ds(pl.multiple_of(base + step * CHUNK, CHUNK), CHUNK)

        def multiply(step, product_ref):
            part = place(step)
            columns = jnp.concatenate([col_mine_ref[part, :], col_other_ref[part, :]], axis=1)
            lines = jnp.concatenate([row_mine_ref[row_part, :], row_other_ref[row_part, :]], axis=1)
            product_ref[...] = dot_nt(lines, columns)

        def weigh(step, product_ref, weight_ref):
            col = decode(col_mine_ref, col_other_ref, code_place(cols, half_vecs, step))
            col = [jnp.broadcast_to(field, (8, CHUNK)) for field in col]
            for first_row in range(0, rows, 16):
                both = []
                for line in (first_row, first_row + 8):
                    row = [
                        jnp.concatenate([spread_ref[field, line : line + 8, :]] * (CHUNK // LANES), axis=1)
                        for field in range(FIELDS)
                    ]
                    same = None
                    if own_block:
                        row_ids = lax.broadcasted_iota(jnp.int32, (8, CHUNK), 0) + (sub * rows + line - step * CHUNK)
                        same = row_ids == lax.broadcasted_iota(jnp.int32, (8, CHUNK), 1)
                    both.append(weights_of(product_ref[line : line + 8, :], row, col, same))
                weight_ref[first_row : first_row + 16, :] = jnp.concatenate(both, axis=0).astype(jnp.bfloat16)

        def total(step, weight_ref):
            col_vecs = vectors_of(col_mine_ref, col_other_ref, vec_place(cols, half_vecs, step))
            row_out_ref[...] += dot_nt(col_vecs, weight_ref[...])[0:OUT_ROWS]
            if col_out_ref is not None:
                col_out_ref[:, place(step, done)] = jnp.dot(
                    row_vecs, weight_ref[...], preferred_element_type=jnp.float32
                )[0:OUT_ROWS]

        def steps(index, carry):
            for parity in range(2):
                step = 2 * index + parity
                multiply(lax.rem(step + 1, chunks), products[1 - parity])
                weigh(step, products[parity], weights[parity])
                total(lax.rem(step + chunks - 1, chunks), weights[1 - parity])
            return carry

        multiply(0, products[0])
        weights[1][...] = jnp.zeros_like(weights[1])
        lax.fori_loop(0, chunks // 2, steps, 0)
        total(chunks - 1, weights[1])

    def compute():
        row_vecs = []
        for chunk in range(rows // CHUNK):
            codes = code_place(row_total, half_vecs, first_chunk + chunk)
            for field, values in enumerate(decode(row_mine_ref, row_other_ref, codes)):
                field_ref[field : field + 1, chunk * CHUNK : (chunk + 1) * CHUNK] = values
            row_vecs.append(vectors_of(row_mine_ref, row_other_ref, vec_place(row_total, half_vecs, first_chunk + chunk)))
        row_vecs = jnp.concatenate(row_vecs, axis=1)
        turned = field_ref[...].T
        for field in range(FIELDS):
            spread_ref[field] = jnp.broadcast_to(turned[:, field : field + 1], (rows, LANES))
        for number in range(blocks):
            block(number, number * 2 * rows, row_vecs)

    if receivers is None:
        compute()
        return
    pair = lax.axis_index("blk") // 2
    takes_part = functools.reduce(jnp.logical_or, [pair == one for one in receivers])

    @pl.when(takes_part)
    def _():
        compute()

    @pl.when(jnp.logical_not(takes_part))
    def _():
        col_out_ref[...] = jnp.zeros_like(col_out_ref)


def tile(row, columns, rows, half_vecs, own_rows=False, own_block=False, col_sums=True, receivers=None):
    features = 2 * row[0].shape[1]
    cols = 2 * rows * len(columns)
    shapes = [jax.ShapeDtypeStruct((OUT_ROWS, rows), jnp.float32)]
    if col_sums:
        shapes.append(jax.ShapeDtypeStruct((OUT_ROWS, cols), jnp.float32))

    def body(*refs):
        inputs = 2 + 2 * len(columns)
        refs = list(refs)
        if not col_sums:
            refs.insert(inputs + 1, None)
        tile_kernel(len(columns), own_rows, own_block, receivers, half_vecs, *refs)

    pairs = rows * cols
    return pl.pallas_call(
        body,
        out_shape=shapes,
        in_specs=[VMEM_SPEC] * (2 + 2 * len(columns)),
        out_specs=[VMEM_SPEC] * len(shapes),
        scratch_shapes=[
            pltpu.VMEM((LANES, rows), jnp.float32),
            pltpu.VMEM((FIELDS, rows, LANES), jnp.float32),
            pltpu.VMEM((rows, CHUNK), jnp.float32),
            pltpu.VMEM((rows, CHUNK), jnp.float32),
            pltpu.VMEM((rows, CHUNK), jnp.bfloat16),
            pltpu.VMEM((rows, CHUNK), jnp.bfloat16),
        ],
        cost_estimate=pl.CostEstimate(
            flops=COST, bytes_accessed=COST, transcendentals=0
        ),
        compiler_params=params(),
        name="tile",
    )(*row, *[array for part in columns for array in part])


def image_kernel(*refs):
    parts, image_ref, grams_ref = refs[:-2], refs[-2], refs[-1]
    total = parts[0][...]
    for part in parts[1:]:
        total = total + part[...]
    vecs = image_ref.shape[0]
    image = total[0:vecs] / total[vecs : vecs + 1]
    image_ref[...] = image
    packed = jnp.zeros((8, LANES), jnp.float32)
    for piece in range(LANES // vecs):
        shifted = [image]
        if piece > 0:
            shifted.insert(0, jnp.zeros((piece * vecs, image.shape[1]), jnp.float32))
        if piece < LANES // vecs - 1:
            shifted.append(jnp.zeros((LANES - (piece + 1) * vecs, image.shape[1]), jnp.float32))
        packed = packed + dot_nt(image[8 * piece : 8 * piece + 8], jnp.concatenate(shifted, axis=0), lax.Precision.HIGHEST)
    for copy in range(grams_ref.shape[0]):
        grams_ref[copy] = packed


def image_of(parts, vecs, copies):
    cols = parts[0].shape[1]
    return pl.pallas_call(
        image_kernel,
        out_shape=[
            jax.ShapeDtypeStruct((vecs, cols), jnp.float32),
            jax.ShapeDtypeStruct((copies, 8, LANES), jnp.float32),
        ],
        in_specs=[VMEM_SPEC] * len(parts),
        out_specs=[VMEM_SPEC] * 2,
        compiler_params=params(),
        name="image",
    )(*parts)


def basis_kernel(total_rows, grams_ref, mine_ref, other_ref, out_ref, inverse_ref):
    vecs, half = mine_ref.shape
    sub = lax.axis_index("sub")
    packed = jnp.sum(grams_ref[...], axis=0) / total_rows
    lane = lax.broadcasted_iota(jnp.int32, (vecs, LANES), 1)
    line = lax.broadcasted_iota(jnp.int32, (vecs, LANES), 0)
    pieces = [packed] + [pltpu.roll(packed, LANES - piece * vecs, 1) for piece in range(1, LANES // vecs)]
    matrix = jnp.where(lane < vecs, jnp.concatenate(pieces, axis=0), 0.0)
    matrix = jnp.where(lane == line + vecs, 1.0, matrix)
    for step in range(vecs - 1):
        column = jnp.broadcast_to(matrix[:, step : step + 1], (vecs, LANES))
        scaled = matrix[step : step + 1, :] / column[step : step + 1, :]
        matrix = jnp.where(line > step, matrix - column * scaled, matrix)
    pivots = jnp.sum(jnp.where(lane == line, matrix, 0.0), axis=1, keepdims=True)
    inverse_ref[...] = pltpu.roll(matrix / jnp.sqrt(pivots), LANES - vecs, 1)
    share = vecs // 2
    own_rows = inverse_ref[pl.ds(pl.multiple_of(sub * share, 8), share), :][:, 0:vecs]
    for ref, place in ((mine_ref, sub), (other_ref, 1 - sub)):
        out_ref[:, pl.ds(pl.multiple_of(place * half, LANES), half)] = jnp.dot(
            own_rows, ref[...], precision=lax.Precision.HIGHEST, preferred_element_type=jnp.float32
        )


def basis_of(grams, mine, other, total_rows):
    vecs, half = mine.shape
    return pl.pallas_call(
        functools.partial(basis_kernel, total_rows),
        out_shape=jax.ShapeDtypeStruct((vecs // 2, 2 * half), jnp.float32),
        in_specs=[VMEM_SPEC] * 3,
        out_specs=VMEM_SPEC,
        scratch_shapes=[pltpu.VMEM((vecs, LANES), jnp.float32)],
        compiler_params=params(),
        name="basis",
    )(grams, mine, other)


def exchanges(pairs):
    plans = []
    for distance in range(1, pairs // 2):
        plans.append(([((p + distance) % pairs, p) for p in range(pairs)], None))
    if pairs > 1:
        half = pairs // 2
        last = [(p, p + half) if p % 2 == 0 else (p + half, p) for p in range(half)]
        plans.append((last, sorted(taker for _, taker in last)))
    return plans


def block_moves(pair_moves):
    return [(2 * source + member, 2 * target + member) for source, target in pair_moves for member in range(2)]


def back(moves):
    return [(target, source) for source, target in moves]


def local(embeddings, vectors, boxes, spans, camera):
    rows = embeddings.shape[0]
    half = rows // 2
    vecs = 2 * vectors.shape[0]
    blocks = lax.axis_size("blk")
    devices = 2 * blocks
    sub = lax.axis_index("sub")
    swap = [(0, 1), (1, 0)]
    beside = [(block, block ^ 1) for block in range(blocks)]
    plans = [(block_moves(moves), takers) for moves, takers in exchanges(blocks // 2)]

    def crossed(moves):
        return [(2 * source + 1 - core, 2 * target + core) for source, target in moves for core in range(2)]

    full, to_same, to_cross = packs_of(embeddings, vectors, boxes, spans, camera)
    sent = [
        (lax.ppermute(to_same, "blk", moves), lax.ppermute(to_cross, ("blk", "sub"), crossed(moves)))
        for moves, _ in plans
    ]
    own = (full, lax.ppermute(full, "sub", swap))
    weigh = functools.partial(tile, rows=half, half_vecs=vecs // 2)
    own_sums = weigh(own, [own], own_rows=True, own_block=True, col_sums=False)[0]
    beside_mine = lax.ppermute(full, "blk", beside)
    own_sums, beside_mine, sent[:1] = lax.optimization_barrier((own_sums, beside_mine, sent[:1]))
    next_to = (beside_mine, lax.ppermute(beside_mine, "sub", swap))
    parts = [own_sums, weigh(own, [next_to], own_rows=True, col_sums=False)[0]]
    col_sums = None
    for (moves, takers), halves in zip(plans, sent):
        if col_sums is not None:
            halves, col_sums = lax.optimization_barrier((halves, col_sums))
        row_sums, sums = weigh(halves, [own, next_to], receivers=takers)
        parts.append(lax.ppermute(row_sums, "blk", back(moves)))
        col_sums = sums if col_sums is None else col_sums + sums

    def piece(place):
        return lax.dynamic_slice_in_dim(col_sums, place * half, half, 1)

    if col_sums is not None:
        parts.append(piece(sub))
        parts.append(lax.ppermute(piece(1 - sub), "sub", swap))
        parts.append(lax.ppermute(piece(2 + sub), "blk", beside))
        parts.append(lax.ppermute(piece(3 - sub), ("blk", "sub"), crossed(beside)))

    image, copies = image_of(parts, vecs, devices)
    image_other = lax.ppermute(image, "sub", swap)
    grams = lax.all_to_all(copies, ("blk", "sub"), 0, 0, tiled=True)
    return basis_of(grams, image, image_other, blocks * rows)


def solution(mesh):
    placed = (
        P(("groups", "blk"), "sub"),
        P("sub", ("groups", "blk")),
        P(None, ("groups", "blk")),
        P(None, ("groups", "blk")),
        P(("groups", "blk")),
    )
    return jax.shard_map(
        local, mesh=mesh, in_specs=placed, out_specs=P("sub", ("groups", "blk")), check_vma=False
    )
```

```python
import functools
import math

import jax
import jax.numpy as jnp
from jax import lax
from jax.experimental import pallas as pl
from jax.experimental.pallas import tpu as pltpu
from jax.sharding import PartitionSpec as P

SHARPNESS = 10.0
HORIZON = 2000.0
MARGIN = 8.0
EPSILON = 1e-06

LOG2E = math.log2(math.e)
COS_SCALE = math.sqrt(SHARPNESS * LOG2E)
GAP_SCALE = LOG2E / HORIZON
BASE = SHARPNESS * LOG2E + 1.0
BARRED_BELOW = BASE - 0.5 * GAP_SCALE

FIELDS = 9
LEFT, RIGHT, BOTTOM, TOP, FIRST, LAST, CAMERA, NORM, AREA = range(FIELDS)
CODE_ROWS = 16
LANES = 128
CHUNK = 256
OUT_ROWS = 40
COST = 1
SWAPS = 2
VMEM_LIMIT = 48 * 1024 * 1024

NT = (((1,), (1,)), ((), ()))
VMEM_SPEC = pl.BlockSpec(memory_space=pltpu.VMEM)


def params():
    return pltpu.CompilerParams(vmem_limit_bytes=VMEM_LIMIT)


def dot_nt(a, b, precision=None):
    return lax.dot_general(a, b, NT, precision=precision, preferred_element_type=jnp.float32)


def pack_rows(half, vecs):
    return half + vecs + CODE_ROWS


def pack_kernel(emb_ref, emb_other_ref, vec_ref, vec_other_ref, meta_ref, own_ref, mine_ref, code_ref):
    sub = lax.axis_index("sub")
    rows, width = emb_ref.shape
    half = rows // 2
    half_vecs = vec_ref.shape[0]
    ones = jnp.ones((8, width), jnp.bfloat16)
    for start in range(0, rows, CHUNK):
        part = pl.ds(start, CHUNK)
        codes = []

        def whole(number, low_bits):
            codes.append((number >> low_bits) << low_bits)
            codes.append(number & ((1 << low_bits) - 1))

        boxes, spans = meta_ref[0:4, part], meta_ref[4:6, part]
        for axis in range(2):
            whole(jnp.minimum(boxes[axis : axis + 1], boxes[axis + 2 : axis + 3]), 5)
            whole(jnp.maximum(boxes[axis : axis + 1], boxes[axis + 2 : axis + 3]), 5)
        whole(jnp.minimum(spans[0:1], spans[1:2]), 7)
        whole(jnp.maximum(spans[0:1], spans[1:2]), 7)
        codes.append(meta_ref[6:7, part])
        codes = [code.astype(jnp.float32) for code in codes]
        rest = jnp.zeros((8, CHUNK), jnp.float32)
        for ref in (emb_ref, emb_other_ref):
            values = ref[part, :].astype(jnp.float32)
            square = values * values
            high = square.astype(jnp.bfloat16)
            low = (square - high.astype(jnp.float32)).astype(jnp.bfloat16)
            rest = rest + (dot_nt(ones, high) + dot_nt(ones, low))
        rest = rest[0:1]
        for _ in range(3):
            piece = rest.astype(jnp.bfloat16).astype(jnp.float32)
            codes.append(piece)
            rest = rest - piece
        code_ref[:, part] = jnp.concatenate(codes, axis=0).astype(jnp.bfloat16)
    size = mine_ref.shape[0]
    targets = [(own_ref, 0, sub), (own_ref, size, 1 - sub), (mine_ref, 0, sub)]
    for ref, base, place in targets:
        source = pl.ds(pl.multiple_of(place * half, half), half)
        sides = ((emb_ref, vec_ref, sub), (emb_other_ref, vec_other_ref, 1 - sub))
        for values_ref, vectors_ref, side in sides:
            ref[base : base + half, pl.ds(pl.multiple_of(side * width, width), width)] = values_ref[source, :]
            first_vec = pl.multiple_of(base + half + side * half_vecs, 16)
            ref[pl.ds(first_vec, half_vecs), :] = vectors_ref[:, source]
        first_code = base + half + 2 * half_vecs
        ref[first_code : first_code + CODE_ROWS, :] = code_ref[:, source]


def packs_of(embeddings, emb_other, vectors, vec_other, meta):
    rows, width = embeddings.shape
    half, features = rows // 2, 2 * width
    assert half == features
    size = pack_rows(half, 2 * vectors.shape[0])
    return pl.pallas_call(
        pack_kernel,
        out_shape=[jax.ShapeDtypeStruct((count * size, features), jnp.bfloat16) for count in (2, 1)],
        in_specs=[VMEM_SPEC] * 5,
        out_specs=[VMEM_SPEC] * 2,
        scratch_shapes=[pltpu.VMEM((CODE_ROWS, rows), jnp.bfloat16)],
        compiler_params=params(),
        name="pack",
    )(embeddings, emb_other, vectors, vec_other, meta)


def decode(codes):
    codes = codes.astype(jnp.float32)
    numbers = [codes[2 * index : 2 * index + 1] + codes[2 * index + 1 : 2 * index + 2] for index in range(6)]
    left, right, bottom, top, first, last = numbers
    right, top = right + MARGIN, top + MARGIN
    square = codes[15:16] + codes[14:15] + codes[13:14]
    norm = lax.rsqrt(square + EPSILON) * COS_SCALE
    area = (right - left) * (top - bottom)
    return [left, right, bottom, top, first * GAP_SCALE + BASE, last * GAP_SCALE, codes[12:13], norm, area]


def with_ones(vectors):
    shape = (CODE_ROWS, vectors.shape[1])
    tail = jnp.where(lax.broadcasted_iota(jnp.int32, shape, 0) == 0, 1.0, 0.0)
    return jnp.concatenate([vectors, tail.astype(jnp.bfloat16)], axis=0)


def weights_of(products, row, col, same):
    logit = products * row[NORM] * col[NORM]
    gap = jnp.maximum(col[FIRST] - row[LAST], row[FIRST] - col[LAST])
    width = jnp.maximum(jnp.minimum(row[RIGHT], col[RIGHT]) - jnp.maximum(row[LEFT], col[LEFT]), 0.0)
    height = jnp.maximum(jnp.minimum(row[TOP], col[TOP]) - jnp.maximum(row[BOTTOM], col[BOTTOM]), 0.0)
    inter = width * height
    both = row[AREA] + col[AREA]
    share = (both + inter) * pl.reciprocal(both - inter, approx=True)
    value = jnp.exp2(logit - jnp.maximum(gap, BASE)) * share
    barred = (row[CAMERA] == col[CAMERA]) & (gap < BARRED_BELOW)
    if same is not None:
        barred = barred & jnp.logical_not(same)
    return jnp.where(barred, 0.0, value)


def tile_kernel(blocks, own_block, receivers, vecs, *refs):
    row_ref, col_refs = refs[0], refs[1 : 1 + blocks]
    row_out_ref, col_out_ref, field_ref, spread_ref = refs[1 + blocks : 5 + blocks]
    products, weights = refs[5 + blocks : 7 + blocks], refs[7 + blocks :]
    rows = row_out_ref.shape[1]
    size = row_ref.shape[0]
    per_pack = rows // CHUNK
    row_out_ref[...] = jnp.zeros_like(row_out_ref)

    def block(col_ref, done, row_vecs):
        chunks = col_ref.shape[0] // size * per_pack

        def within(step):
            pack, chunk = step // per_pack, lax.rem(step, per_pack)
            return pack * size, pl.multiple_of(chunk * CHUNK, CHUNK)

        def multiply(step, product_ref):
            base, start = within(step)
            columns = col_ref[pl.ds(pl.multiple_of(base + start, 16), CHUNK), :]
            product_ref[...] = dot_nt(row_ref[0:rows, :], columns)

        def weigh(step, product_ref, weight_ref):
            base, start = within(step)
            code_part = pl.ds(pl.multiple_of(base + rows + vecs, 16), CODE_ROWS)
            col = decode(col_ref[code_part, pl.ds(start, CHUNK)])
            col = [jnp.broadcast_to(field, (8, CHUNK)) for field in col]
            for first_row in range(0, rows, 16):
                both = []
                for line in (first_row, first_row + 8):
                    row = [
                        jnp.concatenate([spread_ref[field, line : line + 8, :]] * (CHUNK // LANES), axis=1)
                        for field in range(FIELDS)
                    ]
                    same = None
                    if own_block:
                        row_ids = lax.broadcasted_iota(jnp.int32, (8, CHUNK), 0) + (line - step * CHUNK)
                        same = row_ids == lax.broadcasted_iota(jnp.int32, (8, CHUNK), 1)
                    both.append(weights_of(product_ref[line : line + 8, :], row, col, same))
                weight_ref[first_row : first_row + 16, :] = jnp.concatenate(both, axis=0).astype(jnp.bfloat16)

        def total(step, weight_ref):
            base, start = within(step)
            vec_part = pl.ds(pl.multiple_of(base + rows, 16), vecs)
            col_vecs = with_ones(col_ref[vec_part, pl.ds(start, CHUNK)])
            row_out_ref[...] += dot_nt(col_vecs, weight_ref[...])[0:OUT_ROWS]
            if col_out_ref is not None:
                col_out_ref[:, pl.ds(pl.multiple_of(done + step * CHUNK, CHUNK), CHUNK)] = jnp.dot(
                    row_vecs, weight_ref[...], preferred_element_type=jnp.float32
                )[0:OUT_ROWS]

        def steps(index, carry):
            for parity in range(2):
                step = 2 * index + parity
                multiply(lax.rem(step + 1, chunks), products[1 - parity])
                weigh(step, products[parity], weights[parity])
                total(lax.rem(step + chunks - 1, chunks), weights[1 - parity])
            return carry

        multiply(0, products[0])
        weights[1][...] = jnp.zeros_like(weights[1])
        lax.fori_loop(0, chunks // 2, steps, 0)
        total(chunks - 1, weights[1])

    def compute():
        for field, values in enumerate(decode(row_ref[rows + vecs : rows + vecs + CODE_ROWS, :])):
            field_ref[field : field + 1, :] = values
        turned = field_ref[...].T
        for field in range(FIELDS):
            spread_ref[field] = jnp.broadcast_to(turned[:, field : field + 1], (rows, LANES))
        row_vecs = with_ones(row_ref[rows : rows + vecs, :])
        done = 0
        for col_ref in col_refs:
            block(col_ref, done, row_vecs)
            done += col_ref.shape[0] // size * rows

    if receivers is None:
        compute()
        return
    pair = lax.axis_index("blk") // 2
    takes_part = functools.reduce(jnp.logical_or, [pair == one for one in receivers])

    @pl.when(takes_part)
    def _():
        compute()

    @pl.when(jnp.logical_not(takes_part))
    def _():
        col_out_ref[...] = jnp.zeros_like(col_out_ref)


def tile(row, columns, vecs, own_block=False, col_sums=True, receivers=None):
    size, rows = row.shape
    cols = sum(part.shape[0] // size for part in columns) * rows
    shapes = [jax.ShapeDtypeStruct((OUT_ROWS, rows), jnp.float32)]
    if col_sums:
        shapes.append(jax.ShapeDtypeStruct((OUT_ROWS, cols), jnp.float32))

    def body(*refs):
        refs = list(refs)
        if not col_sums:
            refs.insert(2 + len(columns), None)
        tile_kernel(len(columns), own_block, receivers, vecs, *refs)

    return pl.pallas_call(
        body,
        out_shape=shapes,
        in_specs=[VMEM_SPEC] * (1 + len(columns)),
        out_specs=[VMEM_SPEC] * len(shapes),
        scratch_shapes=[
            pltpu.VMEM((LANES, rows), jnp.float32),
            pltpu.VMEM((FIELDS, rows, LANES), jnp.float32),
            pltpu.VMEM((rows, CHUNK), jnp.float32),
            pltpu.VMEM((rows, CHUNK), jnp.float32),
            pltpu.VMEM((rows, CHUNK), jnp.bfloat16),
            pltpu.VMEM((rows, CHUNK), jnp.bfloat16),
        ],
        cost_estimate=pl.CostEstimate(flops=COST, bytes_accessed=COST, transcendentals=0),
        compiler_params=params(),
        name="tile",
    )(row, *columns)


def image_kernel(*refs):
    parts, image_ref, grams_ref = refs[:-2], refs[-2], refs[-1]
    total = parts[0][...]
    for part in parts[1:]:
        total = total + part[...]
    vecs = image_ref.shape[0]
    image = total[0:vecs] / total[vecs : vecs + 1]
    image_ref[...] = image
    packed = jnp.zeros((8, LANES), jnp.float32)
    for piece in range(LANES // vecs):
        shifted = [image]
        if piece > 0:
            shifted.insert(0, jnp.zeros((piece * vecs, image.shape[1]), jnp.float32))
        if piece < LANES // vecs - 1:
            shifted.append(jnp.zeros((LANES - (piece + 1) * vecs, image.shape[1]), jnp.float32))
        packed = packed + dot_nt(image[8 * piece : 8 * piece + 8], jnp.concatenate(shifted, axis=0), lax.Precision.HIGHEST)
    for copy in range(grams_ref.shape[0]):
        grams_ref[copy] = packed


def image_of(parts, vecs, copies):
    cols = parts[0].shape[1]
    return pl.pallas_call(
        image_kernel,
        out_shape=[
            jax.ShapeDtypeStruct((vecs, cols), jnp.float32),
            jax.ShapeDtypeStruct((copies, 8, LANES), jnp.float32),
        ],
        in_specs=[VMEM_SPEC] * len(parts),
        out_specs=[VMEM_SPEC] * 2,
        compiler_params=params(),
        name="image",
    )(*parts)


def basis_kernel(total_rows, grams_ref, mine_ref, other_ref, out_ref, inverse_ref):
    vecs, half = mine_ref.shape
    sub = lax.axis_index("sub")
    packed = jnp.sum(grams_ref[...], axis=0) / total_rows
    lane = lax.broadcasted_iota(jnp.int32, (vecs, LANES), 1)
    line = lax.broadcasted_iota(jnp.int32, (vecs, LANES), 0)
    pieces = [packed] + [pltpu.roll(packed, LANES - piece * vecs, 1) for piece in range(1, LANES // vecs)]
    matrix = jnp.where(lane < vecs, jnp.concatenate(pieces, axis=0), 0.0)
    matrix = jnp.where(lane == line + vecs, 1.0, matrix)
    for step in range(vecs - 1):
        column = jnp.broadcast_to(matrix[:, step : step + 1], (vecs, LANES))
        scaled = matrix[step : step + 1, :] / column[step : step + 1, :]
        matrix = jnp.where(line > step, matrix - column * scaled, matrix)
    pivots = jnp.sum(jnp.where(lane == line, matrix, 0.0), axis=1, keepdims=True)
    inverse_ref[...] = pltpu.roll(matrix / jnp.sqrt(pivots), LANES - vecs, 1)
    share = vecs // 2
    own_rows = inverse_ref[pl.ds(pl.multiple_of(sub * share, 8), share), :][:, 0:vecs]
    for ref, place in ((mine_ref, sub), (other_ref, 1 - sub)):
        out_ref[:, pl.ds(pl.multiple_of(place * half, LANES), half)] = jnp.dot(
            own_rows, ref[...], precision=lax.Precision.HIGHEST, preferred_element_type=jnp.float32
        )


def basis_of(grams, mine, other, total_rows):
    vecs, half = mine.shape
    return pl.pallas_call(
        functools.partial(basis_kernel, total_rows),
        out_shape=jax.ShapeDtypeStruct((vecs // 2, 2 * half), jnp.float32),
        in_specs=[VMEM_SPEC] * 3,
        out_specs=VMEM_SPEC,
        scratch_shapes=[pltpu.VMEM((vecs, LANES), jnp.float32)],
        compiler_params=params(),
        name="basis",
    )(grams, mine, other)


def exchanges(pairs):
    plans = []
    for distance in range(1, pairs // 2):
        plans.append(([((p + distance) % pairs, p) for p in range(pairs)], None))
    if pairs > 1:
        half = pairs // 2
        last = [(p, p + half) if p % 2 == 0 else (p + half, p) for p in range(half)]
        plans.append((last, sorted(taker for _, taker in last)))
    return plans


def block_moves(pair_moves):
    return [(2 * source + member, 2 * target + member) for source, target in pair_moves for member in range(2)]


def back(moves):
    return [(target, source) for source, target in moves]


def local(embeddings, vectors, boxes, spans, camera):
    rows = embeddings.shape[0]
    half = rows // 2
    vecs = 2 * vectors.shape[0]
    blocks = lax.axis_size("blk")
    devices = 2 * blocks
    swap = [(0, 1), (1, 0)]
    beside = [(block, block ^ 1) for block in range(blocks)]
    plans = [(block_moves(moves), takers) for moves, takers in exchanges(blocks // 2)]

    def crossed(moves):
        return [(2 * source + 1 - core, 2 * target + core) for source, target in moves for core in range(2)]

    emb_other = lax.ppermute(embeddings, "sub", swap)
    vec_other = lax.ppermute(vectors, "sub", swap)
    meta = jnp.concatenate([boxes, spans, camera[None, :]], axis=0)
    own, mine = packs_of(embeddings, emb_other, vectors, vec_other, meta)
    sent = [lax.ppermute(mine, "blk", moves) for moves, _ in plans]
    beside_mine = lax.ppermute(mine, "blk", beside)
    weigh = functools.partial(tile, vecs=vecs)
    own_sums = weigh(mine, [own], own_block=True, col_sums=False)[0]
    own_sums, beside_mine, sent[:1] = lax.optimization_barrier((own_sums, beside_mine, sent[:1]))
    cut = beside_mine.shape[0] // SWAPS // 16 * 16
    shares = [beside_mine[at * cut : (at + 1) * cut if at < SWAPS - 1 else None] for at in range(SWAPS)]
    next_to = jnp.concatenate([beside_mine] + [lax.ppermute(share, "sub", swap) for share in shares], axis=0)
    parts = [own_sums, weigh(mine, [next_to], col_sums=False)[0]]
    col_sums = None
    for (moves, takers), pack in zip(plans, sent):
        if col_sums is not None:
            pack, col_sums = lax.optimization_barrier((pack, col_sums))
        row_sums, sums = weigh(pack, [own, next_to], receivers=takers)
        parts.append(lax.ppermute(row_sums, "blk", back(moves)))
        col_sums = sums if col_sums is None else col_sums + sums
    if col_sums is not None:
        pieces = [col_sums[:, place * half : (place + 1) * half] for place in range(4)]
        parts.append(pieces[0])
        parts.append(lax.ppermute(pieces[1], "sub", swap))
        parts.append(lax.ppermute(pieces[2], "blk", beside))
        parts.append(lax.ppermute(pieces[3], ("blk", "sub"), crossed(beside)))

    image, copies = image_of(parts, vecs, devices)
    image_other = lax.ppermute(image, "sub", swap)
    grams = lax.all_to_all(copies, ("blk", "sub"), 0, 0, tiled=True)
    return basis_of(grams, image, image_other, blocks * rows)


def solution(mesh):
    placed = (
        P(("groups", "blk"), "sub"),
        P("sub", ("groups", "blk")),
        P(None, ("groups", "blk")),
        P(None, ("groups", "blk")),
        P(("groups", "blk")),
    )
    return jax.shard_map(
        local, mesh=mesh, in_specs=placed, out_specs=P("sub", ("groups", "blk")), check_vma=False
    )
```

```python
import functools
import math

import jax
import jax.numpy as jnp
from jax import lax
from jax.experimental import pallas as pl
from jax.experimental.pallas import tpu as pltpu
from jax.sharding import PartitionSpec as P

SHARPNESS = 10.0
HORIZON = 2000.0
MARGIN = 8.0
EPSILON = 1e-06

LOG2E = math.log2(math.e)
COS_SCALE = math.sqrt(SHARPNESS * LOG2E)
GAP_SCALE = LOG2E / HORIZON
BASE = SHARPNESS * LOG2E + 1.0
BARRED_BELOW = BASE - 0.5 * GAP_SCALE

FIELDS = 9
LEFT, RIGHT, BOTTOM, TOP, FIRST, LAST, CAMERA, NORM, AREA = range(FIELDS)
CODE_ROWS = 16
LANES = 128
CHUNK = 256
OUT_ROWS = 40
COST = 1
SWAPS = 2
VMEM_LIMIT = 48 * 1024 * 1024

NT = (((1,), (1,)), ((), ()))
VMEM_SPEC = pl.BlockSpec(memory_space=pltpu.VMEM)


def params():
    return pltpu.CompilerParams(vmem_limit_bytes=VMEM_LIMIT)


def dot_nt(a, b, precision=None):
    return lax.dot_general(a, b, NT, precision=precision, preferred_element_type=jnp.float32)


def pack_rows(half, vecs):
    return half + vecs + CODE_ROWS


def pack_kernel(emb_mine_ref, emb_rest_ref, emb_other_ref, vec_other_ref, meta_ref, own_ref, mine_ref, code_ref):
    sub = lax.axis_index("sub")
    half, width = emb_mine_ref.shape
    half_vecs = vec_other_ref.shape[0]
    size = mine_ref.shape[0]
    ones = jnp.ones((8, width), jnp.bfloat16)
    for base, emb_ref, place in ((0, emb_mine_ref, sub), (size, emb_rest_ref, 1 - sub)):
        first = pl.multiple_of(place * half, half)
        for start in range(0, half, CHUNK):
            part = pl.ds(first + start, CHUNK)
            codes = []

            def whole(number, unit):
                high = jnp.floor(number * (1.0 / unit)) * unit
                codes.append(high)
                codes.append(number - high)

            meta = meta_ref[half_vecs:, part]
            for axis in range(2):
                whole(jnp.minimum(meta[axis : axis + 1], meta[axis + 2 : axis + 3]), 32.0)
                whole(jnp.maximum(meta[axis : axis + 1], meta[axis + 2 : axis + 3]), 32.0)
            whole(jnp.minimum(meta[4:5], meta[5:6]), 128.0)
            whole(jnp.maximum(meta[4:5], meta[5:6]), 128.0)
            codes.append(meta[6:7])
            rest = jnp.zeros((8, CHUNK), jnp.float32)
            for values in (emb_ref[start : start + CHUNK, :], emb_other_ref[part, :]):
                values = values.astype(jnp.float32)
                square = values * values
                high = square.astype(jnp.bfloat16)
                low = (square - high.astype(jnp.float32)).astype(jnp.bfloat16)
                rest = rest + (dot_nt(ones, high) + dot_nt(ones, low))
            rest = rest[0:1]
            for _ in range(3):
                piece = rest.astype(jnp.bfloat16).astype(jnp.float32)
                codes.append(piece)
                rest = rest - piece
            code_ref[:, start : start + CHUNK] = jnp.concatenate(codes, axis=0).astype(jnp.bfloat16)
        source = pl.ds(first, half)
        refs = [(own_ref, base)] + ([(mine_ref, 0)] if base == 0 else [])
        sides = (
            (emb_ref[...], meta_ref[0:half_vecs, source].astype(jnp.bfloat16), sub),
            (emb_other_ref[source, :], vec_other_ref[:, source], 1 - sub),
        )
        for ref, top in refs:
            for values, vectors, side in sides:
                ref[top : top + half, pl.ds(pl.multiple_of(side * width, width), width)] = values
                ref[pl.ds(pl.multiple_of(top + half + side * half_vecs, 16), half_vecs), :] = vectors
            first_code = top + half + 2 * half_vecs
            ref[first_code : first_code + CODE_ROWS, :] = code_ref[...]


def packs_of(emb_mine, emb_rest, emb_other, vec_other, meta):
    half, width = emb_mine.shape
    features = 2 * width
    assert half == features
    size = pack_rows(half, 2 * vec_other.shape[0])
    return pl.pallas_call(
        pack_kernel,
        out_shape=[jax.ShapeDtypeStruct((count * size, features), jnp.bfloat16) for count in (2, 1)],
        in_specs=[VMEM_SPEC] * 5,
        out_specs=[VMEM_SPEC] * 2,
        scratch_shapes=[pltpu.VMEM((CODE_ROWS, half), jnp.bfloat16)],
        compiler_params=params(),
        name="pack",
    )(emb_mine, emb_rest, emb_other, vec_other, meta)


def decode(codes):
    codes = codes.astype(jnp.float32)
    numbers = [codes[2 * index : 2 * index + 1] + codes[2 * index + 1 : 2 * index + 2] for index in range(6)]
    left, right, bottom, top, first, last = numbers
    right, top = right + MARGIN, top + MARGIN
    square = codes[15:16] + codes[14:15] + codes[13:14]
    norm = lax.rsqrt(square + EPSILON) * COS_SCALE
    area = (right - left) * (top - bottom)
    return [left, right, bottom, top, first * GAP_SCALE + BASE, last * GAP_SCALE, codes[12:13], norm, area]


def with_ones(vectors):
    shape = (CODE_ROWS, vectors.shape[1])
    tail = jnp.where(lax.broadcasted_iota(jnp.int32, shape, 0) == 0, 1.0, 0.0)
    return jnp.concatenate([vectors, tail.astype(jnp.bfloat16)], axis=0)


def weights_of(products, row, col, same):
    logit = products * row[NORM] * col[NORM]
    gap = jnp.maximum(col[FIRST] - row[LAST], row[FIRST] - col[LAST])
    width = jnp.maximum(jnp.minimum(row[RIGHT], col[RIGHT]) - jnp.maximum(row[LEFT], col[LEFT]), 0.0)
    height = jnp.maximum(jnp.minimum(row[TOP], col[TOP]) - jnp.maximum(row[BOTTOM], col[BOTTOM]), 0.0)
    inter = width * height
    both = row[AREA] + col[AREA]
    share = (both + inter) * pl.reciprocal(both - inter, approx=True)
    value = jnp.exp2(logit - jnp.maximum(gap, BASE)) * share
    barred = (row[CAMERA] == col[CAMERA]) & (gap < BARRED_BELOW)
    if same is not None:
        barred = barred & jnp.logical_not(same)
    return jnp.where(barred, 0.0, value)


def tile_kernel(blocks, own_block, receivers, vecs, *refs):
    row_ref, col_refs = refs[0], refs[1 : 1 + blocks]
    row_out_ref, col_out_ref, field_ref, spread_ref = refs[1 + blocks : 5 + blocks]
    products, weights = refs[5 + blocks : 7 + blocks], refs[7 + blocks :]
    rows = row_out_ref.shape[1]
    size = row_ref.shape[0]
    per_pack = rows // CHUNK
    row_out_ref[...] = jnp.zeros_like(row_out_ref)

    def block(col_ref, done, row_vecs):
        chunks = col_ref.shape[0] // size * per_pack

        def within(step):
            pack, chunk = step // per_pack, lax.rem(step, per_pack)
            return pack * size, pl.multiple_of(chunk * CHUNK, CHUNK)

        def multiply(step, product_ref):
            base, start = within(step)
            columns = col_ref[pl.ds(pl.multiple_of(base + start, 16), CHUNK), :]
            product_ref[...] = dot_nt(row_ref[0:rows, :], columns)

        def weigh(step, product_ref, weight_ref):
            base, start = within(step)
            code_part = pl.ds(pl.multiple_of(base + rows + vecs, 16), CODE_ROWS)
            col = decode(col_ref[code_part, pl.ds(start, CHUNK)])
            col = [jnp.broadcast_to(field, (8, CHUNK)) for field in col]
            for first_row in range(0, rows, 16):
                both = []
                for line in (first_row, first_row + 8):
                    row = [
                        jnp.concatenate([spread_ref[field, line : line + 8, :]] * (CHUNK // LANES), axis=1)
                        for field in range(FIELDS)
                    ]
                    same = None
                    if own_block:
                        row_ids = lax.broadcasted_iota(jnp.int32, (8, CHUNK), 0) + (line - step * CHUNK)
                        same = row_ids == lax.broadcasted_iota(jnp.int32, (8, CHUNK), 1)
                    both.append(weights_of(product_ref[line : line + 8, :], row, col, same))
                weight_ref[first_row : first_row + 16, :] = jnp.concatenate(both, axis=0).astype(jnp.bfloat16)

        def total(step, weight_ref):
            base, start = within(step)
            vec_part = pl.ds(pl.multiple_of(base + rows, 16), vecs)
            col_vecs = with_ones(col_ref[vec_part, pl.ds(start, CHUNK)])
            row_out_ref[...] += dot_nt(col_vecs, weight_ref[...])[0:OUT_ROWS]
            if col_out_ref is not None:
                col_out_ref[:, pl.ds(pl.multiple_of(done + step * CHUNK, CHUNK), CHUNK)] = jnp.dot(
                    row_vecs, weight_ref[...], preferred_element_type=jnp.float32
                )[0:OUT_ROWS]

        def steps(index, carry):
            for parity in range(2):
                step = 2 * index + parity
                multiply(lax.rem(step + 1, chunks), products[1 - parity])
                weigh(step, products[parity], weights[parity])
                total(lax.rem(step + chunks - 1, chunks), weights[1 - parity])
            return carry

        multiply(0, products[0])
        weights[1][...] = jnp.zeros_like(weights[1])
        lax.fori_loop(0, chunks // 2, steps, 0)
        total(chunks - 1, weights[1])

    def compute():
        for field, values in enumerate(decode(row_ref[rows + vecs : rows + vecs + CODE_ROWS, :])):
            field_ref[field : field + 1, :] = values
        turned = field_ref[...].T
        for field in range(FIELDS):
            spread_ref[field] = jnp.broadcast_to(turned[:, field : field + 1], (rows, LANES))
        row_vecs = with_ones(row_ref[rows : rows + vecs, :])
        done = 0
        for col_ref in col_refs:
            block(col_ref, done, row_vecs)
            done += col_ref.shape[0] // size * rows

    if receivers is None:
        compute()
        return
    pair = lax.axis_index("blk") // 2
    takes_part = functools.reduce(jnp.logical_or, [pair == one for one in receivers])

    @pl.when(takes_part)
    def _():
        compute()

    @pl.when(jnp.logical_not(takes_part))
    def _():
        col_out_ref[...] = jnp.zeros_like(col_out_ref)


def tile(row, columns, vecs, own_block=False, col_sums=True, receivers=None):
    size, rows = row.shape
    cols = sum(part.shape[0] // size for part in columns) * rows
    shapes = [jax.ShapeDtypeStruct((OUT_ROWS, rows), jnp.float32)]
    if col_sums:
        shapes.append(jax.ShapeDtypeStruct((OUT_ROWS, cols), jnp.float32))

    def body(*refs):
        refs = list(refs)
        if not col_sums:
            refs.insert(2 + len(columns), None)
        tile_kernel(len(columns), own_block, receivers, vecs, *refs)

    return pl.pallas_call(
        body,
        out_shape=shapes,
        in_specs=[VMEM_SPEC] * (1 + len(columns)),
        out_specs=[VMEM_SPEC] * len(shapes),
        scratch_shapes=[
            pltpu.VMEM((LANES, rows), jnp.float32),
            pltpu.VMEM((FIELDS, rows, LANES), jnp.float32),
            pltpu.VMEM((rows, CHUNK), jnp.float32),
            pltpu.VMEM((rows, CHUNK), jnp.float32),
            pltpu.VMEM((rows, CHUNK), jnp.bfloat16),
            pltpu.VMEM((rows, CHUNK), jnp.bfloat16),
        ],
        cost_estimate=pl.CostEstimate(flops=COST, bytes_accessed=COST, transcendentals=0),
        compiler_params=params(),
        name="tile",
    )(row, *columns)


def image_kernel(*refs):
    parts, image_ref = refs[:-1], refs[-1]
    total = parts[0][...]
    for part in parts[1:]:
        total = total + part[...]
    vecs = image_ref.shape[0]
    image_ref[...] = total[0:vecs] / total[vecs : vecs + 1]


def image_of(parts, vecs):
    return pl.pallas_call(
        image_kernel,
        out_shape=jax.ShapeDtypeStruct((vecs, parts[0].shape[1]), jnp.float32),
        in_specs=[VMEM_SPEC] * len(parts),
        out_specs=VMEM_SPEC,
        compiler_params=params(),
        name="image",
    )(*parts)


def gram_kernel(mine_ref, other_ref, grams_ref):
    vecs, cols = mine_ref.shape
    packed = []
    for ref in (mine_ref, other_ref):
        image = ref[...]
        total = jnp.zeros((8, LANES), jnp.float32)
        for piece in range(LANES // vecs):
            shifted = [image]
            if piece > 0:
                shifted.insert(0, jnp.zeros((piece * vecs, cols), jnp.float32))
            if piece < LANES // vecs - 1:
                shifted.append(jnp.zeros((LANES - (piece + 1) * vecs, cols), jnp.float32))
            lines = image[8 * piece : 8 * piece + 8]
            total = total + dot_nt(lines, jnp.concatenate(shifted, axis=0), lax.Precision.HIGHEST)
        packed.append(total)
    both = packed[0] + packed[1]
    for copy in range(grams_ref.shape[0]):
        grams_ref[copy] = both


def grams_of(mine, other, copies):
    return pl.pallas_call(
        gram_kernel,
        out_shape=jax.ShapeDtypeStruct((copies, 8, LANES), jnp.float32),
        in_specs=[VMEM_SPEC] * 2,
        out_specs=VMEM_SPEC,
        compiler_params=params(),
        name="gram",
    )(mine, other)


def basis_kernel(total_rows, grams_ref, mine_ref, other_ref, out_ref, inverse_ref):
    vecs, half = mine_ref.shape
    sub = lax.axis_index("sub")
    packed = jnp.sum(grams_ref[...], axis=0) / total_rows
    lane = lax.broadcasted_iota(jnp.int32, (vecs, LANES), 1)
    line = lax.broadcasted_iota(jnp.int32, (vecs, LANES), 0)
    pieces = [packed] + [pltpu.roll(packed, LANES - piece * vecs, 1) for piece in range(1, LANES // vecs)]
    matrix = jnp.where(lane < vecs, jnp.concatenate(pieces, axis=0), 0.0)
    matrix = jnp.where(lane == line + vecs, 1.0, matrix)
    for step in range(vecs - 1):
        column = jnp.broadcast_to(matrix[:, step : step + 1], (vecs, LANES))
        scaled = matrix[step : step + 1, :] / column[step : step + 1, :]
        matrix = jnp.where(line > step, matrix - column * scaled, matrix)
    pivots = jnp.sum(jnp.where(lane == line, matrix, 0.0), axis=1, keepdims=True)
    inverse_ref[...] = pltpu.roll(matrix / jnp.sqrt(pivots), LANES - vecs, 1)
    share = vecs // 2
    own_rows = inverse_ref[pl.ds(pl.multiple_of(sub * share, 8), share), :][:, 0:vecs]
    for ref, place in ((mine_ref, sub), (other_ref, 1 - sub)):
        out_ref[:, pl.ds(pl.multiple_of(place * half, LANES), half)] = jnp.dot(
            own_rows, ref[...], precision=lax.Precision.HIGHEST, preferred_element_type=jnp.float32
        )


def basis_of(grams, mine, other, total_rows):
    vecs, half = mine.shape
    return pl.pallas_call(
        functools.partial(basis_kernel, total_rows),
        out_shape=jax.ShapeDtypeStruct((vecs // 2, 2 * half), jnp.float32),
        in_specs=[VMEM_SPEC] * 3,
        out_specs=VMEM_SPEC,
        scratch_shapes=[pltpu.VMEM((vecs, LANES), jnp.float32)],
        compiler_params=params(),
        name="basis",
    )(grams, mine, other)


def exchanges(pairs):
    plans = []
    for distance in range(1, pairs // 2):
        plans.append(([((p + distance) % pairs, p) for p in range(pairs)], None))
    if pairs > 1:
        half = pairs // 2
        last = [(p, p + half) if p % 2 == 0 else (p + half, p) for p in range(half)]
        plans.append((last, sorted(taker for _, taker in last)))
    return plans


def block_moves(pair_moves):
    return [(2 * source + member, 2 * target + member) for source, target in pair_moves for member in range(2)]


def back(moves):
    return [(target, source) for source, target in moves]


def local(embeddings, vectors, boxes, spans, camera):
    rows = embeddings.shape[0]
    half = rows // 2
    vecs = 2 * vectors.shape[0]
    blocks = lax.axis_size("blk")
    swap = [(0, 1), (1, 0)]
    beside = [(block, block ^ 1) for block in range(blocks)]
    plans = [(block_moves(moves), takers) for moves, takers in exchanges(blocks // 2)]

    def crossed(moves):
        return [(2 * source + 1 - core, 2 * target + core) for source, target in moves for core in range(2)]

    emb_other = lax.ppermute(embeddings, "sub", swap)
    vec_other = lax.ppermute(vectors, "sub", swap)
    meta = jnp.concatenate([array.astype(jnp.float32) for array in (vectors, boxes, spans, camera[None, :])], axis=0)
    sub = lax.axis_index("sub")
    halves = [lax.dynamic_slice_in_dim(embeddings, place * half, half, 0) for place in (sub, 1 - sub)]
    own, mine = packs_of(*halves, emb_other, vec_other, meta)
    sent = [lax.ppermute(mine, "blk", moves) for moves, _ in plans]
    beside_mine = lax.ppermute(mine, "blk", beside)
    weigh = functools.partial(tile, vecs=vecs)
    own_sums = weigh(mine, [own], own_block=True, col_sums=False)[0]
    own_sums, beside_mine, sent[:1] = lax.optimization_barrier((own_sums, beside_mine, sent[:1]))
    cut = beside_mine.shape[0] // SWAPS // 16 * 16
    shares = [beside_mine[at * cut : (at + 1) * cut if at < SWAPS - 1 else None] for at in range(SWAPS)]
    next_to = jnp.concatenate([beside_mine] + [lax.ppermute(share, "sub", swap) for share in shares], axis=0)
    parts = [own_sums, weigh(mine, [next_to], col_sums=False)[0]]
    col_sums = None
    for (moves, takers), pack in zip(plans, sent):
        if col_sums is not None:
            pack, col_sums, parts[1:2] = lax.optimization_barrier((pack, col_sums, parts[1:2]))
        row_sums, sums = weigh(pack, [own, next_to], receivers=takers)
        parts.append(lax.ppermute(row_sums, "blk", back(moves)))
        col_sums = sums if col_sums is None else col_sums + sums
    if col_sums is not None:
        pieces = [col_sums[:, place * half : (place + 1) * half] for place in range(4)]
        parts.append(pieces[0])
        parts.append(lax.ppermute(pieces[1], "sub", swap))
        parts.append(lax.ppermute(pieces[2], "blk", beside))
        parts.append(lax.ppermute(pieces[3], ("blk", "sub"), crossed(beside)))

    image = image_of(parts, vecs)
    image_other = lax.ppermute(image, "sub", swap)
    grams = lax.all_to_all(grams_of(image, image_other, blocks), "blk", 0, 0, tiled=True)
    return basis_of(grams, image, image_other, blocks * rows)


def solution(mesh):
    placed = (
        P(("groups", "blk"), "sub"),
        P("sub", ("groups", "blk")),
        P(None, ("groups", "blk")),
        P(None, ("groups", "blk")),
        P(("groups", "blk")),
    )
    return jax.shard_map(
        local, mesh=mesh, in_specs=placed, out_specs=P("sub", ("groups", "blk")), check_vma=False
    )
```

```python
import functools
import math

import jax
import jax.numpy as jnp
from jax import lax
from jax.experimental import pallas as pl
from jax.experimental.pallas import tpu as pltpu
from jax.sharding import PartitionSpec as P

SHARPNESS = 10.0
HORIZON = 2000.0
MARGIN = 8.0
EPSILON = 1e-06

LOG2E = math.log2(math.e)
COS_SCALE = math.sqrt(SHARPNESS * LOG2E)
GAP_SCALE = LOG2E / HORIZON
BASE = SHARPNESS * LOG2E + 1.0
BARRED_BELOW = BASE - 0.5 * GAP_SCALE

FIELDS = 9
LEFT, RIGHT, BOTTOM, TOP, FIRST, LAST, CAMERA, NORM, AREA = range(FIELDS)
CODE_ROWS = 16
LANES = 128
CHUNK = 256
OUT_ROWS = 40
COST = 1
SWAPS = 2
VMEM_LIMIT = 48 * 1024 * 1024

NT = (((1,), (1,)), ((), ()))
VMEM_SPEC = pl.BlockSpec(memory_space=pltpu.VMEM)


def params():
    return pltpu.CompilerParams(vmem_limit_bytes=VMEM_LIMIT)


def dot_nt(a, b, precision=None):
    return lax.dot_general(a, b, NT, precision=precision, preferred_element_type=jnp.float32)


def pack_rows(half, vecs):
    return half + vecs + CODE_ROWS


def pack_kernel(emb_mine_ref, emb_rest_ref, emb_other_ref, vec_ref, vec_other_ref, meta_ref, own_ref, mine_ref, code_ref):
    sub = lax.axis_index("sub")
    half, width = emb_mine_ref.shape
    half_vecs = vec_other_ref.shape[0]
    size = mine_ref.shape[0]
    ones = jnp.ones((8, width), jnp.bfloat16)
    for base, emb_ref, place in ((0, emb_mine_ref, sub), (size, emb_rest_ref, 1 - sub)):
        first = pl.multiple_of(place * half, half)
        for start in range(0, half, CHUNK):
            part = pl.ds(first + start, CHUNK)
            codes = []

            def whole(number, low_bits):
                codes.append((number >> low_bits) << low_bits)
                codes.append(number & ((1 << low_bits) - 1))

            meta = meta_ref[:, part]
            for axis in range(2):
                whole(jnp.minimum(meta[axis : axis + 1], meta[axis + 2 : axis + 3]), 5)
                whole(jnp.maximum(meta[axis : axis + 1], meta[axis + 2 : axis + 3]), 5)
            whole(jnp.minimum(meta[4:5], meta[5:6]), 7)
            whole(jnp.maximum(meta[4:5], meta[5:6]), 7)
            codes.append(meta[6:7])
            codes = [code.astype(jnp.float32) for code in codes]
            rest = jnp.zeros((8, CHUNK), jnp.float32)
            for values in (emb_ref[start : start + CHUNK, :], emb_other_ref[part, :]):
                values = values.astype(jnp.float32)
                square = values * values
                high = square.astype(jnp.bfloat16)
                low = (square - high.astype(jnp.float32)).astype(jnp.bfloat16)
                rest = rest + (dot_nt(ones, high) + dot_nt(ones, low))
            rest = rest[0:1]
            for _ in range(3):
                piece = rest.astype(jnp.bfloat16).astype(jnp.float32)
                codes.append(piece)
                rest = rest - piece
            code_ref[:, start : start + CHUNK] = jnp.concatenate(codes, axis=0).astype(jnp.bfloat16)
        source = pl.ds(first, half)
        refs = [(own_ref, base)] + ([(mine_ref, 0)] if base == 0 else [])
        sides = (
            (emb_ref[...], vec_ref[:, source], sub),
            (emb_other_ref[source, :], vec_other_ref[:, source], 1 - sub),
        )
        for ref, top in refs:
            for values, vectors, side in sides:
                ref[top : top + half, pl.ds(pl.multiple_of(side * width, width), width)] = values
                ref[pl.ds(pl.multiple_of(top + half + side * half_vecs, 16), half_vecs), :] = vectors
            first_code = top + half + 2 * half_vecs
            ref[first_code : first_code + CODE_ROWS, :] = code_ref[...]


def packs_of(emb_mine, emb_rest, emb_other, vec, vec_other, meta):
    half, width = emb_mine.shape
    features = 2 * width
    assert half == features
    size = pack_rows(half, 2 * vec_other.shape[0])
    return pl.pallas_call(
        pack_kernel,
        out_shape=[jax.ShapeDtypeStruct((count * size, features), jnp.bfloat16) for count in (2, 1)],
        in_specs=[VMEM_SPEC] * 6,
        out_specs=[VMEM_SPEC] * 2,
        scratch_shapes=[pltpu.VMEM((CODE_ROWS, half), jnp.bfloat16)],
        compiler_params=params(),
        name="pack",
    )(emb_mine, emb_rest, emb_other, vec, vec_other, meta)


def decode(codes):
    codes = codes.astype(jnp.float32)
    numbers = [codes[2 * index : 2 * index + 1] + codes[2 * index + 1 : 2 * index + 2] for index in range(6)]
    left, right, bottom, top, first, last = numbers
    right, top = right + MARGIN, top + MARGIN
    square = codes[15:16] + codes[14:15] + codes[13:14]
    norm = lax.rsqrt(square + EPSILON) * COS_SCALE
    area = (right - left) * (top - bottom)
    return [left, right, bottom, top, first * GAP_SCALE + BASE, last * GAP_SCALE, codes[12:13], norm, area]


def with_ones(vectors):
    shape = (CODE_ROWS, vectors.shape[1])
    tail = jnp.where(lax.broadcasted_iota(jnp.int32, shape, 0) == 0, 1.0, 0.0)
    return jnp.concatenate([vectors, tail.astype(jnp.bfloat16)], axis=0)


def weights_of(products, row, col, same):
    logit = products * row[NORM] * col[NORM]
    gap = jnp.maximum(col[FIRST] - row[LAST], row[FIRST] - col[LAST])
    width = jnp.maximum(jnp.minimum(row[RIGHT], col[RIGHT]) - jnp.maximum(row[LEFT], col[LEFT]), 0.0)
    height = jnp.maximum(jnp.minimum(row[TOP], col[TOP]) - jnp.maximum(row[BOTTOM], col[BOTTOM]), 0.0)
    inter = width * height
    both = row[AREA] + col[AREA]
    share = (both + inter) * pl.reciprocal(both - inter, approx=True)
    value = jnp.exp2(logit - jnp.maximum(gap, BASE)) * share
    barred = (row[CAMERA] == col[CAMERA]) & (gap < BARRED_BELOW)
    if same is not None:
        barred = barred & jnp.logical_not(same)
    return jnp.where(barred, 0.0, value)


def tile_kernel(blocks, own_block, receivers, vecs, *refs):
    row_ref, col_refs = refs[0], refs[1 : 1 + blocks]
    row_out_ref, col_out_ref, field_ref, spread_ref = refs[1 + blocks : 5 + blocks]
    products, weights = refs[5 + blocks : 7 + blocks], refs[7 + blocks :]
    rows = row_out_ref.shape[1]
    size = row_ref.shape[0]
    per_pack = rows // CHUNK
    row_out_ref[...] = jnp.zeros_like(row_out_ref)

    def block(col_ref, done, row_vecs):
        chunks = col_ref.shape[0] // size * per_pack

        def within(step):
            pack, chunk = step // per_pack, lax.rem(step, per_pack)
            return pack * size, pl.multiple_of(chunk * CHUNK, CHUNK)

        def multiply(step, product_ref):
            base, start = within(step)
            columns = col_ref[pl.ds(pl.multiple_of(base + start, 16), CHUNK), :]
            product_ref[...] = dot_nt(row_ref[0:rows, :], columns)

        def weigh(step, product_ref, weight_ref):
            base, start = within(step)
            code_part = pl.ds(pl.multiple_of(base + rows + vecs, 16), CODE_ROWS)
            col = decode(col_ref[code_part, pl.ds(start, CHUNK)])
            col = [jnp.broadcast_to(field, (8, CHUNK)) for field in col]
            for first_row in range(0, rows, 16):
                both = []
                for line in (first_row, first_row + 8):
                    row = [
                        jnp.concatenate([spread_ref[field, line : line + 8, :]] * (CHUNK // LANES), axis=1)
                        for field in range(FIELDS)
                    ]
                    same = None
                    if own_block:
                        row_ids = lax.broadcasted_iota(jnp.int32, (8, CHUNK), 0) + (line - step * CHUNK)
                        same = row_ids == lax.broadcasted_iota(jnp.int32, (8, CHUNK), 1)
                    both.append(weights_of(product_ref[line : line + 8, :], row, col, same))
                weight_ref[first_row : first_row + 16, :] = jnp.concatenate(both, axis=0).astype(jnp.bfloat16)

        def total(step, weight_ref):
            base, start = within(step)
            vec_part = pl.ds(pl.multiple_of(base + rows, 16), vecs)
            col_vecs = with_ones(col_ref[vec_part, pl.ds(start, CHUNK)])
            row_out_ref[...] += dot_nt(col_vecs, weight_ref[...])[0:OUT_ROWS]
            if col_out_ref is not None:
                col_out_ref[:, pl.ds(pl.multiple_of(done + step * CHUNK, CHUNK), CHUNK)] = jnp.dot(
                    row_vecs, weight_ref[...], preferred_element_type=jnp.float32
                )[0:OUT_ROWS]

        def steps(index, carry):
            for parity in range(2):
                step = 2 * index + parity
                multiply(lax.rem(step + 1, chunks), products[1 - parity])
                weigh(step, products[parity], weights[parity])
                total(lax.rem(step + chunks - 1, chunks), weights[1 - parity])
            return carry

        multiply(0, products[0])
        weights[1][...] = jnp.zeros_like(weights[1])
        lax.fori_loop(0, chunks // 2, steps, 0)
        total(chunks - 1, weights[1])

    def compute():
        for field, values in enumerate(decode(row_ref[rows + vecs : rows + vecs + CODE_ROWS, :])):
            field_ref[field : field + 1, :] = values
        turned = field_ref[...].T
        for field in range(FIELDS):
            spread_ref[field] = jnp.broadcast_to(turned[:, field : field + 1], (rows, LANES))
        row_vecs = with_ones(row_ref[rows : rows + vecs, :])
        done = 0
        for col_ref in col_refs:
            block(col_ref, done, row_vecs)
            done += col_ref.shape[0] // size * rows

    if receivers is None:
        compute()
        return
    pair = lax.axis_index("blk") // 2
    takes_part = functools.reduce(jnp.logical_or, [pair == one for one in receivers])

    @pl.when(takes_part)
    def _():
        compute()

    @pl.when(jnp.logical_not(takes_part))
    def _():
        col_out_ref[...] = jnp.zeros_like(col_out_ref)


def tile(row, columns, vecs, own_block=False, col_sums=True, receivers=None):
    size, rows = row.shape
    cols = sum(part.shape[0] // size for part in columns) * rows
    shapes = [jax.ShapeDtypeStruct((OUT_ROWS, rows), jnp.float32)]
    if col_sums:
        shapes.append(jax.ShapeDtypeStruct((OUT_ROWS, cols), jnp.float32))

    def body(*refs):
        refs = list(refs)
        if not col_sums:
            refs.insert(2 + len(columns), None)
        tile_kernel(len(columns), own_block, receivers, vecs, *refs)

    return pl.pallas_call(
        body,
        out_shape=shapes,
        in_specs=[VMEM_SPEC] * (1 + len(columns)),
        out_specs=[VMEM_SPEC] * len(shapes),
        scratch_shapes=[
            pltpu.VMEM((LANES, rows), jnp.float32),
            pltpu.VMEM((FIELDS, rows, LANES), jnp.float32),
            pltpu.VMEM((rows, CHUNK), jnp.float32),
            pltpu.VMEM((rows, CHUNK), jnp.float32),
            pltpu.VMEM((rows, CHUNK), jnp.bfloat16),
            pltpu.VMEM((rows, CHUNK), jnp.bfloat16),
        ],
        cost_estimate=pl.CostEstimate(flops=COST, bytes_accessed=COST, transcendentals=0),
        compiler_params=params(),
        name="tile",
    )(row, *columns)


def image_kernel(*refs):
    parts, image_ref = refs[:-1], refs[-1]
    total = parts[0][...]
    for part in parts[1:]:
        total = total + part[...]
    vecs = image_ref.shape[0]
    image_ref[...] = total[0:vecs] / total[vecs : vecs + 1]


def image_of(parts, vecs):
    return pl.pallas_call(
        image_kernel,
        out_shape=jax.ShapeDtypeStruct((vecs, parts[0].shape[1]), jnp.float32),
        in_specs=[VMEM_SPEC] * len(parts),
        out_specs=VMEM_SPEC,
        compiler_params=params(),
        name="image",
    )(*parts)


def gram_kernel(mine_ref, other_ref, gram_ref):
    vecs, cols = mine_ref.shape
    totals = []
    for ref in (mine_ref, other_ref):
        image = ref[...]
        padded = jnp.concatenate([image, jnp.zeros((LANES - vecs, cols), jnp.float32)], axis=0)
        totals.append(dot_nt(image, padded, lax.Precision.HIGHEST))
    gram = totals[0] + totals[1]
    packed = gram[0:8]
    for piece in range(1, vecs // 8):
        packed = packed + pltpu.roll(gram[8 * piece : 8 * piece + 8], piece * vecs, 1)
    gram_ref[...] = packed


def gram_of(mine, other):
    return pl.pallas_call(
        gram_kernel,
        out_shape=jax.ShapeDtypeStruct((8, LANES), jnp.float32),
        in_specs=[VMEM_SPEC] * 2,
        out_specs=VMEM_SPEC,
        compiler_params=params(),
        name="gram",
    )(mine, other)


def inverse_of(number):
    guess = pl.reciprocal(number, approx=True)
    guess = guess * (2.0 - number * guess)
    return guess * (2.0 - number * guess)


def basis_kernel(total_rows, gram_ref, mine_ref, other_ref, out_ref, inverse_ref):
    vecs, half = mine_ref.shape
    sub = lax.axis_index("sub")
    packed = gram_ref[...] / total_rows
    lane = lax.broadcasted_iota(jnp.int32, (vecs, LANES), 1)
    line = lax.broadcasted_iota(jnp.int32, (vecs, LANES), 0)
    pieces = [packed] + [pltpu.roll(packed, LANES - piece * vecs, 1) for piece in range(1, LANES // vecs)]
    matrix = jnp.where(lane < vecs, jnp.concatenate(pieces, axis=0), 0.0)
    matrix = jnp.where(lane == line + vecs, 1.0, matrix)
    for step in range(0, vecs, 2):
        left = jnp.broadcast_to(matrix[:, step : step + 1], (vecs, LANES))
        right = jnp.broadcast_to(matrix[:, step + 1 : step + 2], (vecs, LANES))
        upper, lower = matrix[step : step + 1, :], matrix[step + 1 : step + 2, :]
        across = right[step : step + 1, :]
        inverse = inverse_of(left[step : step + 1, :])
        factor = left[step + 1 : step + 2, :] * inverse
        lower = lower - factor * upper
        inverse_next = inverse_of(right[step + 1 : step + 2, :] - factor * across)
        first = left * inverse
        second = (right - first * across) * inverse_next
        reduced = matrix - first * upper - second * lower
        matrix = jnp.where(line > step + 1, reduced, jnp.where(line == step + 1, lower, matrix))
    pivots = jnp.sum(jnp.where(lane == line, matrix, 0.0), axis=1, keepdims=True)
    inverse_ref[...] = pltpu.roll(matrix / jnp.sqrt(pivots), LANES - vecs, 1)
    share = vecs // 2
    own_rows = inverse_ref[pl.ds(pl.multiple_of(sub * share, 8), share), :][:, 0:vecs]
    for ref, place in ((mine_ref, sub), (other_ref, 1 - sub)):
        out_ref[:, pl.ds(pl.multiple_of(place * half, LANES), half)] = jnp.dot(
            own_rows, ref[...], precision=lax.Precision.HIGHEST, preferred_element_type=jnp.float32
        )


def basis_of(gram, mine, other, total_rows):
    vecs, half = mine.shape
    return pl.pallas_call(
        functools.partial(basis_kernel, total_rows),
        out_shape=jax.ShapeDtypeStruct((vecs // 2, 2 * half), jnp.float32),
        in_specs=[VMEM_SPEC] * 3,
        out_specs=VMEM_SPEC,
        scratch_shapes=[pltpu.VMEM((vecs, LANES), jnp.float32)],
        compiler_params=params(),
        name="basis",
    )(gram, mine, other)


def exchanges(pairs):
    plans = []
    for distance in range(1, pairs // 2):
        plans.append(([((p + distance) % pairs, p) for p in range(pairs)], None))
    if pairs > 1:
        half = pairs // 2
        last = [(p, p + half) if p % 2 == 0 else (p + half, p) for p in range(half)]
        plans.append((last, sorted(taker for _, taker in last)))
    return plans


def block_moves(pair_moves):
    return [(2 * source + member, 2 * target + member) for source, target in pair_moves for member in range(2)]


def rounds(blocks):
    bits = blocks.bit_length() - 1
    assert blocks == 1 << bits
    plan, first = ([(1,)], 1) if bits > 0 else ([], 0)
    while first < bits:
        plan.append(tuple(part << first for part in range(1, min(4, 1 << (bits - first)))))
        first += 2
    return plan


def back(moves):
    return [(target, source) for source, target in moves]


def local(embeddings, vectors, boxes, spans, camera):
    rows = embeddings.shape[0]
    half = rows // 2
    vecs = 2 * vectors.shape[0]
    blocks = lax.axis_size("blk")
    swap = [(0, 1), (1, 0)]
    beside = [(block, block ^ 1) for block in range(blocks)]
    plans = [(block_moves(moves), takers) for moves, takers in exchanges(blocks // 2)]

    emb_other = lax.ppermute(embeddings, "sub", swap)
    vec_other = lax.ppermute(vectors, "sub", swap)
    meta = jnp.concatenate([boxes, spans, camera[None, :]], axis=0)
    sub = lax.axis_index("sub")
    halves = [lax.dynamic_slice_in_dim(embeddings, place * half, half, 0) for place in (sub, 1 - sub)]
    own, mine = packs_of(*halves, emb_other, vectors, vec_other, meta)
    sent = [lax.ppermute(mine, "blk", moves) for moves, _ in plans]
    beside_mine = lax.ppermute(mine, "blk", beside)
    weigh = functools.partial(tile, vecs=vecs)
    own_sums = weigh(mine, [own], own_block=True, col_sums=False)[0]
    own_sums, beside_mine, sent[:1] = lax.optimization_barrier((own_sums, beside_mine, sent[:1]))
    cut = beside_mine.shape[0] // SWAPS // 16 * 16
    shares = [beside_mine[at * cut : (at + 1) * cut if at < SWAPS - 1 else None] for at in range(SWAPS)]
    next_to = jnp.concatenate([beside_mine] + [lax.ppermute(share, "sub", swap) for share in shares], axis=0)
    parts = [own_sums, weigh(mine, [next_to], col_sums=False)[0]]
    col_sums = None
    for (moves, takers), pack in zip(plans, sent):
        if col_sums is not None:
            pack, col_sums, parts[1:2] = lax.optimization_barrier((pack, col_sums, parts[1:2]))
        row_sums, sums = weigh(pack, [own, next_to], receivers=takers)
        parts.append(lax.ppermute(row_sums, "blk", back(moves)))
        col_sums = sums if col_sums is None else col_sums + sums
    if col_sums is not None:
        own_mine, own_rest, next_mine, next_rest = [col_sums[:, place * half : (place + 1) * half] for place in range(4)]
        sides = lax.ppermute(jnp.concatenate([own_rest, next_rest], axis=1), "sub", swap)
        parts.append(own_mine)
        parts.append(sides[:, :half])
        parts.append(lax.ppermute(next_mine + sides[:, half:], "blk", beside))
    image = image_of(parts, vecs)
    image_other = lax.ppermute(image, "sub", swap)
    gram = gram_of(image, image_other)
    for offsets in rounds(blocks):
        shares = [lax.ppermute(gram, "blk", [(block, block ^ offset) for block in range(blocks)]) for offset in offsets]
        gram = sum(shares, gram)
    return basis_of(gram, image, image_other, blocks * rows)


def solution(mesh):
    placed = (
        P(("groups", "blk"), "sub"),
        P("sub", ("groups", "blk")),
        P(None, ("groups", "blk")),
        P(None, ("groups", "blk")),
        P(("groups", "blk")),
    )
    return jax.shard_map(
        local, mesh=mesh, in_specs=placed, out_specs=P("sub", ("groups", "blk")), check_vma=False
    )
```

```python
import functools
import math

import jax
import jax.numpy as jnp
from jax import lax
from jax.experimental import pallas as pl
from jax.experimental.pallas import tpu as pltpu
from jax.sharding import PartitionSpec as P

SHARPNESS = 10.0
HORIZON = 2000.0
MARGIN = 8.0
EPSILON = 1e-06

LOG2E = math.log2(math.e)
COS_SCALE = math.sqrt(SHARPNESS * LOG2E)
GAP_SCALE = LOG2E / HORIZON
BASE = SHARPNESS * LOG2E + 1.0
BARRED_BELOW = BASE - 0.5 * GAP_SCALE

FIELDS = 9
LEFT, RIGHT, BOTTOM, TOP, FIRST, LAST, CAMERA, NORM, AREA = range(FIELDS)
CODE_ROWS = 16
LANES = 128
CHUNK = 256
OUT_ROWS = 40
COST = 1
SWAPS = 2
VMEM_LIMIT = 48 * 1024 * 1024

NT = (((1,), (1,)), ((), ()))
VMEM_SPEC = pl.BlockSpec(memory_space=pltpu.VMEM)


def params():
    return pltpu.CompilerParams(vmem_limit_bytes=VMEM_LIMIT)


def dot_nt(a, b, precision=None):
    return lax.dot_general(a, b, NT, precision=precision, preferred_element_type=jnp.float32)


def pack_rows(half, vecs):
    return half + vecs + CODE_ROWS


def pack_kernel(emb_mine_ref, emb_rest_ref, emb_other_ref, vec_ref, vec_other_ref, meta_ref, mine_ref, rest_ref, code_ref):
    sub = lax.axis_index("sub")
    half, width = emb_mine_ref.shape
    half_vecs = vec_other_ref.shape[0]
    ones = jnp.ones((8, width), jnp.bfloat16)
    for ref, emb_ref, place in ((mine_ref, emb_mine_ref, sub), (rest_ref, emb_rest_ref, 1 - sub)):
        first = pl.multiple_of(place * half, half)
        for start in range(0, half, CHUNK):
            part = pl.ds(first + start, CHUNK)
            codes = []

            def whole(number, low_bits):
                codes.append((number >> low_bits) << low_bits)
                codes.append(number & ((1 << low_bits) - 1))

            meta = meta_ref[:, part]
            for axis in range(2):
                whole(jnp.minimum(meta[axis : axis + 1], meta[axis + 2 : axis + 3]), 5)
                whole(jnp.maximum(meta[axis : axis + 1], meta[axis + 2 : axis + 3]), 5)
            whole(jnp.minimum(meta[4:5], meta[5:6]), 7)
            whole(jnp.maximum(meta[4:5], meta[5:6]), 7)
            codes.append(meta[6:7])
            codes = [code.astype(jnp.float32) for code in codes]
            rest = jnp.zeros((8, CHUNK), jnp.float32)
            for values in (emb_ref[start : start + CHUNK, :], emb_other_ref[part, :]):
                values = values.astype(jnp.float32)
                square = values * values
                high = square.astype(jnp.bfloat16)
                low = (square - high.astype(jnp.float32)).astype(jnp.bfloat16)
                rest = rest + (dot_nt(ones, high) + dot_nt(ones, low))
            rest = rest[0:1]
            for _ in range(3):
                piece = rest.astype(jnp.bfloat16).astype(jnp.float32)
                codes.append(piece)
                rest = rest - piece
            code_ref[:, start : start + CHUNK] = jnp.concatenate(codes, axis=0).astype(jnp.bfloat16)
        source = pl.ds(first, half)
        sides = (
            (emb_ref[...], vec_ref[:, source], sub),
            (emb_other_ref[source, :], vec_other_ref[:, source], 1 - sub),
        )
        for values, vectors, side in sides:
            ref[0:half, pl.ds(pl.multiple_of(side * width, width), width)] = values
            ref[pl.ds(pl.multiple_of(half + side * half_vecs, 16), half_vecs), :] = vectors
        first_code = half + 2 * half_vecs
        ref[first_code : first_code + CODE_ROWS, :] = code_ref[...]


def packs_of(emb_mine, emb_rest, emb_other, vec, vec_other, meta):
    half, width = emb_mine.shape
    features = 2 * width
    assert half == features
    size = pack_rows(half, 2 * vec_other.shape[0])
    return pl.pallas_call(
        pack_kernel,
        out_shape=[jax.ShapeDtypeStruct((size, features), jnp.bfloat16)] * 2,
        in_specs=[VMEM_SPEC] * 6,
        out_specs=[VMEM_SPEC] * 2,
        scratch_shapes=[pltpu.VMEM((CODE_ROWS, half), jnp.bfloat16)],
        compiler_params=params(),
        name="pack",
    )(emb_mine, emb_rest, emb_other, vec, vec_other, meta)


def decode(codes):
    codes = codes.astype(jnp.float32)
    numbers = [codes[2 * index : 2 * index + 1] + codes[2 * index + 1 : 2 * index + 2] for index in range(6)]
    left, right, bottom, top, first, last = numbers
    right, top = right + MARGIN, top + MARGIN
    square = codes[15:16] + codes[14:15] + codes[13:14]
    norm = lax.rsqrt(square + EPSILON) * COS_SCALE
    area = (right - left) * (top - bottom)
    return [left, right, bottom, top, first * GAP_SCALE + BASE, last * GAP_SCALE, codes[12:13], norm, area]


def with_ones(vectors):
    shape = (CODE_ROWS, vectors.shape[1])
    tail = jnp.where(lax.broadcasted_iota(jnp.int32, shape, 0) == 0, 1.0, 0.0)
    return jnp.concatenate([vectors, tail.astype(jnp.bfloat16)], axis=0)


def weights_of(products, row, col, same):
    logit = products * row[NORM] * col[NORM]
    gap = jnp.maximum(col[FIRST] - row[LAST], row[FIRST] - col[LAST])
    width = jnp.maximum(jnp.minimum(row[RIGHT], col[RIGHT]) - jnp.maximum(row[LEFT], col[LEFT]), 0.0)
    height = jnp.maximum(jnp.minimum(row[TOP], col[TOP]) - jnp.maximum(row[BOTTOM], col[BOTTOM]), 0.0)
    inter = width * height
    both = row[AREA] + col[AREA]
    share = (both + inter) * pl.reciprocal(both - inter, approx=True)
    value = jnp.exp2(logit - jnp.maximum(gap, BASE)) * share
    barred = (row[CAMERA] == col[CAMERA]) & (gap < BARRED_BELOW)
    if same is not None:
        barred = barred & jnp.logical_not(same)
    return jnp.where(barred, 0.0, value)


def tile_kernel(blocks, turns, own_block, receivers, vecs, *refs):
    row_ref, col_refs = refs[0], refs[1 : 1 + blocks]
    row_out_ref, col_out_ref, field_ref, spread_ref, sum_ref = refs[1 + blocks : 6 + blocks]
    products, weights = refs[6 + blocks : 8 + blocks], refs[8 + blocks :]
    size, rows = row_ref.shape
    features = size - vecs - CODE_ROWS
    vec_rows, code_rows = slice(features, features + vecs), slice(features + vecs, size)
    sum_ref[...] = jnp.zeros_like(sum_ref)

    def block(col_ref, done, row_vecs):
        chunks = col_ref.shape[1] // CHUNK

        def place(step, base=0):
            return pl.ds(pl.multiple_of(base + step * CHUNK, CHUNK), CHUNK)

        def multiply(step, product_ref):
            product_ref[...] = jnp.dot(
                row_ref[0:rows, :], col_ref[0:features, place(step)], preferred_element_type=jnp.float32
            )

        def weigh(step, product_ref, weight_ref):
            col = [jnp.broadcast_to(field, (8, CHUNK)) for field in decode(col_ref[code_rows, place(step)])]
            for first_row in range(0, rows, 16):
                both = []
                for line in (first_row, first_row + 8):
                    row = [
                        jnp.concatenate([spread_ref[field, line : line + 8, :]] * (CHUNK // LANES), axis=1)
                        for field in range(FIELDS)
                    ]
                    same = None
                    if own_block:
                        row_ids = lax.broadcasted_iota(jnp.int32, (8, CHUNK), 0) + (line - step * CHUNK)
                        same = row_ids == lax.broadcasted_iota(jnp.int32, (8, CHUNK), 1)
                    both.append(weights_of(product_ref[line : line + 8, :], row, col, same))
                weight_ref[first_row : first_row + 16, :] = jnp.concatenate(both, axis=0).astype(jnp.bfloat16)

        def total(step, weight_ref):
            sum_ref[:, 0 : vecs + CODE_ROWS] += dot_nt(weight_ref[...], with_ones(col_ref[vec_rows, place(step)]))
            if not turns:
                col_out_ref[:, place(step, done)] = jnp.dot(
                    row_vecs, weight_ref[...], preferred_element_type=jnp.float32
                )[0:OUT_ROWS]

        def steps(index, carry):
            for parity in range(2):
                step = 2 * index + parity
                multiply(lax.rem(step + 1, chunks), products[1 - parity])
                weigh(step, products[parity], weights[parity])
                total(lax.rem(step + chunks - 1, chunks), weights[1 - parity])
            return carry

        multiply(0, products[0])
        weights[1][...] = jnp.zeros_like(weights[1])
        lax.fori_loop(0, chunks // 2, steps, 0)
        total(chunks - 1, weights[1])

    def compute():
        for field, values in enumerate(decode(row_ref[code_rows, :])):
            field_ref[field : field + 1, :] = values
        turned = field_ref[...].T
        for field in range(FIELDS):
            spread_ref[field] = jnp.broadcast_to(turned[:, field : field + 1], (rows, LANES))
        row_vecs = with_ones(row_ref[vec_rows, :])
        if turns:
            for number, pack_ref in enumerate(col_refs):
                part = pl.ds(number * rows, rows)
                col_out_ref[0:features, part] = pack_ref[0:rows, :].T
                col_out_ref[features:size, part] = pack_ref[features:size, :]
            block(col_out_ref, 0, row_vecs)
        else:
            done = 0
            for col_ref in col_refs:
                block(col_ref, done, row_vecs)
                done += col_ref.shape[1]

    def finish():
        row_out_ref[...] = sum_ref[...].T[0:OUT_ROWS]

    if receivers is None:
        compute()
        finish()
        return
    pair = lax.axis_index("blk") // 2
    takes_part = functools.reduce(jnp.logical_or, [pair == one for one in receivers])

    @pl.when(takes_part)
    def _():
        compute()
        finish()

    @pl.when(jnp.logical_not(takes_part))
    def _():
        row_out_ref[...] = jnp.zeros_like(row_out_ref)
        col_out_ref[...] = jnp.zeros_like(col_out_ref)


def tile(row, columns, vecs, turns=False, own_block=False, receivers=None):
    size, rows = row.shape
    cols = len(columns) * rows if turns else sum(part.shape[1] for part in columns)
    second = jax.ShapeDtypeStruct((size, cols), jnp.bfloat16)
    if not turns:
        second = jax.ShapeDtypeStruct((OUT_ROWS, cols), jnp.float32)
    return pl.pallas_call(
        functools.partial(tile_kernel, len(columns), turns, own_block, receivers, vecs),
        out_shape=[jax.ShapeDtypeStruct((OUT_ROWS, rows), jnp.float32), second],
        in_specs=[VMEM_SPEC] * (1 + len(columns)),
        out_specs=[VMEM_SPEC] * 2,
        scratch_shapes=[
            pltpu.VMEM((LANES, rows), jnp.float32),
            pltpu.VMEM((FIELDS, rows, LANES), jnp.float32),
            pltpu.VMEM((rows, LANES), jnp.float32),
            pltpu.VMEM((rows, CHUNK), jnp.float32),
            pltpu.VMEM((rows, CHUNK), jnp.float32),
            pltpu.VMEM((rows, CHUNK), jnp.bfloat16),
            pltpu.VMEM((rows, CHUNK), jnp.bfloat16),
        ],
        cost_estimate=pl.CostEstimate(flops=COST, bytes_accessed=COST, transcendentals=0),
        compiler_params=params(),
        name="tile",
    )(row, *columns)


def image_kernel(*refs):
    parts, image_ref = refs[:-1], refs[-1]
    total = parts[0][...]
    for part in parts[1:]:
        total = total + part[...]
    vecs = image_ref.shape[0]
    image_ref[...] = total[0:vecs] / total[vecs : vecs + 1]


def image_of(parts, vecs):
    return pl.pallas_call(
        image_kernel,
        out_shape=jax.ShapeDtypeStruct((vecs, parts[0].shape[1]), jnp.float32),
        in_specs=[VMEM_SPEC] * len(parts),
        out_specs=VMEM_SPEC,
        compiler_params=params(),
        name="image",
    )(*parts)


def gram_kernel(image_ref, grams_ref):
    vecs, cols = image_ref.shape
    image = image_ref[...]
    padded = jnp.concatenate([image, jnp.zeros((LANES - vecs, cols), jnp.float32)], axis=0)
    gram = dot_nt(image, padded, lax.Precision.HIGHEST)
    packed = gram[0:8]
    for piece in range(1, vecs // 8):
        packed = packed + pltpu.roll(gram[8 * piece : 8 * piece + 8], piece * vecs, 1)
    for copy in range(grams_ref.shape[0]):
        grams_ref[copy] = packed


def grams_of(image, copies):
    return pl.pallas_call(
        gram_kernel,
        out_shape=jax.ShapeDtypeStruct((copies, 8, LANES), jnp.float32),
        in_specs=[VMEM_SPEC],
        out_specs=VMEM_SPEC,
        compiler_params=params(),
        name="gram",
    )(image)


def inverse_of(number):
    guess = pl.reciprocal(number, approx=True)
    guess = guess * (2.0 - number * guess)
    return guess * (2.0 - number * guess)


def basis_kernel(total_rows, grams_ref, mine_ref, other_ref, out_ref, inverse_ref):
    vecs, half = mine_ref.shape
    sub = lax.axis_index("sub")
    packed = jnp.sum(grams_ref[...], axis=0) / total_rows
    lane = lax.broadcasted_iota(jnp.int32, (vecs, LANES), 1)
    line = lax.broadcasted_iota(jnp.int32, (vecs, LANES), 0)
    pieces = [packed] + [pltpu.roll(packed, LANES - piece * vecs, 1) for piece in range(1, LANES // vecs)]
    matrix = jnp.where(lane < vecs, jnp.concatenate(pieces, axis=0), 0.0)
    matrix = jnp.where(lane == line + vecs, 1.0, matrix)
    for step in range(0, vecs, 2):
        left = jnp.broadcast_to(matrix[:, step : step + 1], (vecs, LANES))
        right = jnp.broadcast_to(matrix[:, step + 1 : step + 2], (vecs, LANES))
        upper, lower = matrix[step : step + 1, :], matrix[step + 1 : step + 2, :]
        across = right[step : step + 1, :]
        inverse = inverse_of(left[step : step + 1, :])
        factor = left[step + 1 : step + 2, :] * inverse
        lower = lower - factor * upper
        inverse_next = inverse_of(right[step + 1 : step + 2, :] - factor * across)
        first = left * inverse
        second = (right - first * across) * inverse_next
        reduced = matrix - first * upper - second * lower
        matrix = jnp.where(line > step + 1, reduced, jnp.where(line == step + 1, lower, matrix))
    pivots = jnp.sum(jnp.where(lane == line, matrix, 0.0), axis=1, keepdims=True)
    inverse_ref[...] = pltpu.roll(matrix / jnp.sqrt(pivots), LANES - vecs, 1)
    share = vecs // 2
    own_rows = inverse_ref[pl.ds(pl.multiple_of(sub * share, 8), share), :][:, 0:vecs]
    for ref, place in ((mine_ref, sub), (other_ref, 1 - sub)):
        out_ref[:, pl.ds(pl.multiple_of(place * half, LANES), half)] = jnp.dot(
            own_rows, ref[...], precision=lax.Precision.HIGHEST, preferred_element_type=jnp.float32
        )


def basis_of(grams, mine, other, total_rows):
    vecs, half = mine.shape
    return pl.pallas_call(
        functools.partial(basis_kernel, total_rows),
        out_shape=jax.ShapeDtypeStruct((vecs // 2, 2 * half), jnp.float32),
        in_specs=[VMEM_SPEC] * 3,
        out_specs=VMEM_SPEC,
        scratch_shapes=[pltpu.VMEM((vecs, LANES), jnp.float32)],
        compiler_params=params(),
        name="basis",
    )(grams, mine, other)


def exchanges(pairs):
    plans = []
    for distance in range(1, pairs // 2):
        plans.append(([((p + distance) % pairs, p) for p in range(pairs)], None))
    if pairs > 1:
        half = pairs // 2
        last = [(p, p + half) if p % 2 == 0 else (p + half, p) for p in range(half)]
        plans.append((last, sorted(taker for _, taker in last)))
    return plans


def block_moves(pair_moves):
    return [(2 * source + member, 2 * target + member) for source, target in pair_moves for member in range(2)]


def back(moves):
    return [(target, source) for source, target in moves]


def local(embeddings, vectors, boxes, spans, camera):
    rows = embeddings.shape[0]
    half = rows // 2
    vecs = 2 * vectors.shape[0]
    blocks = lax.axis_size("blk")
    swap = [(0, 1), (1, 0)]
    beside = [(block, block ^ 1) for block in range(blocks)]
    plans = [(block_moves(moves), takers) for moves, takers in exchanges(blocks // 2)]

    emb_other = lax.ppermute(embeddings, "sub", swap)
    vec_other = lax.ppermute(vectors, "sub", swap)
    meta = jnp.concatenate([boxes, spans, camera[None, :]], axis=0)
    sub = lax.axis_index("sub")
    halves = [lax.dynamic_slice_in_dim(embeddings, place * half, half, 0) for place in (sub, 1 - sub)]
    mine, rest = packs_of(*halves, emb_other, vectors, vec_other, meta)
    sent = [lax.ppermute(mine, "blk", moves) for moves, _ in plans]
    beside_mine = lax.ppermute(mine, "blk", beside)
    weigh = functools.partial(tile, vecs=vecs)
    own_sums, own = weigh(mine, [mine, rest], turns=True, own_block=True)
    own_sums, own, beside_mine, sent[:1] = lax.optimization_barrier((own_sums, own, beside_mine, sent[:1]))
    cut = beside_mine.shape[0] // SWAPS // 16 * 16
    shares = [beside_mine[at * cut : (at + 1) * cut if at < SWAPS - 1 else None] for at in range(SWAPS)]
    beside_rest = jnp.concatenate([lax.ppermute(share, "sub", swap) for share in shares], axis=0)
    beside_sums, next_to = weigh(mine, [beside_mine, beside_rest], turns=True)
    parts = [own_sums, beside_sums]
    col_sums = None
    returns = []
    for (moves, takers), pack in zip(plans, sent):
        if col_sums is not None:
            pack, col_sums = lax.optimization_barrier((pack, col_sums))
        row_sums, sums = weigh(pack, [own, next_to], receivers=takers)
        returns.append((row_sums, back(moves)))
        col_sums = sums if col_sums is None else col_sums + sums
    if col_sums is not None:
        own_mine, own_rest, next_mine, next_rest = [col_sums[:, place * half : (place + 1) * half] for place in range(4)]
        sides = lax.ppermute(jnp.concatenate([own_rest, next_rest], axis=1), "sub", swap)
        last_sums, last_moves = returns.pop()
        parts.append(lax.ppermute(last_sums, "blk", last_moves))
        crossing = next_mine + sides[:, half:]
        parts.append(own_mine)
        parts.append(sides[:, :half])
        parts.append(lax.ppermute(crossing, "blk", beside))
        for row_sums, moves in returns:
            row_sums, _ = lax.optimization_barrier((row_sums, crossing))
            parts.append(lax.ppermute(row_sums, "blk", moves))
    image = image_of(parts, vecs)
    image_other = lax.ppermute(image, "sub", swap)
    grams = lax.all_to_all(grams_of(image, 2 * blocks), ("blk", "sub"), 0, 0, tiled=True)
    return basis_of(grams, image, image_other, blocks * rows)


def solution(mesh):
    placed = (
        P(("groups", "blk"), "sub"),
        P("sub", ("groups", "blk")),
        P(None, ("groups", "blk")),
        P(None, ("groups", "blk")),
        P(("groups", "blk")),
    )
    return jax.shard_map(
        local, mesh=mesh, in_specs=placed, out_specs=P("sub", ("groups", "blk")), check_vma=False
    )
```

```python
import functools
import math

import jax
import jax.numpy as jnp
from jax import lax
from jax.experimental import pallas as pl
from jax.experimental.pallas import tpu as pltpu
from jax.sharding import PartitionSpec as P

SHARPNESS = 10.0
HORIZON = 2000.0
MARGIN = 8.0
EPSILON = 1e-06

LOG2E = math.log2(math.e)
COS_SCALE = math.sqrt(SHARPNESS * LOG2E)
GAP_SCALE = LOG2E / HORIZON
BASE = SHARPNESS * LOG2E + 1.0
BARRED_BELOW = BASE - 0.5 * GAP_SCALE

FIELDS = 9
LEFT, RIGHT, BOTTOM, TOP, FIRST, LAST, CAMERA, NORM, AREA = range(FIELDS)
CODE_ROWS = 16
LANES = 128
CHUNK = 256
OUT_ROWS = 40
COST = 1
GROUP = 32
SWAPS = 2
VMEM_LIMIT = 48 * 1024 * 1024

NT = (((1,), (1,)), ((), ()))
VMEM_SPEC = pl.BlockSpec(memory_space=pltpu.VMEM)


def params():
    return pltpu.CompilerParams(vmem_limit_bytes=VMEM_LIMIT)


def dot_nt(a, b, precision=None):
    return lax.dot_general(a, b, NT, precision=precision, preferred_element_type=jnp.float32)


def pack_rows(half, vecs):
    return half + vecs + CODE_ROWS


def pack_kernel(emb_mine_ref, emb_rest_ref, emb_other_ref, vec_ref, vec_other_ref, meta_ref, mine_ref, rest_ref, code_ref):
    sub = lax.axis_index("sub")
    half, width = emb_mine_ref.shape
    half_vecs = vec_other_ref.shape[0]
    ones = jnp.ones((8, width), jnp.bfloat16)
    for ref, emb_ref, place in ((mine_ref, emb_mine_ref, sub), (rest_ref, emb_rest_ref, 1 - sub)):
        first = pl.multiple_of(place * half, half)
        for start in range(0, half, CHUNK):
            part = pl.ds(first + start, CHUNK)
            codes = []

            def whole(number, low_bits):
                codes.append((number >> low_bits) << low_bits)
                codes.append(number & ((1 << low_bits) - 1))

            meta = meta_ref[:, part]
            for axis in range(2):
                whole(jnp.minimum(meta[axis : axis + 1], meta[axis + 2 : axis + 3]), 5)
                whole(jnp.maximum(meta[axis : axis + 1], meta[axis + 2 : axis + 3]), 5)
            whole(jnp.minimum(meta[4:5], meta[5:6]), 7)
            whole(jnp.maximum(meta[4:5], meta[5:6]), 7)
            codes.append(meta[6:7])
            codes = [code.astype(jnp.float32) for code in codes]
            rest = jnp.zeros((8, CHUNK), jnp.float32)
            for values in (emb_ref[start : start + CHUNK, :], emb_other_ref[part, :]):
                values = values.astype(jnp.float32)
                square = values * values
                high = square.astype(jnp.bfloat16)
                low = (square - high.astype(jnp.float32)).astype(jnp.bfloat16)
                rest = rest + (dot_nt(ones, high) + dot_nt(ones, low))
            rest = rest[0:1]
            for _ in range(3):
                piece = rest.astype(jnp.bfloat16).astype(jnp.float32)
                codes.append(piece)
                rest = rest - piece
            code_ref[:, start : start + CHUNK] = jnp.concatenate(codes, axis=0).astype(jnp.bfloat16)
        source = pl.ds(first, half)
        sides = (
            (emb_ref[...], vec_ref[:, source], sub),
            (emb_other_ref[source, :], vec_other_ref[:, source], 1 - sub),
        )
        for values, vectors, side in sides:
            ref[0:half, pl.ds(pl.multiple_of(side * width, width), width)] = values
            ref[pl.ds(pl.multiple_of(half + side * half_vecs, 16), half_vecs), :] = vectors
        first_code = half + 2 * half_vecs
        ref[first_code : first_code + CODE_ROWS, :] = code_ref[...]


def packs_of(emb_mine, emb_rest, emb_other, vec, vec_other, meta):
    half, width = emb_mine.shape
    features = 2 * width
    assert half == features
    size = pack_rows(half, 2 * vec_other.shape[0])
    return pl.pallas_call(
        pack_kernel,
        out_shape=[jax.ShapeDtypeStruct((size, features), jnp.bfloat16)] * 2,
        in_specs=[VMEM_SPEC] * 6,
        out_specs=[VMEM_SPEC] * 2,
        scratch_shapes=[pltpu.VMEM((CODE_ROWS, half), jnp.bfloat16)],
        compiler_params=params(),
        name="pack",
    )(emb_mine, emb_rest, emb_other, vec, vec_other, meta)


def decode(codes):
    codes = codes.astype(jnp.float32)
    numbers = [codes[2 * index : 2 * index + 1] + codes[2 * index + 1 : 2 * index + 2] for index in range(6)]
    left, right, bottom, top, first, last = numbers
    right, top = right + MARGIN, top + MARGIN
    square = codes[15:16] + codes[14:15] + codes[13:14]
    norm = lax.rsqrt(square + EPSILON) * COS_SCALE
    area = (right - left) * (top - bottom)
    return [left, right, bottom, top, first * GAP_SCALE + BASE, last * GAP_SCALE, codes[12:13], norm, area]


def with_ones(vectors):
    shape = (CODE_ROWS, vectors.shape[1])
    tail = jnp.where(lax.broadcasted_iota(jnp.int32, shape, 0) == 0, 1.0, 0.0)
    return jnp.concatenate([vectors, tail.astype(jnp.bfloat16)], axis=0)


def weights_of(products, row, col, same):
    width = jnp.maximum(jnp.minimum(row(RIGHT), col(RIGHT)) - jnp.maximum(row(LEFT), col(LEFT)), 0.0)
    height = jnp.maximum(jnp.minimum(row(TOP), col(TOP)) - jnp.maximum(row(BOTTOM), col(BOTTOM)), 0.0)
    inter = width * height
    both = row(AREA) + col(AREA)
    share = (both + inter) * pl.reciprocal(both - inter, approx=True)
    gap = jnp.maximum(col(FIRST) - row(LAST), row(FIRST) - col(LAST))
    logit = products * row(NORM) * col(NORM)
    value = jnp.exp2(logit - jnp.maximum(gap, BASE)) * share
    barred = (row(CAMERA) == col(CAMERA)) & (gap < BARRED_BELOW)
    if same is not None:
        barred = barred & jnp.logical_not(same)
    return jnp.where(barred, 0.0, value)


def tile_kernel(blocks, turns, own_block, receivers, vecs, *refs):
    row_ref, col_refs = refs[0], refs[1 : 1 + blocks]
    row_out_ref, col_out_ref, field_ref, spread_ref, sum_ref = refs[1 + blocks : 6 + blocks]
    products, weights, col_spreads = [refs[at : at + 2] for at in range(6 + blocks, 12 + blocks, 2)]
    size, rows = row_ref.shape
    features = size - vecs - CODE_ROWS
    vec_rows, code_rows = slice(features, features + vecs), slice(features + vecs, size)
    sum_ref[...] = jnp.zeros_like(sum_ref)

    def block(col_ref, done, row_vecs):
        chunks = col_ref.shape[1] // CHUNK

        def place(step, base=0):
            return pl.ds(pl.multiple_of(base + step * CHUNK, CHUNK), CHUNK)

        def multiply(step, product_ref):
            product_ref[...] = jnp.dot(
                row_ref[0:rows, :], col_ref[0:features, place(step)], preferred_element_type=jnp.float32
            )

        def weigh(step, product_ref, weight_ref, col_spread_ref):
            for field, values in enumerate(decode(col_ref[code_rows, place(step)])):
                col_spread_ref[field] = jnp.broadcast_to(values, (8, CHUNK))
            for first_row in range(0, rows, GROUP):
                row_part = slice(first_row, first_row + GROUP)

                def row(field):
                    return jnp.concatenate([spread_ref[field, row_part, :]] * (CHUNK // LANES), axis=1)

                def col(field):
                    return jnp.concatenate([col_spread_ref[field]] * (GROUP // 8), axis=0)

                same = None
                if own_block:
                    row_ids = lax.broadcasted_iota(jnp.int32, (GROUP, CHUNK), 0) + (first_row - step * CHUNK)
                    same = row_ids == lax.broadcasted_iota(jnp.int32, (GROUP, CHUNK), 1)
                weight_ref[row_part, :] = weights_of(product_ref[row_part, :], row, col, same).astype(jnp.bfloat16)

        def total(step, weight_ref):
            sum_ref[:, 0 : vecs + CODE_ROWS] += dot_nt(weight_ref[...], with_ones(col_ref[vec_rows, place(step)]))
            if not turns:
                col_out_ref[:, place(step, done)] = jnp.dot(
                    row_vecs, weight_ref[...], preferred_element_type=jnp.float32
                )[0:OUT_ROWS]

        def steps(index, carry):
            for parity in range(2):
                step = 2 * index + parity
                multiply(lax.rem(step + 1, chunks), products[1 - parity])
                weigh(step, products[parity], weights[parity], col_spreads[parity])
                total(lax.rem(step + chunks - 1, chunks), weights[1 - parity])
            return carry

        multiply(0, products[0])
        weights[1][...] = jnp.zeros_like(weights[1])
        lax.fori_loop(0, chunks // 2, steps, 0)
        total(chunks - 1, weights[1])

    def compute():
        for field, values in enumerate(decode(row_ref[code_rows, :])):
            field_ref[field : field + 1, :] = values
        turned = field_ref[...].T
        for field in range(FIELDS):
            spread_ref[field] = jnp.broadcast_to(turned[:, field : field + 1], (rows, LANES))
        row_vecs = with_ones(row_ref[vec_rows, :])
        if turns:
            for number, pack_ref in enumerate(col_refs):
                part = pl.ds(number * rows, rows)
                col_out_ref[0:features, part] = pack_ref[0:rows, :].T
                col_out_ref[features:size, part] = pack_ref[features:size, :]
            block(col_out_ref, 0, row_vecs)
        else:
            done = 0
            for col_ref in col_refs:
                block(col_ref, done, row_vecs)
                done += col_ref.shape[1]

    def finish():
        row_out_ref[...] = sum_ref[...].T[0:OUT_ROWS]

    if receivers is None:
        compute()
        finish()
        return
    pair = lax.axis_index("blk") // 2
    takes_part = functools.reduce(jnp.logical_or, [pair == one for one in receivers])

    @pl.when(takes_part)
    def _():
        compute()
        finish()

    @pl.when(jnp.logical_not(takes_part))
    def _():
        row_out_ref[...] = jnp.zeros_like(row_out_ref)
        col_out_ref[...] = jnp.zeros_like(col_out_ref)


def tile(row, columns, vecs, turns=False, own_block=False, receivers=None):
    size, rows = row.shape
    cols = len(columns) * rows if turns else sum(part.shape[1] for part in columns)
    second = jax.ShapeDtypeStruct((size, cols), jnp.bfloat16)
    if not turns:
        second = jax.ShapeDtypeStruct((OUT_ROWS, cols), jnp.float32)
    return pl.pallas_call(
        functools.partial(tile_kernel, len(columns), turns, own_block, receivers, vecs),
        out_shape=[jax.ShapeDtypeStruct((OUT_ROWS, rows), jnp.float32), second],
        in_specs=[VMEM_SPEC] * (1 + len(columns)),
        out_specs=[VMEM_SPEC] * 2,
        scratch_shapes=[
            pltpu.VMEM((LANES, rows), jnp.float32),
            pltpu.VMEM((FIELDS, rows, LANES), jnp.float32),
            pltpu.VMEM((rows, LANES), jnp.float32),
            pltpu.VMEM((rows, CHUNK), jnp.float32),
            pltpu.VMEM((rows, CHUNK), jnp.float32),
            pltpu.VMEM((rows, CHUNK), jnp.bfloat16),
            pltpu.VMEM((rows, CHUNK), jnp.bfloat16),
            pltpu.VMEM((FIELDS, 8, CHUNK), jnp.float32),
            pltpu.VMEM((FIELDS, 8, CHUNK), jnp.float32),
        ],
        cost_estimate=pl.CostEstimate(flops=COST, bytes_accessed=COST, transcendentals=0),
        compiler_params=params(),
        name="tile",
    )(row, *columns)


def image_kernel(*refs):
    parts, image_ref = refs[:-1], refs[-1]
    total = parts[0][...]
    for part in parts[1:]:
        total = total + part[...]
    vecs = image_ref.shape[0]
    image_ref[...] = total[0:vecs] / total[vecs : vecs + 1]


def image_of(parts, vecs):
    return pl.pallas_call(
        image_kernel,
        out_shape=jax.ShapeDtypeStruct((vecs, parts[0].shape[1]), jnp.float32),
        in_specs=[VMEM_SPEC] * len(parts),
        out_specs=VMEM_SPEC,
        compiler_params=params(),
        name="image",
    )(*parts)


def gram_kernel(image_ref, grams_ref):
    vecs, cols = image_ref.shape
    image = image_ref[...]
    padded = jnp.concatenate([image, jnp.zeros((LANES - vecs, cols), jnp.float32)], axis=0)
    gram = dot_nt(image, padded, lax.Precision.HIGHEST)
    packed = gram[0:8]
    for piece in range(1, vecs // 8):
        packed = packed + pltpu.roll(gram[8 * piece : 8 * piece + 8], piece * vecs, 1)
    for copy in range(grams_ref.shape[0]):
        grams_ref[copy] = packed


def grams_of(image, copies):
    return pl.pallas_call(
        gram_kernel,
        out_shape=jax.ShapeDtypeStruct((copies, 8, LANES), jnp.float32),
        in_specs=[VMEM_SPEC],
        out_specs=VMEM_SPEC,
        compiler_params=params(),
        name="gram",
    )(image)


def inverse_of(number):
    guess = pl.reciprocal(number, approx=True)
    guess = guess * (2.0 - number * guess)
    return guess * (2.0 - number * guess)


def basis_kernel(total_rows, grams_ref, mine_ref, other_ref, out_ref, inverse_ref):
    vecs, half = mine_ref.shape
    sub = lax.axis_index("sub")
    packed = jnp.sum(grams_ref[...], axis=0) / total_rows
    lane = lax.broadcasted_iota(jnp.int32, (vecs, LANES), 1)
    line = lax.broadcasted_iota(jnp.int32, (vecs, LANES), 0)
    pieces = [packed] + [pltpu.roll(packed, LANES - piece * vecs, 1) for piece in range(1, LANES // vecs)]
    matrix = jnp.where(lane < vecs, jnp.concatenate(pieces, axis=0), 0.0)
    matrix = jnp.where(lane == line + vecs, 1.0, matrix)
    for step in range(0, vecs, 2):
        left = jnp.broadcast_to(matrix[:, step : step + 1], (vecs, LANES))
        right = jnp.broadcast_to(matrix[:, step + 1 : step + 2], (vecs, LANES))
        upper, lower = matrix[step : step + 1, :], matrix[step + 1 : step + 2, :]
        across = right[step : step + 1, :]
        inverse = inverse_of(left[step : step + 1, :])
        factor = left[step + 1 : step + 2, :] * inverse
        lower = lower - factor * upper
        inverse_next = inverse_of(right[step + 1 : step + 2, :] - factor * across)
        first = left * inverse
        second = (right - first * across) * inverse_next
        reduced = matrix - first * upper - second * lower
        matrix = jnp.where(line > step + 1, reduced, jnp.where(line == step + 1, lower, matrix))
    pivots = jnp.sum(jnp.where(lane == line, matrix, 0.0), axis=1, keepdims=True)
    inverse_ref[...] = pltpu.roll(matrix / jnp.sqrt(pivots), LANES - vecs, 1)
    share = vecs // 2
    own_rows = inverse_ref[pl.ds(pl.multiple_of(sub * share, 8), share), :][:, 0:vecs]
    for ref, place in ((mine_ref, sub), (other_ref, 1 - sub)):
        out_ref[:, pl.ds(pl.multiple_of(place * half, LANES), half)] = jnp.dot(
            own_rows, ref[...], precision=lax.Precision.HIGHEST, preferred_element_type=jnp.float32
        )


def basis_of(grams, mine, other, total_rows):
    vecs, half = mine.shape
    return pl.pallas_call(
        functools.partial(basis_kernel, total_rows),
        out_shape=jax.ShapeDtypeStruct((vecs // 2, 2 * half), jnp.float32),
        in_specs=[VMEM_SPEC] * 3,
        out_specs=VMEM_SPEC,
        scratch_shapes=[pltpu.VMEM((vecs, LANES), jnp.float32)],
        compiler_params=params(),
        name="basis",
    )(grams, mine, other)


def exchanges(pairs):
    plans = []
    for distance in range(1, pairs // 2):
        plans.append(([((p + distance) % pairs, p) for p in range(pairs)], None))
    if pairs > 1:
        half = pairs // 2
        last = [(p, p + half) if p % 2 == 0 else (p + half, p) for p in range(half)]
        plans.append((last, sorted(taker for _, taker in last)))
    return plans


def block_moves(pair_moves):
    return [(2 * source + member, 2 * target + member) for source, target in pair_moves for member in range(2)]


def back(moves):
    return [(target, source) for source, target in moves]


def local(embeddings, vectors, boxes, spans, camera):
    rows = embeddings.shape[0]
    half = rows // 2
    vecs = 2 * vectors.shape[0]
    blocks = lax.axis_size("blk")
    swap = [(0, 1), (1, 0)]
    beside = [(block, block ^ 1) for block in range(blocks)]
    plans = [(block_moves(moves), takers) for moves, takers in exchanges(blocks // 2)]

    emb_other = lax.ppermute(embeddings, "sub", swap)
    vec_other = lax.ppermute(vectors, "sub", swap)
    meta = jnp.concatenate([boxes, spans, camera[None, :]], axis=0)
    sub = lax.axis_index("sub")
    halves = [lax.dynamic_slice_in_dim(embeddings, place * half, half, 0) for place in (sub, 1 - sub)]
    mine, rest = packs_of(*halves, emb_other, vectors, vec_other, meta)
    sent = [lax.ppermute(mine, "blk", moves) for moves, _ in plans]
    beside_mine = lax.ppermute(mine, "blk", beside)
    weigh = functools.partial(tile, vecs=vecs)
    own_sums, own = weigh(mine, [mine, rest], turns=True, own_block=True)
    own_sums, own, beside_mine, sent[:1] = lax.optimization_barrier((own_sums, own, beside_mine, sent[:1]))
    cut = beside_mine.shape[0] // SWAPS // 16 * 16
    shares = [beside_mine[at * cut : (at + 1) * cut if at < SWAPS - 1 else None] for at in range(SWAPS)]
    beside_rest = jnp.concatenate([lax.ppermute(share, "sub", swap) for share in shares], axis=0)
    beside_sums, next_to = weigh(mine, [beside_mine, beside_rest], turns=True)
    parts = [own_sums, beside_sums]
    col_sums = None
    returns = []
    for (moves, takers), pack in zip(plans, sent):
        if col_sums is not None:
            pack, col_sums = lax.optimization_barrier((pack, col_sums))
        row_sums, sums = weigh(pack, [own, next_to], receivers=takers)
        returns.append((row_sums, back(moves)))
        col_sums = sums if col_sums is None else col_sums + sums
    if col_sums is not None:
        own_mine, own_rest, next_mine, next_rest = [col_sums[:, place * half : (place + 1) * half] for place in range(4)]
        sides = lax.ppermute(jnp.concatenate([own_rest, next_rest], axis=1), "sub", swap)
        last_sums, last_moves = returns.pop()
        parts.append(lax.ppermute(last_sums, "blk", last_moves))
        crossing = next_mine + sides[:, half:]
        parts.append(own_mine)
        parts.append(sides[:, :half])
        for row_sums, moves in returns:
            row_sums, _ = lax.optimization_barrier((row_sums, crossing))
            parts.append(lax.ppermute(row_sums, "blk", moves))
        parts.append(lax.ppermute(crossing, "blk", beside))
    image = image_of(parts, vecs)
    image_other = lax.ppermute(image, "sub", swap)
    grams = lax.all_to_all(grams_of(image, 2 * blocks), ("blk", "sub"), 0, 0, tiled=True)
    return basis_of(grams, image, image_other, blocks * rows)


def solution(mesh):
    placed = (
        P(("groups", "blk"), "sub"),
        P("sub", ("groups", "blk")),
        P(None, ("groups", "blk")),
        P(None, ("groups", "blk")),
        P(("groups", "blk")),
    )
    return jax.shard_map(
        local, mesh=mesh, in_specs=placed, out_specs=P("sub", ("groups", "blk")), check_vma=False
    )
```

```python
import functools
import math

import jax
import jax.numpy as jnp
from jax import lax
from jax.experimental import pallas as pl
from jax.experimental.pallas import tpu as pltpu
from jax.sharding import PartitionSpec as P

SHARPNESS = 10.0
HORIZON = 2000.0
MARGIN = 8.0
EPSILON = 1e-06

LOG2E = math.log2(math.e)
COS_SCALE = math.sqrt(SHARPNESS * LOG2E)
GAP_SCALE = LOG2E / HORIZON
BASE = SHARPNESS * LOG2E + 1.0
BARRED_BELOW = BASE - 0.5 * GAP_SCALE

FIELDS = 9
LEFT, RIGHT, BOTTOM, TOP, FIRST, LAST, CAMERA, NORM, AREA = range(FIELDS)
CODE_ROWS = 16
LANES = 128
CHUNK = 256
OUT_ROWS = 40
COST = 1
GROUP = 32
SWAPS = 2
VMEM_LIMIT = 48 * 1024 * 1024

NT = (((1,), (1,)), ((), ()))
VMEM_SPEC = pl.BlockSpec(memory_space=pltpu.VMEM)


def params():
    return pltpu.CompilerParams(vmem_limit_bytes=VMEM_LIMIT)


def dot_nt(a, b, precision=None):
    return lax.dot_general(a, b, NT, precision=precision, preferred_element_type=jnp.float32)


def pack_rows(half, vecs):
    return half + vecs + CODE_ROWS


def pack_kernel(emb_mine_ref, emb_rest_ref, emb_other_ref, vec_ref, vec_other_ref, meta_ref, mine_ref, rest_ref, code_ref):
    sub = lax.axis_index("sub")
    half, width = emb_mine_ref.shape
    half_vecs = vec_other_ref.shape[0]
    ones = jnp.ones((8, width), jnp.bfloat16)
    for ref, emb_ref, place in ((mine_ref, emb_mine_ref, sub), (rest_ref, emb_rest_ref, 1 - sub)):
        first = pl.multiple_of(place * half, half)
        for start in range(0, half, CHUNK):
            part = pl.ds(first + start, CHUNK)
            codes = []

            def whole(number, low_bits):
                codes.append((number >> low_bits) << low_bits)
                codes.append(number & ((1 << low_bits) - 1))

            meta = meta_ref[:, part]
            for axis in range(2):
                whole(jnp.minimum(meta[axis : axis + 1], meta[axis + 2 : axis + 3]), 5)
                whole(jnp.maximum(meta[axis : axis + 1], meta[axis + 2 : axis + 3]), 5)
            whole(jnp.minimum(meta[4:5], meta[5:6]), 7)
            whole(jnp.maximum(meta[4:5], meta[5:6]), 7)
            codes.append(meta[6:7])
            codes = [code.astype(jnp.float32) for code in codes]
            rest = jnp.zeros((8, CHUNK), jnp.float32)
            for values in (emb_ref[start : start + CHUNK, :], emb_other_ref[part, :]):
                values = values.astype(jnp.float32)
                square = values * values
                high = square.astype(jnp.bfloat16)
                low = (square - high.astype(jnp.float32)).astype(jnp.bfloat16)
                rest = rest + (dot_nt(ones, high) + dot_nt(ones, low))
            rest = rest[0:1]
            for _ in range(3):
                piece = rest.astype(jnp.bfloat16).astype(jnp.float32)
                codes.append(piece)
                rest = rest - piece
            code_ref[:, start : start + CHUNK] = jnp.concatenate(codes, axis=0).astype(jnp.bfloat16)
        source = pl.ds(first, half)
        sides = (
            (emb_ref[...], vec_ref[:, source], sub),
            (emb_other_ref[source, :], vec_other_ref[:, source], 1 - sub),
        )
        for values, vectors, side in sides:
            ref[0:half, pl.ds(pl.multiple_of(side * width, width), width)] = values
            ref[pl.ds(pl.multiple_of(half + side * half_vecs, 16), half_vecs), :] = vectors
        first_code = half + 2 * half_vecs
        ref[first_code : first_code + CODE_ROWS, :] = code_ref[...]


def packs_of(emb_mine, emb_rest, emb_other, vec, vec_other, meta):
    half, width = emb_mine.shape
    features = 2 * width
    assert half == features
    size = pack_rows(half, 2 * vec_other.shape[0])
    return pl.pallas_call(
        pack_kernel,
        out_shape=[jax.ShapeDtypeStruct((size, features), jnp.bfloat16)] * 2,
        in_specs=[VMEM_SPEC] * 6,
        out_specs=[VMEM_SPEC] * 2,
        scratch_shapes=[pltpu.VMEM((CODE_ROWS, half), jnp.bfloat16)],
        compiler_params=params(),
        name="pack",
    )(emb_mine, emb_rest, emb_other, vec, vec_other, meta)


def decode(codes):
    codes = codes.astype(jnp.float32)
    numbers = [codes[2 * index : 2 * index + 1] + codes[2 * index + 1 : 2 * index + 2] for index in range(6)]
    left, right, bottom, top, first, last = numbers
    right, top = right + MARGIN, top + MARGIN
    square = codes[15:16] + codes[14:15] + codes[13:14]
    norm = lax.rsqrt(square + EPSILON) * COS_SCALE
    area = (right - left) * (top - bottom)
    return [left, right, bottom, top, first * GAP_SCALE + BASE, last * GAP_SCALE, codes[12:13], norm, area]


def with_ones(vectors):
    shape = (CODE_ROWS, vectors.shape[1])
    tail = jnp.where(lax.broadcasted_iota(jnp.int32, shape, 0) == 0, 1.0, 0.0)
    return jnp.concatenate([vectors, tail.astype(jnp.bfloat16)], axis=0)


def weights_of(products, row, col, same):
    width = jnp.maximum(jnp.minimum(row(RIGHT), col(RIGHT)) - jnp.maximum(row(LEFT), col(LEFT)), 0.0)
    height = jnp.maximum(jnp.minimum(row(TOP), col(TOP)) - jnp.maximum(row(BOTTOM), col(BOTTOM)), 0.0)
    inter = width * height
    both = row(AREA) + col(AREA)
    share = (both + inter) * pltpu.reciprocal(both - inter, approx=True, full_range=False)
    gap = jnp.maximum(col(FIRST) - row(LAST), row(FIRST) - col(LAST))
    logit = products * row(NORM) * col(NORM)
    value = jnp.exp2(logit - jnp.maximum(gap, BASE)) * share
    barred = (row(CAMERA) == col(CAMERA)) & (gap < BARRED_BELOW)
    if same is not None:
        barred = barred & jnp.logical_not(same)
    return jnp.where(barred, 0.0, value)


def tile_kernel(blocks, turns, own_block, receivers, vecs, *refs):
    row_ref, col_refs = refs[0], refs[1 : 1 + blocks]
    row_out_ref, col_out_ref, field_ref, spread_ref, sum_ref = refs[1 + blocks : 6 + blocks]
    products, weights, col_spreads = [refs[at : at + 2] for at in range(6 + blocks, 12 + blocks, 2)]
    size, rows = row_ref.shape
    features = size - vecs - CODE_ROWS
    vec_rows, code_rows = slice(features, features + vecs), slice(features + vecs, size)
    sum_ref[...] = jnp.zeros_like(sum_ref)

    def block(col_ref, done, row_vecs):
        chunks = col_ref.shape[1] // CHUNK

        def place(step, base=0):
            return pl.ds(pl.multiple_of(base + step * CHUNK, CHUNK), CHUNK)

        def multiply(step, product_ref):
            product_ref[...] = jnp.dot(
                row_ref[0:rows, :], col_ref[0:features, place(step)], preferred_element_type=jnp.float32
            )

        def weigh(step, product_ref, weight_ref, col_spread_ref):
            for field, values in enumerate(decode(col_ref[code_rows, place(step)])):
                col_spread_ref[field] = jnp.broadcast_to(values, (8, CHUNK))
            for first_row in range(0, rows, GROUP):
                row_part = slice(first_row, first_row + GROUP)

                def row(field):
                    return jnp.concatenate([spread_ref[field, row_part, :]] * (CHUNK // LANES), axis=1)

                def col(field):
                    return jnp.concatenate([col_spread_ref[field]] * (GROUP // 8), axis=0)

                same = None
                if own_block:
                    row_ids = lax.broadcasted_iota(jnp.int32, (GROUP, CHUNK), 0) + (first_row - step * CHUNK)
                    same = row_ids == lax.broadcasted_iota(jnp.int32, (GROUP, CHUNK), 1)
                weight_ref[row_part, :] = weights_of(product_ref[row_part, :], row, col, same).astype(jnp.bfloat16)

        def total(step, weight_ref):
            sum_ref[:, 0 : vecs + CODE_ROWS] += dot_nt(weight_ref[...], with_ones(col_ref[vec_rows, place(step)]))
            if not turns:
                col_out_ref[:, place(step, done)] = jnp.dot(
                    row_vecs, weight_ref[...], preferred_element_type=jnp.float32
                )[0:OUT_ROWS]

        def steps(index, carry):
            for parity in range(2):
                step = 2 * index + parity
                multiply(lax.rem(step + 1, chunks), products[1 - parity])
                weigh(step, products[parity], weights[parity], col_spreads[parity])
                total(lax.rem(step + chunks - 1, chunks), weights[1 - parity])
            return carry

        multiply(0, products[0])
        weights[1][...] = jnp.zeros_like(weights[1])
        lax.fori_loop(0, chunks // 2, steps, 0)
        total(chunks - 1, weights[1])

    def compute():
        for field, values in enumerate(decode(row_ref[code_rows, :])):
            field_ref[field : field + 1, :] = values
        turned = field_ref[...].T
        for field in range(FIELDS):
            spread_ref[field] = jnp.broadcast_to(turned[:, field : field + 1], (rows, LANES))
        row_vecs = with_ones(row_ref[vec_rows, :])
        if turns:
            for number, pack_ref in enumerate(col_refs):
                part = pl.ds(number * rows, rows)
                col_out_ref[0:features, part] = pack_ref[0:rows, :].T
                col_out_ref[features:size, part] = pack_ref[features:size, :]
            block(col_out_ref, 0, row_vecs)
        else:
            done = 0
            for col_ref in col_refs:
                block(col_ref, done, row_vecs)
                done += col_ref.shape[1]

    def finish():
        row_out_ref[...] = sum_ref[...].T[0:OUT_ROWS]

    if receivers is None:
        compute()
        finish()
        return
    pair = lax.axis_index("blk") // 2
    takes_part = functools.reduce(jnp.logical_or, [pair == one for one in receivers])

    @pl.when(takes_part)
    def _():
        compute()
        finish()

    @pl.when(jnp.logical_not(takes_part))
    def _():
        row_out_ref[...] = jnp.zeros_like(row_out_ref)
        col_out_ref[...] = jnp.zeros_like(col_out_ref)


def tile(row, columns, vecs, turns=False, own_block=False, receivers=None):
    size, rows = row.shape
    cols = len(columns) * rows if turns else sum(part.shape[1] for part in columns)
    second = jax.ShapeDtypeStruct((size, cols), jnp.bfloat16)
    if not turns:
        second = jax.ShapeDtypeStruct((OUT_ROWS, cols), jnp.float32)
    return pl.pallas_call(
        functools.partial(tile_kernel, len(columns), turns, own_block, receivers, vecs),
        out_shape=[jax.ShapeDtypeStruct((OUT_ROWS, rows), jnp.float32), second],
        in_specs=[VMEM_SPEC] * (1 + len(columns)),
        out_specs=[VMEM_SPEC] * 2,
        scratch_shapes=[
            pltpu.VMEM((LANES, rows), jnp.float32),
            pltpu.VMEM((FIELDS, rows, LANES), jnp.float32),
            pltpu.VMEM((rows, LANES), jnp.float32),
            pltpu.VMEM((rows, CHUNK), jnp.float32),
            pltpu.VMEM((rows, CHUNK), jnp.float32),
            pltpu.VMEM((rows, CHUNK), jnp.bfloat16),
            pltpu.VMEM((rows, CHUNK), jnp.bfloat16),
            pltpu.VMEM((FIELDS, 8, CHUNK), jnp.float32),
            pltpu.VMEM((FIELDS, 8, CHUNK), jnp.float32),
        ],
        cost_estimate=pl.CostEstimate(flops=COST, bytes_accessed=COST, transcendentals=0),
        compiler_params=params(),
        name="tile",
    )(row, *columns)


def image_kernel(*refs):
    parts, image_ref = refs[:-1], refs[-1]
    total = parts[0][...]
    for part in parts[1:]:
        total = total + part[...]
    vecs = image_ref.shape[0]
    image_ref[...] = total[0:vecs] / total[vecs : vecs + 1]


def image_of(parts, vecs):
    return pl.pallas_call(
        image_kernel,
        out_shape=jax.ShapeDtypeStruct((vecs, parts[0].shape[1]), jnp.float32),
        in_specs=[VMEM_SPEC] * len(parts),
        out_specs=VMEM_SPEC,
        compiler_params=params(),
        name="image",
    )(*parts)


def gram_kernel(image_ref, grams_ref):
    vecs, cols = image_ref.shape
    image = image_ref[...]
    padded = jnp.concatenate([image, jnp.zeros((LANES - vecs, cols), jnp.float32)], axis=0)
    gram = dot_nt(image, padded, lax.Precision.HIGHEST)
    packed = gram[0:8]
    for piece in range(1, vecs // 8):
        packed = packed + pltpu.roll(gram[8 * piece : 8 * piece + 8], piece * vecs, 1)
    for copy in range(grams_ref.shape[0]):
        grams_ref[copy] = packed


def grams_of(image, copies):
    return pl.pallas_call(
        gram_kernel,
        out_shape=jax.ShapeDtypeStruct((copies, 8, LANES), jnp.float32),
        in_specs=[VMEM_SPEC],
        out_specs=VMEM_SPEC,
        compiler_params=params(),
        name="gram",
    )(image)


def inverse_of(number):
    guess = pltpu.reciprocal(number, approx=True)
    guess = guess * (2.0 - number * guess)
    return guess * (2.0 - number * guess)


def basis_kernel(total_rows, grams_ref, mine_ref, other_ref, out_ref, inverse_ref):
    vecs, half = mine_ref.shape
    sub = lax.axis_index("sub")
    packed = jnp.sum(grams_ref[...], axis=0) / total_rows
    lane = lax.broadcasted_iota(jnp.int32, (vecs, LANES), 1)
    line = lax.broadcasted_iota(jnp.int32, (vecs, LANES), 0)
    pieces = [packed] + [pltpu.roll(packed, LANES - piece * vecs, 1) for piece in range(1, LANES // vecs)]
    matrix = jnp.where(lane < vecs, jnp.concatenate(pieces, axis=0), 0.0)
    matrix = jnp.where(lane == line + vecs, 1.0, matrix)
    for step in range(0, vecs, 2):
        left = jnp.broadcast_to(matrix[:, step : step + 1], (vecs, LANES))
        right = jnp.broadcast_to(matrix[:, step + 1 : step + 2], (vecs, LANES))
        upper, lower = matrix[step : step + 1, :], matrix[step + 1 : step + 2, :]
        across = right[step : step + 1, :]
        inverse = inverse_of(left[step : step + 1, :])
        factor = left[step + 1 : step + 2, :] * inverse
        lower = lower - factor * upper
        inverse_next = inverse_of(right[step + 1 : step + 2, :] - factor * across)
        first = left * inverse
        second = (right - first * across) * inverse_next
        reduced = matrix - first * upper - second * lower
        matrix = jnp.where(line > step + 1, reduced, jnp.where(line == step + 1, lower, matrix))
    pivots = jnp.sum(jnp.where(lane == line, matrix, 0.0), axis=1, keepdims=True)
    inverse_ref[...] = pltpu.roll(matrix / jnp.sqrt(pivots), LANES - vecs, 1)
    share = vecs // 2
    own_rows = inverse_ref[pl.ds(pl.multiple_of(sub * share, 8), share), :][:, 0:vecs]
    for ref, place in ((mine_ref, sub), (other_ref, 1 - sub)):
        out_ref[:, pl.ds(pl.multiple_of(place * half, LANES), half)] = jnp.dot(
            own_rows, ref[...], precision=lax.Precision.HIGHEST, preferred_element_type=jnp.float32
        )


def basis_of(grams, mine, other, total_rows):
    vecs, half = mine.shape
    return pl.pallas_call(
        functools.partial(basis_kernel, total_rows),
        out_shape=jax.ShapeDtypeStruct((vecs // 2, 2 * half), jnp.float32),
        in_specs=[VMEM_SPEC] * 3,
        out_specs=VMEM_SPEC,
        scratch_shapes=[pltpu.VMEM((vecs, LANES), jnp.float32)],
        compiler_params=params(),
        name="basis",
    )(grams, mine, other)


def exchanges(pairs):
    plans = []
    for distance in range(1, pairs // 2):
        plans.append(([((p + distance) % pairs, p) for p in range(pairs)], None))
    if pairs > 1:
        half = pairs // 2
        last = [(p, p + half) if p % 2 == 0 else (p + half, p) for p in range(half)]
        plans.append((last, sorted(taker for _, taker in last)))
    return plans


def block_moves(pair_moves):
    return [(2 * source + member, 2 * target + member) for source, target in pair_moves for member in range(2)]


def back(moves):
    return [(target, source) for source, target in moves]


def local(embeddings, vectors, boxes, spans, camera):
    rows = embeddings.shape[0]
    half = rows // 2
    vecs = 2 * vectors.shape[0]
    blocks = lax.axis_size("blk")
    swap = [(0, 1), (1, 0)]
    beside = [(block, block ^ 1) for block in range(blocks)]
    plans = [(block_moves(moves), takers) for moves, takers in exchanges(blocks // 2)]

    emb_other = lax.ppermute(embeddings, "sub", swap)
    vec_other = lax.ppermute(vectors, "sub", swap)
    meta = jnp.concatenate([boxes, spans, camera[None, :]], axis=0)
    sub = lax.axis_index("sub")
    halves = [lax.dynamic_slice_in_dim(embeddings, place * half, half, 0) for place in (sub, 1 - sub)]
    mine, rest = packs_of(*halves, emb_other, vectors, vec_other, meta)
    sent = [lax.ppermute(mine, "blk", moves) for moves, _ in plans]
    beside_mine = lax.ppermute(mine, "blk", beside)
    weigh = functools.partial(tile, vecs=vecs)
    own_sums, own = weigh(mine, [mine, rest], turns=True, own_block=True)
    own_sums, own, beside_mine, sent[:1] = lax.optimization_barrier((own_sums, own, beside_mine, sent[:1]))
    cut = beside_mine.shape[0] // SWAPS // 16 * 16
    shares = [beside_mine[at * cut : (at + 1) * cut if at < SWAPS - 1 else None] for at in range(SWAPS)]
    beside_rest = jnp.concatenate([lax.ppermute(share, "sub", swap) for share in shares], axis=0)
    beside_sums, next_to = weigh(mine, [beside_mine, beside_rest], turns=True)
    parts = [own_sums, beside_sums]
    col_sums = None
    for (moves, takers), pack in zip(plans, sent):
        if col_sums is not None:
            pack, col_sums, parts[-1] = lax.optimization_barrier((pack, col_sums, parts[-1]))
        row_sums, sums = weigh(pack, [own, next_to], receivers=takers)
        parts.append(lax.ppermute(row_sums, "blk", back(moves)))
        col_sums = sums if col_sums is None else col_sums + sums
    if col_sums is not None:
        own_mine, own_rest, next_mine, next_rest = [col_sums[:, place * half : (place + 1) * half] for place in range(4)]
        sides = lax.ppermute(jnp.concatenate([own_rest, next_rest], axis=1), "sub", swap)
        parts.append(own_mine)
        parts.append(sides[:, :half])
        parts.append(lax.ppermute(next_mine + sides[:, half:], "blk", beside))
    image = image_of(parts, vecs)
    image_other = lax.ppermute(image, "sub", swap)
    grams = lax.all_to_all(grams_of(image, 2 * blocks), ("blk", "sub"), 0, 0, tiled=True)
    return basis_of(grams, image, image_other, blocks * rows)


def solution(mesh):
    placed = (
        P(("groups", "blk"), "sub"),
        P("sub", ("groups", "blk")),
        P(None, ("groups", "blk")),
        P(None, ("groups", "blk")),
        P(("groups", "blk")),
    )
    return jax.shard_map(
        local, mesh=mesh, in_specs=placed, out_specs=P("sub", ("groups", "blk")), check_vma=False
    )
```

```python
import functools
import math

import jax
import jax.numpy as jnp
from jax import lax
from jax.experimental import pallas as pl
from jax.experimental.pallas import tpu as pltpu
from jax.sharding import PartitionSpec as P

SHARPNESS = 10.0
HORIZON = 2000.0
MARGIN = 8.0
EPSILON = 1e-06

LOG2E = math.log2(math.e)
COS_SCALE = math.sqrt(SHARPNESS * LOG2E)
GAP_SCALE = LOG2E / HORIZON
BASE = SHARPNESS * LOG2E + 1.0
BARRED_BELOW = BASE - 0.5 * GAP_SCALE

FIELDS = 9
LEFT, RIGHT, BOTTOM, TOP, FIRST, LAST, CAMERA, NORM, AREA = range(FIELDS)
CODE_ROWS = 16
LANES = 128
CHUNK = 256
OUT_ROWS = 40
COST = 1
GROUP = 32
SWAPS = 2
VMEM_LIMIT = 48 * 1024 * 1024

NT = (((1,), (1,)), ((), ()))
VMEM_SPEC = pl.BlockSpec(memory_space=pltpu.VMEM)


def params():
    return pltpu.CompilerParams(vmem_limit_bytes=VMEM_LIMIT)


def dot_nt(a, b, precision=None):
    return lax.dot_general(a, b, NT, precision=precision, preferred_element_type=jnp.float32)


def pack_rows(half, vecs):
    return half + vecs + CODE_ROWS


def pack_kernel(emb_mine_ref, emb_rest_ref, emb_other_ref, vec_ref, vec_other_ref, meta_ref, mine_ref, rest_ref, code_ref):
    sub = lax.axis_index("sub")
    half, width = emb_mine_ref.shape
    half_vecs = vec_other_ref.shape[0]
    ones = jnp.ones((8, width), jnp.bfloat16)
    for ref, emb_ref, place in ((mine_ref, emb_mine_ref, sub), (rest_ref, emb_rest_ref, 1 - sub)):
        first = pl.multiple_of(place * half, half)
        for start in range(0, half, CHUNK):
            part = pl.ds(first + start, CHUNK)
            codes = []

            def whole(number, low_bits):
                codes.append((number >> low_bits) << low_bits)
                codes.append(number & ((1 << low_bits) - 1))

            meta = meta_ref[:, part]
            for axis in range(2):
                whole(jnp.minimum(meta[axis : axis + 1], meta[axis + 2 : axis + 3]), 5)
                whole(jnp.maximum(meta[axis : axis + 1], meta[axis + 2 : axis + 3]), 5)
            whole(jnp.minimum(meta[4:5], meta[5:6]), 7)
            whole(jnp.maximum(meta[4:5], meta[5:6]), 7)
            codes.append(meta[6:7])
            codes = [code.astype(jnp.float32) for code in codes]
            rest = jnp.zeros((8, CHUNK), jnp.float32)
            for values in (emb_ref[start : start + CHUNK, :], emb_other_ref[part, :]):
                values = values.astype(jnp.float32)
                square = values * values
                high = square.astype(jnp.bfloat16)
                low = (square - high.astype(jnp.float32)).astype(jnp.bfloat16)
                rest = rest + (dot_nt(ones, high) + dot_nt(ones, low))
            rest = rest[0:1]
            for _ in range(3):
                piece = rest.astype(jnp.bfloat16).astype(jnp.float32)
                codes.append(piece)
                rest = rest - piece
            code_ref[:, start : start + CHUNK] = jnp.concatenate(codes, axis=0).astype(jnp.bfloat16)
        source = pl.ds(first, half)
        sides = (
            (emb_ref[...], vec_ref[:, source], sub),
            (emb_other_ref[source, :], vec_other_ref[:, source], 1 - sub),
        )
        for values, vectors, side in sides:
            ref[0:half, pl.ds(pl.multiple_of(side * width, width), width)] = values
            ref[pl.ds(pl.multiple_of(half + side * half_vecs, 16), half_vecs), :] = vectors
        first_code = half + 2 * half_vecs
        ref[first_code : first_code + CODE_ROWS, :] = code_ref[...]


def packs_of(emb_mine, emb_rest, emb_other, vec, vec_other, meta):
    half, width = emb_mine.shape
    features = 2 * width
    assert half == features
    size = pack_rows(half, 2 * vec_other.shape[0])
    return pl.pallas_call(
        pack_kernel,
        out_shape=[jax.ShapeDtypeStruct((size, features), jnp.bfloat16)] * 2,
        in_specs=[VMEM_SPEC] * 6,
        out_specs=[VMEM_SPEC] * 2,
        scratch_shapes=[pltpu.VMEM((CODE_ROWS, half), jnp.bfloat16)],
        compiler_params=params(),
        name="pack",
    )(emb_mine, emb_rest, emb_other, vec, vec_other, meta)


def decode(codes):
    codes = codes.astype(jnp.float32)
    numbers = [codes[2 * index : 2 * index + 1] + codes[2 * index + 1 : 2 * index + 2] for index in range(6)]
    left, right, bottom, top, first, last = numbers
    right, top = right + MARGIN, top + MARGIN
    square = codes[15:16] + codes[14:15] + codes[13:14]
    norm = lax.rsqrt(square + EPSILON) * COS_SCALE
    area = (right - left) * (top - bottom)
    return [left, right, bottom, top, first * GAP_SCALE + BASE, last * GAP_SCALE, codes[12:13], norm, area]


def with_ones(vectors):
    shape = (CODE_ROWS, vectors.shape[1])
    tail = jnp.where(lax.broadcasted_iota(jnp.int32, shape, 0) == 0, 1.0, 0.0)
    return jnp.concatenate([vectors, tail.astype(jnp.bfloat16)], axis=0)


def weights_of(products, row, col, same):
    width = jnp.maximum(jnp.minimum(row(RIGHT), col(RIGHT)) - jnp.maximum(row(LEFT), col(LEFT)), 0.0)
    height = jnp.maximum(jnp.minimum(row(TOP), col(TOP)) - jnp.maximum(row(BOTTOM), col(BOTTOM)), 0.0)
    inter = width * height
    both = row(AREA) + col(AREA)
    share = (both + inter) * pltpu.reciprocal(both - inter, approx=True, full_range=False)
    gap = jnp.maximum(col(FIRST) - row(LAST), row(FIRST) - col(LAST))
    logit = products * row(NORM) * col(NORM)
    value = jnp.exp2(logit - jnp.maximum(gap, BASE)) * share
    barred = (row(CAMERA) == col(CAMERA)) & (gap < BARRED_BELOW)
    if same is not None:
        barred = barred & jnp.logical_not(same)
    return jnp.where(barred, 0.0, value)


def tile_kernel(blocks, turns, own_block, receivers, vecs, lines, *refs):
    row_ref, col_refs = refs[0], refs[1 : 1 + blocks]
    row_out_ref, col_out_ref, field_ref, spread_ref, sum_ref = refs[1 + blocks : 6 + blocks]
    products, weights = [refs[at : at + 2] for at in (6 + blocks, 8 + blocks)]
    col_spread_ref, row_vec_ref, col_vec_ref = refs[10 + blocks :]
    size, rows = row_ref.shape
    features = size - vecs - CODE_ROWS
    vec_rows, code_rows = slice(features, features + vecs), slice(features + vecs, size)
    sum_ref[...] = jnp.zeros_like(sum_ref)

    def block(col_ref, done):
        chunks = col_ref.shape[1] // CHUNK

        def place(step, base=0):
            return pl.ds(pl.multiple_of(base + step * CHUNK, CHUNK), CHUNK)

        def multiply(step, part, product_ref):
            product_ref[part, :] = jnp.dot(
                row_ref[part, :], col_ref[0:features, place(step)], preferred_element_type=jnp.float32
            )

        def weigh(step, first, product_ref, weight_ref):
            for start in range(0, lines, GROUP):
                row_part = pl.ds(pl.multiple_of(first + start, GROUP), GROUP)

                def row(field):
                    return jnp.concatenate([spread_ref[field, row_part, :]] * (CHUNK // LANES), axis=1)

                def col(field):
                    return jnp.concatenate([col_spread_ref[field]] * (GROUP // 8), axis=0)

                same = None
                if own_block:
                    row_ids = lax.broadcasted_iota(jnp.int32, (GROUP, CHUNK), 0) + (first + start - step * CHUNK)
                    same = row_ids == lax.broadcasted_iota(jnp.int32, (GROUP, CHUNK), 1)
                weight_ref[row_part, :] = weights_of(product_ref[row_part, :], row, col, same).astype(jnp.bfloat16)

        def prepare_total(step):
            col_vec_ref[...] = with_ones(col_ref[vec_rows, place(step)])
            if not turns:
                col_out_ref[:, place(step, done)] = jnp.zeros((OUT_ROWS, CHUNK), jnp.float32)

        def total(step, part, weight_ref):
            sum_ref[part, 0 : vecs + CODE_ROWS] += dot_nt(weight_ref[part, :], col_vec_ref[...])
            if not turns:
                col_out_ref[:, place(step, done)] += jnp.dot(
                    row_vec_ref[:, part], weight_ref[part, :], preferred_element_type=jnp.float32
                )[0:OUT_ROWS]

        def steps(index, carry):
            for parity in range(2):
                step = 2 * index + parity
                ahead, behind = lax.rem(step + 1, chunks), lax.rem(step + chunks - 1, chunks)
                for field, values in enumerate(decode(col_ref[code_rows, place(step)])):
                    col_spread_ref[field] = jnp.broadcast_to(values, (8, CHUNK))
                prepare_total(behind)

                def some_lines(number, inner, parity=parity, step=step, ahead=ahead, behind=behind):
                    first = pl.multiple_of(number * lines, lines)
                    part = pl.ds(first, lines)
                    multiply(ahead, part, products[1 - parity])
                    weigh(step, first, products[parity], weights[parity])
                    total(behind, part, weights[1 - parity])
                    return inner

                lax.fori_loop(0, rows // lines, some_lines, 0)
            return carry

        multiply(0, pl.ds(0, rows), products[0])
        weights[1][...] = jnp.zeros_like(weights[1])
        lax.fori_loop(0, chunks // 2, steps, 0)
        prepare_total(chunks - 1)
        total(chunks - 1, pl.ds(0, rows), weights[1])

    def compute():
        for field, values in enumerate(decode(row_ref[code_rows, :])):
            field_ref[field : field + 1, :] = values
        turned = field_ref[...].T
        for field in range(FIELDS):
            spread_ref[field] = jnp.broadcast_to(turned[:, field : field + 1], (rows, LANES))
        row_vec_ref[...] = with_ones(row_ref[vec_rows, :])
        if turns:
            for number, pack_ref in enumerate(col_refs):
                part = pl.ds(number * rows, rows)
                col_out_ref[0:features, part] = pack_ref[0:rows, :].T
                col_out_ref[features:size, part] = pack_ref[features:size, :]
            block(col_out_ref, 0)
        else:
            done = 0
            for col_ref in col_refs:
                block(col_ref, done)
                done += col_ref.shape[1]

    def finish():
        row_out_ref[...] = sum_ref[...].T[0:OUT_ROWS]

    if receivers is None:
        compute()
        finish()
        return
    pair = lax.axis_index("blk") // 2
    takes_part = functools.reduce(jnp.logical_or, [pair == one for one in receivers])

    @pl.when(takes_part)
    def _():
        compute()
        finish()

    @pl.when(jnp.logical_not(takes_part))
    def _():
        row_out_ref[...] = jnp.zeros_like(row_out_ref)
        col_out_ref[...] = jnp.zeros_like(col_out_ref)


def tile(row, columns, vecs, lines, turns=False, own_block=False, receivers=None):
    size, rows = row.shape
    cols = len(columns) * rows if turns else sum(part.shape[1] for part in columns)
    second = jax.ShapeDtypeStruct((size, cols), jnp.bfloat16)
    if not turns:
        second = jax.ShapeDtypeStruct((OUT_ROWS, cols), jnp.float32)
    return pl.pallas_call(
        functools.partial(tile_kernel, len(columns), turns, own_block, receivers, vecs, lines),
        out_shape=[jax.ShapeDtypeStruct((OUT_ROWS, rows), jnp.float32), second],
        in_specs=[VMEM_SPEC] * (1 + len(columns)),
        out_specs=[VMEM_SPEC] * 2,
        scratch_shapes=[
            pltpu.VMEM((LANES, rows), jnp.float32),
            pltpu.VMEM((FIELDS, rows, LANES), jnp.float32),
            pltpu.VMEM((rows, LANES), jnp.float32),
            pltpu.VMEM((rows, CHUNK), jnp.float32),
            pltpu.VMEM((rows, CHUNK), jnp.float32),
            pltpu.VMEM((rows, CHUNK), jnp.bfloat16),
            pltpu.VMEM((rows, CHUNK), jnp.bfloat16),
            pltpu.VMEM((FIELDS, 8, CHUNK), jnp.float32),
            pltpu.VMEM((vecs + CODE_ROWS, rows), jnp.bfloat16),
            pltpu.VMEM((vecs + CODE_ROWS, CHUNK), jnp.bfloat16),
        ],
        cost_estimate=pl.CostEstimate(flops=COST, bytes_accessed=COST, transcendentals=0),
        compiler_params=params(),
        name="tile",
    )(row, *columns)


def image_kernel(*refs):
    parts, image_ref = refs[:-1], refs[-1]
    total = parts[0][...]
    for part in parts[1:]:
        total = total + part[...]
    vecs = image_ref.shape[0]
    image_ref[...] = total[0:vecs] / total[vecs : vecs + 1]


def image_of(parts, vecs):
    return pl.pallas_call(
        image_kernel,
        out_shape=jax.ShapeDtypeStruct((vecs, parts[0].shape[1]), jnp.float32),
        in_specs=[VMEM_SPEC] * len(parts),
        out_specs=VMEM_SPEC,
        compiler_params=params(),
        name="image",
    )(*parts)


def gram_kernel(image_ref, grams_ref):
    vecs, cols = image_ref.shape
    image = image_ref[...]
    padded = jnp.concatenate([image, jnp.zeros((LANES - vecs, cols), jnp.float32)], axis=0)
    gram = dot_nt(image, padded, lax.Precision.HIGHEST)
    packed = gram[0:8]
    for piece in range(1, vecs // 8):
        packed = packed + pltpu.roll(gram[8 * piece : 8 * piece + 8], piece * vecs, 1)
    for copy in range(grams_ref.shape[0]):
        grams_ref[copy] = packed


def grams_of(image, copies):
    return pl.pallas_call(
        gram_kernel,
        out_shape=jax.ShapeDtypeStruct((copies, 8, LANES), jnp.float32),
        in_specs=[VMEM_SPEC],
        out_specs=VMEM_SPEC,
        compiler_params=params(),
        name="gram",
    )(image)


def inverse_of(number):
    guess = pltpu.reciprocal(number, approx=True)
    guess = guess * (2.0 - number * guess)
    return guess * (2.0 - number * guess)


def basis_kernel(total_rows, grams_ref, mine_ref, other_ref, out_ref, inverse_ref):
    vecs, half = mine_ref.shape
    sub = lax.axis_index("sub")
    packed = jnp.sum(grams_ref[...], axis=0) / total_rows
    lane = lax.broadcasted_iota(jnp.int32, (vecs, LANES), 1)
    line = lax.broadcasted_iota(jnp.int32, (vecs, LANES), 0)
    pieces = [packed] + [pltpu.roll(packed, LANES - piece * vecs, 1) for piece in range(1, LANES // vecs)]
    matrix = jnp.where(lane < vecs, jnp.concatenate(pieces, axis=0), 0.0)
    matrix = jnp.where(lane == line + vecs, 1.0, matrix)
    for step in range(0, vecs, 2):
        left = jnp.broadcast_to(matrix[:, step : step + 1], (vecs, LANES))
        right = jnp.broadcast_to(matrix[:, step + 1 : step + 2], (vecs, LANES))
        upper, lower = matrix[step : step + 1, :], matrix[step + 1 : step + 2, :]
        across = right[step : step + 1, :]
        inverse = inverse_of(left[step : step + 1, :])
        factor = left[step + 1 : step + 2, :] * inverse
        lower = lower - factor * upper
        inverse_next = inverse_of(right[step + 1 : step + 2, :] - factor * across)
        first = left * inverse
        second = (right - first * across) * inverse_next
        reduced = matrix - first * upper - second * lower
        matrix = jnp.where(line > step + 1, reduced, jnp.where(line == step + 1, lower, matrix))
    pivots = jnp.sum(jnp.where(lane == line, matrix, 0.0), axis=1, keepdims=True)
    inverse_ref[...] = pltpu.roll(matrix / jnp.sqrt(pivots), LANES - vecs, 1)
    share = vecs // 2
    own_rows = inverse_ref[pl.ds(pl.multiple_of(sub * share, 8), share), :][:, 0:vecs]
    for ref, place in ((mine_ref, sub), (other_ref, 1 - sub)):
        out_ref[:, pl.ds(pl.multiple_of(place * half, LANES), half)] = jnp.dot(
            own_rows, ref[...], precision=lax.Precision.HIGHEST, preferred_element_type=jnp.float32
        )


def basis_of(grams, mine, other, total_rows):
    vecs, half = mine.shape
    return pl.pallas_call(
        functools.partial(basis_kernel, total_rows),
        out_shape=jax.ShapeDtypeStruct((vecs // 2, 2 * half), jnp.float32),
        in_specs=[VMEM_SPEC] * 3,
        out_specs=VMEM_SPEC,
        scratch_shapes=[pltpu.VMEM((vecs, LANES), jnp.float32)],
        compiler_params=params(),
        name="basis",
    )(grams, mine, other)


def exchanges(pairs):
    plans = []
    for distance in range(1, pairs // 2):
        plans.append(([((p + distance) % pairs, p) for p in range(pairs)], None))
    if pairs > 1:
        half = pairs // 2
        last = [(p, p + half) if p % 2 == 0 else (p + half, p) for p in range(half)]
        plans.append((last, sorted(taker for _, taker in last)))
    return plans


def block_moves(pair_moves):
    return [(2 * source + member, 2 * target + member) for source, target in pair_moves for member in range(2)]


def back(moves):
    return [(target, source) for source, target in moves]


def local(embeddings, vectors, boxes, spans, camera):
    rows = embeddings.shape[0]
    half = rows // 2
    vecs = 2 * vectors.shape[0]
    blocks = lax.axis_size("blk")
    swap = [(0, 1), (1, 0)]
    beside = [(block, block ^ 1) for block in range(blocks)]
    plans = [(block_moves(moves), takers) for moves, takers in exchanges(blocks // 2)]

    emb_other = lax.ppermute(embeddings, "sub", swap)
    vec_other = lax.ppermute(vectors, "sub", swap)
    meta = jnp.concatenate([boxes, spans, camera[None, :]], axis=0)
    sub = lax.axis_index("sub")
    halves = [lax.dynamic_slice_in_dim(embeddings, place * half, half, 0) for place in (sub, 1 - sub)]
    mine, rest = packs_of(*halves, emb_other, vectors, vec_other, meta)
    sent = [lax.ppermute(mine, "blk", moves) for moves, _ in plans]
    beside_mine = lax.ppermute(mine, "blk", beside)
    weigh = functools.partial(tile, vecs=vecs)
    own_sums, own = weigh(mine, [mine, rest], lines=128, turns=True, own_block=True)
    own_sums, own, beside_mine, sent[:1] = lax.optimization_barrier((own_sums, own, beside_mine, sent[:1]))
    cut = beside_mine.shape[0] // SWAPS // 16 * 16
    shares = [beside_mine[at * cut : (at + 1) * cut if at < SWAPS - 1 else None] for at in range(SWAPS)]
    beside_rest = jnp.concatenate([lax.ppermute(share, "sub", swap) for share in shares], axis=0)
    beside_sums, next_to = weigh(mine, [beside_mine, beside_rest], lines=256, turns=True)
    parts = [own_sums, beside_sums]
    col_sums = None
    returns = []
    for number, ((moves, takers), pack) in enumerate(zip(plans, sent)):
        if col_sums is not None:
            pack, col_sums = lax.optimization_barrier((pack, col_sums))
        row_sums, sums = weigh(pack, [own, next_to], lines=128 if number == 0 else 256, receivers=takers)
        returns.append((row_sums, back(moves)))
        col_sums = sums if col_sums is None else col_sums + sums
    if col_sums is not None:
        own_mine, own_rest, next_mine, next_rest = [col_sums[:, place * half : (place + 1) * half] for place in range(4)]
        sides = lax.ppermute(jnp.concatenate([own_rest, next_rest], axis=1), "sub", swap)
        last_sums, last_moves = returns.pop()
        parts.append(lax.ppermute(last_sums, "blk", last_moves))
        crossing = next_mine + sides[:, half:]
        parts.append(own_mine)
        parts.append(sides[:, :half])
        for row_sums, moves in returns:
            row_sums, _ = lax.optimization_barrier((row_sums, crossing))
            parts.append(lax.ppermute(row_sums, "blk", moves))
        parts.append(lax.ppermute(crossing, "blk", beside))
    image = image_of(parts, vecs)
    image_other = lax.ppermute(image, "sub", swap)
    grams = lax.all_to_all(grams_of(image, 2 * blocks), ("blk", "sub"), 0, 0, tiled=True)
    return basis_of(grams, image, image_other, blocks * rows)


def solution(mesh):
    placed = (
        P(("groups", "blk"), "sub"),
        P("sub", ("groups", "blk")),
        P(None, ("groups", "blk")),
        P(None, ("groups", "blk")),
        P(("groups", "blk")),
    )
    return jax.shard_map(
        local, mesh=mesh, in_specs=placed, out_specs=P("sub", ("groups", "blk")), check_vma=False
    )
```

```python
import functools
import math

import jax
import jax.numpy as jnp
from jax import lax
from jax.experimental import pallas as pl
from jax.experimental.pallas import tpu as pltpu
from jax.sharding import PartitionSpec as P

SHARPNESS = 10.0
HORIZON = 2000.0
MARGIN = 8.0
EPSILON = 1e-06

LOG2E = math.log2(math.e)
COS_SCALE = math.sqrt(SHARPNESS * LOG2E)
GAP_SCALE = LOG2E / HORIZON
BASE = SHARPNESS * LOG2E + 1.0
BARRED_BELOW = BASE - 0.5 * GAP_SCALE

FIELDS = 9
LEFT, RIGHT, BOTTOM, TOP, FIRST, LAST, CAMERA, NORM, AREA = range(FIELDS)
CODE_ROWS = 16
LANES = 128
CHUNK = 256
OUT_ROWS = 40
COST = 1
WIDE = 512
GROUP = 16
SWAPS = 2
VMEM_LIMIT = 48 * 1024 * 1024

NT = (((1,), (1,)), ((), ()))
VMEM_SPEC = pl.BlockSpec(memory_space=pltpu.VMEM)


def params():
    return pltpu.CompilerParams(vmem_limit_bytes=VMEM_LIMIT)


def dot_nt(a, b, precision=None):
    return lax.dot_general(a, b, NT, precision=precision, preferred_element_type=jnp.float32)


def pack_rows(half, vecs):
    return half + vecs + CODE_ROWS


def pack_kernel(emb_mine_ref, emb_rest_ref, emb_other_ref, vec_ref, vec_other_ref, meta_ref, mine_ref, rest_ref, code_ref):
    sub = lax.axis_index("sub")
    half, width = emb_mine_ref.shape
    half_vecs = vec_other_ref.shape[0]
    ones = jnp.ones((8, width), jnp.bfloat16)
    for ref, emb_ref, place in ((mine_ref, emb_mine_ref, sub), (rest_ref, emb_rest_ref, 1 - sub)):
        first = pl.multiple_of(place * half, half)
        for start in range(0, half, CHUNK):
            part = pl.ds(first + start, CHUNK)
            codes = []

            def whole(number, low_bits):
                codes.append((number >> low_bits) << low_bits)
                codes.append(number & ((1 << low_bits) - 1))

            meta = meta_ref[:, part]
            for axis in range(2):
                whole(jnp.minimum(meta[axis : axis + 1], meta[axis + 2 : axis + 3]), 5)
                whole(jnp.maximum(meta[axis : axis + 1], meta[axis + 2 : axis + 3]), 5)
            whole(jnp.minimum(meta[4:5], meta[5:6]), 7)
            whole(jnp.maximum(meta[4:5], meta[5:6]), 7)
            codes.append(meta[6:7])
            codes = [code.astype(jnp.float32) for code in codes]
            rest = jnp.zeros((8, CHUNK), jnp.float32)
            for values in (emb_ref[start : start + CHUNK, :], emb_other_ref[part, :]):
                values = values.astype(jnp.float32)
                square = values * values
                high = square.astype(jnp.bfloat16)
                low = (square - high.astype(jnp.float32)).astype(jnp.bfloat16)
                rest = rest + (dot_nt(ones, high) + dot_nt(ones, low))
            rest = rest[0:1]
            for _ in range(3):
                piece = rest.astype(jnp.bfloat16).astype(jnp.float32)
                codes.append(piece)
                rest = rest - piece
            code_ref[:, start : start + CHUNK] = jnp.concatenate(codes, axis=0).astype(jnp.bfloat16)
        source = pl.ds(first, half)
        sides = (
            (emb_ref[...], vec_ref[:, source], sub),
            (emb_other_ref[source, :], vec_other_ref[:, source], 1 - sub),
        )
        for values, vectors, side in sides:
            ref[0:half, pl.ds(pl.multiple_of(side * width, width), width)] = values
            ref[pl.ds(pl.multiple_of(half + side * half_vecs, 16), half_vecs), :] = vectors
        first_code = half + 2 * half_vecs
        ref[first_code : first_code + CODE_ROWS, :] = code_ref[...]


def packs_of(emb_mine, emb_rest, emb_other, vec, vec_other, meta):
    half, width = emb_mine.shape
    features = 2 * width
    assert half == features
    size = pack_rows(half, 2 * vec_other.shape[0])
    return pl.pallas_call(
        pack_kernel,
        out_shape=[jax.ShapeDtypeStruct((size, features), jnp.bfloat16)] * 2,
        in_specs=[VMEM_SPEC] * 6,
        out_specs=[VMEM_SPEC] * 2,
        scratch_shapes=[pltpu.VMEM((CODE_ROWS, half), jnp.bfloat16)],
        compiler_params=params(),
        name="pack",
    )(emb_mine, emb_rest, emb_other, vec, vec_other, meta)


def decode(codes):
    codes = codes.astype(jnp.float32)
    numbers = [codes[2 * index : 2 * index + 1] + codes[2 * index + 1 : 2 * index + 2] for index in range(6)]
    left, right, bottom, top, first, last = numbers
    right, top = right + MARGIN, top + MARGIN
    square = codes[15:16] + codes[14:15] + codes[13:14]
    norm = lax.rsqrt(square + EPSILON) * COS_SCALE
    area = (right - left) * (top - bottom)
    return [left, right, bottom, top, first * GAP_SCALE + BASE, last * GAP_SCALE, codes[12:13], norm, area]


def with_ones(vectors):
    shape = (CODE_ROWS, vectors.shape[1])
    tail = jnp.where(lax.broadcasted_iota(jnp.int32, shape, 0) == 0, 1.0, 0.0)
    return jnp.concatenate([vectors, tail.astype(jnp.bfloat16)], axis=0)


def weights_of(products, row, col, same):
    width = jnp.maximum(jnp.minimum(row(RIGHT), col(RIGHT)) - jnp.maximum(row(LEFT), col(LEFT)), 0.0)
    height = jnp.maximum(jnp.minimum(row(TOP), col(TOP)) - jnp.maximum(row(BOTTOM), col(BOTTOM)), 0.0)
    inter = width * height
    both = row(AREA) + col(AREA)
    share = (both + inter) * pltpu.reciprocal(both - inter, approx=True, full_range=False)
    gap = jnp.maximum(col(FIRST) - row(LAST), row(FIRST) - col(LAST))
    logit = products * row(NORM) * col(NORM)
    value = jnp.exp2(logit - jnp.maximum(gap, BASE)) * share
    barred = (row(CAMERA) == col(CAMERA)) & (gap < BARRED_BELOW)
    if same is not None:
        barred = barred & jnp.logical_not(same)
    return jnp.where(barred, 0.0, value)


def tile_kernel(blocks, turns, own_block, receivers, vecs, lines, *refs):
    row_ref, col_refs = refs[0], refs[1 : 1 + blocks]
    row_out_ref, col_out_ref, field_ref, spread_ref = refs[1 + blocks : 5 + blocks]
    products, weights = [refs[at : at + 2] for at in (5 + blocks, 7 + blocks)]
    col_spread_ref, row_vec_ref, col_vec_ref = refs[9 + blocks :]
    size, rows = row_ref.shape
    features = size - vecs - CODE_ROWS
    vec_rows, code_rows = slice(features, features + vecs), slice(features + vecs, size)
    row_out_ref[...] = jnp.zeros_like(row_out_ref)

    def block(col_ref, done):
        chunks = col_ref.shape[1] // WIDE

        def place(step, base=0):
            return pl.ds(pl.multiple_of(base + step * WIDE, WIDE), WIDE)

        def multiply(step, part, product_ref):
            product_ref[part, :] = jnp.dot(
                row_ref[part, :], col_ref[0:features, place(step)], preferred_element_type=jnp.float32
            )

        def weigh(step, first, product_ref, weight_ref):
            for start in range(0, lines, GROUP):
                row_part = pl.ds(pl.multiple_of(first + start, GROUP), GROUP)

                def row(field):
                    return jnp.concatenate([spread_ref[field, row_part, :]] * (WIDE // LANES), axis=1)

                def col(field):
                    return jnp.concatenate([col_spread_ref[field]] * (GROUP // 8), axis=0)

                same = None
                if own_block:
                    row_ids = lax.broadcasted_iota(jnp.int32, (GROUP, WIDE), 0) + (first + start - step * WIDE)
                    same = row_ids == lax.broadcasted_iota(jnp.int32, (GROUP, WIDE), 1)
                weight_ref[row_part, :] = weights_of(product_ref[row_part, :], row, col, same).astype(jnp.bfloat16)

        def prepare_total(step):
            col_vec_ref[...] = with_ones(col_ref[vec_rows, place(step)])
            if not turns:
                col_out_ref[:, place(step, done)] = jnp.zeros((OUT_ROWS, WIDE), jnp.float32)

        def total(step, part, weight_ref):
            row_out_ref[:, part] += dot_nt(col_vec_ref[...], weight_ref[part, :])[0:OUT_ROWS]
            if not turns:
                col_out_ref[:, place(step, done)] += jnp.dot(
                    row_vec_ref[:, part], weight_ref[part, :], preferred_element_type=jnp.float32
                )[0:OUT_ROWS]

        def steps(index, carry):
            for parity in range(2):
                step = 2 * index + parity
                ahead, behind = lax.rem(step + 1, chunks), lax.rem(step + chunks - 1, chunks)
                for field, values in enumerate(decode(col_ref[code_rows, place(step)])):
                    col_spread_ref[field] = jnp.broadcast_to(values, (8, WIDE))
                prepare_total(behind)

                def some_lines(number, inner, parity=parity, step=step, ahead=ahead, behind=behind):
                    first = pl.multiple_of(number * lines, lines)
                    part = pl.ds(first, lines)
                    multiply(ahead, part, products[1 - parity])
                    weigh(step, first, products[parity], weights[parity])
                    total(behind, part, weights[1 - parity])
                    return inner

                lax.fori_loop(0, rows // lines, some_lines, 0)
            return carry

        multiply(0, pl.ds(0, rows), products[0])
        weights[1][...] = jnp.zeros_like(weights[1])
        lax.fori_loop(0, chunks // 2, steps, 0)
        prepare_total(chunks - 1)
        total(chunks - 1, pl.ds(0, rows), weights[1])

    def compute():
        for field, values in enumerate(decode(row_ref[code_rows, :])):
            field_ref[field : field + 1, :] = values
        turned = field_ref[...].T
        for field in range(FIELDS):
            spread_ref[field] = jnp.broadcast_to(turned[:, field : field + 1], (rows, LANES))
        row_vec_ref[...] = with_ones(row_ref[vec_rows, :])
        if turns:
            for number, pack_ref in enumerate(col_refs):
                part = pl.ds(number * rows, rows)
                col_out_ref[0:features, part] = pack_ref[0:rows, :].T
                col_out_ref[features:size, part] = pack_ref[features:size, :]
            block(col_out_ref, 0)
        else:
            done = 0
            for col_ref in col_refs:
                block(col_ref, done)
                done += col_ref.shape[1]

    if receivers is None:
        compute()
        return
    pair = lax.axis_index("blk") // 2
    takes_part = functools.reduce(jnp.logical_or, [pair == one for one in receivers])

    @pl.when(takes_part)
    def _():
        compute()

    @pl.when(jnp.logical_not(takes_part))
    def _():
        col_out_ref[...] = jnp.zeros_like(col_out_ref)


def tile(row, columns, vecs, lines, turns=False, own_block=False, receivers=None):
    size, rows = row.shape
    cols = len(columns) * rows if turns else sum(part.shape[1] for part in columns)
    second = jax.ShapeDtypeStruct((size, cols), jnp.bfloat16)
    if not turns:
        second = jax.ShapeDtypeStruct((OUT_ROWS, cols), jnp.float32)
    return pl.pallas_call(
        functools.partial(tile_kernel, len(columns), turns, own_block, receivers, vecs, lines),
        out_shape=[jax.ShapeDtypeStruct((OUT_ROWS, rows), jnp.float32), second],
        in_specs=[VMEM_SPEC] * (1 + len(columns)),
        out_specs=[VMEM_SPEC] * 2,
        scratch_shapes=[
            pltpu.VMEM((LANES, rows), jnp.float32),
            pltpu.VMEM((FIELDS, rows, LANES), jnp.float32),
            pltpu.VMEM((rows, WIDE), jnp.float32),
            pltpu.VMEM((rows, WIDE), jnp.float32),
            pltpu.VMEM((rows, WIDE), jnp.bfloat16),
            pltpu.VMEM((rows, WIDE), jnp.bfloat16),
            pltpu.VMEM((FIELDS, 8, WIDE), jnp.float32),
            pltpu.VMEM((vecs + CODE_ROWS, rows), jnp.bfloat16),
            pltpu.VMEM((vecs + CODE_ROWS, WIDE), jnp.bfloat16),
        ],
        cost_estimate=pl.CostEstimate(flops=COST, bytes_accessed=COST, transcendentals=0),
        compiler_params=params(),
        name="tile",
    )(row, *columns)


def image_kernel(*refs):
    parts, image_ref = refs[:-1], refs[-1]
    total = parts[0][...]
    for part in parts[1:]:
        total = total + part[...]
    vecs = image_ref.shape[0]
    image_ref[...] = total[0:vecs] / total[vecs : vecs + 1]


def image_of(parts, vecs):
    return pl.pallas_call(
        image_kernel,
        out_shape=jax.ShapeDtypeStruct((vecs, parts[0].shape[1]), jnp.float32),
        in_specs=[VMEM_SPEC] * len(parts),
        out_specs=VMEM_SPEC,
        compiler_params=params(),
        name="image",
    )(*parts)


def gram_kernel(image_ref, grams_ref):
    vecs, cols = image_ref.shape
    image = image_ref[...]
    padded = jnp.concatenate([image, jnp.zeros((LANES - vecs, cols), jnp.float32)], axis=0)
    gram = dot_nt(image, padded, lax.Precision.HIGHEST)
    packed = gram[0:8]
    for piece in range(1, vecs // 8):
        packed = packed + pltpu.roll(gram[8 * piece : 8 * piece + 8], piece * vecs, 1)
    for copy in range(grams_ref.shape[0]):
        grams_ref[copy] = packed


def grams_of(image, copies):
    return pl.pallas_call(
        gram_kernel,
        out_shape=jax.ShapeDtypeStruct((copies, 8, LANES), jnp.float32),
        in_specs=[VMEM_SPEC],
        out_specs=VMEM_SPEC,
        compiler_params=params(),
        name="gram",
    )(image)


def inverse_of(number):
    guess = pltpu.reciprocal(number, approx=True)
    guess = guess * (2.0 - number * guess)
    return guess * (2.0 - number * guess)


def basis_kernel(total_rows, grams_ref, mine_ref, other_ref, out_ref, inverse_ref):
    vecs, half = mine_ref.shape
    sub = lax.axis_index("sub")
    packed = jnp.sum(grams_ref[...], axis=0) / total_rows
    lane = lax.broadcasted_iota(jnp.int32, (vecs, LANES), 1)
    line = lax.broadcasted_iota(jnp.int32, (vecs, LANES), 0)
    pieces = [packed] + [pltpu.roll(packed, LANES - piece * vecs, 1) for piece in range(1, LANES // vecs)]
    matrix = jnp.where(lane < vecs, jnp.concatenate(pieces, axis=0), 0.0)
    matrix = jnp.where(lane == line + vecs, 1.0, matrix)
    for step in range(0, vecs, 2):
        left = jnp.broadcast_to(matrix[:, step : step + 1], (vecs, LANES))
        right = jnp.broadcast_to(matrix[:, step + 1 : step + 2], (vecs, LANES))
        upper, lower = matrix[step : step + 1, :], matrix[step + 1 : step + 2, :]
        across = right[step : step + 1, :]
        inverse = inverse_of(left[step : step + 1, :])
        factor = left[step + 1 : step + 2, :] * inverse
        lower = lower - factor * upper
        inverse_next = inverse_of(right[step + 1 : step + 2, :] - factor * across)
        first = left * inverse
        second = (right - first * across) * inverse_next
        reduced = matrix - first * upper - second * lower
        matrix = jnp.where(line > step + 1, reduced, jnp.where(line == step + 1, lower, matrix))
    pivots = jnp.sum(jnp.where(lane == line, matrix, 0.0), axis=1, keepdims=True)
    inverse_ref[...] = pltpu.roll(matrix / jnp.sqrt(pivots), LANES - vecs, 1)
    share = vecs // 2
    own_rows = inverse_ref[pl.ds(pl.multiple_of(sub * share, 8), share), :][:, 0:vecs]
    for ref, place in ((mine_ref, sub), (other_ref, 1 - sub)):
        out_ref[:, pl.ds(pl.multiple_of(place * half, LANES), half)] = jnp.dot(
            own_rows, ref[...], precision=lax.Precision.HIGHEST, preferred_element_type=jnp.float32
        )


def basis_of(grams, mine, other, total_rows):
    vecs, half = mine.shape
    return pl.pallas_call(
        functools.partial(basis_kernel, total_rows),
        out_shape=jax.ShapeDtypeStruct((vecs // 2, 2 * half), jnp.float32),
        in_specs=[VMEM_SPEC] * 3,
        out_specs=VMEM_SPEC,
        scratch_shapes=[pltpu.VMEM((vecs, LANES), jnp.float32)],
        compiler_params=params(),
        name="basis",
    )(grams, mine, other)


def exchanges(pairs):
    plans = []
    for distance in range(1, pairs // 2):
        plans.append(([((p + distance) % pairs, p) for p in range(pairs)], None))
    if pairs > 1:
        half = pairs // 2
        last = [(p, p + half) if p % 2 == 0 else (p + half, p) for p in range(half)]
        plans.append((last, sorted(taker for _, taker in last)))
    return plans


def block_moves(pair_moves):
    return [(2 * source + member, 2 * target + member) for source, target in pair_moves for member in range(2)]


def back(moves):
    return [(target, source) for source, target in moves]


def local(embeddings, vectors, boxes, spans, camera):
    rows = embeddings.shape[0]
    half = rows // 2
    vecs = 2 * vectors.shape[0]
    blocks = lax.axis_size("blk")
    swap = [(0, 1), (1, 0)]
    beside = [(block, block ^ 1) for block in range(blocks)]
    plans = [(block_moves(moves), takers) for moves, takers in exchanges(blocks // 2)]

    emb_other = lax.ppermute(embeddings, "sub", swap)
    vec_other = lax.ppermute(vectors, "sub", swap)
    meta = jnp.concatenate([boxes, spans, camera[None, :]], axis=0)
    sub = lax.axis_index("sub")
    halves = [lax.dynamic_slice_in_dim(embeddings, place * half, half, 0) for place in (sub, 1 - sub)]
    mine, rest = packs_of(*halves, emb_other, vectors, vec_other, meta)
    sent = [lax.ppermute(mine, "blk", moves) for moves, _ in plans]
    beside_mine = lax.ppermute(mine, "blk", beside)
    weigh = functools.partial(tile, vecs=vecs)
    own_sums, own = weigh(mine, [mine, rest], lines=256, turns=True, own_block=True)
    own_sums, own, beside_mine, sent[:1] = lax.optimization_barrier((own_sums, own, beside_mine, sent[:1]))
    cut = beside_mine.shape[0] // SWAPS // 16 * 16
    shares = [beside_mine[at * cut : (at + 1) * cut if at < SWAPS - 1 else None] for at in range(SWAPS)]
    beside_rest = jnp.concatenate([lax.ppermute(share, "sub", swap) for share in shares], axis=0)
    beside_sums, next_to = weigh(mine, [beside_mine, beside_rest], lines=256, turns=True)
    parts = [own_sums, beside_sums]
    col_sums = None
    returns = []
    for number, ((moves, takers), pack) in enumerate(zip(plans, sent)):
        if col_sums is not None:
            pack, col_sums = lax.optimization_barrier((pack, col_sums))
        row_sums, sums = weigh(pack, [own, next_to], lines=256 if number == 0 else 512, receivers=takers)
        returns.append((row_sums, back(moves)))
        col_sums = sums if col_sums is None else col_sums + sums
    if col_sums is not None:
        own_mine, own_rest, next_mine, next_rest = [col_sums[:, place * half : (place + 1) * half] for place in range(4)]
        sides = lax.ppermute(jnp.concatenate([own_rest, next_rest], axis=1), "sub", swap)
        last_sums, last_moves = returns.pop()
        parts.append(lax.ppermute(last_sums, "blk", last_moves))
        crossing = next_mine + sides[:, half:]
        parts.append(own_mine)
        parts.append(sides[:, :half])
        for row_sums, moves in returns:
            row_sums, _ = lax.optimization_barrier((row_sums, crossing))
            parts.append(lax.ppermute(row_sums, "blk", moves))
        parts.append(lax.ppermute(crossing, "blk", beside))
    image = image_of(parts, vecs)
    image_other = lax.ppermute(image, "sub", swap)
    grams = lax.all_to_all(grams_of(image, 2 * blocks), ("blk", "sub"), 0, 0, tiled=True)
    return basis_of(grams, image, image_other, blocks * rows)


def solution(mesh):
    placed = (
        P(("groups", "blk"), "sub"),
        P("sub", ("groups", "blk")),
        P(None, ("groups", "blk")),
        P(None, ("groups", "blk")),
        P(("groups", "blk")),
    )
    return jax.shard_map(
        local, mesh=mesh, in_specs=placed, out_specs=P("sub", ("groups", "blk")), check_vma=False
    )
```

```python
import functools
import math

import jax
import jax.numpy as jnp
from jax import lax
from jax.experimental import pallas as pl
from jax.experimental.pallas import tpu as pltpu
from jax.sharding import PartitionSpec as P

SHARPNESS = 10.0
HORIZON = 2000.0
MARGIN = 8.0
EPSILON = 1e-06

LOG2E = math.log2(math.e)
COS_SCALE = math.sqrt(SHARPNESS * LOG2E)
GAP_SCALE = LOG2E / HORIZON
BASE = SHARPNESS * LOG2E + 1.0
BARRED_BELOW = BASE - 0.5 * GAP_SCALE

FIELDS = 9
LEFT, RIGHT, BOTTOM, TOP, FIRST, LAST, CAMERA, NORM, AREA = range(FIELDS)
CODE_ROWS = 16
LANES = 128
CHUNK = 256
OUT_ROWS = 40
COST = 1
WIDE = 512
GROUP = 16
SWAPS = 2
VMEM_LIMIT = 48 * 1024 * 1024

NT = (((1,), (1,)), ((), ()))
VMEM_SPEC = pl.BlockSpec(memory_space=pltpu.VMEM)


def params():
    return pltpu.CompilerParams(vmem_limit_bytes=VMEM_LIMIT)


def dot_nt(a, b, precision=None):
    return lax.dot_general(a, b, NT, precision=precision, preferred_element_type=jnp.float32)


def pack_rows(half, vecs):
    return half + vecs + CODE_ROWS


def pack_kernel(emb_mine_ref, emb_rest_ref, emb_other_ref, vec_ref, vec_other_ref, meta_ref, mine_ref, rest_ref, code_ref):
    sub = lax.axis_index("sub")
    half, width = emb_mine_ref.shape
    half_vecs = vec_other_ref.shape[0]
    ones = jnp.ones((8, width), jnp.bfloat16)
    for ref, emb_ref, place in ((mine_ref, emb_mine_ref, sub), (rest_ref, emb_rest_ref, 1 - sub)):
        first = pl.multiple_of(place * half, half)
        for start in range(0, half, CHUNK):
            part = pl.ds(first + start, CHUNK)
            codes = []

            def whole(number, low_bits):
                codes.append((number >> low_bits) << low_bits)
                codes.append(number & ((1 << low_bits) - 1))

            meta = meta_ref[:, part]
            for axis in range(2):
                whole(jnp.minimum(meta[axis : axis + 1], meta[axis + 2 : axis + 3]), 5)
                whole(jnp.maximum(meta[axis : axis + 1], meta[axis + 2 : axis + 3]), 5)
            whole(jnp.minimum(meta[4:5], meta[5:6]), 7)
            whole(jnp.maximum(meta[4:5], meta[5:6]), 7)
            codes.append(meta[6:7])
            codes = [code.astype(jnp.float32) for code in codes]
            rest = jnp.zeros((8, CHUNK), jnp.float32)
            for values in (emb_ref[start : start + CHUNK, :], emb_other_ref[part, :]):
                values = values.astype(jnp.float32)
                square = values * values
                high = square.astype(jnp.bfloat16)
                low = (square - high.astype(jnp.float32)).astype(jnp.bfloat16)
                rest = rest + (dot_nt(ones, high) + dot_nt(ones, low))
            rest = rest[0:1]
            for _ in range(3):
                piece = rest.astype(jnp.bfloat16).astype(jnp.float32)
                codes.append(piece)
                rest = rest - piece
            code_ref[:, start : start + CHUNK] = jnp.concatenate(codes, axis=0).astype(jnp.bfloat16)
        source = pl.ds(first, half)
        sides = (
            (emb_ref[...], vec_ref[:, source], sub),
            (emb_other_ref[source, :], vec_other_ref[:, source], 1 - sub),
        )
        for values, vectors, side in sides:
            ref[0:half, pl.ds(pl.multiple_of(side * width, width), width)] = values
            ref[pl.ds(pl.multiple_of(half + side * half_vecs, 16), half_vecs), :] = vectors
        first_code = half + 2 * half_vecs
        ref[first_code : first_code + CODE_ROWS, :] = code_ref[...]


def packs_of(emb_mine, emb_rest, emb_other, vec, vec_other, meta):
    half, width = emb_mine.shape
    features = 2 * width
    assert half == features
    size = pack_rows(half, 2 * vec_other.shape[0])
    return pl.pallas_call(
        pack_kernel,
        out_shape=[jax.ShapeDtypeStruct((size, features), jnp.bfloat16)] * 2,
        in_specs=[VMEM_SPEC] * 6,
        out_specs=[VMEM_SPEC] * 2,
        scratch_shapes=[pltpu.VMEM((CODE_ROWS, half), jnp.bfloat16)],
        compiler_params=params(),
        name="pack",
    )(emb_mine, emb_rest, emb_other, vec, vec_other, meta)


def decode(codes):
    codes = codes.astype(jnp.float32)
    numbers = [codes[2 * index : 2 * index + 1] + codes[2 * index + 1 : 2 * index + 2] for index in range(6)]
    left, right, bottom, top, first, last = numbers
    right, top = right + MARGIN, top + MARGIN
    square = codes[15:16] + codes[14:15] + codes[13:14]
    norm = lax.rsqrt(square + EPSILON) * COS_SCALE
    area = (right - left) * (top - bottom)
    return [left, right, bottom, top, first * GAP_SCALE + BASE, last * GAP_SCALE, codes[12:13], norm, area]


def with_ones(vectors):
    shape = (CODE_ROWS, vectors.shape[1])
    tail = jnp.where(lax.broadcasted_iota(jnp.int32, shape, 0) == 0, 1.0, 0.0)
    return jnp.concatenate([vectors, tail.astype(jnp.bfloat16)], axis=0)


def weights_of(products, row, col, same):
    width = jnp.maximum(jnp.minimum(row(RIGHT), col(RIGHT)) - jnp.maximum(row(LEFT), col(LEFT)), 0.0)
    height = jnp.maximum(jnp.minimum(row(TOP), col(TOP)) - jnp.maximum(row(BOTTOM), col(BOTTOM)), 0.0)
    inter = width * height
    both = row(AREA) + col(AREA)
    share = (both + inter) * pltpu.reciprocal(both - inter, approx=True, full_range=False)
    gap = jnp.maximum(col(FIRST) - row(LAST), row(FIRST) - col(LAST))
    logit = products * row(NORM) * col(NORM)
    value = jnp.exp2(logit - jnp.maximum(gap, BASE)) * share
    barred = (row(CAMERA) == col(CAMERA)) & (gap < BARRED_BELOW)
    if same is not None:
        barred = barred & jnp.logical_not(same)
    return jnp.where(barred, 0.0, value)


def tile_kernel(blocks, turns, own_block, receivers, vecs, *refs):
    row_ref, col_refs = refs[0], refs[1 : 1 + blocks]
    row_out_ref, col_out_ref, field_ref, spread_ref = refs[1 + blocks : 5 + blocks]
    products, weights = [refs[at : at + 2] for at in (5 + blocks, 7 + blocks)]
    col_spread_ref, row_vec_ref = refs[9 + blocks :]
    size, rows = row_ref.shape
    features = size - vecs - CODE_ROWS
    vec_rows, code_rows = slice(features, features + vecs), slice(features + vecs, size)
    row_out_ref[...] = jnp.zeros_like(row_out_ref)

    def block(col_ref, done):
        chunks = col_ref.shape[1] // WIDE

        def place(step, base=0):
            return pl.ds(pl.multiple_of(base + step * WIDE, WIDE), WIDE)

        def multiply(step, product_ref):
            product_ref[...] = jnp.dot(
                row_ref[0:rows, :], col_ref[0:features, place(step)], preferred_element_type=jnp.float32
            )

        def weigh(step, product_ref, weight_ref):
            for field, values in enumerate(decode(col_ref[code_rows, place(step)])):
                col_spread_ref[field] = jnp.broadcast_to(values, (8, WIDE))
            for start in range(0, rows, GROUP):
                row_part = slice(start, start + GROUP)

                def row(field):
                    return jnp.concatenate([spread_ref[field, row_part, :]] * (WIDE // LANES), axis=1)

                def col(field):
                    return jnp.concatenate([col_spread_ref[field]] * (GROUP // 8), axis=0)

                same = None
                if own_block:
                    row_ids = lax.broadcasted_iota(jnp.int32, (GROUP, WIDE), 0) + (start - step * WIDE)
                    same = row_ids == lax.broadcasted_iota(jnp.int32, (GROUP, WIDE), 1)
                weight_ref[row_part, :] = weights_of(product_ref[row_part, :], row, col, same).astype(jnp.bfloat16)

        def total(step, weight_ref):
            col_vecs = with_ones(col_ref[vec_rows, place(step)])
            row_out_ref[...] += dot_nt(col_vecs, weight_ref[...])[0:OUT_ROWS]
            if not turns:
                col_out_ref[:, place(step, done)] = jnp.dot(
                    row_vec_ref[...], weight_ref[...], preferred_element_type=jnp.float32
                )[0:OUT_ROWS]

        def steps(index, carry):
            for parity in range(2):
                step = 2 * index + parity
                multiply(lax.rem(step + 1, chunks), products[1 - parity])
                weigh(step, products[parity], weights[parity])
                total(lax.rem(step + chunks - 1, chunks), weights[1 - parity])
            return carry

        multiply(0, products[0])
        weights[1][...] = jnp.zeros_like(weights[1])
        lax.fori_loop(0, chunks // 2, steps, 0)
        total(chunks - 1, weights[1])

    def compute():
        for field, values in enumerate(decode(row_ref[code_rows, :])):
            field_ref[field : field + 1, :] = values
        turned = field_ref[...].T
        for field in range(FIELDS):
            spread_ref[field] = jnp.broadcast_to(turned[:, field : field + 1], (rows, LANES))
        row_vec_ref[...] = with_ones(row_ref[vec_rows, :])
        if turns:
            for number, pack_ref in enumerate(col_refs):
                part = pl.ds(number * rows, rows)
                col_out_ref[0:features, part] = pack_ref[0:rows, :].T
                col_out_ref[features:size, part] = pack_ref[features:size, :]
            block(col_out_ref, 0)
        else:
            done = 0
            for col_ref in col_refs:
                block(col_ref, done)
                done += col_ref.shape[1]

    if receivers is None:
        compute()
        return
    pair = lax.axis_index("blk") // 2
    takes_part = functools.reduce(jnp.logical_or, [pair == one for one in receivers])

    @pl.when(takes_part)
    def _():
        compute()

    @pl.when(jnp.logical_not(takes_part))
    def _():
        col_out_ref[...] = jnp.zeros_like(col_out_ref)


def tile(row, columns, vecs, turns=False, own_block=False, receivers=None):
    size, rows = row.shape
    cols = len(columns) * rows if turns else sum(part.shape[1] for part in columns)
    second = jax.ShapeDtypeStruct((size, cols), jnp.bfloat16)
    if not turns:
        second = jax.ShapeDtypeStruct((OUT_ROWS, cols), jnp.float32)
    return pl.pallas_call(
        functools.partial(tile_kernel, len(columns), turns, own_block, receivers, vecs),
        out_shape=[jax.ShapeDtypeStruct((OUT_ROWS, rows), jnp.float32), second],
        in_specs=[VMEM_SPEC] * (1 + len(columns)),
        out_specs=[VMEM_SPEC] * 2,
        scratch_shapes=[
            pltpu.VMEM((LANES, rows), jnp.float32),
            pltpu.VMEM((FIELDS, rows, LANES), jnp.float32),
            pltpu.VMEM((rows, WIDE), jnp.float32),
            pltpu.VMEM((rows, WIDE), jnp.float32),
            pltpu.VMEM((rows, WIDE), jnp.bfloat16),
            pltpu.VMEM((rows, WIDE), jnp.bfloat16),
            pltpu.VMEM((FIELDS, 8, WIDE), jnp.float32),
            pltpu.VMEM((vecs + CODE_ROWS, rows), jnp.bfloat16),
        ],
        cost_estimate=pl.CostEstimate(flops=COST, bytes_accessed=COST, transcendentals=0),
        compiler_params=params(),
        name="tile",
    )(row, *columns)


def image_kernel(*refs):
    parts, image_ref = refs[:-1], refs[-1]
    total = parts[0][...]
    for part in parts[1:]:
        total = total + part[...]
    vecs = image_ref.shape[0]
    image_ref[...] = total[0:vecs] / total[vecs : vecs + 1]


def image_of(parts, vecs):
    return pl.pallas_call(
        image_kernel,
        out_shape=jax.ShapeDtypeStruct((vecs, parts[0].shape[1]), jnp.float32),
        in_specs=[VMEM_SPEC] * len(parts),
        out_specs=VMEM_SPEC,
        compiler_params=params(),
        name="image",
    )(*parts)


def gram_kernel(image_ref, grams_ref):
    vecs, cols = image_ref.shape
    image = image_ref[...]
    padded = jnp.concatenate([image, jnp.zeros((LANES - vecs, cols), jnp.float32)], axis=0)
    gram = dot_nt(image, padded, lax.Precision.HIGHEST)
    packed = gram[0:8]
    for piece in range(1, vecs // 8):
        packed = packed + pltpu.roll(gram[8 * piece : 8 * piece + 8], piece * vecs, 1)
    for copy in range(grams_ref.shape[0]):
        grams_ref[copy] = packed


def grams_of(image, copies):
    return pl.pallas_call(
        gram_kernel,
        out_shape=jax.ShapeDtypeStruct((copies, 8, LANES), jnp.float32),
        in_specs=[VMEM_SPEC],
        out_specs=VMEM_SPEC,
        compiler_params=params(),
        name="gram",
    )(image)


def inverse_of(number):
    guess = pltpu.reciprocal(number, approx=True)
    guess = guess * (2.0 - number * guess)
    return guess * (2.0 - number * guess)


def basis_kernel(total_rows, grams_ref, mine_ref, other_ref, out_ref, inverse_ref):
    vecs, half = mine_ref.shape
    sub = lax.axis_index("sub")
    packed = jnp.sum(grams_ref[...], axis=0) / total_rows
    lane = lax.broadcasted_iota(jnp.int32, (vecs, LANES), 1)
    line = lax.broadcasted_iota(jnp.int32, (vecs, LANES), 0)
    pieces = [packed] + [pltpu.roll(packed, LANES - piece * vecs, 1) for piece in range(1, LANES // vecs)]
    matrix = jnp.where(lane < vecs, jnp.concatenate(pieces, axis=0), 0.0)
    matrix = jnp.where(lane == line + vecs, 1.0, matrix)
    for step in range(0, vecs, 2):
        left = jnp.broadcast_to(matrix[:, step : step + 1], (vecs, LANES))
        right = jnp.broadcast_to(matrix[:, step + 1 : step + 2], (vecs, LANES))
        upper, lower = matrix[step : step + 1, :], matrix[step + 1 : step + 2, :]
        across = right[step : step + 1, :]
        inverse = inverse_of(left[step : step + 1, :])
        factor = left[step + 1 : step + 2, :] * inverse
        lower = lower - factor * upper
        inverse_next = inverse_of(right[step + 1 : step + 2, :] - factor * across)
        first = left * inverse
        second = (right - first * across) * inverse_next
        reduced = matrix - first * upper - second * lower
        matrix = jnp.where(line > step + 1, reduced, jnp.where(line == step + 1, lower, matrix))
    pivots = jnp.sum(jnp.where(lane == line, matrix, 0.0), axis=1, keepdims=True)
    inverse_ref[...] = pltpu.roll(matrix / jnp.sqrt(pivots), LANES - vecs, 1)
    share = vecs // 2
    own_rows = inverse_ref[pl.ds(pl.multiple_of(sub * share, 8), share), :][:, 0:vecs]
    for ref, place in ((mine_ref, sub), (other_ref, 1 - sub)):
        out_ref[:, pl.ds(pl.multiple_of(place * half, LANES), half)] = jnp.dot(
            own_rows, ref[...], precision=lax.Precision.HIGHEST, preferred_element_type=jnp.float32
        )


def basis_of(grams, mine, other, total_rows):
    vecs, half = mine.shape
    return pl.pallas_call(
        functools.partial(basis_kernel, total_rows),
        out_shape=jax.ShapeDtypeStruct((vecs // 2, 2 * half), jnp.float32),
        in_specs=[VMEM_SPEC] * 3,
        out_specs=VMEM_SPEC,
        scratch_shapes=[pltpu.VMEM((vecs, LANES), jnp.float32)],
        compiler_params=params(),
        name="basis",
    )(grams, mine, other)


def exchanges(pairs):
    plans = []
    for distance in range(1, pairs // 2):
        plans.append(([((p + distance) % pairs, p) for p in range(pairs)], None))
    if pairs > 1:
        half = pairs // 2
        last = [(p, p + half) if p % 2 == 0 else (p + half, p) for p in range(half)]
        plans.append((last, sorted(taker for _, taker in last)))
    return plans


def block_moves(pair_moves):
    return [(2 * source + member, 2 * target + member) for source, target in pair_moves for member in range(2)]


def back(moves):
    return [(target, source) for source, target in moves]


def local(embeddings, vectors, boxes, spans, camera):
    rows = embeddings.shape[0]
    half = rows // 2
    vecs = 2 * vectors.shape[0]
    blocks = lax.axis_size("blk")
    swap = [(0, 1), (1, 0)]
    beside = [(block, block ^ 1) for block in range(blocks)]
    plans = [(block_moves(moves), takers) for moves, takers in exchanges(blocks // 2)]

    emb_other = lax.ppermute(embeddings, "sub", swap)
    vec_other = lax.ppermute(vectors, "sub", swap)
    meta = jnp.concatenate([boxes, spans, camera[None, :]], axis=0)
    sub = lax.axis_index("sub")
    halves = [lax.dynamic_slice_in_dim(embeddings, place * half, half, 0) for place in (sub, 1 - sub)]
    mine, rest = packs_of(*halves, emb_other, vectors, vec_other, meta)
    sent = [lax.ppermute(mine, "blk", moves) for moves, _ in plans]
    beside_mine = lax.ppermute(mine, "blk", beside)
    weigh = functools.partial(tile, vecs=vecs)
    own_sums, own = weigh(mine, [mine, rest], turns=True, own_block=True)
    own_sums, own, beside_mine, sent[:1] = lax.optimization_barrier((own_sums, own, beside_mine, sent[:1]))
    cut = beside_mine.shape[0] // SWAPS // 16 * 16
    shares = [beside_mine[at * cut : (at + 1) * cut if at < SWAPS - 1 else None] for at in range(SWAPS)]
    beside_rest = jnp.concatenate([lax.ppermute(share, "sub", swap) for share in shares], axis=0)
    first_sums = [weigh(pack, [own], receivers=takers) for (_, takers), pack in zip(plans[:1], sent[:1])]
    if first_sums:
        first_sums, beside_rest = lax.optimization_barrier((first_sums, beside_rest))
    beside_sums, next_to = weigh(mine, [beside_mine, beside_rest], turns=True)
    parts = [own_sums, beside_sums]
    col_sums = None
    for number, ((moves, takers), pack) in enumerate(zip(plans, sent)):
        if number == 0:
            row_sums, sums = weigh(pack, [next_to], receivers=takers)
            row_sums = row_sums + first_sums[0][0]
            col_sums = jnp.concatenate([first_sums[0][1], sums], axis=1)
        else:
            pack, col_sums, parts[-1] = lax.optimization_barrier((pack, col_sums, parts[-1]))
            row_sums, sums = weigh(pack, [own, next_to], receivers=takers)
            col_sums = col_sums + sums
        parts.append(lax.ppermute(row_sums, "blk", back(moves)))
    if col_sums is not None:
        own_mine, own_rest, next_mine, next_rest = [col_sums[:, place * half : (place + 1) * half] for place in range(4)]
        sides = lax.ppermute(jnp.concatenate([own_rest, next_rest], axis=1), "sub", swap)
        parts.append(own_mine)
        parts.append(sides[:, :half])
        parts.append(lax.ppermute(next_mine + sides[:, half:], "blk", beside))
    image = image_of(parts, vecs)
    image_other = lax.ppermute(image, "sub", swap)
    grams = lax.all_to_all(grams_of(image, 2 * blocks), ("blk", "sub"), 0, 0, tiled=True)
    return basis_of(grams, image, image_other, blocks * rows)


def solution(mesh):
    placed = (
        P(("groups", "blk"), "sub"),
        P("sub", ("groups", "blk")),
        P(None, ("groups", "blk")),
        P(None, ("groups", "blk")),
        P(("groups", "blk")),
    )
    return jax.shard_map(
        local, mesh=mesh, in_specs=placed, out_specs=P("sub", ("groups", "blk")), check_vma=False
    )
```

```python
import functools
import math

import jax
import jax.numpy as jnp
from jax import lax
from jax.experimental import pallas as pl
from jax.experimental.pallas import tpu as pltpu
from jax.sharding import PartitionSpec as P

SHARPNESS = 10.0
HORIZON = 2000.0
MARGIN = 8.0
EPSILON = 1e-06

LOG2E = math.log2(math.e)
COS_SCALE = math.sqrt(SHARPNESS * LOG2E)
GAP_SCALE = LOG2E / HORIZON
BASE = SHARPNESS * LOG2E + 1.0
BARRED_BELOW = BASE - 0.5 * GAP_SCALE

FIELDS = 9
LEFT, RIGHT, BOTTOM, TOP, FIRST, LAST, CAMERA, NORM, AREA = range(FIELDS)
CODE_ROWS = 16
LANES = 128
CHUNK = 256
OUT_ROWS = 40
COST = 1
WIDE = 512
GROUP = 16
SWAPS = 3
VMEM_LIMIT = 48 * 1024 * 1024

NT = (((1,), (1,)), ((), ()))
VMEM_SPEC = pl.BlockSpec(memory_space=pltpu.VMEM)


def params():
    return pltpu.CompilerParams(vmem_limit_bytes=VMEM_LIMIT)


def dot_nt(a, b, precision=None):
    return lax.dot_general(a, b, NT, precision=precision, preferred_element_type=jnp.float32)


def pack_rows(half, vecs):
    return half + vecs + CODE_ROWS


def pack_kernel(emb_mine_ref, emb_rest_ref, emb_other_ref, vec_ref, vec_other_ref, meta_ref, mine_ref, rest_ref, code_ref):
    sub = lax.axis_index("sub")
    half, width = emb_mine_ref.shape
    half_vecs = vec_other_ref.shape[0]
    ones = jnp.ones((8, width), jnp.bfloat16)
    for ref, emb_ref, place in ((mine_ref, emb_mine_ref, sub), (rest_ref, emb_rest_ref, 1 - sub)):
        first = pl.multiple_of(place * half, half)
        for start in range(0, half, CHUNK):
            part = pl.ds(first + start, CHUNK)
            codes = []

            def whole(number, low_bits):
                codes.append((number >> low_bits) << low_bits)
                codes.append(number & ((1 << low_bits) - 1))

            meta = meta_ref[:, part]
            for axis in range(2):
                whole(jnp.minimum(meta[axis : axis + 1], meta[axis + 2 : axis + 3]), 5)
                whole(jnp.maximum(meta[axis : axis + 1], meta[axis + 2 : axis + 3]), 5)
            whole(jnp.minimum(meta[4:5], meta[5:6]), 7)
            whole(jnp.maximum(meta[4:5], meta[5:6]), 7)
            codes.append(meta[6:7])
            codes = [code.astype(jnp.float32) for code in codes]
            rest = jnp.zeros((8, CHUNK), jnp.float32)
            for values in (emb_ref[start : start + CHUNK, :], emb_other_ref[part, :]):
                values = values.astype(jnp.float32)
                square = values * values
                high = square.astype(jnp.bfloat16)
                low = (square - high.astype(jnp.float32)).astype(jnp.bfloat16)
                rest = rest + (dot_nt(ones, high) + dot_nt(ones, low))
            rest = rest[0:1]
            for _ in range(3):
                piece = rest.astype(jnp.bfloat16).astype(jnp.float32)
                codes.append(piece)
                rest = rest - piece
            code_ref[:, start : start + CHUNK] = jnp.concatenate(codes, axis=0).astype(jnp.bfloat16)
        source = pl.ds(first, half)
        sides = (
            (emb_ref[...], vec_ref[:, source], sub),
            (emb_other_ref[source, :], vec_other_ref[:, source], 1 - sub),
        )
        for values, vectors, side in sides:
            ref[0:half, pl.ds(pl.multiple_of(side * width, width), width)] = values
            ref[pl.ds(pl.multiple_of(half + side * half_vecs, 16), half_vecs), :] = vectors
        first_code = half + 2 * half_vecs
        ref[first_code : first_code + CODE_ROWS, :] = code_ref[...]


def packs_of(emb_mine, emb_rest, emb_other, vec, vec_other, meta):
    half, width = emb_mine.shape
    features = 2 * width
    assert half == features
    size = pack_rows(half, 2 * vec_other.shape[0])
    return pl.pallas_call(
        pack_kernel,
        out_shape=[jax.ShapeDtypeStruct((size, features), jnp.bfloat16)] * 2,
        in_specs=[VMEM_SPEC] * 6,
        out_specs=[VMEM_SPEC] * 2,
        scratch_shapes=[pltpu.VMEM((CODE_ROWS, half), jnp.bfloat16)],
        compiler_params=params(),
        name="pack",
    )(emb_mine, emb_rest, emb_other, vec, vec_other, meta)


def decode(codes):
    codes = codes.astype(jnp.float32)
    numbers = [codes[2 * index : 2 * index + 1] + codes[2 * index + 1 : 2 * index + 2] for index in range(6)]
    left, right, bottom, top, first, last = numbers
    right, top = right + MARGIN, top + MARGIN
    square = codes[15:16] + codes[14:15] + codes[13:14]
    norm = lax.rsqrt(square + EPSILON) * COS_SCALE
    area = (right - left) * (top - bottom)
    return [left, right, bottom, top, first * GAP_SCALE + BASE, last * GAP_SCALE, codes[12:13], norm, area]


def with_ones(vectors):
    shape = (CODE_ROWS, vectors.shape[1])
    tail = jnp.where(lax.broadcasted_iota(jnp.int32, shape, 0) == 0, 1.0, 0.0)
    return jnp.concatenate([vectors, tail.astype(jnp.bfloat16)], axis=0)


def weights_of(products, row, col, same):
    width = jnp.maximum(jnp.minimum(row(RIGHT), col(RIGHT)) - jnp.maximum(row(LEFT), col(LEFT)), 0.0)
    height = jnp.maximum(jnp.minimum(row(TOP), col(TOP)) - jnp.maximum(row(BOTTOM), col(BOTTOM)), 0.0)
    inter = width * height
    both = row(AREA) + col(AREA)
    share = (both + inter) * pltpu.reciprocal(both - inter, approx=True, full_range=False)
    gap = jnp.maximum(col(FIRST) - row(LAST), row(FIRST) - col(LAST))
    logit = products * row(NORM) * col(NORM)
    value = jnp.exp2(logit - jnp.maximum(gap, BASE)) * share
    barred = (row(CAMERA) == col(CAMERA)) & (gap < BARRED_BELOW)
    if same is not None:
        barred = barred & jnp.logical_not(same)
    return jnp.where(barred, 0.0, value)


def tile_kernel(blocks, turns, own_block, streams, receivers, vecs, *refs):
    row_ref, col_refs = refs[0], refs[1 : 1 + blocks]
    row_out_ref, col_out_ref, field_ref, spread_ref = refs[1 + blocks : 5 + blocks]
    products, weights = [refs[at : at + 2] for at in (5 + blocks, 7 + blocks)]
    col_spread_ref, row_vec_ref, sum_ref = refs[9 + blocks :]
    size, rows = row_ref.shape
    features = size - vecs - CODE_ROWS
    vec_rows, code_rows = slice(features, features + vecs), slice(features + vecs, size)
    if streams:
        sum_ref[...] = jnp.zeros_like(sum_ref)
    row_out_ref[...] = jnp.zeros_like(row_out_ref)

    def block(col_ref, done):
        chunks = col_ref.shape[1] // WIDE

        def place(step, base=0):
            return pl.ds(pl.multiple_of(base + step * WIDE, WIDE), WIDE)

        def multiply(step, product_ref):
            product_ref[...] = jnp.dot(
                row_ref[0:rows, :], col_ref[0:features, place(step)], preferred_element_type=jnp.float32
            )

        def weigh(step, product_ref, weight_ref):
            for field, values in enumerate(decode(col_ref[code_rows, place(step)])):
                col_spread_ref[field] = jnp.broadcast_to(values, (8, WIDE))
            for start in range(0, rows, GROUP):
                row_part = slice(start, start + GROUP)

                def row(field):
                    return jnp.concatenate([spread_ref[field, row_part, :]] * (WIDE // LANES), axis=1)

                def col(field):
                    return jnp.concatenate([col_spread_ref[field]] * (GROUP // 8), axis=0)

                same = None
                if own_block:
                    row_ids = lax.broadcasted_iota(jnp.int32, (GROUP, WIDE), 0) + (start - step * WIDE)
                    same = row_ids == lax.broadcasted_iota(jnp.int32, (GROUP, WIDE), 1)
                weight_ref[row_part, :] = weights_of(product_ref[row_part, :], row, col, same).astype(jnp.bfloat16)

        def total(step, weight_ref):
            col_vecs = with_ones(col_ref[vec_rows, place(step)])
            if streams:
                sum_ref[:, 0 : vecs + CODE_ROWS] += dot_nt(weight_ref[...], col_vecs)
            else:
                row_out_ref[...] += dot_nt(col_vecs, weight_ref[...])[0:OUT_ROWS]
            if not turns:
                col_out_ref[:, place(step, done)] = jnp.dot(
                    row_vec_ref[...], weight_ref[...], preferred_element_type=jnp.float32
                )[0:OUT_ROWS]

        def steps(index, carry):
            for parity in range(2):
                step = 2 * index + parity
                multiply(lax.rem(step + 1, chunks), products[1 - parity])
                weigh(step, products[parity], weights[parity])
                total(lax.rem(step + chunks - 1, chunks), weights[1 - parity])
            return carry

        multiply(0, products[0])
        weights[1][...] = jnp.zeros_like(weights[1])
        lax.fori_loop(0, chunks // 2, steps, 0)
        total(chunks - 1, weights[1])

    def compute():
        for field, values in enumerate(decode(row_ref[code_rows, :])):
            field_ref[field : field + 1, :] = values
        turned = field_ref[...].T
        for field in range(FIELDS):
            spread_ref[field] = jnp.broadcast_to(turned[:, field : field + 1], (rows, LANES))
        row_vec_ref[...] = with_ones(row_ref[vec_rows, :])
        if turns:
            for number, pack_ref in enumerate(col_refs):
                part = pl.ds(number * rows, rows)
                col_out_ref[0:features, part] = pack_ref[0:rows, :].T
                col_out_ref[features:size, part] = pack_ref[features:size, :]
            block(col_out_ref, 0)
        else:
            done = 0
            for col_ref in col_refs:
                block(col_ref, done)
                done += col_ref.shape[1]
        if streams:
            row_out_ref[...] = sum_ref[...].T[0:OUT_ROWS]

    if receivers is None:
        compute()
        return
    pair = lax.axis_index("blk") // 2
    takes_part = functools.reduce(jnp.logical_or, [pair == one for one in receivers])

    @pl.when(takes_part)
    def _():
        compute()

    @pl.when(jnp.logical_not(takes_part))
    def _():
        col_out_ref[...] = jnp.zeros_like(col_out_ref)


def tile(row, columns, vecs, turns=False, own_block=False, streams=False, receivers=None):
    size, rows = row.shape
    cols = len(columns) * rows if turns else sum(part.shape[1] for part in columns)
    second = jax.ShapeDtypeStruct((size, cols), jnp.bfloat16)
    if not turns:
        second = jax.ShapeDtypeStruct((OUT_ROWS, cols), jnp.float32)
    return pl.pallas_call(
        functools.partial(tile_kernel, len(columns), turns, own_block, streams, receivers, vecs),
        out_shape=[jax.ShapeDtypeStruct((OUT_ROWS, rows), jnp.float32), second],
        in_specs=[VMEM_SPEC] * (1 + len(columns)),
        out_specs=[VMEM_SPEC] * 2,
        scratch_shapes=[
            pltpu.VMEM((LANES, rows), jnp.float32),
            pltpu.VMEM((FIELDS, rows, LANES), jnp.float32),
            pltpu.VMEM((rows, WIDE), jnp.float32),
            pltpu.VMEM((rows, WIDE), jnp.float32),
            pltpu.VMEM((rows, WIDE), jnp.bfloat16),
            pltpu.VMEM((rows, WIDE), jnp.bfloat16),
            pltpu.VMEM((FIELDS, 8, WIDE), jnp.float32),
            pltpu.VMEM((vecs + CODE_ROWS, rows), jnp.bfloat16),
            pltpu.VMEM((rows, LANES), jnp.float32),
        ],
        cost_estimate=pl.CostEstimate(flops=COST, bytes_accessed=COST, transcendentals=0),
        compiler_params=params(),
        name="tile",
    )(row, *columns)


def image_kernel(*refs):
    parts, image_ref = refs[:-1], refs[-1]
    total = parts[0][...]
    for part in parts[1:]:
        total = total + part[...]
    vecs = image_ref.shape[0]
    image_ref[...] = total[0:vecs] / total[vecs : vecs + 1]


def image_of(parts, vecs):
    return pl.pallas_call(
        image_kernel,
        out_shape=jax.ShapeDtypeStruct((vecs, parts[0].shape[1]), jnp.float32),
        in_specs=[VMEM_SPEC] * len(parts),
        out_specs=VMEM_SPEC,
        compiler_params=params(),
        name="image",
    )(*parts)


def gram_kernel(image_ref, grams_ref):
    vecs, cols = image_ref.shape
    image = image_ref[...]
    padded = jnp.concatenate([image, jnp.zeros((LANES - vecs, cols), jnp.float32)], axis=0)
    gram = dot_nt(image, padded, lax.Precision.HIGHEST)
    packed = gram[0:8]
    for piece in range(1, vecs // 8):
        packed = packed + pltpu.roll(gram[8 * piece : 8 * piece + 8], piece * vecs, 1)
    for copy in range(grams_ref.shape[0]):
        grams_ref[copy] = packed


def grams_of(image, copies):
    return pl.pallas_call(
        gram_kernel,
        out_shape=jax.ShapeDtypeStruct((copies, 8, LANES), jnp.float32),
        in_specs=[VMEM_SPEC],
        out_specs=VMEM_SPEC,
        compiler_params=params(),
        name="gram",
    )(image)


def inverse_of(number):
    guess = pltpu.reciprocal(number, approx=True)
    guess = guess * (2.0 - number * guess)
    return guess * (2.0 - number * guess)


def basis_kernel(total_rows, grams_ref, mine_ref, other_ref, out_ref, inverse_ref):
    vecs, half = mine_ref.shape
    sub = lax.axis_index("sub")
    packed = jnp.sum(grams_ref[...], axis=0) / total_rows
    lane = lax.broadcasted_iota(jnp.int32, (vecs, LANES), 1)
    line = lax.broadcasted_iota(jnp.int32, (vecs, LANES), 0)
    pieces = [packed] + [pltpu.roll(packed, LANES - piece * vecs, 1) for piece in range(1, LANES // vecs)]
    matrix = jnp.where(lane < vecs, jnp.concatenate(pieces, axis=0), 0.0)
    matrix = jnp.where(lane == line + vecs, 1.0, matrix)
    for step in range(0, vecs, 2):
        left = jnp.broadcast_to(matrix[:, step : step + 1], (vecs, LANES))
        right = jnp.broadcast_to(matrix[:, step + 1 : step + 2], (vecs, LANES))
        upper, lower = matrix[step : step + 1, :], matrix[step + 1 : step + 2, :]
        across = right[step : step + 1, :]
        inverse = inverse_of(left[step : step + 1, :])
        factor = left[step + 1 : step + 2, :] * inverse
        lower = lower - factor * upper
        inverse_next = inverse_of(right[step + 1 : step + 2, :] - factor * across)
        first = left * inverse
        second = (right - first * across) * inverse_next
        reduced = matrix - first * upper - second * lower
        matrix = jnp.where(line > step + 1, reduced, jnp.where(line == step + 1, lower, matrix))
    pivots = jnp.sum(jnp.where(lane == line, matrix, 0.0), axis=1, keepdims=True)
    inverse_ref[...] = pltpu.roll(matrix / jnp.sqrt(pivots), LANES - vecs, 1)
    share = vecs // 2
    own_rows = inverse_ref[pl.ds(pl.multiple_of(sub * share, 8), share), :][:, 0:vecs]
    for ref, place in ((mine_ref, sub), (other_ref, 1 - sub)):
        out_ref[:, pl.ds(pl.multiple_of(place * half, LANES), half)] = jnp.dot(
            own_rows, ref[...], precision=lax.Precision.HIGHEST, preferred_element_type=jnp.float32
        )


def basis_of(grams, mine, other, total_rows):
    vecs, half = mine.shape
    return pl.pallas_call(
        functools.partial(basis_kernel, total_rows),
        out_shape=jax.ShapeDtypeStruct((vecs // 2, 2 * half), jnp.float32),
        in_specs=[VMEM_SPEC] * 3,
        out_specs=VMEM_SPEC,
        scratch_shapes=[pltpu.VMEM((vecs, LANES), jnp.float32)],
        compiler_params=params(),
        name="basis",
    )(grams, mine, other)


def exchanges(pairs):
    plans = []
    for distance in range(1, pairs // 2):
        plans.append(([((p + distance) % pairs, p) for p in range(pairs)], None))
    if pairs > 1:
        half = pairs // 2
        last = [(p, p + half) if p % 2 == 0 else (p + half, p) for p in range(half)]
        plans.append((last, sorted(taker for _, taker in last)))
    return plans


def block_moves(pair_moves):
    return [(2 * source + member, 2 * target + member) for source, target in pair_moves for member in range(2)]


def back(moves):
    return [(target, source) for source, target in moves]


def local(embeddings, vectors, boxes, spans, camera):
    rows = embeddings.shape[0]
    half = rows // 2
    vecs = 2 * vectors.shape[0]
    blocks = lax.axis_size("blk")
    swap = [(0, 1), (1, 0)]
    beside = [(block, block ^ 1) for block in range(blocks)]
    plans = [(block_moves(moves), takers) for moves, takers in exchanges(blocks // 2)]

    emb_other = lax.ppermute(embeddings, "sub", swap)
    vec_other = lax.ppermute(vectors, "sub", swap)
    meta = jnp.concatenate([boxes, spans, camera[None, :]], axis=0)
    sub = lax.axis_index("sub")
    halves = [lax.dynamic_slice_in_dim(embeddings, place * half, half, 0) for place in (sub, 1 - sub)]
    mine, rest = packs_of(*halves, emb_other, vectors, vec_other, meta)
    sent = [lax.ppermute(mine, "blk", moves) for moves, _ in plans]
    beside_mine = lax.ppermute(mine, "blk", beside)
    weigh = functools.partial(tile, vecs=vecs)
    own_sums, own = weigh(mine, [mine, rest], turns=True, own_block=True)
    own_sums, own, beside_mine, sent[:1] = lax.optimization_barrier((own_sums, own, beside_mine, sent[:1]))
    cut = beside_mine.shape[0] // SWAPS // 16 * 16
    shares = [beside_mine[at * cut : (at + 1) * cut if at < SWAPS - 1 else None] for at in range(SWAPS)]
    beside_rest = jnp.concatenate([lax.ppermute(share, "sub", swap) for share in shares], axis=0)
    first_sums = [weigh(pack, [own], receivers=takers) for (_, takers), pack in zip(plans[:1], sent[:1])]
    if first_sums:
        first_sums, beside_rest = lax.optimization_barrier((first_sums, beside_rest))
    beside_sums, next_to = weigh(mine, [beside_mine, beside_rest], turns=True)
    parts = [own_sums, beside_sums]
    col_sums = None
    for number, ((moves, takers), pack) in enumerate(zip(plans, sent)):
        if number == 0:
            row_sums, sums = weigh(pack, [next_to], receivers=takers)
            row_sums = row_sums + first_sums[0][0]
            col_sums = jnp.concatenate([first_sums[0][1], sums], axis=1)
        else:
            pack, col_sums, parts[-1] = lax.optimization_barrier((pack, col_sums, parts[-1]))
            row_sums, sums = weigh(pack, [own, next_to], streams=True, receivers=takers)
            col_sums = col_sums + sums
        parts.append(lax.ppermute(row_sums, "blk", back(moves)))
    if col_sums is not None:
        own_mine, own_rest, next_mine, next_rest = [col_sums[:, place * half : (place + 1) * half] for place in range(4)]
        sides = lax.ppermute(jnp.concatenate([own_rest, next_rest], axis=1), "sub", swap)
        parts.append(own_mine)
        parts.append(sides[:, :half])
        parts.append(lax.ppermute(next_mine + sides[:, half:], "blk", beside))
    image = image_of(parts, vecs)
    image_other = lax.ppermute(image, "sub", swap)
    grams = lax.all_to_all(grams_of(image, 2 * blocks), ("blk", "sub"), 0, 0, tiled=True)
    return basis_of(grams, image, image_other, blocks * rows)


def solution(mesh):
    placed = (
        P(("groups", "blk"), "sub"),
        P("sub", ("groups", "blk")),
        P(None, ("groups", "blk")),
        P(None, ("groups", "blk")),
        P(("groups", "blk")),
    )
    return jax.shard_map(
        local, mesh=mesh, in_specs=placed, out_specs=P("sub", ("groups", "blk")), check_vma=False
    )
```

```python
import functools
import math

import jax
import jax.numpy as jnp
from jax import lax
from jax.experimental import pallas as pl
from jax.experimental.pallas import tpu as pltpu
from jax.sharding import PartitionSpec as P

SHARPNESS = 10.0
HORIZON = 2000.0
MARGIN = 8.0
EPSILON = 1e-06

LOG2E = math.log2(math.e)
COS_SCALE = math.sqrt(SHARPNESS * LOG2E)
GAP_SCALE = LOG2E / HORIZON
BASE = SHARPNESS * LOG2E + 1.0
BARRED_BELOW = BASE - 0.5 * GAP_SCALE

FIELDS = 9
LEFT, RIGHT, BOTTOM, TOP, FIRST, LAST, CAMERA, NORM, AREA = range(FIELDS)
CODE_ROWS = 16
LANES = 128
CHUNK = 256
OUT_ROWS = 40
COST = 1
LAST_COST = 4 * 1024 * 1024 * 1024
WIDE = 512
GROUP = 16
SWAPS = 3
VMEM_LIMIT = 48 * 1024 * 1024

NT = (((1,), (1,)), ((), ()))
VMEM_SPEC = pl.BlockSpec(memory_space=pltpu.VMEM)


def params():
    return pltpu.CompilerParams(vmem_limit_bytes=VMEM_LIMIT)


def dot_nt(a, b, precision=None):
    return lax.dot_general(a, b, NT, precision=precision, preferred_element_type=jnp.float32)


def pack_rows(half, vecs):
    return half + vecs + CODE_ROWS


def pack_kernel(emb_mine_ref, emb_rest_ref, emb_other_ref, vec_ref, vec_other_ref, meta_ref, mine_ref, rest_ref, code_ref):
    sub = lax.axis_index("sub")
    half, width = emb_mine_ref.shape
    half_vecs = vec_other_ref.shape[0]
    ones = jnp.ones((8, width), jnp.bfloat16)
    for ref, emb_ref, place in ((mine_ref, emb_mine_ref, sub), (rest_ref, emb_rest_ref, 1 - sub)):
        first = pl.multiple_of(place * half, half)
        for start in range(0, half, CHUNK):
            part = pl.ds(first + start, CHUNK)
            codes = []

            def whole(number, low_bits):
                codes.append((number >> low_bits) << low_bits)
                codes.append(number & ((1 << low_bits) - 1))

            meta = meta_ref[:, part]
            for axis in range(2):
                whole(jnp.minimum(meta[axis : axis + 1], meta[axis + 2 : axis + 3]), 5)
                whole(jnp.maximum(meta[axis : axis + 1], meta[axis + 2 : axis + 3]), 5)
            whole(jnp.minimum(meta[4:5], meta[5:6]), 7)
            whole(jnp.maximum(meta[4:5], meta[5:6]), 7)
            codes.append(meta[6:7])
            codes = [code.astype(jnp.float32) for code in codes]
            rest = jnp.zeros((8, CHUNK), jnp.float32)
            for values in (emb_ref[start : start + CHUNK, :], emb_other_ref[part, :]):
                values = values.astype(jnp.float32)
                square = values * values
                high = square.astype(jnp.bfloat16)
                low = (square - high.astype(jnp.float32)).astype(jnp.bfloat16)
                rest = rest + (dot_nt(ones, high) + dot_nt(ones, low))
            rest = rest[0:1]
            for _ in range(3):
                piece = rest.astype(jnp.bfloat16).astype(jnp.float32)
                codes.append(piece)
                rest = rest - piece
            code_ref[:, start : start + CHUNK] = jnp.concatenate(codes, axis=0).astype(jnp.bfloat16)
        source = pl.ds(first, half)
        sides = (
            (emb_ref[...], vec_ref[:, source], sub),
            (emb_other_ref[source, :], vec_other_ref[:, source], 1 - sub),
        )
        for values, vectors, side in sides:
            ref[0:half, pl.ds(pl.multiple_of(side * width, width), width)] = values
            ref[pl.ds(pl.multiple_of(half + side * half_vecs, 16), half_vecs), :] = vectors
        first_code = half + 2 * half_vecs
        ref[first_code : first_code + CODE_ROWS, :] = code_ref[...]


def packs_of(emb_mine, emb_rest, emb_other, vec, vec_other, meta):
    half, width = emb_mine.shape
    features = 2 * width
    assert half == features
    size = pack_rows(half, 2 * vec_other.shape[0])
    return pl.pallas_call(
        pack_kernel,
        out_shape=[jax.ShapeDtypeStruct((size, features), jnp.bfloat16)] * 2,
        in_specs=[VMEM_SPEC] * 6,
        out_specs=[VMEM_SPEC] * 2,
        scratch_shapes=[pltpu.VMEM((CODE_ROWS, half), jnp.bfloat16)],
        compiler_params=params(),
        name="pack",
    )(emb_mine, emb_rest, emb_other, vec, vec_other, meta)


def decode(codes):
    codes = codes.astype(jnp.float32)
    numbers = [codes[2 * index : 2 * index + 1] + codes[2 * index + 1 : 2 * index + 2] for index in range(6)]
    left, right, bottom, top, first, last = numbers
    right, top = right + MARGIN, top + MARGIN
    square = codes[15:16] + codes[14:15] + codes[13:14]
    norm = lax.rsqrt(square + EPSILON) * COS_SCALE
    area = (right - left) * (top - bottom)
    return [left, right, bottom, top, first * GAP_SCALE + BASE, last * GAP_SCALE, codes[12:13], norm, area]


def with_ones(vectors):
    shape = (CODE_ROWS, vectors.shape[1])
    tail = jnp.where(lax.broadcasted_iota(jnp.int32, shape, 0) == 0, 1.0, 0.0)
    return jnp.concatenate([vectors, tail.astype(jnp.bfloat16)], axis=0)


def weights_of(products, row, col, same):
    width = jnp.maximum(jnp.minimum(row(RIGHT), col(RIGHT)) - jnp.maximum(row(LEFT), col(LEFT)), 0.0)
    height = jnp.maximum(jnp.minimum(row(TOP), col(TOP)) - jnp.maximum(row(BOTTOM), col(BOTTOM)), 0.0)
    inter = width * height
    both = row(AREA) + col(AREA)
    share = (both + inter) * pltpu.reciprocal(both - inter, approx=True, full_range=False)
    gap = jnp.maximum(col(FIRST) - row(LAST), row(FIRST) - col(LAST))
    logit = products * row(NORM) * col(NORM)
    value = jnp.exp2(logit - jnp.maximum(gap, BASE)) * share
    barred = (row(CAMERA) == col(CAMERA)) & (gap < BARRED_BELOW)
    if same is not None:
        barred = barred & jnp.logical_not(same)
    return jnp.where(barred, 0.0, value)


def tile_kernel(blocks, turns, own_block, receivers, vecs, *refs):
    row_ref, col_refs = refs[0], refs[1 : 1 + blocks]
    row_out_ref, col_out_ref, field_ref, spread_ref = refs[1 + blocks : 5 + blocks]
    products, weights = [refs[at : at + 2] for at in (5 + blocks, 7 + blocks)]
    col_spread_ref, row_vec_ref = refs[9 + blocks :]
    size, rows = row_ref.shape
    features = size - vecs - CODE_ROWS
    vec_rows, code_rows = slice(features, features + vecs), slice(features + vecs, size)
    row_out_ref[...] = jnp.zeros_like(row_out_ref)

    def block(col_ref, done):
        chunks = col_ref.shape[1] // WIDE

        def place(step, base=0):
            return pl.ds(pl.multiple_of(base + step * WIDE, WIDE), WIDE)

        def multiply(step, product_ref):
            product_ref[...] = jnp.dot(
                row_ref[0:rows, :], col_ref[0:features, place(step)], preferred_element_type=jnp.float32
            )

        def weigh(step, product_ref, weight_ref):
            for field, values in enumerate(decode(col_ref[code_rows, place(step)])):
                col_spread_ref[field] = jnp.broadcast_to(values, (8, WIDE))
            for start in range(0, rows, GROUP):
                row_part = slice(start, start + GROUP)

                def row(field):
                    return jnp.concatenate([spread_ref[field, row_part, :]] * (WIDE // LANES), axis=1)

                def col(field):
                    return jnp.concatenate([col_spread_ref[field]] * (GROUP // 8), axis=0)

                same = None
                if own_block:
                    row_ids = lax.broadcasted_iota(jnp.int32, (GROUP, WIDE), 0) + (start - step * WIDE)
                    same = row_ids == lax.broadcasted_iota(jnp.int32, (GROUP, WIDE), 1)
                weight_ref[row_part, :] = weights_of(product_ref[row_part, :], row, col, same).astype(jnp.bfloat16)

        def total(step, weight_ref):
            col_vecs = with_ones(col_ref[vec_rows, place(step)])
            row_out_ref[...] += dot_nt(col_vecs, weight_ref[...])[0:OUT_ROWS]
            if not turns:
                col_out_ref[:, place(step, done)] = jnp.dot(
                    row_vec_ref[...], weight_ref[...], preferred_element_type=jnp.float32
                )[0:OUT_ROWS]

        def steps(index, carry):
            for parity in range(2):
                step = 2 * index + parity
                multiply(lax.rem(step + 1, chunks), products[1 - parity])
                weigh(step, products[parity], weights[parity])
                total(lax.rem(step + chunks - 1, chunks), weights[1 - parity])
            return carry

        multiply(0, products[0])
        weights[1][...] = jnp.zeros_like(weights[1])
        lax.fori_loop(0, chunks // 2, steps, 0)
        total(chunks - 1, weights[1])

    def compute():
        for field, values in enumerate(decode(row_ref[code_rows, :])):
            field_ref[field : field + 1, :] = values
        turned = field_ref[...].T
        for field in range(FIELDS):
            spread_ref[field] = jnp.broadcast_to(turned[:, field : field + 1], (rows, LANES))
        row_vec_ref[...] = with_ones(row_ref[vec_rows, :])
        if turns:
            for number, pack_ref in enumerate(col_refs):
                part = pl.ds(number * rows, rows)
                col_out_ref[0:features, part] = pack_ref[0:rows, :].T
                col_out_ref[features:size, part] = pack_ref[features:size, :]
            block(col_out_ref, 0)
        else:
            done = 0
            for col_ref in col_refs:
                block(col_ref, done)
                done += col_ref.shape[1]

    if receivers is None:
        compute()
        return
    pair = lax.axis_index("blk") // 2
    takes_part = functools.reduce(jnp.logical_or, [pair == one for one in receivers])

    @pl.when(takes_part)
    def _():
        compute()

    @pl.when(jnp.logical_not(takes_part))
    def _():
        col_out_ref[...] = jnp.zeros_like(col_out_ref)


def tile(row, columns, vecs, turns=False, own_block=False, receivers=None, last=False):
    size, rows = row.shape
    cols = len(columns) * rows if turns else sum(part.shape[1] for part in columns)
    second = jax.ShapeDtypeStruct((size, cols), jnp.bfloat16)
    if not turns:
        second = jax.ShapeDtypeStruct((OUT_ROWS, cols), jnp.float32)
    return pl.pallas_call(
        functools.partial(tile_kernel, len(columns), turns, own_block, receivers, vecs),
        out_shape=[jax.ShapeDtypeStruct((OUT_ROWS, rows), jnp.float32), second],
        in_specs=[VMEM_SPEC] * (1 + len(columns)),
        out_specs=[VMEM_SPEC] * 2,
        scratch_shapes=[
            pltpu.VMEM((LANES, rows), jnp.float32),
            pltpu.VMEM((FIELDS, rows, LANES), jnp.float32),
            pltpu.VMEM((rows, WIDE), jnp.float32),
            pltpu.VMEM((rows, WIDE), jnp.float32),
            pltpu.VMEM((rows, WIDE), jnp.bfloat16),
            pltpu.VMEM((rows, WIDE), jnp.bfloat16),
            pltpu.VMEM((FIELDS, 8, WIDE), jnp.float32),
            pltpu.VMEM((vecs + CODE_ROWS, rows), jnp.bfloat16),
        ],
        cost_estimate=pl.CostEstimate(flops=LAST_COST if last else COST, bytes_accessed=COST, transcendentals=0),
        compiler_params=params(),
        name="tile",
    )(row, *columns)


def image_kernel(*refs):
    parts, image_ref = refs[:-1], refs[-1]
    total = parts[0][...]
    for part in parts[1:]:
        total = total + part[...]
    vecs = image_ref.shape[0]
    image_ref[...] = total[0:vecs] / total[vecs : vecs + 1]


def image_of(parts, vecs):
    return pl.pallas_call(
        image_kernel,
        out_shape=jax.ShapeDtypeStruct((vecs, parts[0].shape[1]), jnp.float32),
        in_specs=[VMEM_SPEC] * len(parts),
        out_specs=VMEM_SPEC,
        compiler_params=params(),
        name="image",
    )(*parts)


def gram_kernel(image_ref, grams_ref):
    vecs, cols = image_ref.shape
    image = image_ref[...]
    padded = jnp.concatenate([image, jnp.zeros((LANES - vecs, cols), jnp.float32)], axis=0)
    gram = dot_nt(image, padded, lax.Precision.HIGHEST)
    packed = gram[0:8]
    for piece in range(1, vecs // 8):
        packed = packed + pltpu.roll(gram[8 * piece : 8 * piece + 8], piece * vecs, 1)
    for copy in range(grams_ref.shape[0]):
        grams_ref[copy] = packed


def grams_of(image, copies):
    return pl.pallas_call(
        gram_kernel,
        out_shape=jax.ShapeDtypeStruct((copies, 8, LANES), jnp.float32),
        in_specs=[VMEM_SPEC],
        out_specs=VMEM_SPEC,
        compiler_params=params(),
        name="gram",
    )(image)


def inverse_of(number):
    guess = pltpu.reciprocal(number, approx=True)
    guess = guess * (2.0 - number * guess)
    return guess * (2.0 - number * guess)


def basis_kernel(total_rows, grams_ref, mine_ref, other_ref, out_ref, inverse_ref):
    vecs, half = mine_ref.shape
    sub = lax.axis_index("sub")
    packed = jnp.sum(grams_ref[...], axis=0) / total_rows
    lane = lax.broadcasted_iota(jnp.int32, (vecs, LANES), 1)
    line = lax.broadcasted_iota(jnp.int32, (vecs, LANES), 0)
    pieces = [packed] + [pltpu.roll(packed, LANES - piece * vecs, 1) for piece in range(1, LANES // vecs)]
    matrix = jnp.where(lane < vecs, jnp.concatenate(pieces, axis=0), 0.0)
    matrix = jnp.where(lane == line + vecs, 1.0, matrix)
    for step in range(0, vecs, 2):
        left = jnp.broadcast_to(matrix[:, step : step + 1], (vecs, LANES))
        right = jnp.broadcast_to(matrix[:, step + 1 : step + 2], (vecs, LANES))
        upper, lower = matrix[step : step + 1, :], matrix[step + 1 : step + 2, :]
        across = right[step : step + 1, :]
        inverse = inverse_of(left[step : step + 1, :])
        factor = left[step + 1 : step + 2, :] * inverse
        lower = lower - factor * upper
        inverse_next = inverse_of(right[step + 1 : step + 2, :] - factor * across)
        first = left * inverse
        second = (right - first * across) * inverse_next
        reduced = matrix - first * upper - second * lower
        matrix = jnp.where(line > step + 1, reduced, jnp.where(line == step + 1, lower, matrix))
    pivots = jnp.sum(jnp.where(lane == line, matrix, 0.0), axis=1, keepdims=True)
    inverse_ref[...] = pltpu.roll(matrix / jnp.sqrt(pivots), LANES - vecs, 1)
    share = vecs // 2
    own_rows = inverse_ref[pl.ds(pl.multiple_of(sub * share, 8), share), :][:, 0:vecs]
    for ref, place in ((mine_ref, sub), (other_ref, 1 - sub)):
        out_ref[:, pl.ds(pl.multiple_of(place * half, LANES), half)] = jnp.dot(
            own_rows, ref[...], precision=lax.Precision.HIGHEST, preferred_element_type=jnp.float32
        )


def basis_of(grams, mine, other, total_rows):
    vecs, half = mine.shape
    return pl.pallas_call(
        functools.partial(basis_kernel, total_rows),
        out_shape=jax.ShapeDtypeStruct((vecs // 2, 2 * half), jnp.float32),
        in_specs=[VMEM_SPEC] * 3,
        out_specs=VMEM_SPEC,
        scratch_shapes=[pltpu.VMEM((vecs, LANES), jnp.float32)],
        compiler_params=params(),
        name="basis",
    )(grams, mine, other)


def exchanges(pairs):
    plans = []
    for distance in range(1, pairs // 2):
        plans.append(([((p + distance) % pairs, p) for p in range(pairs)], None))
    if pairs > 1:
        half = pairs // 2
        last = [(p, p + half) if p % 2 == 0 else (p + half, p) for p in range(half)]
        plans.append((last, sorted(taker for _, taker in last)))
    return plans


def block_moves(pair_moves):
    return [(2 * source + member, 2 * target + member) for source, target in pair_moves for member in range(2)]


def back(moves):
    return [(target, source) for source, target in moves]


def local(embeddings, vectors, boxes, spans, camera):
    rows = embeddings.shape[0]
    half = rows // 2
    vecs = 2 * vectors.shape[0]
    blocks = lax.axis_size("blk")
    swap = [(0, 1), (1, 0)]
    beside = [(block, block ^ 1) for block in range(blocks)]
    plans = [(block_moves(moves), takers) for moves, takers in exchanges(blocks // 2)]

    emb_other = lax.ppermute(embeddings, "sub", swap)
    vec_other = lax.ppermute(vectors, "sub", swap)
    meta = jnp.concatenate([boxes, spans, camera[None, :]], axis=0)
    sub = lax.axis_index("sub")
    halves = [lax.dynamic_slice_in_dim(embeddings, place * half, half, 0) for place in (sub, 1 - sub)]
    mine, rest = packs_of(*halves, emb_other, vectors, vec_other, meta)
    sent = [lax.ppermute(mine, "blk", moves) for moves, _ in plans]
    beside_mine = lax.ppermute(mine, "blk", beside)
    weigh = functools.partial(tile, vecs=vecs)
    own_sums, own = weigh(mine, [mine, rest], turns=True, own_block=True)
    own_sums, own, beside_mine, sent[:1] = lax.optimization_barrier((own_sums, own, beside_mine, sent[:1]))
    cut = beside_mine.shape[0] // SWAPS // 16 * 16
    shares = [beside_mine[at * cut : (at + 1) * cut if at < SWAPS - 1 else None] for at in range(SWAPS)]
    beside_rest = jnp.concatenate([lax.ppermute(share, "sub", swap) for share in shares], axis=0)
    parts = [own_sums]
    if not plans:
        parts.append(weigh(mine, [beside_mine, beside_rest], turns=True)[0])
    for number, ((moves, takers), pack) in enumerate(zip(plans, sent)):
        last = number == len(plans) - 1
        if number == 0:
            own_lines, own_cols = weigh(pack, [own], receivers=takers)
            own_lines, own_cols, beside_rest = lax.optimization_barrier((own_lines, own_cols, beside_rest))
            beside_sums, next_to = weigh(mine, [beside_mine, beside_rest], turns=True)
            parts.append(beside_sums)
            next_lines, next_cols = weigh(pack, [next_to], receivers=takers)
        else:
            pack, own_cols, next_cols = lax.optimization_barrier((pack, own_cols, next_cols))
            next_lines, cols = weigh(pack, [next_to], receivers=takers)
            next_cols = next_cols + cols
            pack, next_cols, parts[-1] = lax.optimization_barrier((pack, next_cols, parts[-1]))
            own_lines, cols = weigh(pack, [own], receivers=takers, last=last)
            own_cols = own_cols + cols
        if last:
            next_rest = lax.ppermute(next_cols[:, half:], "sub", swap)
            crossing = next_cols[:, :half] + next_rest
            crossed = lax.ppermute(crossing, "blk", beside)
            own_lines, _ = lax.optimization_barrier((own_lines, crossing))
            parts += [crossed, own_cols[:, :half], lax.ppermute(own_cols[:, half:], "sub", swap)]
        parts.append(lax.ppermute(own_lines + next_lines, "blk", back(moves)))
    image = image_of(parts, vecs)
    image_other = lax.ppermute(image, "sub", swap)
    grams = lax.all_to_all(grams_of(image, 2 * blocks), ("blk", "sub"), 0, 0, tiled=True)
    return basis_of(grams, image, image_other, blocks * rows)


def solution(mesh):
    placed = (
        P(("groups", "blk"), "sub"),
        P("sub", ("groups", "blk")),
        P(None, ("groups", "blk")),
        P(None, ("groups", "blk")),
        P(("groups", "blk")),
    )
    return jax.shard_map(
        local, mesh=mesh, in_specs=placed, out_specs=P("sub", ("groups", "blk")), check_vma=False
    )
```

```python
import functools
import math

import jax
import jax.numpy as jnp
from jax import lax
from jax.experimental import pallas as pl
from jax.experimental.pallas import tpu as pltpu
from jax.sharding import PartitionSpec as P

SHARPNESS = 10.0
HORIZON = 2000.0
MARGIN = 8.0
EPSILON = 1e-06

LOG2E = math.log2(math.e)
COS_SCALE = math.sqrt(SHARPNESS * LOG2E)
GAP_SCALE = LOG2E / HORIZON
BASE = SHARPNESS * LOG2E + 1.0
BARRED_BELOW = BASE - 0.5 * GAP_SCALE

FIELDS = 9
LEFT, RIGHT, BOTTOM, TOP, FIRST, LAST, CAMERA, NORM, AREA = range(FIELDS)
CODE_ROWS = 16
LANES = 128
CHUNK = 256
OUT_ROWS = 40
COST = 1
LAST_COST = 4 * 1024 * 1024 * 1024
WIDE = 512
GROUP = 16
SWAPS = 3
VMEM_LIMIT = 48 * 1024 * 1024

NT = (((1,), (1,)), ((), ()))
VMEM_SPEC = pl.BlockSpec(memory_space=pltpu.VMEM)


def params():
    return pltpu.CompilerParams(vmem_limit_bytes=VMEM_LIMIT)


def dot_nt(a, b, precision=None):
    return lax.dot_general(a, b, NT, precision=precision, preferred_element_type=jnp.float32)


def pack_rows(half, vecs):
    return half + vecs + CODE_ROWS


def pack_kernel(emb_mine_ref, emb_rest_ref, emb_other_ref, vec_ref, vec_other_ref, meta_ref, mine_ref, rest_ref, code_ref):
    sub = lax.axis_index("sub")
    half, width = emb_mine_ref.shape
    half_vecs = vec_other_ref.shape[0]
    ones = jnp.ones((8, width), jnp.bfloat16)
    for ref, emb_ref, place in ((mine_ref, emb_mine_ref, sub), (rest_ref, emb_rest_ref, 1 - sub)):
        first = pl.multiple_of(place * half, half)
        for start in range(0, half, CHUNK):
            part = pl.ds(first + start, CHUNK)
            codes = []

            def whole(number, low_bits):
                codes.append((number >> low_bits) << low_bits)
                codes.append(number & ((1 << low_bits) - 1))

            meta = meta_ref[:, part]
            for axis in range(2):
                whole(jnp.minimum(meta[axis : axis + 1], meta[axis + 2 : axis + 3]), 5)
                whole(jnp.maximum(meta[axis : axis + 1], meta[axis + 2 : axis + 3]), 5)
            whole(jnp.minimum(meta[4:5], meta[5:6]), 7)
            whole(jnp.maximum(meta[4:5], meta[5:6]), 7)
            codes.append(meta[6:7])
            codes = [code.astype(jnp.float32) for code in codes]
            rest = jnp.zeros((8, CHUNK), jnp.float32)
            for values in (emb_ref[start : start + CHUNK, :], emb_other_ref[part, :]):
                values = values.astype(jnp.float32)
                square = values * values
                high = square.astype(jnp.bfloat16)
                low = (square - high.astype(jnp.float32)).astype(jnp.bfloat16)
                rest = rest + (dot_nt(ones, high) + dot_nt(ones, low))
            rest = rest[0:1]
            for _ in range(3):
                piece = rest.astype(jnp.bfloat16).astype(jnp.float32)
                codes.append(piece)
                rest = rest - piece
            code_ref[:, start : start + CHUNK] = jnp.concatenate(codes, axis=0).astype(jnp.bfloat16)
        source = pl.ds(first, half)
        sides = (
            (emb_ref[...], vec_ref[:, source], sub),
            (emb_other_ref[source, :], vec_other_ref[:, source], 1 - sub),
        )
        for values, vectors, side in sides:
            ref[0:half, pl.ds(pl.multiple_of(side * width, width), width)] = values
            ref[pl.ds(pl.multiple_of(half + side * half_vecs, 16), half_vecs), :] = vectors
        first_code = half + 2 * half_vecs
        ref[first_code : first_code + CODE_ROWS, :] = code_ref[...]


def packs_of(emb_mine, emb_rest, emb_other, vec, vec_other, meta):
    half, width = emb_mine.shape
    features = 2 * width
    assert half == features
    size = pack_rows(half, 2 * vec_other.shape[0])
    return pl.pallas_call(
        pack_kernel,
        out_shape=[jax.ShapeDtypeStruct((size, features), jnp.bfloat16)] * 2,
        in_specs=[VMEM_SPEC] * 6,
        out_specs=[VMEM_SPEC] * 2,
        scratch_shapes=[pltpu.VMEM((CODE_ROWS, half), jnp.bfloat16)],
        compiler_params=params(),
        name="pack",
    )(emb_mine, emb_rest, emb_other, vec, vec_other, meta)


def decode(codes):
    codes = codes.astype(jnp.float32)
    numbers = [codes[2 * index : 2 * index + 1] + codes[2 * index + 1 : 2 * index + 2] for index in range(6)]
    left, right, bottom, top, first, last = numbers
    right, top = right + MARGIN, top + MARGIN
    square = codes[15:16] + codes[14:15] + codes[13:14]
    norm = lax.rsqrt(square + EPSILON) * COS_SCALE
    area = (right - left) * (top - bottom)
    return [left, right, bottom, top, first * GAP_SCALE + BASE, last * GAP_SCALE, codes[12:13], norm, area]


def with_ones(vectors):
    shape = (CODE_ROWS, vectors.shape[1])
    tail = jnp.where(lax.broadcasted_iota(jnp.int32, shape, 0) == 0, 1.0, 0.0)
    return jnp.concatenate([vectors, tail.astype(jnp.bfloat16)], axis=0)


def weights_of(products, row, col, same):
    width = jnp.maximum(jnp.minimum(row(RIGHT), col(RIGHT)) - jnp.maximum(row(LEFT), col(LEFT)), 0.0)
    height = jnp.maximum(jnp.minimum(row(TOP), col(TOP)) - jnp.maximum(row(BOTTOM), col(BOTTOM)), 0.0)
    inter = width * height
    both = row(AREA) + col(AREA)
    share = (both + inter) * pltpu.reciprocal(both - inter, approx=True, full_range=False)
    gap = jnp.maximum(col(FIRST) - row(LAST), row(FIRST) - col(LAST))
    logit = products * row(NORM) * col(NORM)
    value = jnp.exp2(logit - jnp.maximum(gap, BASE)) * share
    barred = (row(CAMERA) == col(CAMERA)) & (gap < BARRED_BELOW)
    if same is not None:
        barred = barred & jnp.logical_not(same)
    return jnp.where(barred, 0.0, value)


def tile_kernel(blocks, turns, own_block, receivers, vecs, *refs):
    row_ref, col_refs = refs[0], refs[1 : 1 + blocks]
    row_out_ref, col_out_ref, field_ref, spread_ref = refs[1 + blocks : 5 + blocks]
    products, weights = [refs[at : at + 2] for at in (5 + blocks, 7 + blocks)]
    col_spread_ref, row_vec_ref = refs[9 + blocks :]
    size, rows = row_ref.shape
    features = size - vecs - CODE_ROWS
    vec_rows, code_rows = slice(features, features + vecs), slice(features + vecs, size)
    row_out_ref[...] = jnp.zeros_like(row_out_ref)

    def block(col_ref, done):
        chunks = col_ref.shape[1] // WIDE

        def place(step, base=0):
            return pl.ds(pl.multiple_of(base + step * WIDE, WIDE), WIDE)

        def multiply(step, product_ref):
            product_ref[...] = jnp.dot(
                row_ref[0:rows, :], col_ref[0:features, place(step)], preferred_element_type=jnp.float32
            )

        def weigh(step, product_ref, weight_ref):
            for field, values in enumerate(decode(col_ref[code_rows, place(step)])):
                col_spread_ref[field] = jnp.broadcast_to(values, (8, WIDE))
            for start in range(0, rows, GROUP):
                row_part = slice(start, start + GROUP)

                def row(field):
                    return jnp.concatenate([spread_ref[field, row_part, :]] * (WIDE // LANES), axis=1)

                def col(field):
                    return jnp.concatenate([col_spread_ref[field]] * (GROUP // 8), axis=0)

                same = None
                if own_block:
                    row_ids = lax.broadcasted_iota(jnp.int32, (GROUP, WIDE), 0) + (start - step * WIDE)
                    same = row_ids == lax.broadcasted_iota(jnp.int32, (GROUP, WIDE), 1)
                weight_ref[row_part, :] = weights_of(product_ref[row_part, :], row, col, same).astype(jnp.bfloat16)

        def total(step, weight_ref):
            col_vecs = with_ones(col_ref[vec_rows, place(step)])
            row_out_ref[...] += dot_nt(col_vecs, weight_ref[...])[0:OUT_ROWS]
            if not turns:
                col_out_ref[:, place(step, done)] = jnp.dot(
                    row_vec_ref[...], weight_ref[...], preferred_element_type=jnp.float32
                )[0:OUT_ROWS]

        def steps(index, carry):
            for parity in range(2):
                step = 2 * index + parity
                multiply(lax.rem(step + 1, chunks), products[1 - parity])
                weigh(step, products[parity], weights[parity])
                total(lax.rem(step + chunks - 1, chunks), weights[1 - parity])
            return carry

        multiply(0, products[0])
        weights[1][...] = jnp.zeros_like(weights[1])
        lax.fori_loop(0, chunks // 2, steps, 0)
        total(chunks - 1, weights[1])

    def compute():
        for field, values in enumerate(decode(row_ref[code_rows, :])):
            field_ref[field : field + 1, :] = values
        turned = field_ref[...].T
        for field in range(FIELDS):
            spread_ref[field] = jnp.broadcast_to(turned[:, field : field + 1], (rows, LANES))
        row_vec_ref[...] = with_ones(row_ref[vec_rows, :])
        if turns:
            for number, pack_ref in enumerate(col_refs):
                part = pl.ds(number * rows, rows)
                col_out_ref[0:features, part] = pack_ref[0:rows, :].T
                col_out_ref[features:size, part] = pack_ref[features:size, :]
            block(col_out_ref, 0)
        else:
            done = 0
            for col_ref in col_refs:
                block(col_ref, done)
                done += col_ref.shape[1]

    if receivers is None:
        compute()
        return
    pair = lax.axis_index("blk") // 2
    takes_part = functools.reduce(jnp.logical_or, [pair == one for one in receivers])

    @pl.when(takes_part)
    def _():
        compute()

    @pl.when(jnp.logical_not(takes_part))
    def _():
        col_out_ref[...] = jnp.zeros_like(col_out_ref)


def tile(row, columns, vecs, turns=False, own_block=False, receivers=None, last=False):
    size, rows = row.shape
    cols = len(columns) * rows if turns else sum(part.shape[1] for part in columns)
    second = jax.ShapeDtypeStruct((size, cols), jnp.bfloat16)
    if not turns:
        second = jax.ShapeDtypeStruct((OUT_ROWS, cols), jnp.float32)
    return pl.pallas_call(
        functools.partial(tile_kernel, len(columns), turns, own_block, receivers, vecs),
        out_shape=[jax.ShapeDtypeStruct((OUT_ROWS, rows), jnp.float32), second],
        in_specs=[VMEM_SPEC] * (1 + len(columns)),
        out_specs=[VMEM_SPEC] * 2,
        scratch_shapes=[
            pltpu.VMEM((LANES, rows), jnp.float32),
            pltpu.VMEM((FIELDS, rows, LANES), jnp.float32),
            pltpu.VMEM((rows, WIDE), jnp.float32),
            pltpu.VMEM((rows, WIDE), jnp.float32),
            pltpu.VMEM((rows, WIDE), jnp.bfloat16),
            pltpu.VMEM((rows, WIDE), jnp.bfloat16),
            pltpu.VMEM((FIELDS, 8, WIDE), jnp.float32),
            pltpu.VMEM((vecs + CODE_ROWS, rows), jnp.bfloat16),
        ],
        cost_estimate=pl.CostEstimate(flops=LAST_COST if last else COST, bytes_accessed=COST, transcendentals=0),
        compiler_params=params(),
        name="tile",
    )(row, *columns)


def image_kernel(*refs):
    parts, image_ref = refs[:-1], refs[-1]
    total = parts[0][...]
    for part in parts[1:]:
        total = total + part[...]
    vecs = image_ref.shape[0]
    image_ref[...] = total[0:vecs] / total[vecs : vecs + 1]


def image_of(parts, vecs):
    return pl.pallas_call(
        image_kernel,
        out_shape=jax.ShapeDtypeStruct((vecs, parts[0].shape[1]), jnp.float32),
        in_specs=[VMEM_SPEC] * len(parts),
        out_specs=VMEM_SPEC,
        compiler_params=params(),
        name="image",
    )(*parts)


def gram_kernel(image_ref, grams_ref):
    vecs, cols = image_ref.shape
    image = image_ref[...]
    padded = jnp.concatenate([image, jnp.zeros((LANES - vecs, cols), jnp.float32)], axis=0)
    gram = dot_nt(image, padded, lax.Precision.HIGHEST)
    packed = gram[0:8]
    for piece in range(1, vecs // 8):
        packed = packed + pltpu.roll(gram[8 * piece : 8 * piece + 8], piece * vecs, 1)
    for copy in range(grams_ref.shape[0]):
        grams_ref[copy] = packed


def grams_of(image, copies):
    return pl.pallas_call(
        gram_kernel,
        out_shape=jax.ShapeDtypeStruct((copies, 8, LANES), jnp.float32),
        in_specs=[VMEM_SPEC],
        out_specs=VMEM_SPEC,
        compiler_params=params(),
        name="gram",
    )(image)


def inverse_of(number):
    guess = pltpu.reciprocal(number, approx=True)
    guess = guess * (2.0 - number * guess)
    return guess * (2.0 - number * guess)


def basis_kernel(total_rows, grams_ref, mine_ref, other_ref, out_ref, inverse_ref):
    vecs, half = mine_ref.shape
    sub = lax.axis_index("sub")
    packed = jnp.sum(grams_ref[...], axis=0) / total_rows
    lane = lax.broadcasted_iota(jnp.int32, (vecs, LANES), 1)
    line = lax.broadcasted_iota(jnp.int32, (vecs, LANES), 0)
    pieces = [packed] + [pltpu.roll(packed, LANES - piece * vecs, 1) for piece in range(1, LANES // vecs)]
    matrix = jnp.where(lane < vecs, jnp.concatenate(pieces, axis=0), 0.0)
    matrix = jnp.where(lane == line + vecs, 1.0, matrix)
    for step in range(0, vecs, 2):
        left = jnp.broadcast_to(matrix[:, step : step + 1], (vecs, LANES))
        right = jnp.broadcast_to(matrix[:, step + 1 : step + 2], (vecs, LANES))
        upper, lower = matrix[step : step + 1, :], matrix[step + 1 : step + 2, :]
        across = right[step : step + 1, :]
        inverse = inverse_of(left[step : step + 1, :])
        factor = left[step + 1 : step + 2, :] * inverse
        lower = lower - factor * upper
        inverse_next = inverse_of(right[step + 1 : step + 2, :] - factor * across)
        first = left * inverse
        second = (right - first * across) * inverse_next
        reduced = matrix - first * upper - second * lower
        matrix = jnp.where(line > step + 1, reduced, jnp.where(line == step + 1, lower, matrix))
    pivots = jnp.sum(jnp.where(lane == line, matrix, 0.0), axis=1, keepdims=True)
    inverse_ref[...] = pltpu.roll(matrix / jnp.sqrt(pivots), LANES - vecs, 1)
    share = vecs // 2
    own_rows = inverse_ref[pl.ds(pl.multiple_of(sub * share, 8), share), :][:, 0:vecs]
    for ref, place in ((mine_ref, sub), (other_ref, 1 - sub)):
        out_ref[:, pl.ds(pl.multiple_of(place * half, LANES), half)] = jnp.dot(
            own_rows, ref[...], precision=lax.Precision.HIGHEST, preferred_element_type=jnp.float32
        )


def basis_of(grams, mine, other, total_rows):
    vecs, half = mine.shape
    return pl.pallas_call(
        functools.partial(basis_kernel, total_rows),
        out_shape=jax.ShapeDtypeStruct((vecs // 2, 2 * half), jnp.float32),
        in_specs=[VMEM_SPEC] * 3,
        out_specs=VMEM_SPEC,
        scratch_shapes=[pltpu.VMEM((vecs, LANES), jnp.float32)],
        compiler_params=params(),
        name="basis",
    )(grams, mine, other)


def exchanges(pairs):
    if pairs == 4:
        return [([(0, 2), (3, 1), (1, 0), (2, 3)], None), ([(2, 1), (0, 3)], [1, 3])]
    plans = []
    for distance in range(1, pairs // 2):
        plans.append(([((p + distance) % pairs, p) for p in range(pairs)], None))
    if pairs > 1:
        half = pairs // 2
        last = [(p, p + half) if p % 2 == 0 else (p + half, p) for p in range(half)]
        plans.append((last, sorted(taker for _, taker in last)))
    return plans


def block_moves(pair_moves):
    return [(2 * source + member, 2 * target + member) for source, target in pair_moves for member in range(2)]


def back(moves):
    return [(target, source) for source, target in moves]


def local(embeddings, vectors, boxes, spans, camera):
    rows = embeddings.shape[0]
    half = rows // 2
    vecs = 2 * vectors.shape[0]
    blocks = lax.axis_size("blk")
    swap = [(0, 1), (1, 0)]
    beside = [(block, block ^ 1) for block in range(blocks)]
    plans = [(block_moves(moves), takers) for moves, takers in exchanges(blocks // 2)]

    emb_other = lax.ppermute(embeddings, "sub", swap)
    vec_other = lax.ppermute(vectors, "sub", swap)
    meta = jnp.concatenate([boxes, spans, camera[None, :]], axis=0)
    sub = lax.axis_index("sub")
    halves = [lax.dynamic_slice_in_dim(embeddings, place * half, half, 0) for place in (sub, 1 - sub)]
    mine, rest = packs_of(*halves, emb_other, vectors, vec_other, meta)
    sent = [lax.ppermute(mine, "blk", moves) for moves, _ in plans]
    beside_mine = lax.ppermute(mine, "blk", beside)
    weigh = functools.partial(tile, vecs=vecs)
    own_sums, own = weigh(mine, [mine, rest], turns=True, own_block=True)
    own_sums, own, beside_mine, sent[:1] = lax.optimization_barrier((own_sums, own, beside_mine, sent[:1]))
    cut = beside_mine.shape[0] // SWAPS // 16 * 16
    shares = [beside_mine[at * cut : (at + 1) * cut if at < SWAPS - 1 else None] for at in range(SWAPS)]
    beside_rest = jnp.concatenate([lax.ppermute(share, "sub", swap) for share in shares], axis=0)
    parts = [own_sums]
    if not plans:
        parts.append(weigh(mine, [beside_mine, beside_rest], turns=True)[0])
    for number, ((moves, takers), pack) in enumerate(zip(plans, sent)):
        last = number == len(plans) - 1
        if number == 0:
            own_lines, own_cols = weigh(pack, [own], receivers=takers)
            own_lines, own_cols, beside_rest = lax.optimization_barrier((own_lines, own_cols, beside_rest))
            beside_sums, next_to = weigh(mine, [beside_mine, beside_rest], turns=True)
            parts.append(beside_sums)
            next_lines, next_cols = weigh(pack, [next_to], receivers=takers)
        else:
            pack, own_cols, next_cols = lax.optimization_barrier((pack, own_cols, next_cols))
            next_lines, cols = weigh(pack, [next_to], receivers=takers)
            next_cols = next_cols + cols
            pack, next_cols, parts[-1] = lax.optimization_barrier((pack, next_cols, parts[-1]))
            own_lines, cols = weigh(pack, [own], receivers=takers, last=last)
            own_cols = own_cols + cols
        if last:
            next_rest = lax.ppermute(next_cols[:, half:], "sub", swap)
            crossing = next_cols[:, :half] + next_rest
            crossed = lax.ppermute(crossing, "blk", beside)
            own_lines, _ = lax.optimization_barrier((own_lines, crossing))
            parts += [crossed, own_cols[:, :half], lax.ppermute(own_cols[:, half:], "sub", swap)]
        parts.append(lax.ppermute(own_lines + next_lines, "blk", back(moves)))
    image = image_of(parts, vecs)
    image_other = lax.ppermute(image, "sub", swap)
    grams = lax.all_to_all(grams_of(image, 2 * blocks), ("blk", "sub"), 0, 0, tiled=True)
    return basis_of(grams, image, image_other, blocks * rows)


def solution(mesh):
    placed = (
        P(("groups", "blk"), "sub"),
        P("sub", ("groups", "blk")),
        P(None, ("groups", "blk")),
        P(None, ("groups", "blk")),
        P(("groups", "blk")),
    )
    return jax.shard_map(
        local, mesh=mesh, in_specs=placed, out_specs=P("sub", ("groups", "blk")), check_vma=False
    )
```

```python
import functools
import math

import jax
import jax.numpy as jnp
from jax import lax
from jax.experimental import pallas as pl
from jax.experimental.pallas import tpu as pltpu
from jax.sharding import PartitionSpec as P

SHARPNESS = 10.0
HORIZON = 2000.0
MARGIN = 8.0
EPSILON = 1e-06

LOG2E = math.log2(math.e)
COS_SCALE = math.sqrt(SHARPNESS * LOG2E)
GAP_SCALE = LOG2E / HORIZON
BASE = SHARPNESS * LOG2E + 1.0
BARRED_BELOW = BASE - 0.5 * GAP_SCALE

FIELDS = 9
LEFT, RIGHT, BOTTOM, TOP, FIRST, LAST, CAMERA, NORM, AREA = range(FIELDS)
CODE_ROWS = 16
LANES = 128
CHUNK = 256
OUT_ROWS = 40
COST = 1
LAST_COST = 4 * 1024 * 1024 * 1024
WIDE = 512
GROUP = 16
SWAPS = 3
VMEM_LIMIT = 48 * 1024 * 1024

NT = (((1,), (1,)), ((), ()))
VMEM_SPEC = pl.BlockSpec(memory_space=pltpu.VMEM)


def params():
    return pltpu.CompilerParams(vmem_limit_bytes=VMEM_LIMIT)


def dot_nt(a, b, precision=None):
    return lax.dot_general(a, b, NT, precision=precision, preferred_element_type=jnp.float32)


def pack_rows(half, vecs):
    return half + vecs + CODE_ROWS


def pack_kernel(emb_mine_ref, emb_rest_ref, emb_other_ref, vec_ref, vec_other_ref, meta_ref, mine_ref, rest_ref, code_ref):
    sub = lax.axis_index("sub")
    half, width = emb_mine_ref.shape
    half_vecs = vec_other_ref.shape[0]
    ones = jnp.ones((8, width), jnp.bfloat16)
    for ref, emb_ref, place in ((mine_ref, emb_mine_ref, sub), (rest_ref, emb_rest_ref, 1 - sub)):
        first = pl.multiple_of(place * half, half)
        for start in range(0, half, CHUNK):
            part = pl.ds(first + start, CHUNK)
            codes = []

            def whole(number, low_bits):
                codes.append((number >> low_bits) << low_bits)
                codes.append(number & ((1 << low_bits) - 1))

            meta = meta_ref[:, part]
            for axis in range(2):
                whole(jnp.minimum(meta[axis : axis + 1], meta[axis + 2 : axis + 3]), 5)
                whole(jnp.maximum(meta[axis : axis + 1], meta[axis + 2 : axis + 3]), 5)
            whole(jnp.minimum(meta[4:5], meta[5:6]), 7)
            whole(jnp.maximum(meta[4:5], meta[5:6]), 7)
            codes.append(meta[6:7])
            codes = [code.astype(jnp.float32) for code in codes]
            rest = jnp.zeros((8, CHUNK), jnp.float32)
            for values in (emb_ref[start : start + CHUNK, :], emb_other_ref[part, :]):
                values = values.astype(jnp.float32)
                square = values * values
                high = square.astype(jnp.bfloat16)
                low = (square - high.astype(jnp.float32)).astype(jnp.bfloat16)
                rest = rest + (dot_nt(ones, high) + dot_nt(ones, low))
            rest = rest[0:1]
            for _ in range(3):
                piece = rest.astype(jnp.bfloat16).astype(jnp.float32)
                codes.append(piece)
                rest = rest - piece
            code_ref[:, start : start + CHUNK] = jnp.concatenate(codes, axis=0).astype(jnp.bfloat16)
        source = pl.ds(first, half)
        sides = (
            (emb_ref[...], vec_ref[:, source], sub),
            (emb_other_ref[source, :], vec_other_ref[:, source], 1 - sub),
        )
        for values, vectors, side in sides:
            ref[0:half, pl.ds(pl.multiple_of(side * width, width), width)] = values
            ref[pl.ds(pl.multiple_of(half + side * half_vecs, 16), half_vecs), :] = vectors
        first_code = half + 2 * half_vecs
        ref[first_code : first_code + CODE_ROWS, :] = code_ref[...]


def packs_of(emb_mine, emb_rest, emb_other, vec, vec_other, meta):
    half, width = emb_mine.shape
    features = 2 * width
    assert half == features
    size = pack_rows(half, 2 * vec_other.shape[0])
    return pl.pallas_call(
        pack_kernel,
        out_shape=[jax.ShapeDtypeStruct((size, features), jnp.bfloat16)] * 2,
        in_specs=[VMEM_SPEC] * 6,
        out_specs=[VMEM_SPEC] * 2,
        scratch_shapes=[pltpu.VMEM((CODE_ROWS, half), jnp.bfloat16)],
        compiler_params=params(),
        name="pack",
    )(emb_mine, emb_rest, emb_other, vec, vec_other, meta)


def decode(codes):
    codes = codes.astype(jnp.float32)
    numbers = [codes[2 * index : 2 * index + 1] + codes[2 * index + 1 : 2 * index + 2] for index in range(6)]
    left, right, bottom, top, first, last = numbers
    right, top = right + MARGIN, top + MARGIN
    square = codes[15:16] + codes[14:15] + codes[13:14]
    norm = lax.rsqrt(square + EPSILON) * COS_SCALE
    area = (right - left) * (top - bottom)
    return [left, right, bottom, top, first * GAP_SCALE + BASE, last * GAP_SCALE, codes[12:13], norm, area]


def with_ones(vectors):
    shape = (CODE_ROWS, vectors.shape[1])
    tail = jnp.where(lax.broadcasted_iota(jnp.int32, shape, 0) == 0, 1.0, 0.0)
    return jnp.concatenate([vectors, tail.astype(jnp.bfloat16)], axis=0)


def weights_of(products, row, col, same):
    width = jnp.maximum(jnp.minimum(row(RIGHT), col(RIGHT)) - jnp.maximum(row(LEFT), col(LEFT)), 0.0)
    height = jnp.maximum(jnp.minimum(row(TOP), col(TOP)) - jnp.maximum(row(BOTTOM), col(BOTTOM)), 0.0)
    inter = width * height
    both = row(AREA) + col(AREA)
    share = (both + inter) * pltpu.reciprocal(both - inter, approx=True, full_range=False)
    gap = jnp.maximum(col(FIRST) - row(LAST), row(FIRST) - col(LAST))
    logit = products * row(NORM) * col(NORM)
    value = jnp.exp2(logit - jnp.maximum(gap, BASE)) * share
    barred = (row(CAMERA) == col(CAMERA)) & (gap < BARRED_BELOW)
    if same is not None:
        barred = barred & jnp.logical_not(same)
    return jnp.where(barred, 0.0, value)


def tile_kernel(blocks, turns, own_block, receivers, vecs, *refs):
    row_ref, col_refs = refs[0], refs[1 : 1 + blocks]
    row_out_ref, col_out_ref, field_ref, spread_ref = refs[1 + blocks : 5 + blocks]
    products, weights = [refs[at : at + 2] for at in (5 + blocks, 7 + blocks)]
    col_spread_ref, row_vec_ref = refs[9 + blocks :]
    size, rows = row_ref.shape
    features = size - vecs - CODE_ROWS
    vec_rows, code_rows = slice(features, features + vecs), slice(features + vecs, size)
    row_out_ref[...] = jnp.zeros_like(row_out_ref)

    def block(col_ref, done):
        chunks = col_ref.shape[1] // WIDE

        def place(step, base=0):
            return pl.ds(pl.multiple_of(base + step * WIDE, WIDE), WIDE)

        def multiply(step, product_ref):
            product_ref[...] = jnp.dot(
                row_ref[0:rows, :], col_ref[0:features, place(step)], preferred_element_type=jnp.float32
            )

        def weigh(step, product_ref, weight_ref):
            for field, values in enumerate(decode(col_ref[code_rows, place(step)])):
                col_spread_ref[field] = jnp.broadcast_to(values, (8, WIDE))
            for start in range(0, rows, GROUP):
                row_part = slice(start, start + GROUP)

                def row(field):
                    return jnp.concatenate([spread_ref[field, row_part, :]] * (WIDE // LANES), axis=1)

                def col(field):
                    return jnp.concatenate([col_spread_ref[field]] * (GROUP // 8), axis=0)

                same = None
                if own_block:
                    row_ids = lax.broadcasted_iota(jnp.int32, (GROUP, WIDE), 0) + (start - step * WIDE)
                    same = row_ids == lax.broadcasted_iota(jnp.int32, (GROUP, WIDE), 1)
                weight_ref[row_part, :] = weights_of(product_ref[row_part, :], row, col, same).astype(jnp.bfloat16)

        def total(step, weight_ref):
            col_vecs = with_ones(col_ref[vec_rows, place(step)])
            row_out_ref[...] += dot_nt(col_vecs, weight_ref[...])[0:OUT_ROWS]
            if not turns:
                col_out_ref[:, place(step, done)] = jnp.dot(
                    row_vec_ref[...], weight_ref[...], preferred_element_type=jnp.float32
                )[0:OUT_ROWS]

        def steps(index, carry):
            for parity in range(2):
                step = 2 * index + parity
                multiply(lax.rem(step + 1, chunks), products[1 - parity])
                weigh(step, products[parity], weights[parity])
                total(lax.rem(step + chunks - 1, chunks), weights[1 - parity])
            return carry

        multiply(0, products[0])
        weights[1][...] = jnp.zeros_like(weights[1])
        lax.fori_loop(0, chunks // 2, steps, 0)
        total(chunks - 1, weights[1])

    def compute():
        for field, values in enumerate(decode(row_ref[code_rows, :])):
            field_ref[field : field + 1, :] = values
        turned = field_ref[...].T
        for field in range(FIELDS):
            spread_ref[field] = jnp.broadcast_to(turned[:, field : field + 1], (rows, LANES))
        row_vec_ref[...] = with_ones(row_ref[vec_rows, :])
        if turns:
            for number, pack_ref in enumerate(col_refs):
                part = pl.ds(number * rows, rows)
                col_out_ref[0:features, part] = pack_ref[0:rows, :].T
                col_out_ref[features:size, part] = pack_ref[features:size, :]
            block(col_out_ref, 0)
        else:
            done = 0
            for col_ref in col_refs:
                block(col_ref, done)
                done += col_ref.shape[1]

    if receivers is None:
        compute()
        return
    pair = lax.axis_index("blk") // 2
    takes_part = functools.reduce(jnp.logical_or, [pair == one for one in receivers])

    @pl.when(takes_part)
    def _():
        compute()

    @pl.when(jnp.logical_not(takes_part))
    def _():
        col_out_ref[...] = jnp.zeros_like(col_out_ref)


def tile(row, columns, vecs, turns=False, own_block=False, receivers=None, last=False):
    size, rows = row.shape
    cols = len(columns) * rows if turns else sum(part.shape[1] for part in columns)
    second = jax.ShapeDtypeStruct((size, cols), jnp.bfloat16)
    if not turns:
        second = jax.ShapeDtypeStruct((OUT_ROWS, cols), jnp.float32)
    return pl.pallas_call(
        functools.partial(tile_kernel, len(columns), turns, own_block, receivers, vecs),
        out_shape=[jax.ShapeDtypeStruct((OUT_ROWS, rows), jnp.float32), second],
        in_specs=[VMEM_SPEC] * (1 + len(columns)),
        out_specs=[VMEM_SPEC] * 2,
        scratch_shapes=[
            pltpu.VMEM((LANES, rows), jnp.float32),
            pltpu.VMEM((FIELDS, rows, LANES), jnp.float32),
            pltpu.VMEM((rows, WIDE), jnp.float32),
            pltpu.VMEM((rows, WIDE), jnp.float32),
            pltpu.VMEM((rows, WIDE), jnp.bfloat16),
            pltpu.VMEM((rows, WIDE), jnp.bfloat16),
            pltpu.VMEM((FIELDS, 8, WIDE), jnp.float32),
            pltpu.VMEM((vecs + CODE_ROWS, rows), jnp.bfloat16),
        ],
        cost_estimate=pl.CostEstimate(flops=LAST_COST if last else COST, bytes_accessed=COST, transcendentals=0),
        compiler_params=params(),
        name="tile",
    )(row, *columns)


def image_kernel(*refs):
    parts, image_ref = refs[:-1], refs[-1]
    total = parts[0][...]
    for part in parts[1:]:
        total = total + part[...]
    vecs = image_ref.shape[0]
    image_ref[...] = total[0:vecs] / total[vecs : vecs + 1]


def image_of(parts, vecs):
    return pl.pallas_call(
        image_kernel,
        out_shape=jax.ShapeDtypeStruct((vecs, parts[0].shape[1]), jnp.float32),
        in_specs=[VMEM_SPEC] * len(parts),
        out_specs=VMEM_SPEC,
        compiler_params=params(),
        name="image",
    )(*parts)


def gram_kernel(image_ref, grams_ref):
    vecs, cols = image_ref.shape
    image = image_ref[...]
    padded = jnp.concatenate([image, jnp.zeros((LANES - vecs, cols), jnp.float32)], axis=0)
    gram = dot_nt(image, padded, lax.Precision.HIGHEST)
    packed = gram[0:8]
    for piece in range(1, vecs // 8):
        packed = packed + pltpu.roll(gram[8 * piece : 8 * piece + 8], piece * vecs, 1)
    for copy in range(grams_ref.shape[0]):
        grams_ref[copy] = packed


def grams_of(image, copies):
    return pl.pallas_call(
        gram_kernel,
        out_shape=jax.ShapeDtypeStruct((copies, 8, LANES), jnp.float32),
        in_specs=[VMEM_SPEC],
        out_specs=VMEM_SPEC,
        compiler_params=params(),
        name="gram",
    )(image)


def inverse_of(number):
    guess = pltpu.reciprocal(number, approx=True)
    guess = guess * (2.0 - number * guess)
    return guess * (2.0 - number * guess)


def basis_kernel(total_rows, grams_ref, mine_ref, other_ref, out_ref, inverse_ref):
    vecs, half = mine_ref.shape
    sub = lax.axis_index("sub")
    packed = jnp.sum(grams_ref[...], axis=0) / total_rows
    lane = lax.broadcasted_iota(jnp.int32, (vecs, LANES), 1)
    line = lax.broadcasted_iota(jnp.int32, (vecs, LANES), 0)
    pieces = [packed] + [pltpu.roll(packed, LANES - piece * vecs, 1) for piece in range(1, LANES // vecs)]
    matrix = jnp.where(lane < vecs, jnp.concatenate(pieces, axis=0), 0.0)
    matrix = jnp.where(lane == line + vecs, 1.0, matrix)
    for step in range(0, vecs, 2):
        left = jnp.broadcast_to(matrix[:, step : step + 1], (vecs, LANES))
        right = jnp.broadcast_to(matrix[:, step + 1 : step + 2], (vecs, LANES))
        upper, lower = matrix[step : step + 1, :], matrix[step + 1 : step + 2, :]
        across = right[step : step + 1, :]
        inverse = inverse_of(left[step : step + 1, :])
        factor = left[step + 1 : step + 2, :] * inverse
        lower = lower - factor * upper
        inverse_next = inverse_of(right[step + 1 : step + 2, :] - factor * across)
        first = left * inverse
        second = (right - first * across) * inverse_next
        reduced = matrix - first * upper - second * lower
        matrix = jnp.where(line > step + 1, reduced, jnp.where(line == step + 1, lower, matrix))
    pivots = jnp.sum(jnp.where(lane == line, matrix, 0.0), axis=1, keepdims=True)
    inverse_ref[...] = pltpu.roll(matrix / jnp.sqrt(pivots), LANES - vecs, 1)
    share = vecs // 2
    own_rows = inverse_ref[pl.ds(pl.multiple_of(sub * share, 8), share), :][:, 0:vecs]
    for ref, place in ((mine_ref, sub), (other_ref, 1 - sub)):
        out_ref[:, pl.ds(pl.multiple_of(place * half, LANES), half)] = jnp.dot(
            own_rows, ref[...], precision=lax.Precision.HIGHEST, preferred_element_type=jnp.float32
        )


def basis_of(grams, mine, other, total_rows):
    vecs, half = mine.shape
    return pl.pallas_call(
        functools.partial(basis_kernel, total_rows),
        out_shape=jax.ShapeDtypeStruct((vecs // 2, 2 * half), jnp.float32),
        in_specs=[VMEM_SPEC] * 3,
        out_specs=VMEM_SPEC,
        scratch_shapes=[pltpu.VMEM((vecs, LANES), jnp.float32)],
        compiler_params=params(),
        name="basis",
    )(grams, mine, other)


def exchanges(pairs):
    if pairs == 4:
        return [([(0, 2), (3, 1), (1, 0), (2, 3)], None), ([(2, 1), (0, 3)], [1, 3])]
    plans = []
    for distance in range(1, pairs // 2):
        plans.append(([((p + distance) % pairs, p) for p in range(pairs)], None))
    if pairs > 1:
        half = pairs // 2
        last = [(p, p + half) if p % 2 == 0 else (p + half, p) for p in range(half)]
        plans.append((last, sorted(taker for _, taker in last)))
    return plans


def block_moves(pair_moves):
    return [(2 * source + member, 2 * target + member) for source, target in pair_moves for member in range(2)]


def back(moves):
    return [(target, source) for source, target in moves]


def local(embeddings, vectors, boxes, spans, camera):
    rows = embeddings.shape[0]
    half = rows // 2
    vecs = 2 * vectors.shape[0]
    blocks = lax.axis_size("blk")
    swap = [(0, 1), (1, 0)]
    beside = [(block, block ^ 1) for block in range(blocks)]
    plans = [(block_moves(moves), takers) for moves, takers in exchanges(blocks // 2)]

    emb_other = lax.ppermute(embeddings, "sub", swap)
    vec_other = lax.ppermute(vectors, "sub", swap)
    meta = jnp.concatenate([boxes, spans, camera[None, :]], axis=0)
    sub = lax.axis_index("sub")
    halves = [lax.dynamic_slice_in_dim(embeddings, place * half, half, 0) for place in (sub, 1 - sub)]
    mine, rest = packs_of(*halves, emb_other, vectors, vec_other, meta)
    sent = [lax.ppermute(mine, "blk", moves) for moves, _ in plans]
    beside_mine = lax.ppermute(mine, "blk", beside)
    weigh = functools.partial(tile, vecs=vecs)
    own_sums, own = weigh(mine, [mine, rest], turns=True, own_block=True)
    own_sums, own, sent[:1] = lax.optimization_barrier((own_sums, own, sent[:1]))
    beside_mine, sent[:1] = lax.optimization_barrier((beside_mine, sent[:1]))
    cut = beside_mine.shape[0] // SWAPS // 16 * 16
    shares = [beside_mine[at * cut : (at + 1) * cut if at < SWAPS - 1 else None] for at in range(SWAPS)]
    beside_rest = jnp.concatenate([lax.ppermute(share, "sub", swap) for share in shares], axis=0)
    parts = [own_sums]
    if not plans:
        parts.append(weigh(mine, [beside_mine, beside_rest], turns=True)[0])
    for number, ((moves, takers), pack) in enumerate(zip(plans, sent)):
        last = number == len(plans) - 1
        if number == 0:
            own_lines, own_cols = weigh(pack, [own], receivers=takers)
            own_lines, own_cols, beside_rest = lax.optimization_barrier((own_lines, own_cols, beside_rest))
            beside_sums, next_to = weigh(mine, [beside_mine, beside_rest], turns=True)
            parts.append(beside_sums)
            next_lines, next_cols = weigh(pack, [next_to], receivers=takers)
        else:
            pack, own_cols, next_cols = lax.optimization_barrier((pack, own_cols, next_cols))
            next_lines, cols = weigh(pack, [next_to], receivers=takers)
            next_cols = next_cols + cols
            pack, next_cols, parts[-1] = lax.optimization_barrier((pack, next_cols, parts[-1]))
            own_lines, cols = weigh(pack, [own], receivers=takers, last=last)
            own_cols = own_cols + cols
        if last:
            next_rest = lax.ppermute(next_cols[:, half:], "sub", swap)
            crossing = next_cols[:, :half] + next_rest
            crossed = lax.ppermute(crossing, "blk", beside)
            own_lines, _ = lax.optimization_barrier((own_lines, crossing))
            parts += [crossed, own_cols[:, :half], lax.ppermute(own_cols[:, half:], "sub", swap)]
        parts.append(lax.ppermute(own_lines + next_lines, "blk", back(moves)))
    image = image_of(parts, vecs)
    image_other = lax.ppermute(image, "sub", swap)
    grams = lax.all_to_all(grams_of(image, 2 * blocks), ("blk", "sub"), 0, 0, tiled=True)
    return basis_of(grams, image, image_other, blocks * rows)


def solution(mesh):
    placed = (
        P(("groups", "blk"), "sub"),
        P("sub", ("groups", "blk")),
        P(None, ("groups", "blk")),
        P(None, ("groups", "blk")),
        P(("groups", "blk")),
    )
    return jax.shard_map(
        local, mesh=mesh, in_specs=placed, out_specs=P("sub", ("groups", "blk")), check_vma=False
    )
```

```python
import functools
import math

import jax
import jax.numpy as jnp
from jax import lax
from jax.experimental import pallas as pl
from jax.experimental.pallas import tpu as pltpu
from jax.sharding import PartitionSpec as P

SHARPNESS = 10.0
HORIZON = 2000.0
MARGIN = 8.0
EPSILON = 1e-06

LOG2E = math.log2(math.e)
COS_SCALE = math.sqrt(SHARPNESS * LOG2E)
GAP_SCALE = LOG2E / HORIZON
BASE = SHARPNESS * LOG2E + 1.0
BARRED_BELOW = BASE - 0.5 * GAP_SCALE

FIELDS = 9
LEFT, RIGHT, BOTTOM, TOP, FIRST, LAST, CAMERA, NORM, AREA = range(FIELDS)
CODE_ROWS = 16
LANES = 128
CHUNK = 256
OUT_ROWS = 40
COST = 1
LAST_COST = 4 * 1024 * 1024 * 1024
WIDE = 512
GROUP = 16
SWAPS = 3
VMEM_LIMIT = 48 * 1024 * 1024

NT = (((1,), (1,)), ((), ()))
VMEM_SPEC = pl.BlockSpec(memory_space=pltpu.VMEM)


def params():
    return pltpu.CompilerParams(vmem_limit_bytes=VMEM_LIMIT)


def dot_nt(a, b, precision=None):
    return lax.dot_general(a, b, NT, precision=precision, preferred_element_type=jnp.float32)


def pack_rows(half, vecs):
    return half + vecs + CODE_ROWS


def pack_kernel(emb_mine_ref, emb_rest_ref, emb_other_ref, vec_ref, vec_other_ref, meta_ref, mine_ref, rest_ref, code_ref):
    sub = lax.axis_index("sub")
    half, width = emb_mine_ref.shape
    half_vecs = vec_other_ref.shape[0]
    ones = jnp.ones((8, width), jnp.bfloat16)
    for ref, emb_ref, place in ((mine_ref, emb_mine_ref, sub), (rest_ref, emb_rest_ref, 1 - sub)):
        first = pl.multiple_of(place * half, half)
        for start in range(0, half, CHUNK):
            part = pl.ds(first + start, CHUNK)
            codes = []

            def whole(number, low_bits):
                codes.append((number >> low_bits) << low_bits)
                codes.append(number & ((1 << low_bits) - 1))

            meta = meta_ref[:, part]
            for axis in range(2):
                whole(jnp.minimum(meta[axis : axis + 1], meta[axis + 2 : axis + 3]), 5)
                whole(jnp.maximum(meta[axis : axis + 1], meta[axis + 2 : axis + 3]), 5)
            whole(jnp.minimum(meta[4:5], meta[5:6]), 7)
            whole(jnp.maximum(meta[4:5], meta[5:6]), 7)
            codes.append(meta[6:7])
            codes = [code.astype(jnp.float32) for code in codes]
            rest = jnp.zeros((8, CHUNK), jnp.float32)
            for values in (emb_ref[start : start + CHUNK, :], emb_other_ref[part, :]):
                values = values.astype(jnp.float32)
                square = values * values
                high = square.astype(jnp.bfloat16)
                low = (square - high.astype(jnp.float32)).astype(jnp.bfloat16)
                rest = rest + (dot_nt(ones, high) + dot_nt(ones, low))
            rest = rest[0:1]
            for _ in range(3):
                piece = rest.astype(jnp.bfloat16).astype(jnp.float32)
                codes.append(piece)
                rest = rest - piece
            code_ref[:, start : start + CHUNK] = jnp.concatenate(codes, axis=0).astype(jnp.bfloat16)
        source = pl.ds(first, half)
        sides = (
            (emb_ref[...], vec_ref[:, source], sub),
            (emb_other_ref[source, :], vec_other_ref[:, source], 1 - sub),
        )
        for values, vectors, side in sides:
            ref[0:half, pl.ds(pl.multiple_of(side * width, width), width)] = values
            ref[pl.ds(pl.multiple_of(half + side * half_vecs, 16), half_vecs), :] = vectors
        first_code = half + 2 * half_vecs
        ref[first_code : first_code + CODE_ROWS, :] = code_ref[...]


def packs_of(emb_mine, emb_rest, emb_other, vec, vec_other, meta):
    half, width = emb_mine.shape
    features = 2 * width
    assert half == features
    size = pack_rows(half, 2 * vec_other.shape[0])
    return pl.pallas_call(
        pack_kernel,
        out_shape=[jax.ShapeDtypeStruct((size, features), jnp.bfloat16)] * 2,
        in_specs=[VMEM_SPEC] * 6,
        out_specs=[VMEM_SPEC] * 2,
        scratch_shapes=[pltpu.VMEM((CODE_ROWS, half), jnp.bfloat16)],
        compiler_params=params(),
        name="pack",
    )(emb_mine, emb_rest, emb_other, vec, vec_other, meta)


def decode(codes):
    codes = codes.astype(jnp.float32)
    numbers = [codes[2 * index : 2 * index + 1] + codes[2 * index + 1 : 2 * index + 2] for index in range(6)]
    left, right, bottom, top, first, last = numbers
    right, top = right + MARGIN, top + MARGIN
    square = codes[15:16] + codes[14:15] + codes[13:14]
    norm = lax.rsqrt(square + EPSILON) * COS_SCALE
    area = (right - left) * (top - bottom)
    return [left, right, bottom, top, first * GAP_SCALE + BASE, last * GAP_SCALE, codes[12:13], norm, area]


def with_ones(vectors):
    shape = (CODE_ROWS, vectors.shape[1])
    tail = jnp.where(lax.broadcasted_iota(jnp.int32, shape, 0) == 0, 1.0, 0.0)
    return jnp.concatenate([vectors, tail.astype(jnp.bfloat16)], axis=0)


def weights_of(products, row, col, same):
    width = jnp.maximum(jnp.minimum(row(RIGHT), col(RIGHT)) - jnp.maximum(row(LEFT), col(LEFT)), 0.0)
    height = jnp.maximum(jnp.minimum(row(TOP), col(TOP)) - jnp.maximum(row(BOTTOM), col(BOTTOM)), 0.0)
    inter = width * height
    both = row(AREA) + col(AREA)
    share = (both + inter) * pltpu.reciprocal(both - inter, approx=True, full_range=False)
    gap = jnp.maximum(col(FIRST) - row(LAST), row(FIRST) - col(LAST))
    logit = products * row(NORM) * col(NORM)
    value = jnp.exp2(logit - jnp.maximum(gap, BASE)) * share
    barred = (row(CAMERA) == col(CAMERA)) & (gap < BARRED_BELOW)
    if same is not None:
        barred = barred & jnp.logical_not(same)
    return jnp.where(barred, 0.0, value)


def tile_kernel(blocks, turns, own_block, receivers, vecs, *refs):
    row_ref, col_refs = refs[0], refs[1 : 1 + blocks]
    row_out_ref, col_out_ref, field_ref, spread_ref = refs[1 + blocks : 5 + blocks]
    products, weights = [refs[at : at + 2] for at in (5 + blocks, 7 + blocks)]
    col_spread_ref, row_vec_ref = refs[9 + blocks :]
    size, rows = row_ref.shape
    features = size - vecs - CODE_ROWS
    vec_rows, code_rows = slice(features, features + vecs), slice(features + vecs, size)
    row_out_ref[...] = jnp.zeros_like(row_out_ref)

    def block(col_ref, done):
        chunks = col_ref.shape[1] // WIDE

        def place(step, base=0):
            return pl.ds(pl.multiple_of(base + step * WIDE, WIDE), WIDE)

        def multiply(step, product_ref):
            product_ref[...] = jnp.dot(
                row_ref[0:rows, :], col_ref[0:features, place(step)], preferred_element_type=jnp.float32
            )

        def weigh(step, product_ref, weight_ref):
            for field, values in enumerate(decode(col_ref[code_rows, place(step)])):
                col_spread_ref[field] = jnp.broadcast_to(values, (8, WIDE))
            for start in range(0, rows, GROUP):
                row_part = slice(start, start + GROUP)

                def row(field):
                    return jnp.concatenate([spread_ref[field, row_part, :]] * (WIDE // LANES), axis=1)

                def col(field):
                    return jnp.concatenate([col_spread_ref[field]] * (GROUP // 8), axis=0)

                same = None
                if own_block:
                    row_ids = lax.broadcasted_iota(jnp.int32, (GROUP, WIDE), 0) + (start - step * WIDE)
                    same = row_ids == lax.broadcasted_iota(jnp.int32, (GROUP, WIDE), 1)
                weight_ref[row_part, :] = weights_of(product_ref[row_part, :], row, col, same).astype(jnp.bfloat16)

        def total(step, weight_ref):
            col_vecs = with_ones(col_ref[vec_rows, place(step)])
            row_out_ref[...] += dot_nt(col_vecs, weight_ref[...])[0:OUT_ROWS]
            if not turns:
                col_out_ref[:, place(step, done)] = jnp.dot(
                    row_vec_ref[...], weight_ref[...], preferred_element_type=jnp.float32
                )[0:OUT_ROWS]

        def steps(index, carry):
            for parity in range(2):
                step = 2 * index + parity
                multiply(lax.rem(step + 1, chunks), products[1 - parity])
                weigh(step, products[parity], weights[parity])
                total(lax.rem(step + chunks - 1, chunks), weights[1 - parity])
            return carry

        multiply(0, products[0])
        weights[1][...] = jnp.zeros_like(weights[1])
        lax.fori_loop(0, chunks // 2, steps, 0)
        total(chunks - 1, weights[1])

    def compute():
        for field, values in enumerate(decode(row_ref[code_rows, :])):
            field_ref[field : field + 1, :] = values
        turned = field_ref[...].T
        for field in range(FIELDS):
            spread_ref[field] = jnp.broadcast_to(turned[:, field : field + 1], (rows, LANES))
        row_vec_ref[...] = with_ones(row_ref[vec_rows, :])
        if turns:
            for number, pack_ref in enumerate(col_refs):
                part = pl.ds(number * rows, rows)
                col_out_ref[0:features, part] = pack_ref[0:rows, :].T
                col_out_ref[features:size, part] = pack_ref[features:size, :]
            block(col_out_ref, 0)
        else:
            done = 0
            for col_ref in col_refs:
                block(col_ref, done)
                done += col_ref.shape[1]

    if receivers is None:
        compute()
        return
    pair = lax.axis_index("blk") // 2
    takes_part = functools.reduce(jnp.logical_or, [pair == one for one in receivers])

    @pl.when(takes_part)
    def _():
        compute()

    @pl.when(jnp.logical_not(takes_part))
    def _():
        col_out_ref[...] = jnp.zeros_like(col_out_ref)


def tile(row, columns, vecs, turns=False, own_block=False, receivers=None, last=False):
    size, rows = row.shape
    cols = len(columns) * rows if turns else sum(part.shape[1] for part in columns)
    second = jax.ShapeDtypeStruct((size, cols), jnp.bfloat16)
    if not turns:
        second = jax.ShapeDtypeStruct((OUT_ROWS, cols), jnp.float32)
    return pl.pallas_call(
        functools.partial(tile_kernel, len(columns), turns, own_block, receivers, vecs),
        out_shape=[jax.ShapeDtypeStruct((OUT_ROWS, rows), jnp.float32), second],
        in_specs=[VMEM_SPEC] * (1 + len(columns)),
        out_specs=[VMEM_SPEC] * 2,
        scratch_shapes=[
            pltpu.VMEM((LANES, rows), jnp.float32),
            pltpu.VMEM((FIELDS, rows, LANES), jnp.float32),
            pltpu.VMEM((rows, WIDE), jnp.float32),
            pltpu.VMEM((rows, WIDE), jnp.float32),
            pltpu.VMEM((rows, WIDE), jnp.bfloat16),
            pltpu.VMEM((rows, WIDE), jnp.bfloat16),
            pltpu.VMEM((FIELDS, 8, WIDE), jnp.float32),
            pltpu.VMEM((vecs + CODE_ROWS, rows), jnp.bfloat16),
        ],
        cost_estimate=pl.CostEstimate(flops=LAST_COST if last else COST, bytes_accessed=COST, transcendentals=0),
        compiler_params=params(),
        name="tile",
    )(row, *columns)


def image_kernel(*refs):
    parts, image_ref = refs[:-1], refs[-1]
    total = parts[0][...]
    for part in parts[1:]:
        total = total + part[...]
    vecs = image_ref.shape[0]
    image_ref[...] = total[0:vecs] / total[vecs : vecs + 1]


def image_of(parts, vecs):
    return pl.pallas_call(
        image_kernel,
        out_shape=jax.ShapeDtypeStruct((vecs, parts[0].shape[1]), jnp.float32),
        in_specs=[VMEM_SPEC] * len(parts),
        out_specs=VMEM_SPEC,
        compiler_params=params(),
        name="image",
    )(*parts)


def gram_kernel(image_ref, grams_ref):
    vecs, cols = image_ref.shape
    image = image_ref[...]
    padded = jnp.concatenate([image, jnp.zeros((LANES - vecs, cols), jnp.float32)], axis=0)
    gram = dot_nt(image, padded, lax.Precision.HIGHEST)
    packed = gram[0:8]
    for piece in range(1, vecs // 8):
        packed = packed + pltpu.roll(gram[8 * piece : 8 * piece + 8], piece * vecs, 1)
    for copy in range(grams_ref.shape[0]):
        grams_ref[copy] = packed


def grams_of(image, copies):
    return pl.pallas_call(
        gram_kernel,
        out_shape=jax.ShapeDtypeStruct((copies, 8, LANES), jnp.float32),
        in_specs=[VMEM_SPEC],
        out_specs=VMEM_SPEC,
        compiler_params=params(),
        name="gram",
    )(image)


def inverse_of(number):
    guess = pltpu.reciprocal(number, approx=True)
    guess = guess * (2.0 - number * guess)
    return guess * (2.0 - number * guess)


def basis_kernel(total_rows, grams_ref, mine_ref, other_ref, out_ref, inverse_ref):
    vecs, half = mine_ref.shape
    sub = lax.axis_index("sub")
    packed = jnp.sum(grams_ref[...], axis=0) / total_rows
    lane = lax.broadcasted_iota(jnp.int32, (vecs, LANES), 1)
    line = lax.broadcasted_iota(jnp.int32, (vecs, LANES), 0)
    pieces = [packed] + [pltpu.roll(packed, LANES - piece * vecs, 1) for piece in range(1, LANES // vecs)]
    matrix = jnp.where(lane < vecs, jnp.concatenate(pieces, axis=0), 0.0)
    matrix = jnp.where(lane == line + vecs, 1.0, matrix)
    for step in range(0, vecs, 2):
        left = jnp.broadcast_to(matrix[:, step : step + 1], (vecs, LANES))
        right = jnp.broadcast_to(matrix[:, step + 1 : step + 2], (vecs, LANES))
        upper, lower = matrix[step : step + 1, :], matrix[step + 1 : step + 2, :]
        across = right[step : step + 1, :]
        inverse = inverse_of(left[step : step + 1, :])
        factor = left[step + 1 : step + 2, :] * inverse
        lower = lower - factor * upper
        inverse_next = inverse_of(right[step + 1 : step + 2, :] - factor * across)
        first = left * inverse
        second = (right - first * across) * inverse_next
        reduced = matrix - first * upper - second * lower
        matrix = jnp.where(line > step + 1, reduced, jnp.where(line == step + 1, lower, matrix))
    pivots = jnp.sum(jnp.where(lane == line, matrix, 0.0), axis=1, keepdims=True)
    inverse_ref[...] = pltpu.roll(matrix / jnp.sqrt(pivots), LANES - vecs, 1)
    share = vecs // 2
    own_rows = inverse_ref[pl.ds(pl.multiple_of(sub * share, 8), share), :][:, 0:vecs]
    for ref, place in ((mine_ref, sub), (other_ref, 1 - sub)):
        out_ref[:, pl.ds(pl.multiple_of(place * half, LANES), half)] = jnp.dot(
            own_rows, ref[...], precision=lax.Precision.HIGHEST, preferred_element_type=jnp.float32
        )


def basis_of(grams, mine, other, total_rows):
    vecs, half = mine.shape
    return pl.pallas_call(
        functools.partial(basis_kernel, total_rows),
        out_shape=jax.ShapeDtypeStruct((vecs // 2, 2 * half), jnp.float32),
        in_specs=[VMEM_SPEC] * 3,
        out_specs=VMEM_SPEC,
        scratch_shapes=[pltpu.VMEM((vecs, LANES), jnp.float32)],
        compiler_params=params(),
        name="basis",
    )(grams, mine, other)


def exchanges(pairs):
    if pairs == 4:
        return [([(0, 2), (3, 1), (1, 0), (2, 3)], None), ([(2, 1), (0, 3)], [1, 3])]
    plans = []
    for distance in range(1, pairs // 2):
        plans.append(([((p + distance) % pairs, p) for p in range(pairs)], None))
    if pairs > 1:
        half = pairs // 2
        last = [(p, p + half) if p % 2 == 0 else (p + half, p) for p in range(half)]
        plans.append((last, sorted(taker for _, taker in last)))
    return plans


def block_moves(pair_moves):
    return [(2 * source + member, 2 * target + member) for source, target in pair_moves for member in range(2)]


def back(moves):
    return [(target, source) for source, target in moves]


def local(embeddings, vectors, boxes, spans, camera):
    rows = embeddings.shape[0]
    half = rows // 2
    vecs = 2 * vectors.shape[0]
    blocks = lax.axis_size("blk")
    swap = [(0, 1), (1, 0)]
    beside = [(block, block ^ 1) for block in range(blocks)]
    plans = [(block_moves(moves), takers) for moves, takers in exchanges(blocks // 2)]

    emb_other = lax.ppermute(embeddings, "sub", swap)
    vec_other = lax.ppermute(vectors, "sub", swap)
    meta = jnp.concatenate([boxes, spans, camera[None, :]], axis=0)
    sub = lax.axis_index("sub")
    halves = [lax.dynamic_slice_in_dim(embeddings, place * half, half, 0) for place in (sub, 1 - sub)]
    mine, rest = packs_of(*halves, emb_other, vectors, vec_other, meta)
    sent = [lax.ppermute(mine, "blk", moves) for moves, _ in plans]
    beside_mine = lax.ppermute(mine, "blk", beside)
    weigh = functools.partial(tile, vecs=vecs)
    own_sums, own = weigh(mine, [mine, rest], turns=True, own_block=True)
    own_sums, own, sent[:1] = lax.optimization_barrier((own_sums, own, sent[:1]))
    beside_mine, sent[:1] = lax.optimization_barrier((beside_mine, sent[:1]))
    cut = beside_mine.shape[0] // SWAPS // 16 * 16
    shares = [beside_mine[at * cut : (at + 1) * cut if at < SWAPS - 1 else None] for at in range(SWAPS)]
    beside_rest = jnp.concatenate([lax.ppermute(share, "sub", swap) for share in shares], axis=0)
    parts = [own_sums]
    if not plans:
        parts.append(weigh(mine, [beside_mine, beside_rest], turns=True)[0])
    for number, ((moves, takers), pack) in enumerate(zip(plans, sent)):
        last = number == len(plans) - 1
        if number == 0:
            own_lines, own_cols = weigh(pack, [own], receivers=takers)
            own_lines, own_cols, beside_rest = lax.optimization_barrier((own_lines, own_cols, beside_rest))
            beside_sums, next_to = weigh(mine, [beside_mine, beside_rest], turns=True)
            parts.append(beside_sums)
            next_lines, next_cols = weigh(pack, [next_to], receivers=takers)
        else:
            pack, own_cols, next_cols = lax.optimization_barrier((pack, own_cols, next_cols))
            next_lines, cols = weigh(pack, [next_to], receivers=takers)
            next_cols = next_cols + cols
            pack, next_cols, parts[-1] = lax.optimization_barrier((pack, next_cols, parts[-1]))
            own_lines, cols = weigh(pack, [own], receivers=takers, last=last)
            own_cols = own_cols + cols
        parts.append(lax.ppermute(own_lines + next_lines, "blk", back(moves)))
        if last:
            next_rest = lax.ppermute(next_cols[:, half:], "sub", swap)
            crossing = next_cols[:, :half] + next_rest
            parts.append(lax.ppermute(crossing, "blk", beside))
            own_cols, _ = lax.optimization_barrier((own_cols, crossing))
            parts += [own_cols[:, :half], lax.ppermute(own_cols[:, half:], "sub", swap)]
    image = image_of(parts, vecs)
    image_other = lax.ppermute(image, "sub", swap)
    grams = lax.all_to_all(grams_of(image, 2 * blocks), ("blk", "sub"), 0, 0, tiled=True)
    return basis_of(grams, image, image_other, blocks * rows)


def solution(mesh):
    placed = (
        P(("groups", "blk"), "sub"),
        P("sub", ("groups", "blk")),
        P(None, ("groups", "blk")),
        P(None, ("groups", "blk")),
        P(("groups", "blk")),
    )
    return jax.shard_map(
        local, mesh=mesh, in_specs=placed, out_specs=P("sub", ("groups", "blk")), check_vma=False
    )
```

```python
import functools
import math

import jax
import jax.numpy as jnp
from jax import lax
from jax.experimental import pallas as pl
from jax.experimental.pallas import tpu as pltpu
from jax.sharding import PartitionSpec as P

SHARPNESS = 10.0
HORIZON = 2000.0
MARGIN = 8.0
EPSILON = 1e-06

LOG2E = math.log2(math.e)
COS_SCALE = math.sqrt(SHARPNESS * LOG2E)
GAP_SCALE = LOG2E / HORIZON
BASE = SHARPNESS * LOG2E + 1.0
BARRED_BELOW = BASE - 0.5 * GAP_SCALE

FIELDS = 9
LEFT, RIGHT, BOTTOM, TOP, FIRST, LAST, CAMERA, NORM, AREA = range(FIELDS)
CODE_ROWS = 16
LANES = 128
CHUNK = 256
OUT_ROWS = 40
COST = 1
LAST_COST = 4 * 1024 * 1024 * 1024
WIDE = 512
GROUP = 16
SWAPS = 3
VMEM_LIMIT = 48 * 1024 * 1024

NT = (((1,), (1,)), ((), ()))
VMEM_SPEC = pl.BlockSpec(memory_space=pltpu.VMEM)


def params():
    return pltpu.CompilerParams(vmem_limit_bytes=VMEM_LIMIT)


def dot_nt(a, b, precision=None):
    return lax.dot_general(a, b, NT, precision=precision, preferred_element_type=jnp.float32)


def pack_rows(half, vecs):
    return half + vecs + CODE_ROWS


def pack_kernel(emb_mine_ref, emb_rest_ref, emb_other_ref, vec_ref, vec_other_ref, meta_ref, mine_ref, rest_ref, code_ref):
    sub = lax.axis_index("sub")
    half, width = emb_mine_ref.shape
    half_vecs = vec_other_ref.shape[0]
    ones = jnp.ones((8, width), jnp.bfloat16)
    for ref, emb_ref, place in ((mine_ref, emb_mine_ref, sub), (rest_ref, emb_rest_ref, 1 - sub)):
        first = pl.multiple_of(place * half, half)
        for start in range(0, half, CHUNK):
            part = pl.ds(first + start, CHUNK)
            codes = []

            def whole(number, low_bits):
                codes.append((number >> low_bits) << low_bits)
                codes.append(number & ((1 << low_bits) - 1))

            meta = meta_ref[:, part]
            for axis in range(2):
                whole(jnp.minimum(meta[axis : axis + 1], meta[axis + 2 : axis + 3]), 5)
                whole(jnp.maximum(meta[axis : axis + 1], meta[axis + 2 : axis + 3]), 5)
            whole(jnp.minimum(meta[4:5], meta[5:6]), 7)
            whole(jnp.maximum(meta[4:5], meta[5:6]), 7)
            codes.append(meta[6:7])
            codes = [code.astype(jnp.float32) for code in codes]
            rest = jnp.zeros((8, CHUNK), jnp.float32)
            for values in (emb_ref[start : start + CHUNK, :], emb_other_ref[part, :]):
                values = values.astype(jnp.float32)
                square = values * values
                high = square.astype(jnp.bfloat16)
                low = (square - high.astype(jnp.float32)).astype(jnp.bfloat16)
                rest = rest + (dot_nt(ones, high) + dot_nt(ones, low))
            rest = rest[0:1]
            for _ in range(3):
                piece = rest.astype(jnp.bfloat16).astype(jnp.float32)
                codes.append(piece)
                rest = rest - piece
            code_ref[:, start : start + CHUNK] = jnp.concatenate(codes, axis=0).astype(jnp.bfloat16)
        source = pl.ds(first, half)
        sides = (
            (emb_ref[...], vec_ref[:, source], sub),
            (emb_other_ref[source, :], vec_other_ref[:, source], 1 - sub),
        )
        for values, vectors, side in sides:
            ref[0:half, pl.ds(pl.multiple_of(side * width, width), width)] = values
            ref[pl.ds(pl.multiple_of(half + side * half_vecs, 16), half_vecs), :] = vectors
        first_code = half + 2 * half_vecs
        ref[first_code : first_code + CODE_ROWS, :] = code_ref[...]


def packs_of(emb_mine, emb_rest, emb_other, vec, vec_other, meta):
    half, width = emb_mine.shape
    features = 2 * width
    assert half == features
    size = pack_rows(half, 2 * vec_other.shape[0])
    return pl.pallas_call(
        pack_kernel,
        out_shape=[jax.ShapeDtypeStruct((size, features), jnp.bfloat16)] * 2,
        in_specs=[VMEM_SPEC] * 6,
        out_specs=[VMEM_SPEC] * 2,
        scratch_shapes=[pltpu.VMEM((CODE_ROWS, half), jnp.bfloat16)],
        compiler_params=params(),
        name="pack",
    )(emb_mine, emb_rest, emb_other, vec, vec_other, meta)


def decode(codes):
    codes = codes.astype(jnp.float32)
    numbers = [codes[2 * index : 2 * index + 1] + codes[2 * index + 1 : 2 * index + 2] for index in range(6)]
    left, right, bottom, top, first, last = numbers
    right, top = right + MARGIN, top + MARGIN
    square = codes[15:16] + codes[14:15] + codes[13:14]
    norm = lax.rsqrt(square + EPSILON) * COS_SCALE
    area = (right - left) * (top - bottom)
    return [left, right, bottom, top, first * GAP_SCALE + BASE, last * GAP_SCALE, codes[12:13], norm, area]


def with_ones(vectors):
    shape = (CODE_ROWS, vectors.shape[1])
    tail = jnp.where(lax.broadcasted_iota(jnp.int32, shape, 0) == 0, 1.0, 0.0)
    return jnp.concatenate([vectors, tail.astype(jnp.bfloat16)], axis=0)


def weights_of(products, row, col, same):
    width = jnp.maximum(jnp.minimum(row(RIGHT), col(RIGHT)) - jnp.maximum(row(LEFT), col(LEFT)), 0.0)
    height = jnp.maximum(jnp.minimum(row(TOP), col(TOP)) - jnp.maximum(row(BOTTOM), col(BOTTOM)), 0.0)
    inter = width * height
    both = row(AREA) + col(AREA)
    share = (both + inter) * pltpu.reciprocal(both - inter, approx=True, full_range=False)
    gap = jnp.maximum(col(FIRST) - row(LAST), row(FIRST) - col(LAST))
    logit = products * row(NORM) * col(NORM)
    value = jnp.exp2(logit - jnp.maximum(gap, BASE)) * share
    barred = (row(CAMERA) == col(CAMERA)) & (gap < BARRED_BELOW)
    if same is not None:
        barred = barred & jnp.logical_not(same)
    return jnp.where(barred, 0.0, value)


def tile_kernel(blocks, turns, own_block, receivers, vecs, *refs):
    row_ref, col_refs = refs[0], refs[1 : 1 + blocks]
    row_out_ref, col_out_ref, field_ref, spread_ref = refs[1 + blocks : 5 + blocks]
    products, weights = [refs[at : at + 2] for at in (5 + blocks, 7 + blocks)]
    col_spread_ref, row_vec_ref = refs[9 + blocks :]
    size, rows = row_ref.shape
    features = size - vecs - CODE_ROWS
    vec_rows, code_rows = slice(features, features + vecs), slice(features + vecs, size)
    row_out_ref[...] = jnp.zeros_like(row_out_ref)

    def block(col_ref, done):
        chunks = col_ref.shape[1] // WIDE

        def place(step, base=0):
            return pl.ds(pl.multiple_of(base + step * WIDE, WIDE), WIDE)

        def multiply(step, product_ref):
            product_ref[...] = jnp.dot(
                row_ref[0:rows, :], col_ref[0:features, place(step)], preferred_element_type=jnp.float32
            )

        def weigh(step, product_ref, weight_ref):
            for field, values in enumerate(decode(col_ref[code_rows, place(step)])):
                col_spread_ref[field] = jnp.broadcast_to(values, (8, WIDE))
            for start in range(0, rows, GROUP):
                row_part = slice(start, start + GROUP)

                def row(field):
                    return jnp.concatenate([spread_ref[field, row_part, :]] * (WIDE // LANES), axis=1)

                def col(field):
                    return jnp.concatenate([col_spread_ref[field]] * (GROUP // 8), axis=0)

                same = None
                if own_block:
                    row_ids = lax.broadcasted_iota(jnp.int32, (GROUP, WIDE), 0) + (start - step * WIDE)
                    same = row_ids == lax.broadcasted_iota(jnp.int32, (GROUP, WIDE), 1)
                weight_ref[row_part, :] = weights_of(product_ref[row_part, :], row, col, same).astype(jnp.bfloat16)

        def total(step, weight_ref):
            col_vecs = with_ones(col_ref[vec_rows, place(step)])
            row_out_ref[...] += dot_nt(col_vecs, weight_ref[...])[0:OUT_ROWS]
            if not turns:
                col_out_ref[:, place(step, done)] = jnp.dot(
                    row_vec_ref[...], weight_ref[...], preferred_element_type=jnp.float32
                )[0:OUT_ROWS]

        def steps(index, carry):
            for parity in range(2):
                step = 2 * index + parity
                multiply(lax.rem(step + 1, chunks), products[1 - parity])
                weigh(step, products[parity], weights[parity])
                total(lax.rem(step + chunks - 1, chunks), weights[1 - parity])
            return carry

        multiply(0, products[0])
        weights[1][...] = jnp.zeros_like(weights[1])
        lax.fori_loop(0, chunks // 2, steps, 0)
        total(chunks - 1, weights[1])

    def compute():
        for field, values in enumerate(decode(row_ref[code_rows, :])):
            field_ref[field : field + 1, :] = values
        turned = field_ref[...].T
        for field in range(FIELDS):
            spread_ref[field] = jnp.broadcast_to(turned[:, field : field + 1], (rows, LANES))
        row_vec_ref[...] = with_ones(row_ref[vec_rows, :])
        if turns:
            for number, pack_ref in enumerate(col_refs):
                part = pl.ds(number * rows, rows)
                col_out_ref[0:features, part] = pack_ref[0:rows, :].T
                col_out_ref[features:size, part] = pack_ref[features:size, :]
            block(col_out_ref, 0)
        else:
            done = 0
            for col_ref in col_refs:
                block(col_ref, done)
                done += col_ref.shape[1]

    if receivers is None:
        compute()
        return
    pair = lax.axis_index("blk") // 2
    takes_part = functools.reduce(jnp.logical_or, [pair == one for one in receivers])

    @pl.when(takes_part)
    def _():
        compute()

    @pl.when(jnp.logical_not(takes_part))
    def _():
        col_out_ref[...] = jnp.zeros_like(col_out_ref)


def tile(row, columns, vecs, turns=False, own_block=False, receivers=None, last=False):
    size, rows = row.shape
    cols = len(columns) * rows if turns else sum(part.shape[1] for part in columns)
    second = jax.ShapeDtypeStruct((size, cols), jnp.bfloat16)
    if not turns:
        second = jax.ShapeDtypeStruct((OUT_ROWS, cols), jnp.float32)
    return pl.pallas_call(
        functools.partial(tile_kernel, len(columns), turns, own_block, receivers, vecs),
        out_shape=[jax.ShapeDtypeStruct((OUT_ROWS, rows), jnp.float32), second],
        in_specs=[VMEM_SPEC] * (1 + len(columns)),
        out_specs=[VMEM_SPEC] * 2,
        scratch_shapes=[
            pltpu.VMEM((LANES, rows), jnp.float32),
            pltpu.VMEM((FIELDS, rows, LANES), jnp.float32),
            pltpu.VMEM((rows, WIDE), jnp.float32),
            pltpu.VMEM((rows, WIDE), jnp.float32),
            pltpu.VMEM((rows, WIDE), jnp.bfloat16),
            pltpu.VMEM((rows, WIDE), jnp.bfloat16),
            pltpu.VMEM((FIELDS, 8, WIDE), jnp.float32),
            pltpu.VMEM((vecs + CODE_ROWS, rows), jnp.bfloat16),
        ],
        cost_estimate=pl.CostEstimate(flops=LAST_COST if last else COST, bytes_accessed=COST, transcendentals=0),
        compiler_params=params(),
        name="tile",
    )(row, *columns)


def image_kernel(*refs):
    parts, image_ref = refs[:-1], refs[-1]
    total = parts[0][...]
    for part in parts[1:]:
        total = total + part[...]
    vecs = image_ref.shape[0]
    image_ref[...] = total[0:vecs] / total[vecs : vecs + 1]


def image_of(parts, vecs):
    return pl.pallas_call(
        image_kernel,
        out_shape=jax.ShapeDtypeStruct((vecs, parts[0].shape[1]), jnp.float32),
        in_specs=[VMEM_SPEC] * len(parts),
        out_specs=VMEM_SPEC,
        compiler_params=params(),
        name="image",
    )(*parts)


def gram_kernel(image_ref, grams_ref):
    vecs, cols = image_ref.shape
    image = image_ref[...]
    padded = jnp.concatenate([image, jnp.zeros((LANES - vecs, cols), jnp.float32)], axis=0)
    gram = dot_nt(image, padded, lax.Precision.HIGHEST)
    packed = gram[0:8]
    for piece in range(1, vecs // 8):
        packed = packed + pltpu.roll(gram[8 * piece : 8 * piece + 8], piece * vecs, 1)
    for copy in range(grams_ref.shape[0]):
        grams_ref[copy] = packed


def grams_of(image, copies):
    return pl.pallas_call(
        gram_kernel,
        out_shape=jax.ShapeDtypeStruct((copies, 8, LANES), jnp.float32),
        in_specs=[VMEM_SPEC],
        out_specs=VMEM_SPEC,
        compiler_params=params(),
        name="gram",
    )(image)


def inverse_of(number):
    guess = pltpu.reciprocal(number, approx=True)
    guess = guess * (2.0 - number * guess)
    return guess * (2.0 - number * guess)


def basis_kernel(total_rows, grams_ref, mine_ref, other_ref, out_ref, inverse_ref):
    vecs, half = mine_ref.shape
    sub = lax.axis_index("sub")
    packed = jnp.sum(grams_ref[...], axis=0) / total_rows
    lane = lax.broadcasted_iota(jnp.int32, (vecs, LANES), 1)
    line = lax.broadcasted_iota(jnp.int32, (vecs, LANES), 0)
    pieces = [packed] + [pltpu.roll(packed, LANES - piece * vecs, 1) for piece in range(1, LANES // vecs)]
    matrix = jnp.where(lane < vecs, jnp.concatenate(pieces, axis=0), 0.0)
    matrix = jnp.where(lane == line + vecs, 1.0, matrix)
    for step in range(0, vecs, 2):
        left = jnp.broadcast_to(matrix[:, step : step + 1], (vecs, LANES))
        right = jnp.broadcast_to(matrix[:, step + 1 : step + 2], (vecs, LANES))
        upper, lower = matrix[step : step + 1, :], matrix[step + 1 : step + 2, :]
        across = right[step : step + 1, :]
        inverse = inverse_of(left[step : step + 1, :])
        factor = left[step + 1 : step + 2, :] * inverse
        lower = lower - factor * upper
        inverse_next = inverse_of(right[step + 1 : step + 2, :] - factor * across)
        first = left * inverse
        second = (right - first * across) * inverse_next
        reduced = matrix - first * upper - second * lower
        matrix = jnp.where(line > step + 1, reduced, jnp.where(line == step + 1, lower, matrix))
    pivots = jnp.sum(jnp.where(lane == line, matrix, 0.0), axis=1, keepdims=True)
    inverse_ref[...] = pltpu.roll(matrix / jnp.sqrt(pivots), LANES - vecs, 1)
    share = vecs // 2
    own_rows = inverse_ref[pl.ds(pl.multiple_of(sub * share, 8), share), :][:, 0:vecs]
    for ref, place in ((mine_ref, sub), (other_ref, 1 - sub)):
        out_ref[:, pl.ds(pl.multiple_of(place * half, LANES), half)] = jnp.dot(
            own_rows, ref[...], precision=lax.Precision.HIGHEST, preferred_element_type=jnp.float32
        )


def basis_of(grams, mine, other, total_rows):
    vecs, half = mine.shape
    return pl.pallas_call(
        functools.partial(basis_kernel, total_rows),
        out_shape=jax.ShapeDtypeStruct((vecs // 2, 2 * half), jnp.float32),
        in_specs=[VMEM_SPEC] * 3,
        out_specs=VMEM_SPEC,
        scratch_shapes=[pltpu.VMEM((vecs, LANES), jnp.float32)],
        compiler_params=params(),
        name="basis",
    )(grams, mine, other)


def exchanges(pairs):
    plans = []
    for distance in range(1, pairs // 2):
        plans.append(([((p + distance) % pairs, p) for p in range(pairs)], None))
    if pairs > 1:
        half = pairs // 2
        last = [(p, p + half) if p % 2 == 0 else (p + half, p) for p in range(half)]
        plans.append((last, sorted(taker for _, taker in last)))
    return plans


def block_moves(pair_moves):
    return [(2 * source + member, 2 * target + member) for source, target in pair_moves for member in range(2)]


def back(moves):
    return [(target, source) for source, target in moves]


def local(embeddings, vectors, boxes, spans, camera):
    rows = embeddings.shape[0]
    half = rows // 2
    vecs = 2 * vectors.shape[0]
    blocks = lax.axis_size("blk")
    swap = [(0, 1), (1, 0)]
    beside = [(block, block ^ 1) for block in range(blocks)]
    plans = [(block_moves(moves), takers) for moves, takers in exchanges(blocks // 2)]

    emb_other = lax.ppermute(embeddings, "sub", swap)
    vec_other = lax.ppermute(vectors, "sub", swap)
    meta = jnp.concatenate([boxes, spans, camera[None, :]], axis=0)
    sub = lax.axis_index("sub")
    halves = [lax.dynamic_slice_in_dim(embeddings, place * half, half, 0) for place in (sub, 1 - sub)]
    mine, rest = packs_of(*halves, emb_other, vectors, vec_other, meta)
    sent = [lax.ppermute(mine, "blk", moves) for moves, _ in plans]
    beside_mine = lax.ppermute(mine, "blk", beside)
    weigh = functools.partial(tile, vecs=vecs)
    own_sums, own = weigh(mine, [mine, rest], turns=True, own_block=True)
    own_sums, own, sent[:1] = lax.optimization_barrier((own_sums, own, sent[:1]))
    beside_mine, sent[:1] = lax.optimization_barrier((beside_mine, sent[:1]))
    cut = beside_mine.shape[0] // SWAPS // 16 * 16
    shares = [beside_mine[at * cut : (at + 1) * cut if at < SWAPS - 1 else None] for at in range(SWAPS)]
    beside_rest = jnp.concatenate([lax.ppermute(share, "sub", swap) for share in shares], axis=0)
    parts = [own_sums]
    if not plans:
        parts.append(weigh(mine, [beside_mine, beside_rest], turns=True)[0])
    for number, ((moves, takers), pack) in enumerate(zip(plans, sent)):
        last = number == len(plans) - 1
        if number == 0:
            own_lines, own_cols = weigh(pack, [own], receivers=takers)
            own_lines, own_cols, beside_rest = lax.optimization_barrier((own_lines, own_cols, beside_rest))
            beside_sums, next_to = weigh(mine, [beside_mine, beside_rest], turns=True)
            parts.append(beside_sums)
            next_lines, next_cols = weigh(pack, [next_to], receivers=takers)
        else:
            pack, own_cols, next_cols = lax.optimization_barrier((pack, own_cols, next_cols))
            next_lines, cols = weigh(pack, [next_to], receivers=takers)
            next_cols = next_cols + cols
            pack, next_cols, parts[-1] = lax.optimization_barrier((pack, next_cols, parts[-1]))
            own_lines, cols = weigh(pack, [own], receivers=takers, last=last)
            own_cols = own_cols + cols
        parts.append(lax.ppermute(own_lines + next_lines, "blk", back(moves)))
        if last:
            next_rest = lax.ppermute(next_cols[:, half:], "sub", swap)
            crossing = next_cols[:, :half] + next_rest
            parts.append(lax.ppermute(crossing, "blk", beside))
            own_cols, _ = lax.optimization_barrier((own_cols, crossing))
            parts += [own_cols[:, :half], lax.ppermute(own_cols[:, half:], "sub", swap)]
    image = image_of(parts, vecs)
    image_other = lax.ppermute(image, "sub", swap)
    grams = lax.all_to_all(grams_of(image, 2 * blocks), ("blk", "sub"), 0, 0, tiled=True)
    return basis_of(grams, image, image_other, blocks * rows)


def solution(mesh):
    placed = (
        P(("groups", "blk"), "sub"),
        P("sub", ("groups", "blk")),
        P(None, ("groups", "blk")),
        P(None, ("groups", "blk")),
        P(("groups", "blk")),
    )
    return jax.shard_map(
        local, mesh=mesh, in_specs=placed, out_specs=P("sub", ("groups", "blk")), check_vma=False
    )
```

```python
import functools
import math

import jax
import jax.numpy as jnp
from jax import lax
from jax.experimental import pallas as pl
from jax.experimental.pallas import tpu as pltpu
from jax.sharding import PartitionSpec as P

SHARPNESS = 10.0
HORIZON = 2000.0
MARGIN = 8.0
EPSILON = 1e-06

LOG2E = math.log2(math.e)
COS_SCALE = math.sqrt(SHARPNESS * LOG2E)
GAP_SCALE = LOG2E / HORIZON
BASE = SHARPNESS * LOG2E + 1.0
BARRED_BELOW = BASE - 0.5 * GAP_SCALE

FIELDS = 9
LEFT, RIGHT, BOTTOM, TOP, FIRST, LAST, CAMERA, NORM, AREA = range(FIELDS)
CODE_ROWS = 16
LANES = 128
CHUNK = 256
OUT_ROWS = 40
COST = 1
LAST_COST = 4 * 1024 * 1024 * 1024
WIDE = 512
GROUP = 16
SWAPS = 3
VMEM_LIMIT = 48 * 1024 * 1024

NT = (((1,), (1,)), ((), ()))
VMEM_SPEC = pl.BlockSpec(memory_space=pltpu.VMEM)


def params():
    return pltpu.CompilerParams(vmem_limit_bytes=VMEM_LIMIT)


def dot_nt(a, b, precision=None):
    return lax.dot_general(a, b, NT, precision=precision, preferred_element_type=jnp.float32)


def pack_rows(half, vecs):
    return half + vecs + CODE_ROWS


def pack_kernel(emb_mine_ref, emb_rest_ref, emb_other_ref, vec_ref, vec_other_ref, meta_ref, mine_ref, rest_ref, code_ref):
    sub = lax.axis_index("sub")
    half, width = emb_mine_ref.shape
    half_vecs = vec_other_ref.shape[0]
    ones = jnp.ones((8, width), jnp.bfloat16)
    for ref, emb_ref, place in ((mine_ref, emb_mine_ref, sub), (rest_ref, emb_rest_ref, 1 - sub)):
        first = pl.multiple_of(place * half, half)
        for start in range(0, half, CHUNK):
            part = pl.ds(first + start, CHUNK)
            codes = []

            def whole(number, low_bits):
                codes.append((number >> low_bits) << low_bits)
                codes.append(number & ((1 << low_bits) - 1))

            meta = meta_ref[:, part]
            for axis in range(2):
                whole(jnp.minimum(meta[axis : axis + 1], meta[axis + 2 : axis + 3]), 5)
                whole(jnp.maximum(meta[axis : axis + 1], meta[axis + 2 : axis + 3]), 5)
            whole(jnp.minimum(meta[4:5], meta[5:6]), 7)
            whole(jnp.maximum(meta[4:5], meta[5:6]), 7)
            codes.append(meta[6:7])
            codes = [code.astype(jnp.float32) for code in codes]
            rest = jnp.zeros((8, CHUNK), jnp.float32)
            for values in (emb_ref[start : start + CHUNK, :], emb_other_ref[part, :]):
                values = values.astype(jnp.float32)
                square = values * values
                high = square.astype(jnp.bfloat16)
                low = (square - high.astype(jnp.float32)).astype(jnp.bfloat16)
                rest = rest + (dot_nt(ones, high) + dot_nt(ones, low))
            rest = rest[0:1]
            for _ in range(3):
                piece = rest.astype(jnp.bfloat16).astype(jnp.float32)
                codes.append(piece)
                rest = rest - piece
            code_ref[:, start : start + CHUNK] = jnp.concatenate(codes, axis=0).astype(jnp.bfloat16)
        source = pl.ds(first, half)
        sides = (
            (emb_ref[...], vec_ref[:, source], sub),
            (emb_other_ref[source, :], vec_other_ref[:, source], 1 - sub),
        )
        for values, vectors, side in sides:
            ref[0:half, pl.ds(pl.multiple_of(side * width, width), width)] = values
            ref[pl.ds(pl.multiple_of(half + side * half_vecs, 16), half_vecs), :] = vectors
        first_code = half + 2 * half_vecs
        ref[first_code : first_code + CODE_ROWS, :] = code_ref[...]


def packs_of(emb_mine, emb_rest, emb_other, vec, vec_other, meta):
    half, width = emb_mine.shape
    features = 2 * width
    assert half == features
    size = pack_rows(half, 2 * vec_other.shape[0])
    return pl.pallas_call(
        pack_kernel,
        out_shape=[jax.ShapeDtypeStruct((size, features), jnp.bfloat16)] * 2,
        in_specs=[VMEM_SPEC] * 6,
        out_specs=[VMEM_SPEC] * 2,
        scratch_shapes=[pltpu.VMEM((CODE_ROWS, half), jnp.bfloat16)],
        compiler_params=params(),
        name="pack",
    )(emb_mine, emb_rest, emb_other, vec, vec_other, meta)


def decode(codes):
    codes = codes.astype(jnp.float32)
    numbers = [codes[2 * index : 2 * index + 1] + codes[2 * index + 1 : 2 * index + 2] for index in range(6)]
    left, right, bottom, top, first, last = numbers
    right, top = right + MARGIN, top + MARGIN
    square = codes[15:16] + codes[14:15] + codes[13:14]
    norm = lax.rsqrt(square + EPSILON) * COS_SCALE
    area = (right - left) * (top - bottom)
    return [left, right, bottom, top, first * GAP_SCALE + BASE, last * GAP_SCALE, codes[12:13], norm, area]


def with_ones(vectors):
    shape = (CODE_ROWS, vectors.shape[1])
    tail = jnp.where(lax.broadcasted_iota(jnp.int32, shape, 0) == 0, 1.0, 0.0)
    return jnp.concatenate([vectors, tail.astype(jnp.bfloat16)], axis=0)


def weights_of(products, row, col, same):
    width = jnp.maximum(jnp.minimum(row(RIGHT), col(RIGHT)) - jnp.maximum(row(LEFT), col(LEFT)), 0.0)
    height = jnp.maximum(jnp.minimum(row(TOP), col(TOP)) - jnp.maximum(row(BOTTOM), col(BOTTOM)), 0.0)
    inter = width * height
    both = row(AREA) + col(AREA)
    share = (both + inter) * pltpu.reciprocal(both - inter, approx=True, full_range=False)
    gap = jnp.maximum(col(FIRST) - row(LAST), row(FIRST) - col(LAST))
    logit = products * row(NORM) * col(NORM)
    value = jnp.exp2(logit - jnp.maximum(gap, BASE)) * share
    barred = (row(CAMERA) == col(CAMERA)) & (gap < BARRED_BELOW)
    if same is not None:
        barred = barred & jnp.logical_not(same)
    return jnp.where(barred, 0.0, value)


def tile_kernel(blocks, turns, own_block, receivers, vecs, *refs):
    row_ref, col_refs = refs[0], refs[1 : 1 + blocks]
    row_out_ref, col_out_ref, field_ref, spread_ref = refs[1 + blocks : 5 + blocks]
    products, weights = [refs[at : at + 2] for at in (5 + blocks, 7 + blocks)]
    col_spread_ref, row_vec_ref = refs[9 + blocks :]
    size, rows = row_ref.shape
    features = size - vecs - CODE_ROWS
    vec_rows, code_rows = slice(features, features + vecs), slice(features + vecs, size)
    row_out_ref[...] = jnp.zeros_like(row_out_ref)

    def multiply(chunk, product_ref):
        col_ref, part, _ = chunk
        product_ref[...] = jnp.dot(row_ref[0:rows, :], col_ref[0:features, part], preferred_element_type=jnp.float32)

    def weigh(chunk, product_ref, weight_ref):
        col_ref, part, done = chunk
        for field, values in enumerate(decode(col_ref[code_rows, part])):
            col_spread_ref[field] = jnp.broadcast_to(values, (8, WIDE))
        for start in range(0, rows, GROUP):
            row_part = slice(start, start + GROUP)

            def row(field):
                return jnp.concatenate([spread_ref[field, row_part, :]] * (WIDE // LANES), axis=1)

            def col(field):
                return jnp.concatenate([col_spread_ref[field]] * (GROUP // 8), axis=0)

            same = None
            if own_block and done < rows:
                row_ids = lax.broadcasted_iota(jnp.int32, (GROUP, WIDE), 0) + (start - done)
                same = row_ids == lax.broadcasted_iota(jnp.int32, (GROUP, WIDE), 1)
            weight_ref[row_part, :] = weights_of(product_ref[row_part, :], row, col, same).astype(jnp.bfloat16)

    def total(chunk, weight_ref):
        col_ref, part, done = chunk
        row_out_ref[...] += dot_nt(with_ones(col_ref[vec_rows, part]), weight_ref[...])[0:OUT_ROWS]
        if not turns:
            col_out_ref[:, done : done + WIDE] = jnp.dot(
                row_vec_ref[...], weight_ref[...], preferred_element_type=jnp.float32
            )[0:OUT_ROWS]

    def pipeline(chunks):
        multiply(chunks[0], products[0])
        for step, chunk in enumerate(chunks):
            now, later = step % 2, (step + 1) % 2
            if step + 1 < len(chunks):
                multiply(chunks[step + 1], products[later])
            weigh(chunk, products[now], weights[now])
            if step > 0:
                total(chunks[step - 1], weights[later])
        total(chunks[-1], weights[(len(chunks) - 1) % 2])

    def compute():
        for field, values in enumerate(decode(row_ref[code_rows, :])):
            field_ref[field : field + 1, :] = values
        turned = field_ref[...].T
        for field in range(FIELDS):
            spread_ref[field] = jnp.broadcast_to(turned[:, field : field + 1], (rows, LANES))
        row_vec_ref[...] = with_ones(row_ref[vec_rows, :])
        if turns:
            for number, pack_ref in enumerate(col_refs):
                part = pl.ds(number * rows, rows)
                col_out_ref[0:features, part] = pack_ref[0:rows, :].T
                col_out_ref[features:size, part] = pack_ref[features:size, :]
        sources = [col_out_ref] if turns else col_refs
        chunks = []
        for source in sources:
            for start in range(0, source.shape[1], WIDE):
                chunks.append((source, slice(start, start + WIDE), len(chunks) * WIDE))
        pipeline(chunks)

    if receivers is None:
        compute()
        return
    pair = lax.axis_index("blk") // 2
    takes_part = functools.reduce(jnp.logical_or, [pair == one for one in receivers])

    @pl.when(takes_part)
    def _():
        compute()

    @pl.when(jnp.logical_not(takes_part))
    def _():
        col_out_ref[...] = jnp.zeros_like(col_out_ref)


def tile(row, columns, vecs, turns=False, own_block=False, receivers=None, last=False):
    size, rows = row.shape
    cols = len(columns) * rows if turns else sum(part.shape[1] for part in columns)
    second = jax.ShapeDtypeStruct((size, cols), jnp.bfloat16)
    if not turns:
        second = jax.ShapeDtypeStruct((OUT_ROWS, cols), jnp.float32)
    return pl.pallas_call(
        functools.partial(tile_kernel, len(columns), turns, own_block, receivers, vecs),
        out_shape=[jax.ShapeDtypeStruct((OUT_ROWS, rows), jnp.float32), second],
        in_specs=[VMEM_SPEC] * (1 + len(columns)),
        out_specs=[VMEM_SPEC] * 2,
        scratch_shapes=[
            pltpu.VMEM((LANES, rows), jnp.float32),
            pltpu.VMEM((FIELDS, rows, LANES), jnp.float32),
            pltpu.VMEM((rows, WIDE), jnp.float32),
            pltpu.VMEM((rows, WIDE), jnp.float32),
            pltpu.VMEM((rows, WIDE), jnp.bfloat16),
            pltpu.VMEM((rows, WIDE), jnp.bfloat16),
            pltpu.VMEM((FIELDS, 8, WIDE), jnp.float32),
            pltpu.VMEM((vecs + CODE_ROWS, rows), jnp.bfloat16),
        ],
        cost_estimate=pl.CostEstimate(flops=LAST_COST if last else COST, bytes_accessed=COST, transcendentals=0),
        compiler_params=params(),
        name="tile",
    )(row, *columns)


def image_kernel(*refs):
    parts, image_ref = refs[:-1], refs[-1]
    total = parts[0][...]
    for part in parts[1:]:
        total = total + part[...]
    vecs = image_ref.shape[0]
    image_ref[...] = total[0:vecs] / total[vecs : vecs + 1]


def image_of(parts, vecs):
    return pl.pallas_call(
        image_kernel,
        out_shape=jax.ShapeDtypeStruct((vecs, parts[0].shape[1]), jnp.float32),
        in_specs=[VMEM_SPEC] * len(parts),
        out_specs=VMEM_SPEC,
        compiler_params=params(),
        name="image",
    )(*parts)


def gram_kernel(image_ref, grams_ref):
    vecs, cols = image_ref.shape
    image = image_ref[...]
    padded = jnp.concatenate([image, jnp.zeros((LANES - vecs, cols), jnp.float32)], axis=0)
    gram = dot_nt(image, padded, lax.Precision.HIGHEST)
    packed = gram[0:8]
    for piece in range(1, vecs // 8):
        packed = packed + pltpu.roll(gram[8 * piece : 8 * piece + 8], piece * vecs, 1)
    for copy in range(grams_ref.shape[0]):
        grams_ref[copy] = packed


def grams_of(image, copies):
    return pl.pallas_call(
        gram_kernel,
        out_shape=jax.ShapeDtypeStruct((copies, 8, LANES), jnp.float32),
        in_specs=[VMEM_SPEC],
        out_specs=VMEM_SPEC,
        compiler_params=params(),
        name="gram",
    )(image)


def inverse_of(number):
    guess = pltpu.reciprocal(number, approx=True)
    guess = guess * (2.0 - number * guess)
    return guess * (2.0 - number * guess)


def basis_kernel(total_rows, grams_ref, mine_ref, other_ref, out_ref, inverse_ref):
    vecs, half = mine_ref.shape
    sub = lax.axis_index("sub")
    packed = jnp.sum(grams_ref[...], axis=0) / total_rows
    lane = lax.broadcasted_iota(jnp.int32, (vecs, LANES), 1)
    line = lax.broadcasted_iota(jnp.int32, (vecs, LANES), 0)
    pieces = [packed] + [pltpu.roll(packed, LANES - piece * vecs, 1) for piece in range(1, LANES // vecs)]
    matrix = jnp.where(lane < vecs, jnp.concatenate(pieces, axis=0), 0.0)
    matrix = jnp.where(lane == line + vecs, 1.0, matrix)
    for step in range(0, vecs, 2):
        left = jnp.broadcast_to(matrix[:, step : step + 1], (vecs, LANES))
        right = jnp.broadcast_to(matrix[:, step + 1 : step + 2], (vecs, LANES))
        upper, lower = matrix[step : step + 1, :], matrix[step + 1 : step + 2, :]
        across = right[step : step + 1, :]
        inverse = inverse_of(left[step : step + 1, :])
        factor = left[step + 1 : step + 2, :] * inverse
        lower = lower - factor * upper
        inverse_next = inverse_of(right[step + 1 : step + 2, :] - factor * across)
        first = left * inverse
        second = (right - first * across) * inverse_next
        reduced = matrix - first * upper - second * lower
        matrix = jnp.where(line > step + 1, reduced, jnp.where(line == step + 1, lower, matrix))
    pivots = jnp.sum(jnp.where(lane == line, matrix, 0.0), axis=1, keepdims=True)
    inverse_ref[...] = pltpu.roll(matrix / jnp.sqrt(pivots), LANES - vecs, 1)
    share = vecs // 2
    own_rows = inverse_ref[pl.ds(pl.multiple_of(sub * share, 8), share), :][:, 0:vecs]
    for ref, place in ((mine_ref, sub), (other_ref, 1 - sub)):
        out_ref[:, pl.ds(pl.multiple_of(place * half, LANES), half)] = jnp.dot(
            own_rows, ref[...], precision=lax.Precision.HIGHEST, preferred_element_type=jnp.float32
        )


def basis_of(grams, mine, other, total_rows):
    vecs, half = mine.shape
    return pl.pallas_call(
        functools.partial(basis_kernel, total_rows),
        out_shape=jax.ShapeDtypeStruct((vecs // 2, 2 * half), jnp.float32),
        in_specs=[VMEM_SPEC] * 3,
        out_specs=VMEM_SPEC,
        scratch_shapes=[pltpu.VMEM((vecs, LANES), jnp.float32)],
        compiler_params=params(),
        name="basis",
    )(grams, mine, other)


def exchanges(pairs):
    if pairs == 4:
        return [([(0, 2), (3, 1), (1, 0), (2, 3)], None), ([(2, 1), (0, 3)], [1, 3])]
    plans = []
    for distance in range(1, pairs // 2):
        plans.append(([((p + distance) % pairs, p) for p in range(pairs)], None))
    if pairs > 1:
        half = pairs // 2
        last = [(p, p + half) if p % 2 == 0 else (p + half, p) for p in range(half)]
        plans.append((last, sorted(taker for _, taker in last)))
    return plans


def block_moves(pair_moves):
    return [(2 * source + member, 2 * target + member) for source, target in pair_moves for member in range(2)]


def back(moves):
    return [(target, source) for source, target in moves]


def local(embeddings, vectors, boxes, spans, camera):
    rows = embeddings.shape[0]
    half = rows // 2
    vecs = 2 * vectors.shape[0]
    blocks = lax.axis_size("blk")
    swap = [(0, 1), (1, 0)]
    beside = [(block, block ^ 1) for block in range(blocks)]
    plans = [(block_moves(moves), takers) for moves, takers in exchanges(blocks // 2)]

    emb_other = lax.ppermute(embeddings, "sub", swap)
    vec_other = lax.ppermute(vectors, "sub", swap)
    meta = jnp.concatenate([boxes, spans, camera[None, :]], axis=0)
    sub = lax.axis_index("sub")
    halves = [lax.dynamic_slice_in_dim(embeddings, place * half, half, 0) for place in (sub, 1 - sub)]
    mine, rest = packs_of(*halves, emb_other, vectors, vec_other, meta)
    sent = [lax.ppermute(mine, "blk", moves) for moves, _ in plans]
    beside_mine = lax.ppermute(mine, "blk", beside)
    weigh = functools.partial(tile, vecs=vecs)
    own_sums, own = weigh(mine, [mine, rest], turns=True, own_block=True)
    own_sums, own, sent[:1] = lax.optimization_barrier((own_sums, own, sent[:1]))
    beside_mine, sent[:1] = lax.optimization_barrier((beside_mine, sent[:1]))
    cut = beside_mine.shape[0] // SWAPS // 16 * 16
    shares = [beside_mine[at * cut : (at + 1) * cut if at < SWAPS - 1 else None] for at in range(SWAPS)]
    beside_rest = jnp.concatenate([lax.ppermute(share, "sub", swap) for share in shares], axis=0)
    parts = [own_sums]
    if not plans:
        parts.append(weigh(mine, [beside_mine, beside_rest], turns=True)[0])
    for number, ((moves, takers), pack) in enumerate(zip(plans, sent)):
        last = number == len(plans) - 1
        if number == 0:
            own_lines, own_cols = weigh(pack, [own], receivers=takers)
            own_lines, own_cols, beside_rest = lax.optimization_barrier((own_lines, own_cols, beside_rest))
            beside_sums, next_to = weigh(mine, [beside_mine, beside_rest], turns=True)
            parts.append(beside_sums)
            next_lines, next_cols = weigh(pack, [next_to], receivers=takers)
        else:
            pack, own_cols, next_cols = lax.optimization_barrier((pack, own_cols, next_cols))
            next_lines, cols = weigh(pack, [next_to], receivers=takers)
            next_cols = next_cols + cols
            pack, next_cols, parts[-1] = lax.optimization_barrier((pack, next_cols, parts[-1]))
            own_lines, cols = weigh(pack, [own], receivers=takers, last=last)
            own_cols = own_cols + cols
        parts.append(lax.ppermute(own_lines + next_lines, "blk", back(moves)))
        if last:
            next_rest = lax.ppermute(next_cols[:, half:], "sub", swap)
            crossing = next_cols[:, :half] + next_rest
            parts.append(lax.ppermute(crossing, "blk", beside))
            own_cols, _ = lax.optimization_barrier((own_cols, crossing))
            parts += [own_cols[:, :half], lax.ppermute(own_cols[:, half:], "sub", swap)]
    image = image_of(parts, vecs)
    image_other = lax.ppermute(image, "sub", swap)
    grams = lax.all_to_all(grams_of(image, 2 * blocks), ("blk", "sub"), 0, 0, tiled=True)
    return basis_of(grams, image, image_other, blocks * rows)


def solution(mesh):
    placed = (
        P(("groups", "blk"), "sub"),
        P("sub", ("groups", "blk")),
        P(None, ("groups", "blk")),
        P(None, ("groups", "blk")),
        P(("groups", "blk")),
    )
    return jax.shard_map(
        local, mesh=mesh, in_specs=placed, out_specs=P("sub", ("groups", "blk")), check_vma=False
    )
```

```python
import functools
import math

import jax
import jax.numpy as jnp
from jax import lax
from jax.experimental import pallas as pl
from jax.experimental.pallas import tpu as pltpu
from jax.sharding import PartitionSpec as P

SHARPNESS = 10.0
HORIZON = 2000.0
MARGIN = 8.0
EPSILON = 1e-06

LOG2E = math.log2(math.e)
COS_SCALE = math.sqrt(SHARPNESS * LOG2E)
GAP_SCALE = LOG2E / HORIZON
BASE = SHARPNESS * LOG2E + 1.0
BARRED_BELOW = BASE - 0.5 * GAP_SCALE

FIELDS = 9
LEFT, RIGHT, BOTTOM, TOP, FIRST, LAST, CAMERA, NORM, AREA = range(FIELDS)
CODE_ROWS = 16
LANES = 128
CHUNK = 256
OUT_ROWS = 40
COST = 1
LAST_COST = 4 * 1024 * 1024 * 1024
WIDE = 512
GROUP = 16
SWAPS = 3
VMEM_LIMIT = 48 * 1024 * 1024

NT = (((1,), (1,)), ((), ()))
VMEM_SPEC = pl.BlockSpec(memory_space=pltpu.VMEM)


def params():
    return pltpu.CompilerParams(vmem_limit_bytes=VMEM_LIMIT)


def dot_nt(a, b, precision=None):
    return lax.dot_general(a, b, NT, precision=precision, preferred_element_type=jnp.float32)


def pack_rows(half, vecs):
    return half + vecs + CODE_ROWS


def pack_kernel(emb_mine_ref, emb_rest_ref, emb_other_ref, vec_ref, vec_other_ref, meta_ref, mine_ref, rest_ref, code_ref):
    sub = lax.axis_index("sub")
    half, width = emb_mine_ref.shape
    half_vecs = vec_other_ref.shape[0]
    ones = jnp.ones((8, width), jnp.bfloat16)
    for ref, emb_ref, place in ((mine_ref, emb_mine_ref, sub), (rest_ref, emb_rest_ref, 1 - sub)):
        first = pl.multiple_of(place * half, half)
        for start in range(0, half, CHUNK):
            part = pl.ds(first + start, CHUNK)
            codes = []

            def whole(number, low_bits):
                codes.append((number >> low_bits) << low_bits)
                codes.append(number & ((1 << low_bits) - 1))

            meta = meta_ref[:, part]
            for axis in range(2):
                whole(jnp.minimum(meta[axis : axis + 1], meta[axis + 2 : axis + 3]), 5)
                whole(jnp.maximum(meta[axis : axis + 1], meta[axis + 2 : axis + 3]), 5)
            whole(jnp.minimum(meta[4:5], meta[5:6]), 7)
            whole(jnp.maximum(meta[4:5], meta[5:6]), 7)
            codes.append(meta[6:7])
            codes = [code.astype(jnp.float32) for code in codes]
            rest = jnp.zeros((8, CHUNK), jnp.float32)
            for values in (emb_ref[start : start + CHUNK, :], emb_other_ref[part, :]):
                values = values.astype(jnp.float32)
                square = values * values
                high = square.astype(jnp.bfloat16)
                low = (square - high.astype(jnp.float32)).astype(jnp.bfloat16)
                rest = rest + (dot_nt(ones, high) + dot_nt(ones, low))
            rest = rest[0:1]
            for _ in range(3):
                piece = rest.astype(jnp.bfloat16).astype(jnp.float32)
                codes.append(piece)
                rest = rest - piece
            code_ref[:, start : start + CHUNK] = jnp.concatenate(codes, axis=0).astype(jnp.bfloat16)
        source = pl.ds(first, half)
        sides = (
            (emb_ref[...], vec_ref[:, source], sub),
            (emb_other_ref[source, :], vec_other_ref[:, source], 1 - sub),
        )
        for values, vectors, side in sides:
            ref[0:half, pl.ds(pl.multiple_of(side * width, width), width)] = values
            ref[pl.ds(pl.multiple_of(half + side * half_vecs, 16), half_vecs), :] = vectors
        first_code = half + 2 * half_vecs
        ref[first_code : first_code + CODE_ROWS, :] = code_ref[...]


def packs_of(emb_mine, emb_rest, emb_other, vec, vec_other, meta):
    half, width = emb_mine.shape
    features = 2 * width
    assert half == features
    size = pack_rows(half, 2 * vec_other.shape[0])
    return pl.pallas_call(
        pack_kernel,
        out_shape=[jax.ShapeDtypeStruct((size, features), jnp.bfloat16)] * 2,
        in_specs=[VMEM_SPEC] * 6,
        out_specs=[VMEM_SPEC] * 2,
        scratch_shapes=[pltpu.VMEM((CODE_ROWS, half), jnp.bfloat16)],
        compiler_params=params(),
        name="pack",
    )(emb_mine, emb_rest, emb_other, vec, vec_other, meta)


def decode(codes):
    codes = codes.astype(jnp.float32)
    numbers = [codes[2 * index : 2 * index + 1] + codes[2 * index + 1 : 2 * index + 2] for index in range(6)]
    left, right, bottom, top, first, last = numbers
    right, top = right + MARGIN, top + MARGIN
    square = codes[15:16] + codes[14:15] + codes[13:14]
    norm = lax.rsqrt(square + EPSILON) * COS_SCALE
    area = (right - left) * (top - bottom)
    return [left, right, bottom, top, first * GAP_SCALE + BASE, last * GAP_SCALE, codes[12:13], norm, area]


def with_ones(vectors):
    shape = (CODE_ROWS, vectors.shape[1])
    tail = jnp.where(lax.broadcasted_iota(jnp.int32, shape, 0) == 0, 1.0, 0.0)
    return jnp.concatenate([vectors, tail.astype(jnp.bfloat16)], axis=0)


def weights_of(products, row, col, same):
    width = jnp.maximum(jnp.minimum(row(RIGHT), col(RIGHT)) - jnp.maximum(row(LEFT), col(LEFT)), 0.0)
    height = jnp.maximum(jnp.minimum(row(TOP), col(TOP)) - jnp.maximum(row(BOTTOM), col(BOTTOM)), 0.0)
    inter = width * height
    both = row(AREA) + col(AREA)
    share = (both + inter) * pltpu.reciprocal(both - inter, approx=True, full_range=False)
    gap = jnp.maximum(col(FIRST) - row(LAST), row(FIRST) - col(LAST))
    logit = products * row(NORM) * col(NORM)
    value = jnp.exp2(logit - jnp.maximum(gap, BASE)) * share
    barred = (row(CAMERA) == col(CAMERA)) & (gap < BARRED_BELOW)
    if same is not None:
        barred = barred & jnp.logical_not(same)
    return jnp.where(barred, 0.0, value)


def tile_kernel(blocks, turns, own_block, receivers, vecs, *refs):
    row_ref, col_refs = refs[0], refs[1 : 1 + blocks]
    row_out_ref, col_out_ref, field_ref, spread_ref = refs[1 + blocks : 5 + blocks]
    products, weights = [refs[at : at + 2] for at in (5 + blocks, 7 + blocks)]
    col_spread_ref, row_vec_ref = refs[9 + blocks :]
    size, rows = row_ref.shape
    features = size - vecs - CODE_ROWS
    vec_rows, code_rows = slice(features, features + vecs), slice(features + vecs, size)
    row_out_ref[...] = jnp.zeros_like(row_out_ref)

    def multiply(chunk, product_ref):
        col_ref, part, _ = chunk
        product_ref[...] = jnp.dot(row_ref[0:rows, :], col_ref[0:features, part], preferred_element_type=jnp.float32)

    def weigh(chunk, product_ref, weight_ref):
        col_ref, part, done = chunk
        for field, values in enumerate(decode(col_ref[code_rows, part])):
            col_spread_ref[field] = jnp.broadcast_to(values, (8, WIDE))
        for start in range(0, rows, GROUP):
            row_part = slice(start, start + GROUP)

            def row(field):
                return jnp.concatenate([spread_ref[field, row_part, :]] * (WIDE // LANES), axis=1)

            def col(field):
                return jnp.concatenate([col_spread_ref[field]] * (GROUP // 8), axis=0)

            same = None
            if own_block and done < rows:
                row_ids = lax.broadcasted_iota(jnp.int32, (GROUP, WIDE), 0) + (start - done)
                same = row_ids == lax.broadcasted_iota(jnp.int32, (GROUP, WIDE), 1)
            weight_ref[row_part, :] = weights_of(product_ref[row_part, :], row, col, same).astype(jnp.bfloat16)

    def total(chunk, weight_ref):
        col_ref, part, done = chunk
        row_out_ref[...] += dot_nt(with_ones(col_ref[vec_rows, part]), weight_ref[...])[0:OUT_ROWS]
        if not turns:
            col_out_ref[:, done : done + WIDE] = jnp.dot(
                row_vec_ref[...], weight_ref[...], preferred_element_type=jnp.float32
            )[0:OUT_ROWS]

    def pipeline(chunks):
        for step, chunk in enumerate(chunks):
            now, later = step % 2, (step + 1) % 2
            if step + 1 < len(chunks):
                multiply(chunks[step + 1], products[later])
            weigh(chunk, products[now], weights[now])
            if step > 0:
                total(chunks[step - 1], weights[later])
        total(chunks[-1], weights[(len(chunks) - 1) % 2])

    def compute():
        if turns:
            for number, pack_ref in enumerate(col_refs):
                part = pl.ds(number * rows, rows)
                col_out_ref[0:features, part] = pack_ref[0:rows, :].T
                col_out_ref[features:size, part] = pack_ref[features:size, :]
        sources = [col_out_ref] if turns else col_refs
        chunks = []
        for source in sources:
            for start in range(0, source.shape[1], WIDE):
                chunks.append((source, slice(start, start + WIDE), len(chunks) * WIDE))
        multiply(chunks[0], products[0])
        for field, values in enumerate(decode(row_ref[code_rows, :])):
            field_ref[field : field + 1, :] = values
        turned = field_ref[...].T
        for field in range(FIELDS):
            spread_ref[field] = jnp.broadcast_to(turned[:, field : field + 1], (rows, LANES))
        row_vec_ref[...] = with_ones(row_ref[vec_rows, :])
        pipeline(chunks)

    if receivers is None:
        compute()
        return
    pair = lax.axis_index("blk") // 2
    takes_part = functools.reduce(jnp.logical_or, [pair == one for one in receivers])

    @pl.when(takes_part)
    def _():
        compute()

    @pl.when(jnp.logical_not(takes_part))
    def _():
        col_out_ref[...] = jnp.zeros_like(col_out_ref)


def tile(row, columns, vecs, turns=False, own_block=False, receivers=None, last=False):
    size, rows = row.shape
    cols = len(columns) * rows if turns else sum(part.shape[1] for part in columns)
    second = jax.ShapeDtypeStruct((size, cols), jnp.bfloat16)
    if not turns:
        second = jax.ShapeDtypeStruct((OUT_ROWS, cols), jnp.float32)
    return pl.pallas_call(
        functools.partial(tile_kernel, len(columns), turns, own_block, receivers, vecs),
        out_shape=[jax.ShapeDtypeStruct((OUT_ROWS, rows), jnp.float32), second],
        in_specs=[VMEM_SPEC] * (1 + len(columns)),
        out_specs=[VMEM_SPEC] * 2,
        scratch_shapes=[
            pltpu.VMEM((LANES, rows), jnp.float32),
            pltpu.VMEM((FIELDS, rows, LANES), jnp.float32),
            pltpu.VMEM((rows, WIDE), jnp.float32),
            pltpu.VMEM((rows, WIDE), jnp.float32),
            pltpu.VMEM((rows, WIDE), jnp.bfloat16),
            pltpu.VMEM((rows, WIDE), jnp.bfloat16),
            pltpu.VMEM((FIELDS, 8, WIDE), jnp.float32),
            pltpu.VMEM((vecs + CODE_ROWS, rows), jnp.bfloat16),
        ],
        cost_estimate=pl.CostEstimate(flops=LAST_COST if last else COST, bytes_accessed=COST, transcendentals=0),
        compiler_params=params(),
        name="tile",
    )(row, *columns)


def image_kernel(*refs):
    parts, image_ref = refs[:-1], refs[-1]
    total = parts[0][...]
    for part in parts[1:]:
        total = total + part[...]
    vecs = image_ref.shape[0]
    image_ref[...] = total[0:vecs] / total[vecs : vecs + 1]


def image_of(parts, vecs):
    return pl.pallas_call(
        image_kernel,
        out_shape=jax.ShapeDtypeStruct((vecs, parts[0].shape[1]), jnp.float32),
        in_specs=[VMEM_SPEC] * len(parts),
        out_specs=VMEM_SPEC,
        compiler_params=params(),
        name="image",
    )(*parts)


def gram_kernel(image_ref, grams_ref):
    vecs, cols = image_ref.shape
    image = image_ref[...]
    padded = jnp.concatenate([image, jnp.zeros((LANES - vecs, cols), jnp.float32)], axis=0)
    gram = dot_nt(image, padded, lax.Precision.HIGHEST)
    packed = gram[0:8]
    for piece in range(1, vecs // 8):
        packed = packed + pltpu.roll(gram[8 * piece : 8 * piece + 8], piece * vecs, 1)
    for copy in range(grams_ref.shape[0]):
        grams_ref[copy] = packed


def grams_of(image, copies):
    return pl.pallas_call(
        gram_kernel,
        out_shape=jax.ShapeDtypeStruct((copies, 8, LANES), jnp.float32),
        in_specs=[VMEM_SPEC],
        out_specs=VMEM_SPEC,
        compiler_params=params(),
        name="gram",
    )(image)


def inverse_of(number):
    guess = pltpu.reciprocal(number, approx=True)
    guess = guess * (2.0 - number * guess)
    return guess * (2.0 - number * guess)


def basis_kernel(total_rows, grams_ref, mine_ref, other_ref, out_ref, inverse_ref):
    vecs, half = mine_ref.shape
    sub = lax.axis_index("sub")
    packed = jnp.sum(grams_ref[...], axis=0) / total_rows
    lane = lax.broadcasted_iota(jnp.int32, (vecs, LANES), 1)
    line = lax.broadcasted_iota(jnp.int32, (vecs, LANES), 0)
    pieces = [packed] + [pltpu.roll(packed, LANES - piece * vecs, 1) for piece in range(1, LANES // vecs)]
    matrix = jnp.where(lane < vecs, jnp.concatenate(pieces, axis=0), 0.0)
    matrix = jnp.where(lane == line + vecs, 1.0, matrix)
    for step in range(0, vecs, 2):
        left = jnp.broadcast_to(matrix[:, step : step + 1], (vecs, LANES))
        right = jnp.broadcast_to(matrix[:, step + 1 : step + 2], (vecs, LANES))
        upper, lower = matrix[step : step + 1, :], matrix[step + 1 : step + 2, :]
        across = right[step : step + 1, :]
        inverse = inverse_of(left[step : step + 1, :])
        factor = left[step + 1 : step + 2, :] * inverse
        lower = lower - factor * upper
        inverse_next = inverse_of(right[step + 1 : step + 2, :] - factor * across)
        first = left * inverse
        second = (right - first * across) * inverse_next
        reduced = matrix - first * upper - second * lower
        matrix = jnp.where(line > step + 1, reduced, jnp.where(line == step + 1, lower, matrix))
    pivots = jnp.sum(jnp.where(lane == line, matrix, 0.0), axis=1, keepdims=True)
    inverse_ref[...] = pltpu.roll(matrix / jnp.sqrt(pivots), LANES - vecs, 1)
    share = vecs // 2
    own_rows = inverse_ref[pl.ds(pl.multiple_of(sub * share, 8), share), :][:, 0:vecs]
    for ref, place in ((mine_ref, sub), (other_ref, 1 - sub)):
        out_ref[:, pl.ds(pl.multiple_of(place * half, LANES), half)] = jnp.dot(
            own_rows, ref[...], precision=lax.Precision.HIGHEST, preferred_element_type=jnp.float32
        )


def basis_of(grams, mine, other, total_rows):
    vecs, half = mine.shape
    return pl.pallas_call(
        functools.partial(basis_kernel, total_rows),
        out_shape=jax.ShapeDtypeStruct((vecs // 2, 2 * half), jnp.float32),
        in_specs=[VMEM_SPEC] * 3,
        out_specs=VMEM_SPEC,
        scratch_shapes=[pltpu.VMEM((vecs, LANES), jnp.float32)],
        compiler_params=params(),
        name="basis",
    )(grams, mine, other)


def exchanges(pairs):
    if pairs == 4:
        return [([(0, 2), (3, 1), (1, 0), (2, 3)], None), ([(2, 1), (0, 3)], [1, 3])]
    plans = []
    for distance in range(1, pairs // 2):
        plans.append(([((p + distance) % pairs, p) for p in range(pairs)], None))
    if pairs > 1:
        half = pairs // 2
        last = [(p, p + half) if p % 2 == 0 else (p + half, p) for p in range(half)]
        plans.append((last, sorted(taker for _, taker in last)))
    return plans


def block_moves(pair_moves):
    return [(2 * source + member, 2 * target + member) for source, target in pair_moves for member in range(2)]


def back(moves):
    return [(target, source) for source, target in moves]


def local(embeddings, vectors, boxes, spans, camera):
    rows = embeddings.shape[0]
    half = rows // 2
    vecs = 2 * vectors.shape[0]
    blocks = lax.axis_size("blk")
    swap = [(0, 1), (1, 0)]
    beside = [(block, block ^ 1) for block in range(blocks)]
    plans = [(block_moves(moves), takers) for moves, takers in exchanges(blocks // 2)]

    emb_other = lax.ppermute(embeddings, "sub", swap)
    vec_other = lax.ppermute(vectors, "sub", swap)
    meta = jnp.concatenate([boxes, spans, camera[None, :]], axis=0)
    sub = lax.axis_index("sub")
    halves = [lax.dynamic_slice_in_dim(embeddings, place * half, half, 0) for place in (sub, 1 - sub)]
    mine, rest = packs_of(*halves, emb_other, vectors, vec_other, meta)
    sent = [lax.ppermute(mine, "blk", moves) for moves, _ in plans]
    beside_mine = lax.ppermute(mine, "blk", beside)
    weigh = functools.partial(tile, vecs=vecs)
    own_sums, own = weigh(mine, [mine, rest], turns=True, own_block=True)
    own_sums, own, sent[:1] = lax.optimization_barrier((own_sums, own, sent[:1]))
    beside_mine, sent[:1] = lax.optimization_barrier((beside_mine, sent[:1]))
    cut = beside_mine.shape[0] // SWAPS // 16 * 16
    shares = [beside_mine[at * cut : (at + 1) * cut if at < SWAPS - 1 else None] for at in range(SWAPS)]
    beside_rest = jnp.concatenate([lax.ppermute(share, "sub", swap) for share in shares], axis=0)
    parts = [own_sums]
    if not plans:
        parts.append(weigh(mine, [beside_mine, beside_rest], turns=True)[0])
    for number, ((moves, takers), pack) in enumerate(zip(plans, sent)):
        last = number == len(plans) - 1
        if number == 0:
            own_lines, own_cols = weigh(pack, [own], receivers=takers)
            own_lines, own_cols, beside_rest = lax.optimization_barrier((own_lines, own_cols, beside_rest))
            beside_sums, next_to = weigh(mine, [beside_mine, beside_rest], turns=True)
            parts.append(beside_sums)
            next_lines, next_cols = weigh(pack, [next_to], receivers=takers)
        else:
            pack, own_cols, next_cols = lax.optimization_barrier((pack, own_cols, next_cols))
            next_lines, cols = weigh(pack, [next_to], receivers=takers)
            next_cols = next_cols + cols
            pack, next_cols, parts[-1] = lax.optimization_barrier((pack, next_cols, parts[-1]))
            own_lines, cols = weigh(pack, [own], receivers=takers, last=last)
            own_cols = own_cols + cols
        parts.append(lax.ppermute(own_lines + next_lines, "blk", back(moves)))
        if last:
            next_rest = lax.ppermute(next_cols[:, half:], "sub", swap)
            crossing = next_cols[:, :half] + next_rest
            parts.append(lax.ppermute(crossing, "blk", beside))
            own_cols, _ = lax.optimization_barrier((own_cols, crossing))
            parts += [own_cols[:, :half], lax.ppermute(own_cols[:, half:], "sub", swap)]
    image = image_of(parts, vecs)
    image_other = lax.ppermute(image, "sub", swap)
    grams = lax.all_to_all(grams_of(image, 2 * blocks), ("blk", "sub"), 0, 0, tiled=True)
    return basis_of(grams, image, image_other, blocks * rows)


def solution(mesh):
    placed = (
        P(("groups", "blk"), "sub"),
        P("sub", ("groups", "blk")),
        P(None, ("groups", "blk")),
        P(None, ("groups", "blk")),
        P(("groups", "blk")),
    )
    return jax.shard_map(
        local, mesh=mesh, in_specs=placed, out_specs=P("sub", ("groups", "blk")), check_vma=False
    )
```

```python
import functools
import math

import jax
import jax.numpy as jnp
from jax import lax
from jax.experimental import pallas as pl
from jax.experimental.pallas import tpu as pltpu
from jax.sharding import PartitionSpec as P

SHARPNESS = 10.0
HORIZON = 2000.0
MARGIN = 8.0
EPSILON = 1e-06

LOG2E = math.log2(math.e)
COS_SCALE = math.sqrt(SHARPNESS * LOG2E)
GAP_SCALE = LOG2E / HORIZON
BASE = SHARPNESS * LOG2E + 1.0
BARRED_BELOW = BASE - 0.5 * GAP_SCALE

FIELDS = 9
LEFT, RIGHT, BOTTOM, TOP, FIRST, LAST, CAMERA, NORM, AREA = range(FIELDS)
CODE_ROWS = 16
LANES = 128
CHUNK = 256
OUT_ROWS = 40
COST = 1
LAST_COST = 4 * 1024 * 1024 * 1024
WIDE = 512
GROUP = 16
SWAPS = 3
VMEM_LIMIT = 48 * 1024 * 1024

NT = (((1,), (1,)), ((), ()))
VMEM_SPEC = pl.BlockSpec(memory_space=pltpu.VMEM)


def params():
    return pltpu.CompilerParams(vmem_limit_bytes=VMEM_LIMIT)


def dot_nt(a, b, precision=None):
    return lax.dot_general(a, b, NT, precision=precision, preferred_element_type=jnp.float32)


def pack_rows(half, vecs):
    return half + vecs + CODE_ROWS


def pack_kernel(emb_mine_ref, emb_rest_ref, emb_other_ref, vec_ref, vec_other_ref, meta_ref, mine_ref, rest_ref, code_ref):
    sub = lax.axis_index("sub")
    half, width = emb_mine_ref.shape
    half_vecs = vec_other_ref.shape[0]
    ones = jnp.ones((8, width), jnp.bfloat16)
    for ref, emb_ref, place in ((mine_ref, emb_mine_ref, sub), (rest_ref, emb_rest_ref, 1 - sub)):
        first = pl.multiple_of(place * half, half)
        for start in range(0, half, CHUNK):
            part = pl.ds(first + start, CHUNK)
            codes = []

            def whole(number, low_bits):
                codes.append((number >> low_bits) << low_bits)
                codes.append(number & ((1 << low_bits) - 1))

            meta = meta_ref[:, part]
            for axis in range(2):
                whole(jnp.minimum(meta[axis : axis + 1], meta[axis + 2 : axis + 3]), 5)
                whole(jnp.maximum(meta[axis : axis + 1], meta[axis + 2 : axis + 3]), 5)
            whole(jnp.minimum(meta[4:5], meta[5:6]), 7)
            whole(jnp.maximum(meta[4:5], meta[5:6]), 7)
            codes.append(meta[6:7])
            codes = [code.astype(jnp.float32) for code in codes]
            rest = jnp.zeros((8, CHUNK), jnp.float32)
            for values in (emb_ref[start : start + CHUNK, :], emb_other_ref[part, :]):
                values = values.astype(jnp.float32)
                square = values * values
                high = square.astype(jnp.bfloat16)
                low = (square - high.astype(jnp.float32)).astype(jnp.bfloat16)
                rest = rest + (dot_nt(ones, high) + dot_nt(ones, low))
            rest = rest[0:1]
            for _ in range(3):
                piece = rest.astype(jnp.bfloat16).astype(jnp.float32)
                codes.append(piece)
                rest = rest - piece
            code_ref[:, start : start + CHUNK] = jnp.concatenate(codes, axis=0).astype(jnp.bfloat16)
        source = pl.ds(first, half)
        sides = (
            (emb_ref[...], vec_ref[:, source], sub),
            (emb_other_ref[source, :], vec_other_ref[:, source], 1 - sub),
        )
        for values, vectors, side in sides:
            ref[0:half, pl.ds(pl.multiple_of(side * width, width), width)] = values
            ref[pl.ds(pl.multiple_of(half + side * half_vecs, 16), half_vecs), :] = vectors
        first_code = half + 2 * half_vecs
        ref[first_code : first_code + CODE_ROWS, :] = code_ref[...]


def packs_of(emb_mine, emb_rest, emb_other, vec, vec_other, meta):
    half, width = emb_mine.shape
    features = 2 * width
    assert half == features
    size = pack_rows(half, 2 * vec_other.shape[0])
    return pl.pallas_call(
        pack_kernel,
        out_shape=[jax.ShapeDtypeStruct((size, features), jnp.bfloat16)] * 2,
        in_specs=[VMEM_SPEC] * 6,
        out_specs=[VMEM_SPEC] * 2,
        scratch_shapes=[pltpu.VMEM((CODE_ROWS, half), jnp.bfloat16)],
        compiler_params=params(),
        name="pack",
    )(emb_mine, emb_rest, emb_other, vec, vec_other, meta)


def decode(codes):
    codes = codes.astype(jnp.float32)
    numbers = [codes[2 * index : 2 * index + 1] + codes[2 * index + 1 : 2 * index + 2] for index in range(6)]
    left, right, bottom, top, first, last = numbers
    right, top = right + MARGIN, top + MARGIN
    square = codes[15:16] + codes[14:15] + codes[13:14]
    norm = lax.rsqrt(square + EPSILON) * COS_SCALE
    area = (right - left) * (top - bottom)
    return [left, right, bottom, top, first * GAP_SCALE + BASE, last * GAP_SCALE, codes[12:13], norm, area]


def with_ones(vectors):
    shape = (CODE_ROWS, vectors.shape[1])
    tail = jnp.where(lax.broadcasted_iota(jnp.int32, shape, 0) == 0, 1.0, 0.0)
    return jnp.concatenate([vectors, tail.astype(jnp.bfloat16)], axis=0)


def weights_of(products, row, col, same):
    width = jnp.maximum(jnp.minimum(row(RIGHT), col(RIGHT)) - jnp.maximum(row(LEFT), col(LEFT)), 0.0)
    height = jnp.maximum(jnp.minimum(row(TOP), col(TOP)) - jnp.maximum(row(BOTTOM), col(BOTTOM)), 0.0)
    inter = width * height
    both = row(AREA) + col(AREA)
    share = (both + inter) * pltpu.reciprocal(both - inter, approx=True, full_range=False)
    gap = jnp.maximum(col(FIRST) - row(LAST), row(FIRST) - col(LAST))
    logit = products * row(NORM) * col(NORM)
    value = jnp.exp2(logit - jnp.maximum(gap, BASE)) * share
    barred = (row(CAMERA) == col(CAMERA)) & (gap < BARRED_BELOW)
    if same is not None:
        barred = barred & jnp.logical_not(same)
    return jnp.where(barred, 0.0, value)


def tile_kernel(blocks, turns, own_block, receivers, vecs, *refs):
    row_ref, col_refs = refs[0], refs[1 : 1 + blocks]
    row_out_ref, col_out_ref, field_ref, spread_ref = refs[1 + blocks : 5 + blocks]
    products, weights = [refs[at : at + 2] for at in (5 + blocks, 7 + blocks)]
    col_spread_ref, row_vec_ref = refs[9 + blocks :]
    size, rows = row_ref.shape
    features = size - vecs - CODE_ROWS
    vec_rows, code_rows = slice(features, features + vecs), slice(features + vecs, size)
    row_out_ref[...] = jnp.zeros_like(row_out_ref)

    def multiply(chunk, product_ref):
        col_ref, part, _ = chunk
        product_ref[...] = jnp.dot(row_ref[0:rows, :], col_ref[0:features, part], preferred_element_type=jnp.float32)

    def weigh(chunk, product_ref, weight_ref):
        col_ref, part, done = chunk
        for field, values in enumerate(decode(col_ref[code_rows, part])):
            col_spread_ref[field] = jnp.broadcast_to(values, (8, WIDE))
        for start in range(0, rows, GROUP):
            row_part = slice(start, start + GROUP)

            def row(field):
                return jnp.concatenate([spread_ref[field, row_part, :]] * (WIDE // LANES), axis=1)

            def col(field):
                return jnp.concatenate([col_spread_ref[field]] * (GROUP // 8), axis=0)

            same = None
            if own_block and done < rows:
                row_ids = lax.broadcasted_iota(jnp.int32, (GROUP, WIDE), 0) + (start - done)
                same = row_ids == lax.broadcasted_iota(jnp.int32, (GROUP, WIDE), 1)
            weight_ref[row_part, :] = weights_of(product_ref[row_part, :], row, col, same).astype(jnp.bfloat16)

    def total(chunk, weight_ref):
        col_ref, part, done = chunk
        row_out_ref[...] += dot_nt(with_ones(col_ref[vec_rows, part]), weight_ref[...])[0:OUT_ROWS]
        if not turns:
            col_out_ref[:, done : done + WIDE] = jnp.dot(
                row_vec_ref[...], weight_ref[...], preferred_element_type=jnp.float32
            )[0:OUT_ROWS]

    def pipeline(chunks):
        multiply(chunks[0], products[0])
        for step, chunk in enumerate(chunks):
            now, later = step % 2, (step + 1) % 2
            if step + 1 < len(chunks):
                multiply(chunks[step + 1], products[later])
            weigh(chunk, products[now], weights[now])
            if step > 0:
                total(chunks[step - 1], weights[later])
        total(chunks[-1], weights[(len(chunks) - 1) % 2])

    def compute():
        for field, values in enumerate(decode(row_ref[code_rows, :])):
            field_ref[field : field + 1, :] = values
        turned = field_ref[...].T
        for field in range(FIELDS):
            spread_ref[field] = jnp.broadcast_to(turned[:, field : field + 1], (rows, LANES))
        row_vec_ref[...] = with_ones(row_ref[vec_rows, :])
        if turns:
            for number, pack_ref in enumerate(col_refs):
                part = pl.ds(number * rows, rows)
                col_out_ref[0:features, part] = pack_ref[0:rows, :].T
                col_out_ref[features:size, part] = pack_ref[features:size, :]
        sources = [col_out_ref] if turns else col_refs
        chunks = []
        for source in sources:
            for start in range(0, source.shape[1], WIDE):
                chunks.append((source, slice(start, start + WIDE), len(chunks) * WIDE))
        pipeline(chunks)

    if receivers is None:
        compute()
        return
    pair = lax.axis_index("blk") // 2
    takes_part = functools.reduce(jnp.logical_or, [pair == one for one in receivers])

    @pl.when(takes_part)
    def _():
        compute()

    @pl.when(jnp.logical_not(takes_part))
    def _():
        col_out_ref[...] = jnp.zeros_like(col_out_ref)


def tile(row, columns, vecs, turns=False, own_block=False, receivers=None, last=False):
    size, rows = row.shape
    cols = len(columns) * rows if turns else sum(part.shape[1] for part in columns)
    second = jax.ShapeDtypeStruct((size, cols), jnp.bfloat16)
    if not turns:
        second = jax.ShapeDtypeStruct((OUT_ROWS, cols), jnp.float32)
    return pl.pallas_call(
        functools.partial(tile_kernel, len(columns), turns, own_block, receivers, vecs),
        out_shape=[jax.ShapeDtypeStruct((OUT_ROWS, rows), jnp.float32), second],
        in_specs=[VMEM_SPEC] * (1 + len(columns)),
        out_specs=[VMEM_SPEC] * 2,
        scratch_shapes=[
            pltpu.VMEM((LANES, rows), jnp.float32),
            pltpu.VMEM((FIELDS, rows, LANES), jnp.float32),
            pltpu.VMEM((rows, WIDE), jnp.float32),
            pltpu.VMEM((rows, WIDE), jnp.float32),
            pltpu.VMEM((rows, WIDE), jnp.bfloat16),
            pltpu.VMEM((rows, WIDE), jnp.bfloat16),
            pltpu.VMEM((FIELDS, 8, WIDE), jnp.float32),
            pltpu.VMEM((vecs + CODE_ROWS, rows), jnp.bfloat16),
        ],
        cost_estimate=pl.CostEstimate(flops=LAST_COST if last else COST, bytes_accessed=COST, transcendentals=0),
        compiler_params=params(),
        name="tile",
    )(row, *columns)


def image_kernel(*refs):
    parts, image_ref, grams_ref = refs[:-2], refs[-2], refs[-1]
    total = parts[0][...]
    for part in parts[1:]:
        total = total + part[...]
    vecs, cols = image_ref.shape
    image = total[0:vecs] / total[vecs : vecs + 1]
    image_ref[...] = image
    padded = jnp.concatenate([image, jnp.zeros((LANES - vecs, cols), jnp.float32)], axis=0)
    gram = dot_nt(image, padded, lax.Precision.HIGHEST)
    packed = gram[0:8]
    for piece in range(1, vecs // 8):
        packed = packed + pltpu.roll(gram[8 * piece : 8 * piece + 8], piece * vecs, 1)
    for copy in range(grams_ref.shape[0]):
        grams_ref[copy] = packed


def image_of(parts, vecs, copies):
    return pl.pallas_call(
        image_kernel,
        out_shape=[
            jax.ShapeDtypeStruct((vecs, parts[0].shape[1]), jnp.float32),
            jax.ShapeDtypeStruct((copies, 8, LANES), jnp.float32),
        ],
        in_specs=[VMEM_SPEC] * len(parts),
        out_specs=[VMEM_SPEC] * 2,
        compiler_params=params(),
        name="image",
    )(*parts)


def inverse_of(number):
    guess = pltpu.reciprocal(number, approx=True)
    guess = guess * (2.0 - number * guess)
    return guess * (2.0 - number * guess)


def basis_kernel(total_rows, grams_ref, mine_ref, other_ref, out_ref, inverse_ref):
    vecs, half = mine_ref.shape
    sub = lax.axis_index("sub")
    packed = jnp.sum(grams_ref[...], axis=0) / total_rows
    lane = lax.broadcasted_iota(jnp.int32, (vecs, LANES), 1)
    line = lax.broadcasted_iota(jnp.int32, (vecs, LANES), 0)
    pieces = [packed] + [pltpu.roll(packed, LANES - piece * vecs, 1) for piece in range(1, LANES // vecs)]
    matrix = jnp.where(lane < vecs, jnp.concatenate(pieces, axis=0), 0.0)
    matrix = jnp.where(lane == line + vecs, 1.0, matrix)
    for step in range(0, vecs, 2):
        left = jnp.broadcast_to(matrix[:, step : step + 1], (vecs, LANES))
        right = jnp.broadcast_to(matrix[:, step + 1 : step + 2], (vecs, LANES))
        upper, lower = matrix[step : step + 1, :], matrix[step + 1 : step + 2, :]
        across = right[step : step + 1, :]
        inverse = inverse_of(left[step : step + 1, :])
        factor = left[step + 1 : step + 2, :] * inverse
        lower = lower - factor * upper
        inverse_next = inverse_of(right[step + 1 : step + 2, :] - factor * across)
        first = left * inverse
        second = (right - first * across) * inverse_next
        reduced = matrix - first * upper - second * lower
        matrix = jnp.where(line > step + 1, reduced, jnp.where(line == step + 1, lower, matrix))
    pivots = jnp.sum(jnp.where(lane == line, matrix, 0.0), axis=1, keepdims=True)
    inverse_ref[...] = pltpu.roll(matrix / jnp.sqrt(pivots), LANES - vecs, 1)
    share = vecs // 2
    own_rows = inverse_ref[pl.ds(pl.multiple_of(sub * share, 8), share), :][:, 0:vecs]
    for ref, place in ((mine_ref, sub), (other_ref, 1 - sub)):
        out_ref[:, pl.ds(pl.multiple_of(place * half, LANES), half)] = jnp.dot(
            own_rows, ref[...], precision=lax.Precision.HIGHEST, preferred_element_type=jnp.float32
        )


def basis_of(grams, mine, other, total_rows):
    vecs, half = mine.shape
    return pl.pallas_call(
        functools.partial(basis_kernel, total_rows),
        out_shape=jax.ShapeDtypeStruct((vecs // 2, 2 * half), jnp.float32),
        in_specs=[VMEM_SPEC] * 3,
        out_specs=VMEM_SPEC,
        scratch_shapes=[pltpu.VMEM((vecs, LANES), jnp.float32)],
        compiler_params=params(),
        name="basis",
    )(grams, mine, other)


def exchanges(pairs):
    if pairs == 4:
        return [([(0, 2), (3, 1), (1, 0), (2, 3)], None), ([(2, 1), (0, 3)], [1, 3])]
    plans = []
    for distance in range(1, pairs // 2):
        plans.append(([((p + distance) % pairs, p) for p in range(pairs)], None))
    if pairs > 1:
        half = pairs // 2
        last = [(p, p + half) if p % 2 == 0 else (p + half, p) for p in range(half)]
        plans.append((last, sorted(taker for _, taker in last)))
    return plans


def block_moves(pair_moves):
    return [(2 * source + member, 2 * target + member) for source, target in pair_moves for member in range(2)]


def back(moves):
    return [(target, source) for source, target in moves]


def local(embeddings, vectors, boxes, spans, camera):
    rows = embeddings.shape[0]
    half = rows // 2
    vecs = 2 * vectors.shape[0]
    blocks = lax.axis_size("blk")
    swap = [(0, 1), (1, 0)]
    beside = [(block, block ^ 1) for block in range(blocks)]
    plans = [(block_moves(moves), takers) for moves, takers in exchanges(blocks // 2)]

    emb_other = lax.ppermute(embeddings, "sub", swap)
    vec_other = lax.ppermute(vectors, "sub", swap)
    meta = jnp.concatenate([boxes, spans, camera[None, :]], axis=0)
    sub = lax.axis_index("sub")
    halves = [lax.dynamic_slice_in_dim(embeddings, place * half, half, 0) for place in (sub, 1 - sub)]
    mine, rest = packs_of(*halves, emb_other, vectors, vec_other, meta)
    sent = [lax.ppermute(mine, "blk", moves) for moves, _ in plans]
    beside_mine = lax.ppermute(mine, "blk", beside)
    weigh = functools.partial(tile, vecs=vecs)
    own_sums, own = weigh(mine, [mine, rest], turns=True, own_block=True)
    own_sums, own, sent[:1] = lax.optimization_barrier((own_sums, own, sent[:1]))
    beside_mine, sent[:1] = lax.optimization_barrier((beside_mine, sent[:1]))
    cut = beside_mine.shape[0] // SWAPS // 16 * 16
    shares = [beside_mine[at * cut : (at + 1) * cut if at < SWAPS - 1 else None] for at in range(SWAPS)]
    beside_rest = jnp.concatenate([lax.ppermute(share, "sub", swap) for share in shares], axis=0)
    parts = [own_sums]
    if not plans:
        parts.append(weigh(mine, [beside_mine, beside_rest], turns=True)[0])
    for number, ((moves, takers), pack) in enumerate(zip(plans, sent)):
        last = number == len(plans) - 1
        if number == 0:
            own_lines, own_cols = weigh(pack, [own], receivers=takers)
            own_lines, own_cols, beside_rest = lax.optimization_barrier((own_lines, own_cols, beside_rest))
            beside_sums, next_to = weigh(mine, [beside_mine, beside_rest], turns=True)
            parts.append(beside_sums)
            next_lines, next_cols = weigh(pack, [next_to], receivers=takers)
        else:
            pack, own_cols, next_cols = lax.optimization_barrier((pack, own_cols, next_cols))
            next_lines, cols = weigh(pack, [next_to], receivers=takers)
            next_cols = next_cols + cols
            pack, next_cols, parts[-1] = lax.optimization_barrier((pack, next_cols, parts[-1]))
            own_lines, cols = weigh(pack, [own], receivers=takers, last=last)
            own_cols = own_cols + cols
        parts.append(lax.ppermute(own_lines + next_lines, "blk", back(moves)))
        if last:
            next_rest = lax.ppermute(next_cols[:, half:], "sub", swap)
            crossing = next_cols[:, :half] + next_rest
            parts.append(lax.ppermute(crossing, "blk", beside))
            own_cols, _ = lax.optimization_barrier((own_cols, crossing))
            parts += [own_cols[:, :half], lax.ppermute(own_cols[:, half:], "sub", swap)]
    image, copies = image_of(parts, vecs, 2 * blocks)
    image_other = lax.ppermute(image, "sub", swap)
    grams = lax.all_to_all(copies, ("blk", "sub"), 0, 0, tiled=True)
    return basis_of(grams, image, image_other, blocks * rows)


def solution(mesh):
    placed = (
        P(("groups", "blk"), "sub"),
        P("sub", ("groups", "blk")),
        P(None, ("groups", "blk")),
        P(None, ("groups", "blk")),
        P(("groups", "blk")),
    )
    return jax.shard_map(
        local, mesh=mesh, in_specs=placed, out_specs=P("sub", ("groups", "blk")), check_vma=False
    )
```
